32 devices in a mesh: seq: 8 (over z, y), head: 4 (over x, core).
Axes of the slice: x: 2, y: 2, z: 4, core: 2. Of those that a mesh axis runs over, the one named last changes fastest.
Arguments:
- tokens: bfloat16 [8192, 2048], P('seq', 'head'), may hold values from -20 to 20
- w_query: bfloat16 [2048, 2048], P(None, 'head'), may hold values from -1 to 1
- w_key: bfloat16 [2048, 2048], P(None, 'head'), may hold values from -1 to 1
- w_value: bfloat16 [2048, 2048], P(None, 'head'), may hold values from -0.125 to 0.125
- w_out: bfloat16 [2048, 2048], P('head'), may hold values from -0.125 to 0.125
Outputs:
- attended: bfloat16 [8192, 2048], P(('seq', 'head'))
The draws below stay inside these ranges and needn't reach their ends.
All inputs are finite; a program needn't handle non-finite values.
Results may differ from the reference program's by a relative error of at most 0.04.
Values may be sent and summed in bfloat16 or wider, within the bound.
No kernel may reach another device: no remote copies, remote signals or barrier semaphores. Data moves between devices by JAX's collectives and lax.ppermute only.
A program may use at most 128 MiB of HBM per device.

```python
import math
import jax
import jax.numpy as jnp
from jax import lax

D = 2048
H = 16
DH = 128
STRIDE = 256
TOKENS = 8192
ROWS = 32
N_HEAD = 4


def draw_tokens(key, part):
    drawn = jax.random.normal(jax.random.fold_in(key, 1), (TOKENS, D), jnp.float32)
    return jnp.clip(drawn, -6.0, 6.0).astype(jnp.bfloat16)


def paired_normals(key):
    first = jnp.clip(jax.random.normal(jax.random.fold_in(key, 11), (D, D), jnp.float32), -6.0, 6.0)
    second = jnp.clip(jax.random.normal(jax.random.fold_in(key, 12), (D, D), jnp.float32), -6.0, 6.0)
    return (first, second)


def draw_w_query(key, part):
    first, second = paired_normals(key)
    return jnp.clip(first * (1.6 / math.sqrt(D)), -0.2, 0.2).astype(jnp.bfloat16)


def draw_w_key(key, part):
    first, second = paired_normals(key)
    blended = second
    return jnp.clip(blended * (1.6 / math.sqrt(D)), -0.3, 0.3).astype(jnp.bfloat16)


def steps_of(stream_key, shape, shards, low, top_value):
    level, own = 1.0, jax.random.fold_in(stream_key, 6)
    for dim, parts in shards:
        steps = jnp.exp(jax.random.uniform(jax.random.fold_in(own, dim), (parts,), jnp.float32, low / len(shards), top_value / len(shards)))
        level = level * jnp.repeat(steps, shape[dim] // parts).reshape([-1 if axis == dim else 1 for axis in range(len(shape))])
    return level


def noise(rng, extent, width, bound, cuts=(), kind=jnp.bfloat16):
    entries = width * jax.random.normal(rng, extent, jnp.float32)
    if cuts:
        entries = entries * steps_of(rng, extent, cuts, -0.22, 0.18)
    return jnp.clip(entries, -bound, bound).astype(kind)


def setup_inputs(seed: int = 0) -> dict:
    key_of = jax.random.split(jax.random.key(seed), 6)
    return {
        "tokens": draw_tokens(jax.random.fold_in(key_of[5], 71), 0),
        "w_query": draw_w_query(jax.random.fold_in(key_of[5], 71), 0),
        "w_key": draw_w_key(jax.random.fold_in(key_of[5], 71), 0),
        "w_value": noise(key_of[3], (D, D), D ** -0.5, 0.125, ((1, 4),)),
        "w_out": noise(key_of[4], (D, D), D ** -0.5, 0.125, ((0, 4),)),
    }


def local_part(query_one, key_one, value_one):
    score_scale = DH ** -0.5
    query_rows = query_one.reshape(ROWS, STRIDE, DH).astype(jnp.float32)
    key_rows = key_one.reshape(ROWS, STRIDE, DH)
    value_rows = value_one.reshape(ROWS, STRIDE, DH)
    padding = jnp.zeros((1, STRIDE, DH), key_one.dtype)
    key_window = jnp.concatenate([jnp.concatenate([padding, key_rows[:-1]], 0), key_rows], 1).astype(jnp.float32)
    value_window = jnp.concatenate([jnp.concatenate([padding, value_rows[:-1]], 0), value_rows], 1).astype(jnp.float32)
    scores = jnp.einsum('rtd,rud->rtu', query_rows, key_window) * score_scale
    query_index = jnp.arange(STRIDE)[None, :, None]
    key_index = jnp.arange(2 * STRIDE)[None, None, :]
    row_index = jnp.arange(ROWS)[:, None, None]
    allowed = (key_index > query_index) & (key_index <= query_index + STRIDE) & (row_index * STRIDE + key_index - STRIDE >= 0)
    top_score = jnp.max(jnp.where(allowed, scores, -1e30), axis=-1)
    prob_weights = jnp.where(allowed, jnp.exp(scores - top_score[..., None]), 0.0)
    total_weight = jnp.sum(prob_weights, axis=-1)
    rounded = prob_weights.astype(jnp.bfloat16).astype(jnp.float32)
    result = jnp.einsum('rtu,rud->rtd', rounded, value_window)
    return result.reshape(TOKENS, DH), top_score.reshape(TOKENS), total_weight.reshape(TOKENS)


def column_part(query_one, key_one, value_one):
    score_scale = DH ** -0.5
    query_rows = query_one.reshape(ROWS, STRIDE, DH).astype(jnp.float32)
    key_rows = key_one.reshape(ROWS, STRIDE, DH).astype(jnp.float32)
    value_rows = value_one.reshape(ROWS, STRIDE, DH).astype(jnp.float32)
    scores = jnp.einsum('rcd,scd->crs', query_rows, key_rows) * score_scale
    allowed = jnp.arange(ROWS)[None, :, None] > jnp.arange(ROWS)[None, None, :]
    top_score = jnp.max(jnp.where(allowed, scores, -1e30), axis=-1)
    prob_weights = jnp.where(allowed, jnp.exp(scores - top_score[..., None]), 0.0)
    total_weight = jnp.sum(prob_weights, axis=-1)
    rounded = prob_weights.astype(jnp.bfloat16).astype(jnp.float32)
    summed = jnp.einsum('crs,scd->rcd', rounded, value_rows)
    result = (summed / jnp.maximum(total_weight.T, 1.0)[..., None]).astype(jnp.bfloat16)
    return result.reshape(TOKENS, DH), top_score.T.reshape(TOKENS), total_weight.T.reshape(TOKENS)


def attend_head(pieces):
    query_one, key_one, value_one = pieces
    local_out, local_top, local_total = local_part(query_one, key_one, value_one)
    column_out, column_top, column_total = column_part(query_one, key_one, value_one)
    top_score = jnp.maximum(local_top, column_top)
    local_weight = jnp.exp(local_top - top_score)
    column_weight = column_total * jnp.exp(column_top - top_score)
    denominator = local_total * local_weight + column_weight
    mixed = (local_out * local_weight[:, None] + column_out.astype(jnp.float32) * column_weight[:, None]) / denominator[:, None]
    return mixed.astype(jnp.bfloat16)


def reference(tokens, w_query, w_key, w_value, w_out):
    query = jnp.dot(tokens, w_query, preferred_element_type=jnp.float32).astype(jnp.bfloat16)
    key_all = jnp.dot(tokens, w_key, preferred_element_type=jnp.float32).astype(jnp.bfloat16)
    value = jnp.dot(tokens, w_value, preferred_element_type=jnp.float32).astype(jnp.bfloat16)
    query_heads = query.reshape(TOKENS, H, DH).transpose(1, 0, 2)
    key_heads = key_all.reshape(TOKENS, H, DH).transpose(1, 0, 2)
    value_heads = value.reshape(TOKENS, H, DH).transpose(1, 0, 2)
    mixed = lax.map(attend_head, (query_heads, key_heads, value_heads))
    mixed = mixed.transpose(1, 0, 2).reshape(TOKENS, D)
    group_width = D // N_HEAD
    running = jnp.zeros((TOKENS, D), jnp.float32)
    for group in range(N_HEAD):
        group_term = jnp.dot(mixed[:, group * group_width:(group + 1) * group_width], w_out[group * group_width:(group + 1) * group_width], preferred_element_type=jnp.float32).astype(jnp.bfloat16)
        group_term = lax.optimization_barrier(group_term)
        running = running + group_term.astype(jnp.float32)
    return running.astype(jnp.bfloat16)
```

```python
import functools

import jax
import jax.numpy as jnp
from jax import lax
from jax.experimental import pallas as pl
from jax.experimental.pallas import tpu as pltpu
from jax.sharding import PartitionSpec as P

DH = 128
STRIDE = 256
HEADS = 4
ROWS = 4
SUB = 8
CHUNKS = 2
SCALE2 = DH ** (-0.5) * 1.4426950408889634
FLOOR = -1e29
MIB = 1024 * 1024
F32 = jnp.float32
BF16 = jnp.bfloat16


def params(mib, **kw):
    return pltpu.CompilerParams(vmem_limit_bytes=mib * MIB, **kw)


def cost(flops, moved, exps=0):
    return pl.CostEstimate(flops=flops, bytes_accessed=moved, transcendentals=exps)


def dot(a, b):
    return jnp.dot(a, b, preferred_element_type=F32)


def dot_t(a, b):
    return lax.dot_general(a, b, (((1,), (1,)), ((), ())), preferred_element_type=F32)


def pack_kernel(tok_ref, *out_refs):
    owners = out_refs[0].shape[0]
    per_owner = STRIDE // owners
    groups = per_owner // SUB
    per_chunk = groups // len(out_refs)
    for d in range(owners):
        rows = [
            tok_ref[r * STRIDE + d * per_owner : r * STRIDE + (d + 1) * per_owner, :].astype(F32)
            for r in range(ROWS)
        ]
        for g in range(groups):
            piece = jnp.concatenate([x[g * SUB : (g + 1) * SUB] for x in rows], 0)
            at = (g % per_chunk) * ROWS * SUB
            out_refs[g // per_chunk][d, at : at + ROWS * SUB, :] = piece.astype(BF16)


def pack(tokens, owners):
    width = tokens.shape[1]
    message = tokens.shape[0] // owners // CHUNKS
    return pl.pallas_call(
        pack_kernel,
        out_shape=[jax.ShapeDtypeStruct((owners, message, width), BF16)] * CHUNKS,
        compiler_params=params(16),
        cost_estimate=cost(0, 2 * tokens.size * 2),
        name="pack_tokens",
    )(tokens)


def project_kernel(order_ref, x0, x1, x2, x3, wq, wk, wv, q_ref, k_ref, v_ref, halo_ref):
    for n, (w_ref, out_ref) in enumerate(((wq, q_ref), (wk, k_ref), (wv, v_ref))):
        total = None
        for p, x_ref in enumerate((x0, x1, x2, x3)):
            rows = pl.ds(pl.multiple_of(order_ref[p] * 512, 512), 512)
            term = dot(x_ref[...], w_ref[rows, :])
            total = term if total is None else total + term
        total = total.astype(BF16)
        out_ref[...] = total
        if n:
            halo_ref[(n - 1) * STRIDE : n * STRIDE, :] = total[-STRIDE:]


def project(order, pieces, weights):
    rows, width = pieces[0].shape
    tile = 512
    full = lambda m, s: (0, 0)
    tiled = lambda m, s: (m, 0)
    return pl.pallas_call(
        project_kernel,
        grid_spec=pltpu.PrefetchScalarGridSpec(
            num_scalar_prefetch=1,
            grid=(rows // tile,),
            in_specs=[pl.BlockSpec((tile, width), tiled)] * 4
            + [pl.BlockSpec(weights[0].shape, full)] * 3,
            out_specs=[pl.BlockSpec((tile, width), tiled)] * 3
            + [pl.BlockSpec((2 * STRIDE, width), full)],
        ),
        out_shape=[jax.ShapeDtypeStruct((rows, width), BF16)] * 3
        + [jax.ShapeDtypeStruct((2 * STRIDE, width), BF16)],
        compiler_params=params(32),
        cost_estimate=cost(2 * rows * 2048 * 3 * width, 14 * MIB),
        name="project_block",
    )(order, *pieces, *weights)


def local_kernel(pos_ref, q_ref, k_ref, v_ref, kp_ref, vp_ref, halo_ref, out_ref, lse_ref):
    r = pl.program_id(0)
    first = r == 0
    no_prev = jnp.logical_and(first, pos_ref[0] == 0)
    t = lax.broadcasted_iota(jnp.int32, (STRIDE, STRIDE), 0)
    u = lax.broadcasted_iota(jnp.int32, (STRIDE, STRIDE), 1)
    current = u <= t
    lane = lax.broadcasted_iota(jnp.int32, (STRIDE, 128), 1)
    low = jnp.where(no_prev, -1e30, 0.0).astype(F32)
    lses = jnp.zeros((STRIDE, 128), F32)
    for h in range(HEADS):
        cols = slice(h * DH, (h + 1) * DH)
        q = q_ref[:, cols]
        k_prev = jnp.where(first, halo_ref[:STRIDE, cols], kp_ref[:, cols])
        v_prev = jnp.where(first, halo_ref[STRIDE:, cols], vp_ref[:, cols])
        s = jnp.where(current, dot_t(q, k_ref[:, cols]), dot_t(q, k_prev) + low)
        m = jnp.max(s, -1, keepdims=True)
        p = jnp.exp2((s - m) * SCALE2)
        total = jnp.sum(p, -1, keepdims=True)
        p_now = jnp.where(current, p, 0.0).astype(BF16)
        p_prev = jnp.where(current, 0.0, p).astype(BF16)
        o = dot(p_now, v_ref[:, cols]) + dot(p_prev, v_prev)
        out_ref[:, cols] = o / total
        lses = jnp.where(lane == h, m * SCALE2 + jnp.log2(total), lses)
    lse_ref[...] = lses


def local_part(pos, q, k, v, halo):
    rows, width = q.shape
    tile = lambda r, s: (r, 0)
    back = lambda r, s: (jnp.maximum(r - 1, 0), 0)
    block = (STRIDE, width)
    return pl.pallas_call(
        local_kernel,
        grid_spec=pltpu.PrefetchScalarGridSpec(
            num_scalar_prefetch=1,
            grid=(rows // STRIDE,),
            in_specs=[pl.BlockSpec(block, tile)] * 3
            + [pl.BlockSpec(block, back)] * 2
            + [pl.BlockSpec((2 * STRIDE, width), lambda r, s: (0, 0))],
            out_specs=[pl.BlockSpec(block, tile), pl.BlockSpec((STRIDE, 128), tile)],
        ),
        out_shape=[
            jax.ShapeDtypeStruct((rows, width), F32),
            jax.ShapeDtypeStruct((rows, 128), F32),
        ],
        compiler_params=params(24),
        cost_estimate=cost(8 * rows * STRIDE * width, 8 * MIB, rows * STRIDE * HEADS),
        name="local_part",
    )(pos, q, k, v, k, v, halo)


def column_kernel(order_ref, x0, x1, x2, x3, wq, wk, wv, out_ref, aq, ak, av):
    step = pl.program_id(0)
    owners, message, width = x0.shape
    groups = message // (ROWS * SUB)
    for p, x_ref in enumerate((x0, x1, x2, x3)):

        @pl.when(step == p)
        def _(p=p, x_ref=x_ref):
            x = x_ref[...].reshape(owners * message, width)
            for w_ref, acc in ((wq, aq), (wk, ak), (wv, av)):
                term = dot(x, w_ref[...]).reshape(acc.shape)
                acc[...] = term if p == 0 else acc[...] + term

    @pl.when(step == 3)
    def _():
        size = owners * ROWS * SUB
        i = lax.broadcasted_iota(jnp.int32, (size, size), 0)
        j = lax.broadcasted_iota(jnp.int32, (size, size), 1)
        earlier = jnp.logical_and(i % SUB == j % SUB, i > j)
        part = ROWS * SUB
        lane = lax.broadcasted_iota(jnp.int32, (part, 128), 1)
        stats = []
        for g in range(groups):
            at = slice(g * part, (g + 1) * part)
            stat = jnp.zeros((part, 128), F32)
            for h in range(HEADS):
                cols = slice(h * DH, (h + 1) * DH)
                q, k, v = (a[:, at, cols].reshape(size, DH).astype(BF16) for a in (aq, ak, av))
                s = jnp.where(earlier, dot_t(q, k), -1e30)
                m = jnp.maximum(jnp.max(s, -1, keepdims=True), FLOOR)
                e = jnp.exp2((s - m) * SCALE2)
                total = jnp.maximum(jnp.sum(e, -1, keepdims=True), 1.0)
                o = dot(e.astype(BF16), v) / total
                rows = slice(h * message + g * part, h * message + (g + 1) * part)
                out_ref[:, rows, :] = o.astype(BF16).reshape(owners, part, DH)
                lse = (m * SCALE2 + jnp.log2(total)).reshape(owners, part, 1)
                for d in range(owners):
                    mine = jnp.logical_and(lane // 8 == d, lane % 4 == h)
                    stat = jnp.where(mine, lse[d], stat)
            stats.append(stat)
        if message < 128:
            stats.append(jnp.zeros((128 - message, 128), F32))
        turned = jnp.concatenate(stats, 0).T
        upper = lax.broadcasted_iota(jnp.int32, (8, 128), 0) < 4
        for d in range(owners):
            x = turned[8 * d : 8 * d + 8]
            hi = x.astype(BF16).astype(F32)
            mid = (x - hi).astype(BF16).astype(F32)
            lo = x - hi - mid
            tail = jnp.concatenate([jnp.where(upper, hi, lo), jnp.where(upper, mid, 0.0)], 0)
            out_ref[d, HEADS * message : HEADS * message + 16, :] = tail.astype(BF16)


def column_part(order, pieces, weights):
    owners, message, width = pieces[0].shape
    rows_out = HEADS * message + 16
    whole = lambda p, s: (0, 0, 0)
    tokens = owners * message
    return pl.pallas_call(
        column_kernel,
        grid_spec=pltpu.PrefetchScalarGridSpec(
            num_scalar_prefetch=1,
            grid=(4,),
            in_specs=[pl.BlockSpec(pieces[0].shape, whole)] * 4
            + [pl.BlockSpec((512, width), lambda p, s: (s[p], 0))] * 3,
            out_specs=pl.BlockSpec((owners, rows_out, DH), whole),
            scratch_shapes=[pltpu.VMEM((owners, message, width), F32)] * 3,
        ),
        out_shape=jax.ShapeDtypeStruct((owners, rows_out, DH), BF16),
        compiler_params=params(32),
        cost_estimate=cost(2 * tokens * 2048 * 3 * width, 10 * MIB, tokens * 256 * HEADS),
        name="column_part",
    )(order, *pieces, *weights)


def mix_kernel(chunk, pos_ref, col_ref, loc_ref, lse_ref, own_ref, send_ref, mixed):
    owners = col_ref.shape[0]
    message = (col_ref.shape[1] - 16) // HEADS
    groups = message // (ROWS * SUB)
    per_owner = STRIDE // owners
    base = HEADS * message
    tiles = []
    for d in range(owners):
        tail = col_ref[d, base : base + 16, :].astype(F32)
        tiles.append(tail[:8] + tail[8:])
    tiles.append(jnp.zeros((128 - 8 * owners, 128), F32))
    turned = jnp.concatenate(tiles, 0).T[:message]
    for d in range(owners):
        spots = [
            r * STRIDE + d * per_owner + (chunk * groups + g) * SUB
            for g in range(groups)
            for r in range(ROWS)
        ]
        local_lse = jnp.concatenate([lse_ref[s : s + SUB, :] for s in spots], 0)
        for h in range(HEADS):
            cols = slice(h * DH, (h + 1) * DH)
            col = col_ref[d, h * message : (h + 1) * message, :].astype(F32)
            loc = jnp.concatenate([loc_ref[s : s + SUB, cols] for s in spots], 0)
            at = 8 * d + h
            col_lse = turned[:, at : at + 1] + turned[:, at + 4 : at + 5]
            loc_lse = local_lse[:, h : h + 1]
            top = jnp.maximum(col_lse, loc_lse)
            w_col = jnp.exp2(col_lse - top)
            w_loc = jnp.exp2(loc_lse - top)
            both = (loc * w_loc + col * w_col) / (w_loc + w_col)
            for r in range(ROWS):
                piece = jnp.concatenate(
                    [both[(g * ROWS + r) * SUB : (g * ROWS + r + 1) * SUB] for g in range(groups)], 0
                )
                span = groups * SUB
                mixed[r, d * span : (d + 1) * span, cols] = piece.astype(BF16)
    core = pos_ref[1]
    for x in range(2):
        own_ref[x] = mixed[2 * x + core]
        send_ref[x] = mixed[2 * x + 1 - core]


def mix(pos, chunk, column, local, lse):
    owners = column.shape[0]
    message = (column.shape[1] - 16) // HEADS
    tokens = owners * message // ROWS
    width = local.shape[1]
    vmem = pl.BlockSpec(memory_space=pltpu.VMEM)
    return pl.pallas_call(
        functools.partial(mix_kernel, chunk),
        in_specs=[pl.BlockSpec(memory_space=pltpu.SMEM), vmem, vmem, vmem],
        out_specs=[vmem, vmem],
        out_shape=[jax.ShapeDtypeStruct((2, tokens, width), BF16)] * 2,
        scratch_shapes=[pltpu.VMEM((ROWS, tokens, width), BF16)],
        compiler_params=params(16),
        cost_estimate=cost(8 * tokens * ROWS * width, 4 * MIB),
        name="mix",
    )(pos, column, local, lse)


def out_kernel(which_ref, a_ref, b_ref, wa_ref, wb_ref, out_ref):
    total = dot(a_ref[0], wa_ref[...]) + dot(b_ref[0], wb_ref[...])
    out_ref[...] = total.astype(out_ref.dtype)


def out_project(which, own, other, w_own, w_other, dtype):
    _, tokens, width = own.shape
    columns = w_own.shape[1]
    tile = 512
    rows = pl.BlockSpec((1, tokens, width), lambda n, s: (s[0], 0, 0))
    cols = pl.BlockSpec((width, tile), lambda n, s: (0, n))
    return pl.pallas_call(
        out_kernel,
        grid_spec=pltpu.PrefetchScalarGridSpec(
            num_scalar_prefetch=1,
            grid=(columns // tile,),
            in_specs=[rows, rows, cols, cols],
            out_specs=pl.BlockSpec((tokens, tile), lambda n, s: (0, n)),
        ),
        out_shape=jax.ShapeDtypeStruct((tokens, columns), dtype),
        compiler_params=params(16),
        cost_estimate=cost(4 * tokens * width * columns, 5 * MIB),
        name="out_project",
    )(which, own, other, w_own, w_other)


def join_kernel(*refs):
    out_ref = refs[-1]
    chunks = (len(refs) - 1) // 2
    tokens = refs[0].shape[0]
    owners = STRIDE // 32
    span = tokens // owners
    for i in range(chunks):
        keep, got = refs[2 * i], refs[2 * i + 1]
        for d in range(owners):
            rows = slice(d * span, (d + 1) * span)
            at = (d * chunks + i) * span
            total = keep[rows, :] + got[rows, :].astype(F32)
            out_ref[at : at + span, :] = total.astype(BF16)


def join(pairs):
    tokens, columns = pairs[0][0].shape
    tile = 512
    spec = pl.BlockSpec((tokens, tile), lambda n: (0, n))
    return pl.pallas_call(
        join_kernel,
        grid=(columns // tile,),
        in_specs=[spec] * (2 * len(pairs)),
        out_specs=pl.BlockSpec((STRIDE, tile), lambda n: (0, n)),
        out_shape=jax.ShapeDtypeStruct((STRIDE, columns), BF16),
        compiler_params=params(16),
        cost_estimate=cost(STRIDE * columns, 4 * MIB),
        name="join",
    )(*[x for pair in pairs for x in pair])


def swap(value, distance):
    return lax.ppermute(value, "head", [(i, i ^ distance) for i in range(4)])


def exchange(value):
    return lax.all_to_all(value, "seq", split_axis=0, concat_axis=0, tiled=True)


def gather(own):
    far = swap(own, 2)
    return own, swap(own, 1), far, swap(far, 1)


def chunked(tokens, w_query, w_key, w_value, w_out):
    owners = lax.axis_size("seq")
    head = lax.axis_index("head")
    block = lax.axis_index("seq")
    weights = (w_query, w_key, w_value)
    order = jnp.bitwise_xor(jnp.arange(4, dtype=jnp.int32), head.astype(jnp.int32))
    pos = jnp.stack([block, head % 2]).astype(jnp.int32)
    side = (head // 2).astype(jnp.int32).reshape(1)

    messages = pack(tokens, owners)
    block_pieces = gather(tokens)
    w_other = swap(w_out, 1)
    classes = [exchange(m) for m in messages]
    q, k, v, halo = project(order, block_pieces, weights)
    peers = owners
    halo = lax.ppermute(halo, "seq", [(i, i + 1) for i in range(peers - 1)])
    local, lse = local_part(pos, q, k, v, halo)
    columns = [exchange(column_part(order, gather(c), weights)) for c in classes]
    pairs = []
    for i, column in enumerate(columns):
        own, send = mix(pos, i, column, local, lse)
        other = swap(send, 1)
        out = out_project(1 - side, own, other, w_out, w_other, BF16)
        got = swap(out, 2)
        keep = out_project(side, own, other, w_out, w_other, F32)
        pairs.append((keep, got))
    return join(pairs)


def from_behind(value, axis, by):
    peers = lax.axis_size(axis)
    pairs = [(i, i + by) for i in range(peers) if 0 <= i + by < peers]
    return lax.ppermute(value, axis, pairs)


def general(tokens, w_query, w_key, w_value, w_out):
    tok_rows = tokens.shape[0]
    head_width = w_query.shape[1]
    head_count = head_width // DH
    score_scale = DH ** (-0.5)
    shard_piece = lax.all_gather(tokens, "head", axis=1, tiled=True)
    query_full, key_full, value_full = tuple(
        (
            jnp.dot(shard_piece, weight, preferred_element_type=jnp.float32)
            for weight in (w_query, w_key, w_value)
        )
    )
    query = query_full.astype(jnp.bfloat16).reshape(tok_rows, head_count, DH)
    key_heads = key_full.astype(jnp.bfloat16).reshape(tok_rows, head_count, DH)
    value_heads = value_full.astype(jnp.bfloat16).reshape(tok_rows, head_count, DH)
    prev_keys, prev_values = from_behind((key_heads[-STRIDE:], value_heads[-STRIDE:]), "seq", 1)
    blocks = tok_rows // STRIDE
    extended_keys = jnp.concatenate([prev_keys, key_heads], 0)
    extended_values = jnp.concatenate([prev_values, value_heads], 0)
    window_keys = jnp.concatenate(
        [
            extended_keys[:tok_rows].reshape(blocks, STRIDE, head_count, DH),
            extended_keys[STRIDE:].reshape(blocks, STRIDE, head_count, DH),
        ],
        1,
    )
    window_values = jnp.concatenate(
        [
            extended_values[:tok_rows].reshape(blocks, STRIDE, head_count, DH),
            extended_values[STRIDE:].reshape(blocks, STRIDE, head_count, DH),
        ],
        1,
    )
    query_blocks = query.reshape(blocks, STRIDE, head_count, DH)
    scores = (
        jnp.einsum("bthd,buhd->bhtu", query_blocks, window_keys, preferred_element_type=jnp.float32)
        * score_scale
    )
    first_position = lax.axis_index("seq") * tok_rows
    block_index = jnp.arange(blocks)[:, None, None, None]
    query_index = jnp.arange(STRIDE)[None, None, :, None]
    key_index = jnp.arange(2 * STRIDE)[None, None, None, :]
    allowed = (
        (key_index > query_index)
        & (key_index <= query_index + STRIDE)
        & (first_position + block_index * STRIDE + key_index - STRIDE >= 0)
    )
    local_top = jnp.max(jnp.where(allowed, scores, -1e30), axis=-1)
    local_weights = jnp.where(allowed, jnp.exp(scores - local_top[..., None]), 0.0)
    local_total = jnp.sum(local_weights, axis=-1)
    local_out = jnp.einsum(
        "bhtu,buhd->bthd",
        local_weights.astype(jnp.bfloat16),
        window_values,
        preferred_element_type=jnp.float32,
    )
    local_out = local_out.reshape(tok_rows, head_count, DH)
    local_top = local_top.transpose(0, 2, 1).reshape(tok_rows, head_count)
    local_total = local_total.transpose(0, 2, 1).reshape(tok_rows, head_count)
    row_count = tok_rows // STRIDE
    query_class = lax.all_to_all(
        query.reshape(row_count, STRIDE, head_count, DH),
        "seq",
        split_axis=1,
        concat_axis=0,
        tiled=True,
    )
    key_class = lax.all_to_all(
        key_heads.reshape(row_count, STRIDE, head_count, DH),
        "seq",
        split_axis=1,
        concat_axis=0,
        tiled=True,
    )
    value_class = lax.all_to_all(
        value_heads.reshape(row_count, STRIDE, head_count, DH),
        "seq",
        split_axis=1,
        concat_axis=0,
        tiled=True,
    )
    row_total = query_class.shape[0]
    class_scores = (
        jnp.einsum("rchd,schd->chrs", query_class, key_class, preferred_element_type=jnp.float32)
        * score_scale
    )
    earlier = (
        jnp.arange(row_total)[None, None, :, None] > jnp.arange(row_total)[None, None, None, :]
    )
    class_top = jnp.max(jnp.where(earlier, class_scores, -1e30), axis=-1)
    class_weights = jnp.where(earlier, jnp.exp(class_scores - class_top[..., None]), 0.0)
    class_total = jnp.sum(class_weights, axis=-1)
    summed = jnp.einsum(
        "chrs,schd->rchd",
        class_weights.astype(jnp.bfloat16),
        value_class,
        preferred_element_type=jnp.float32,
    )
    floor_total = jnp.maximum(class_total, 1.0).transpose(2, 0, 1)
    class_out = (summed / floor_total[..., None]).astype(jnp.bfloat16)
    class_top_rows = class_top.transpose(2, 0, 1)
    class_total_rows = class_total.transpose(2, 0, 1)
    column_out = class_out
    column_top = class_top_rows
    column_total = class_total_rows
    column_out, column_top, column_total = (
        lax.all_to_all(column_out, "seq", split_axis=0, concat_axis=1, tiled=True),
        lax.all_to_all(
            column_top.astype(jnp.bfloat16), "seq", split_axis=0, concat_axis=1, tiled=True
        ).astype(column_top.dtype),
        lax.all_to_all(
            column_total.astype(jnp.bfloat16), "seq", split_axis=0, concat_axis=1, tiled=True
        ).astype(column_total.dtype),
    )
    column_out = column_out.reshape(tok_rows, head_count, DH)
    column_top = column_top.reshape(tok_rows, head_count)
    column_total = column_total.reshape(tok_rows, head_count)
    top_score = jnp.maximum(local_top, column_top)
    local_weight = jnp.exp(local_top - top_score)
    column_weight = column_total * jnp.exp(column_top - top_score)
    denominator = local_total * local_weight + column_weight
    mixed = (
        local_out * local_weight[..., None]
        + column_out.astype(jnp.float32) * column_weight[..., None]
    ) / denominator[..., None]
    mixed = mixed.astype(jnp.bfloat16).reshape(tok_rows, head_width)
    return lax.psum_scatter(
        jnp.dot(mixed, w_out, preferred_element_type=jnp.float32).astype(jnp.bfloat16),
        "head",
        scatter_dimension=0,
        tiled=True,
    )


def shards(tokens, w_query, w_key, w_value, w_out):
    rows, width = w_query.shape
    fits = (
        lax.axis_size("seq") == STRIDE // 32
        and lax.axis_size("head") == 4
        and tokens.shape == (ROWS * STRIDE, HEADS * DH)
        and (rows, width) == (4 * HEADS * DH, HEADS * DH)
    )
    plan = chunked if fits else general
    return plan(tokens, w_query, w_key, w_value, w_out)


def solution(mesh):
    in_specs = (
        P("seq", "head"),
        P(None, "head"),
        P(None, "head"),
        P(None, "head"),
        P("head", None),
    )
    out_specs = P(("seq", "head"), None)
    return jax.shard_map(shards, mesh=mesh, in_specs=in_specs, out_specs=out_specs, check_vma=False)
```

```python
import functools

import jax
import jax.numpy as jnp
from jax import lax
from jax.experimental import pallas as pl
from jax.experimental.pallas import tpu as pltpu
from jax.sharding import PartitionSpec as P

DH = 128
STRIDE = 256
HEADS = 4
ROWS = 4
SUB = 8
CHUNKS = 2
SCALE2 = DH ** (-0.5) * 1.4426950408889634
FLOOR = -1e29
MIB = 1024 * 1024
F32 = jnp.float32
BF16 = jnp.bfloat16


ANYWHERE = pl.BlockSpec(memory_space=pl.ANY)


def params():
    return pltpu.CompilerParams(vmem_limit_bytes=56 * MIB)


def cost():
    return pl.CostEstimate(flops=0, bytes_accessed=MIB, transcendentals=0)


def dot(a, b):
    return jnp.dot(a, b, preferred_element_type=F32)


def dot_t(a, b):
    return lax.dot_general(a, b, (((1,), (1,)), ((), ())), preferred_element_type=F32)


def dot_l(a, b):
    return lax.dot_general(a, b, (((0,), (0,)), ((), ())), preferred_element_type=F32)


def pack_kernel(tok_ref, *out_refs):
    owners = out_refs[0].shape[0]
    per_owner = STRIDE // owners
    groups = per_owner // SUB
    per_chunk = groups // len(out_refs)
    for d in range(owners):
        rows = [
            tok_ref[r * STRIDE + d * per_owner : r * STRIDE + (d + 1) * per_owner, :].astype(F32)
            for r in range(ROWS)
        ]
        for g in range(groups):
            piece = jnp.concatenate([x[g * SUB : (g + 1) * SUB] for x in rows], 0)
            at = (g % per_chunk) * ROWS * SUB
            out_refs[g // per_chunk][d, at : at + ROWS * SUB, :] = piece.astype(BF16)


def pack(tokens, owners):
    width = tokens.shape[1]
    message = tokens.shape[0] // owners // CHUNKS
    return pl.pallas_call(
        pack_kernel,
        out_shape=[jax.ShapeDtypeStruct((owners, message, width), BF16)] * CHUNKS,
        compiler_params=params(),
        cost_estimate=cost(),
        name="pack_tokens",
    )(tokens)


def project_kernel(order_ref, x0, x1, x2, x3, wq, wk, wv, after, q_ref, k_ref, v_ref, halo_ref):
    for n, (w_ref, out_ref) in enumerate(((wq, q_ref), (wk, k_ref), (wv, v_ref))):
        total = None
        for p, x_ref in enumerate((x0, x1, x2, x3)):
            rows = pl.ds(pl.multiple_of(order_ref[p] * 512, 512), 512)
            term = dot(x_ref[...], w_ref[rows, :])
            total = term if total is None else total + term
        total = total.astype(BF16)
        out_ref[...] = total
        if n:
            halo_ref[(n - 1) * STRIDE : n * STRIDE, :] = total[-STRIDE:]


def project(order, pieces, weights, after):
    rows, width = pieces[0].shape
    tile = 256
    full = lambda n, s: (0, 0)
    tiled = lambda n, s: (0, n)
    return pl.pallas_call(
        project_kernel,
        grid_spec=pltpu.PrefetchScalarGridSpec(
            num_scalar_prefetch=1,
            grid=(width // tile,),
            in_specs=[pl.BlockSpec((rows, width), full)] * 4
            + [pl.BlockSpec((weights[0].shape[0], tile), tiled)] * 3
            + [ANYWHERE],
            out_specs=[pl.BlockSpec((rows, tile), tiled)] * 3
            + [pl.BlockSpec((2 * STRIDE, tile), tiled)],
        ),
        out_shape=[jax.ShapeDtypeStruct((rows, width), BF16)] * 3
        + [jax.ShapeDtypeStruct((2 * STRIDE, width), BF16)],
        compiler_params=params(),
        cost_estimate=cost(),
        name="project_block",
    )(order, *pieces, *weights, after)


def softmax_columns(s):
    m = jnp.maximum(jnp.max(s, 0, keepdims=True), FLOOR)
    p = jnp.exp2((s - m) * SCALE2)
    total = jnp.maximum(jnp.sum(p, 0, keepdims=True), 1.0)
    return p, total, m * SCALE2 + jnp.log2(total)


def local_kernel(pos_ref, q_ref, k_ref, v_ref, kp_ref, vp_ref, halo_ref, after, *outs):
    out_refs, lse_refs = outs[:CHUNKS], outs[CHUNKS:]
    owners, groups = out_refs[0].shape[:2]
    r = pl.program_id(0)
    first = r == 0
    no_prev = jnp.logical_and(first, pos_ref[0] == 0)
    u = lax.broadcasted_iota(jnp.int32, (STRIDE, STRIDE), 0)
    t = lax.broadcasted_iota(jnp.int32, (STRIDE, STRIDE), 1)
    current = u <= t
    low = jnp.where(no_prev, -1e30, 0.0).astype(F32)

    def spots():
        for d in range(owners):
            for i in range(CHUNKS):
                for g in range(groups):
                    at = ((d * CHUNKS + i) * groups + g) * SUB
                    yield d, i, g, slice(at, at + SUB)

    lses = []
    for h in range(HEADS):
        cols = slice(h * DH, (h + 1) * DH)
        q = q_ref[:, cols]
        k_prev = jnp.where(first, halo_ref[:STRIDE, cols], kp_ref[:, cols])
        v_prev = jnp.where(first, halo_ref[STRIDE:, cols], vp_ref[:, cols])
        s = jnp.where(current, dot_t(k_ref[:, cols], q), dot_t(k_prev, q) + low)
        p, total, lse = softmax_columns(s)
        p_now = jnp.where(current, p, 0.0).astype(BF16)
        p_prev = jnp.where(current, 0.0, p).astype(BF16)
        o = dot_l(v_ref[:, cols], p_now) + dot_l(v_prev, p_prev)
        o = (o / total).T
        lses.append(lse)
        for d, i, g, at in spots():
            out_refs[i][d, g, r, :, cols] = o[at]
    lses.append(jnp.zeros((128 - HEADS, STRIDE), F32))
    turned = jnp.concatenate(lses, 0).T
    for d, i, g, at in spots():
        lse_refs[i][d, g, r] = turned[at]


def local_part(pos, q, k, v, halo, owners, after):
    rows, width = q.shape
    tile = lambda r, s: (r, 0)
    back = lambda r, s: (jnp.maximum(r - 1, 0), 0)
    block = (STRIDE, width)
    lead = (owners, STRIDE // owners // SUB // CHUNKS, ROWS, SUB)
    shapes = [lead + (width,)] * CHUNKS + [lead + (128,)] * CHUNKS
    outs = pl.pallas_call(
        local_kernel,
        grid_spec=pltpu.PrefetchScalarGridSpec(
            num_scalar_prefetch=1,
            grid=(rows // STRIDE,),
            in_specs=[pl.BlockSpec(block, tile)] * 3
            + [pl.BlockSpec(block, back)] * 2
            + [pl.BlockSpec((2 * STRIDE, width), lambda r, s: (0, 0)), ANYWHERE],
            out_specs=[pl.BlockSpec(shape, lambda r, s: (0, 0, 0, 0, 0)) for shape in shapes],
        ),
        out_shape=[jax.ShapeDtypeStruct(shape, F32) for shape in shapes],
        compiler_params=params(),
        cost_estimate=cost(),
        name="local_part",
    )(pos, q, k, v, k, v, halo, after)
    outs = [x.reshape(owners, -1, x.shape[-1]) for x in outs]
    return list(zip(outs[:CHUNKS], outs[CHUNKS:]))


def column_kernel(order_ref, x0, x1, x2, x3, wq, wk, wv, after, out_ref, aq, ak, av):
    step = pl.program_id(0)
    owners, message, width = x0.shape
    groups = message // (ROWS * SUB)
    for p, x_ref in enumerate((x0, x1, x2, x3)):

        @pl.when(step == p)
        def _(p=p, x_ref=x_ref):
            x = x_ref[...].reshape(owners * message, width)
            for w_ref, acc in ((wq, aq), (wk, ak), (wv, av)):
                term = dot(x, w_ref[...]).reshape(acc.shape)
                acc[...] = term if p == 0 else acc[...] + term

    @pl.when(step == 3)
    def _():
        part = ROWS * SUB
        size = owners * part
        j = lax.broadcasted_iota(jnp.int32, (size, size), 0)
        i = lax.broadcasted_iota(jnp.int32, (size, size), 1)
        earlier = jnp.logical_and(i % SUB == j % SUB, i > j)
        stats = []
        for g in range(groups):
            at = slice(g * part, (g + 1) * part)
            lses = []
            for h in range(HEADS):
                cols = slice(h * DH, (h + 1) * DH)
                q, k, v = (a[:, at, cols].reshape(size, DH).astype(BF16) for a in (aq, ak, av))
                p, total, lse = softmax_columns(jnp.where(earlier, dot_t(k, q), -1e30))
                o = (dot_l(v, p.astype(BF16)) / total).T
                rows = slice(h * message + g * part, h * message + (g + 1) * part)
                out_ref[:, rows, :] = o.astype(BF16).reshape(owners, part, DH)
                lses.append(lse)
            stats.append(jnp.concatenate(lses + lses, 0))
        upper = lax.broadcasted_iota(jnp.int32, (8, 128), 0) < HEADS
        blank = [jnp.zeros((8, 128 - message), F32)] if message < 128 else []
        for d in range(owners):
            x = jnp.concatenate([s[:, d * part : (d + 1) * part] for s in stats] + blank, 1)
            hi = x.astype(BF16).astype(F32)
            mid = (x - hi).astype(BF16).astype(F32)
            lo = x - hi - mid
            tail = jnp.concatenate([jnp.where(upper, hi, lo), jnp.where(upper, mid, 0.0)], 0)
            out_ref[d, HEADS * message : HEADS * message + 16, :] = tail.astype(BF16)


def column_part(order, pieces, weights, after):
    owners, message, width = pieces[0].shape
    rows_out = HEADS * message + 16
    whole = lambda p, s: (0, 0, 0)
    return pl.pallas_call(
        column_kernel,
        grid_spec=pltpu.PrefetchScalarGridSpec(
            num_scalar_prefetch=1,
            grid=(4,),
            in_specs=[pl.BlockSpec(pieces[0].shape, whole)] * 4
            + [pl.BlockSpec((512, width), lambda p, s: (s[p], 0))] * 3
            + [ANYWHERE],
            out_specs=pl.BlockSpec((owners, rows_out, DH), whole),
            scratch_shapes=[pltpu.VMEM((owners, message, width), F32)] * 3,
        ),
        out_shape=jax.ShapeDtypeStruct((owners, rows_out, DH), BF16),
        compiler_params=params(),
        cost_estimate=cost(),
        name="column_part",
    )(order, *pieces, *weights, after)


def mix_kernel(pos_ref, col_ref, loc_ref, lse_ref, after, own_ref, send_ref, mixed):
    owners, message, _ = loc_ref.shape
    groups = message // (ROWS * SUB)
    base = HEADS * message
    tiles = []
    for d in range(owners):
        tail = col_ref[d, base : base + 16, :].astype(F32)
        tiles.append(tail[:8] + tail[8:])
    tiles.append(jnp.zeros((128 - 8 * owners, 128), F32))
    turned = jnp.concatenate(tiles, 0).T[:message]
    span = groups * SUB
    for d in range(owners):
        for h in range(HEADS):
            cols = slice(h * DH, (h + 1) * DH)
            col = col_ref[d, h * message : (h + 1) * message, :].astype(F32)
            at = 8 * d + h
            col_lse = turned[:, at : at + 1] + turned[:, at + 4 : at + 5]
            loc_lse = lse_ref[d, :, h : h + 1]
            top = jnp.maximum(col_lse, loc_lse)
            w_col = jnp.exp2(col_lse - top)
            w_loc = jnp.exp2(loc_lse - top)
            both = (loc_ref[d, :, cols] * w_loc + col * w_col) / (w_loc + w_col)
            for r in range(ROWS):
                starts = [(g * ROWS + r) * SUB for g in range(groups)]
                piece = jnp.concatenate([both[s : s + SUB] for s in starts], 0)
                mixed[r, d * span : (d + 1) * span, cols] = piece.astype(BF16)
    core = pos_ref[1]
    for x in range(2):
        own_ref[x] = mixed[2 * x + core]
        send_ref[x] = mixed[2 * x + 1 - core]


def mix(pos, column, local, lse, after):
    owners, message, width = local.shape
    tokens = owners * message // ROWS
    vmem = pl.BlockSpec(memory_space=pltpu.VMEM)
    return pl.pallas_call(
        mix_kernel,
        in_specs=[pl.BlockSpec(memory_space=pltpu.SMEM), vmem, vmem, vmem, ANYWHERE],
        out_specs=[vmem, vmem],
        out_shape=[jax.ShapeDtypeStruct((2, tokens, width), BF16)] * 2,
        scratch_shapes=[pltpu.VMEM((ROWS, tokens, width), BF16)],
        compiler_params=params(),
        cost_estimate=cost(),
        name="mix",
    )(pos, column, local, lse, after)


def out_kernel(pos_ref, a_ref, b_ref, wa_ref, wb_ref, send_ref, keep_ref):
    tokens = send_ref.shape[0]
    a = a_ref[...].reshape(2 * tokens, -1)
    b = b_ref[...].reshape(2 * tokens, -1)
    total = dot(a, wa_ref[...]) + dot(b, wb_ref[...])
    low_side = pos_ref[2] == 0
    send_ref[...] = jnp.where(low_side, total[tokens:], total[:tokens]).astype(BF16)
    keep_ref[...] = jnp.where(low_side, total[:tokens], total[tokens:])


def out_project(pos, own, other, w_own, w_other):
    _, tokens, width = own.shape
    columns = w_own.shape[1]
    tile = 512
    rows = pl.BlockSpec((2, tokens, width), lambda n, s: (0, 0, 0))
    cols = pl.BlockSpec((width, tile), lambda n, s: (0, n))
    return pl.pallas_call(
        out_kernel,
        grid_spec=pltpu.PrefetchScalarGridSpec(
            num_scalar_prefetch=1,
            grid=(columns // tile,),
            in_specs=[rows, rows, cols, cols],
            out_specs=[pl.BlockSpec((tokens, tile), lambda n, s: (0, n))] * 2,
        ),
        out_shape=[
            jax.ShapeDtypeStruct((tokens, columns), BF16),
            jax.ShapeDtypeStruct((tokens, columns), F32),
        ],
        compiler_params=params(),
        cost_estimate=cost(),
        name="out_project",
    )(pos, own, other, w_own, w_other)


def join_kernel(*refs):
    out_ref = refs[-1]
    chunks = (len(refs) - 1) // 2
    tokens = refs[0].shape[0]
    owners = STRIDE // 32
    span = tokens // owners
    for i in range(chunks):
        keep, got = refs[2 * i], refs[2 * i + 1]
        for d in range(owners):
            rows = slice(d * span, (d + 1) * span)
            at = (d * chunks + i) * span
            total = keep[rows, :] + got[rows, :].astype(F32)
            out_ref[at : at + span, :] = total.astype(BF16)


def join(pairs):
    tokens, columns = pairs[0][0].shape
    tile = 512
    spec = pl.BlockSpec((tokens, tile), lambda n: (0, n))
    return pl.pallas_call(
        join_kernel,
        grid=(columns // tile,),
        in_specs=[spec] * (2 * len(pairs)),
        out_specs=pl.BlockSpec((STRIDE, tile), lambda n: (0, n)),
        out_shape=jax.ShapeDtypeStruct((STRIDE, columns), BF16),
        compiler_params=params(),
        cost_estimate=cost(),
        name="join",
    )(*[x for pair in pairs for x in pair])


def swap(value, distance):
    return lax.ppermute(value, "head", [(i, i ^ distance) for i in range(4)])


def exchange(value):
    return lax.all_to_all(value, "seq", split_axis=0, concat_axis=0, tiled=True)


def gather(own):
    far = swap(own, 2)
    return own, swap(own, 1), far, swap(far, 1)


def chunked(tokens, w_query, w_key, w_value, w_out):
    owners = lax.axis_size("seq")
    head = lax.axis_index("head")
    block = lax.axis_index("seq")
    weights = (w_query, w_key, w_value)
    order = jnp.bitwise_xor(jnp.arange(4, dtype=jnp.int32), head.astype(jnp.int32))
    pos = jnp.stack([block, head % 2, head // 2]).astype(jnp.int32)

    block_pieces = gather(tokens)
    classes = [exchange(m) for m in pack(tokens, owners)]
    w_other = swap(w_out, 1)
    q, k, v, halo = project(order, block_pieces, weights, classes[0])
    halo = lax.ppermute(halo, "seq", [(i, i + 1) for i in range(owners - 1)])
    columns, after = [], q
    for i, c in enumerate(classes):
        columns.append(column_part(order, gather(c), weights, after))
        if i == 0:
            locals_ = local_part(pos, q, k, v, halo, owners, columns[0])
            after = locals_[-1][-1]
    pairs, after = [], columns[-1]
    for column, (local, lse) in zip(columns, locals_):
        own, send = mix(pos, exchange(column), local, lse, after)
        out, keep = out_project(pos, own, swap(send, 1), w_out, w_other)
        after = keep
        pairs.append((keep, swap(out, 2)))
    return join(pairs)


def from_behind(value, axis, by):
    peers = lax.axis_size(axis)
    pairs = [(i, i + by) for i in range(peers) if 0 <= i + by < peers]
    return lax.ppermute(value, axis, pairs)


def general(tokens, w_query, w_key, w_value, w_out):
    tok_rows = tokens.shape[0]
    head_width = w_query.shape[1]
    head_count = head_width // DH
    score_scale = DH ** (-0.5)
    shard_piece = lax.all_gather(tokens, "head", axis=1, tiled=True)
    query_full, key_full, value_full = tuple(
        (
            jnp.dot(shard_piece, weight, preferred_element_type=jnp.float32)
            for weight in (w_query, w_key, w_value)
        )
    )
    query = query_full.astype(jnp.bfloat16).reshape(tok_rows, head_count, DH)
    key_heads = key_full.astype(jnp.bfloat16).reshape(tok_rows, head_count, DH)
    value_heads = value_full.astype(jnp.bfloat16).reshape(tok_rows, head_count, DH)
    prev_keys, prev_values = from_behind((key_heads[-STRIDE:], value_heads[-STRIDE:]), "seq", 1)
    blocks = tok_rows // STRIDE
    extended_keys = jnp.concatenate([prev_keys, key_heads], 0)
    extended_values = jnp.concatenate([prev_values, value_heads], 0)
    window_keys = jnp.concatenate(
        [
            extended_keys[:tok_rows].reshape(blocks, STRIDE, head_count, DH),
            extended_keys[STRIDE:].reshape(blocks, STRIDE, head_count, DH),
        ],
        1,
    )
    window_values = jnp.concatenate(
        [
            extended_values[:tok_rows].reshape(blocks, STRIDE, head_count, DH),
            extended_values[STRIDE:].reshape(blocks, STRIDE, head_count, DH),
        ],
        1,
    )
    query_blocks = query.reshape(blocks, STRIDE, head_count, DH)
    scores = (
        jnp.einsum("bthd,buhd->bhtu", query_blocks, window_keys, preferred_element_type=jnp.float32)
        * score_scale
    )
    first_position = lax.axis_index("seq") * tok_rows
    block_index = jnp.arange(blocks)[:, None, None, None]
    query_index = jnp.arange(STRIDE)[None, None, :, None]
    key_index = jnp.arange(2 * STRIDE)[None, None, None, :]
    allowed = (
        (key_index > query_index)
        & (key_index <= query_index + STRIDE)
        & (first_position + block_index * STRIDE + key_index - STRIDE >= 0)
    )
    local_top = jnp.max(jnp.where(allowed, scores, -1e30), axis=-1)
    local_weights = jnp.where(allowed, jnp.exp(scores - local_top[..., None]), 0.0)
    local_total = jnp.sum(local_weights, axis=-1)
    local_out = jnp.einsum(
        "bhtu,buhd->bthd",
        local_weights.astype(jnp.bfloat16),
        window_values,
        preferred_element_type=jnp.float32,
    )
    local_out = local_out.reshape(tok_rows, head_count, DH)
    local_top = local_top.transpose(0, 2, 1).reshape(tok_rows, head_count)
    local_total = local_total.transpose(0, 2, 1).reshape(tok_rows, head_count)
    row_count = tok_rows // STRIDE
    query_class = lax.all_to_all(
        query.reshape(row_count, STRIDE, head_count, DH),
        "seq",
        split_axis=1,
        concat_axis=0,
        tiled=True,
    )
    key_class = lax.all_to_all(
        key_heads.reshape(row_count, STRIDE, head_count, DH),
        "seq",
        split_axis=1,
        concat_axis=0,
        tiled=True,
    )
    value_class = lax.all_to_all(
        value_heads.reshape(row_count, STRIDE, head_count, DH),
        "seq",
        split_axis=1,
        concat_axis=0,
        tiled=True,
    )
    row_total = query_class.shape[0]
    class_scores = (
        jnp.einsum("rchd,schd->chrs", query_class, key_class, preferred_element_type=jnp.float32)
        * score_scale
    )
    earlier = (
        jnp.arange(row_total)[None, None, :, None] > jnp.arange(row_total)[None, None, None, :]
    )
    class_top = jnp.max(jnp.where(earlier, class_scores, -1e30), axis=-1)
    class_weights = jnp.where(earlier, jnp.exp(class_scores - class_top[..., None]), 0.0)
    class_total = jnp.sum(class_weights, axis=-1)
    summed = jnp.einsum(
        "chrs,schd->rchd",
        class_weights.astype(jnp.bfloat16),
        value_class,
        preferred_element_type=jnp.float32,
    )
    floor_total = jnp.maximum(class_total, 1.0).transpose(2, 0, 1)
    class_out = (summed / floor_total[..., None]).astype(jnp.bfloat16)
    class_top_rows = class_top.transpose(2, 0, 1)
    class_total_rows = class_total.transpose(2, 0, 1)
    column_out = class_out
    column_top = class_top_rows
    column_total = class_total_rows
    column_out, column_top, column_total = (
        lax.all_to_all(column_out, "seq", split_axis=0, concat_axis=1, tiled=True),
        lax.all_to_all(
            column_top.astype(jnp.bfloat16), "seq", split_axis=0, concat_axis=1, tiled=True
        ).astype(column_top.dtype),
        lax.all_to_all(
            column_total.astype(jnp.bfloat16), "seq", split_axis=0, concat_axis=1, tiled=True
        ).astype(column_total.dtype),
    )
    column_out = column_out.reshape(tok_rows, head_count, DH)
    column_top = column_top.reshape(tok_rows, head_count)
    column_total = column_total.reshape(tok_rows, head_count)
    top_score = jnp.maximum(local_top, column_top)
    local_weight = jnp.exp(local_top - top_score)
    column_weight = column_total * jnp.exp(column_top - top_score)
    denominator = local_total * local_weight + column_weight
    mixed = (
        local_out * local_weight[..., None]
        + column_out.astype(jnp.float32) * column_weight[..., None]
    ) / denominator[..., None]
    mixed = mixed.astype(jnp.bfloat16).reshape(tok_rows, head_width)
    return lax.psum_scatter(
        jnp.dot(mixed, w_out, preferred_element_type=jnp.float32).astype(jnp.bfloat16),
        "head",
        scatter_dimension=0,
        tiled=True,
    )


def shards(tokens, w_query, w_key, w_value, w_out):
    rows, width = w_query.shape
    fits = (
        lax.axis_size("seq") == STRIDE // 32
        and lax.axis_size("head") == 4
        and tokens.shape == (ROWS * STRIDE, HEADS * DH)
        and (rows, width) == (4 * HEADS * DH, HEADS * DH)
    )
    plan = chunked if fits else general
    return plan(tokens, w_query, w_key, w_value, w_out)


def solution(mesh):
    in_specs = (
        P("seq", "head"),
        P(None, "head"),
        P(None, "head"),
        P(None, "head"),
        P("head", None),
    )
    out_specs = P(("seq", "head"), None)
    return jax.shard_map(shards, mesh=mesh, in_specs=in_specs, out_specs=out_specs, check_vma=False)
```

```python
import jax
import jax.numpy as jnp
from jax import lax
from jax.experimental import pallas as pl
from jax.experimental.pallas import tpu as pltpu
from jax.sharding import PartitionSpec as P

DH = 128
STRIDE = 256
HEADS = 4
ROWS = 4
SUB = 8
CHUNKS = 2
SCALE2 = DH ** (-0.5) * 1.4426950408889634
FLOOR = -1e29
MIB = 1024 * 1024
F32 = jnp.float32
BF16 = jnp.bfloat16


ANYWHERE = pl.BlockSpec(memory_space=pl.ANY)
IN_VMEM = pl.BlockSpec(memory_space=pltpu.VMEM)
IN_SMEM = pl.BlockSpec(memory_space=pltpu.SMEM)


def call(body, name, micros, out_shape, args, after=(), scratch=(), mib=24):
    specs = [IN_SMEM if x.dtype == jnp.int32 else IN_VMEM for x in args]
    extra = len(after)

    def run(*refs):
        n = len(args)
        body(*refs[:n], *refs[n + extra :])

    return pl.pallas_call(
        run,
        in_specs=specs + [ANYWHERE] * extra,
        out_specs=jax.tree.map(lambda _: IN_VMEM, out_shape),
        out_shape=out_shape,
        scratch_shapes=list(scratch),
        compiler_params=pltpu.CompilerParams(vmem_limit_bytes=mib * MIB),
        cost_estimate=pl.CostEstimate(
            flops=int(micros * 1.1e9), bytes_accessed=MIB, transcendentals=0
        ),
        name=name,
    )(*args, *after)


def shape(dims, dtype=BF16):
    return jax.ShapeDtypeStruct(tuple(dims), dtype)


def dot(a, b):
    return jnp.dot(a, b, preferred_element_type=F32)


def dot_t(a, b):
    return lax.dot_general(a, b, (((1,), (1,)), ((), ())), preferred_element_type=F32)


def dot_l(a, b):
    return lax.dot_general(a, b, (((0,), (0,)), ((), ())), preferred_element_type=F32)


def pack_kernel(pos_ref, tok_ref, *out_refs):
    owners = len(out_refs) // CHUNKS
    per_owner = STRIDE // owners
    groups = per_owner // SUB
    per_chunk = groups // CHUNKS
    for k in range(owners):
        d = pos_ref[0] ^ k
        rows = [
            tok_ref[pl.ds(pl.multiple_of(r * STRIDE + d * per_owner, per_owner), per_owner), :]
            for r in range(ROWS)
        ]
        rows = [x.astype(F32) for x in rows]
        for g in range(groups):
            piece = jnp.concatenate([x[g * SUB : (g + 1) * SUB] for x in rows], 0)
            at = (g % per_chunk) * ROWS * SUB
            out = out_refs[(g // per_chunk) * owners + k]
            out[at : at + ROWS * SUB, :] = piece.astype(BF16)


def pack(pos, tokens, owners):
    message = tokens.shape[0] // owners // CHUNKS
    shapes = [shape((message, tokens.shape[1]))] * (CHUNKS * owners)
    outs = call(pack_kernel, "pack_tokens", 2, shapes, (pos, tokens))
    return [outs[i * owners : (i + 1) * owners] for i in range(CHUNKS)]


def stage_kernel(order_ref, wq, wk, wv, oq, ok, ov, sems):
    copies = []
    for n, (w, o) in enumerate(((wq, oq), (wk, ok), (wv, ov))):
        for p in range(4):
            rows = pl.ds(pl.multiple_of(order_ref[p] * 512, 512), 512)
            copies.append(
                pltpu.make_async_copy(w.at[rows], o.at[p * 512 : (p + 1) * 512], sems.at[4 * n + p])
            )
    for c in copies:
        c.start()
    for c in copies:
        c.wait()


def stage(order, weights, after):
    def body(order_ref, wq, wk, wv, _, *rest):
        stage_kernel(order_ref, wq, wk, wv, *rest)

    return pl.pallas_call(
        body,
        in_specs=[IN_SMEM] + [ANYWHERE] * 4,
        out_specs=[IN_VMEM] * 3,
        out_shape=[shape(w.shape) for w in weights],
        scratch_shapes=[pltpu.SemaphoreType.DMA((12,))],
        compiler_params=pltpu.CompilerParams(vmem_limit_bytes=16 * MIB),
        cost_estimate=pl.CostEstimate(flops=0, bytes_accessed=6 * MIB, transcendentals=0),
        name="stage_weights",
    )(order, *weights, after)


def gathered(x_refs, at, w_ref):
    width = x_refs[0].shape[1]
    total = None
    for p, x_ref in enumerate(x_refs):
        term = dot(x_ref[at, :], w_ref[p * width : (p + 1) * width, :])
        total = term if total is None else total + term
    return total.astype(BF16)


def halo_kernel(x0, x1, x2, x3, wk, wv, out_ref):
    rows = x0.shape[0]
    at = slice(rows - STRIDE, rows)
    out_ref[:STRIDE, :] = gathered((x0, x1, x2, x3), at, wk)
    out_ref[STRIDE:, :] = gathered((x0, x1, x2, x3), at, wv)


def project_kernel(x0, x1, x2, x3, wq, wk, wv, halo, q_ref, k_ref, v_ref):
    rows = x0.shape[0]
    xs = (x0, x1, x2, x3)
    last = slice(rows - STRIDE, rows)
    k_ref[last, :] = halo[:STRIDE, :]
    v_ref[last, :] = halo[STRIDE:, :]
    for w, out, upto in ((wq, q_ref, rows), (wk, k_ref, rows - STRIDE), (wv, v_ref, rows - STRIDE)):
        out[:upto, :] = gathered(xs, slice(0, upto), w)


def softmax_columns(s):
    m = jnp.maximum(jnp.max(s, 0, keepdims=True), FLOOR)
    p = jnp.exp2((s - m) * SCALE2)
    total = jnp.maximum(jnp.sum(p, 0, keepdims=True), 1.0)
    return p, total, m * SCALE2 + jnp.log2(total)


def local_kernel(pos_ref, q_ref, k_ref, v_ref, halo_ref, *outs):
    out_refs, lse_refs = outs[:CHUNKS], outs[CHUNKS:]
    owners, message, _ = out_refs[0].shape
    groups = message // ROWS // SUB
    block = pos_ref[0]
    u = lax.broadcasted_iota(jnp.int32, (STRIDE, STRIDE), 0)
    t = lax.broadcasted_iota(jnp.int32, (STRIDE, STRIDE), 1)
    current = u <= t
    low = jnp.where(block == 0, -1e30, 0.0).astype(F32)
    for r in range(ROWS):
        lses = []
        here = slice(r * STRIDE, (r + 1) * STRIDE)
        back = slice((r - 1) * STRIDE, r * STRIDE)
        for h in range(HEADS):
            cols = slice(h * DH, (h + 1) * DH)
            q = q_ref[here, cols]
            k_prev = k_ref[back, cols] if r else halo_ref[:STRIDE, cols]
            v_prev = v_ref[back, cols] if r else halo_ref[STRIDE:, cols]
            s_prev = dot_t(k_prev, q)
            if r == 0:
                s_prev = s_prev + low
            p, total, lse = softmax_columns(jnp.where(current, dot_t(k_ref[here, cols], q), s_prev))
            p_now = jnp.where(current, p, 0.0).astype(BF16)
            p_prev = jnp.where(current, 0.0, p).astype(BF16)
            o = dot_l(v_ref[here, cols], p_now) + dot_l(v_prev, p_prev)
            o = (o * (1.0 / total)).T
            lses.append(lse)
            for d in range(owners):
                for i in range(CHUNKS):
                    for g in range(groups):
                        at = ((d * CHUNKS + i) * groups + g) * SUB
                        to = (g * ROWS + r) * SUB
                        out_refs[i][d, to : to + SUB, cols] = o[at : at + SUB]
        lses.append(jnp.zeros((128 - HEADS, STRIDE), F32))
        turned = jnp.concatenate(lses, 0).T
        for i in range(CHUNKS):
            for g in range(groups):
                total = None
                for d in range(owners):
                    at = ((d * CHUNKS + i) * groups + g) * SUB
                    moved = pltpu.roll(turned[at : at + SUB], 8 * (block ^ d), 1)
                    total = moved if total is None else total + moved
                to = (g * ROWS + r) * SUB
                lse_refs[i][to : to + SUB, :] = total


def local_part(pos, q, k, v, halo, owners, after):
    rows, width = q.shape
    message = rows // owners // CHUNKS
    shapes = [shape((owners, message, width), F32)] * CHUNKS + [shape((message, 128), F32)] * CHUNKS
    outs = call(local_kernel, "local_part", 5, shapes, (pos, q, k, v, halo), after)
    return list(zip(outs[:CHUNKS], outs[CHUNKS:]))


def column_kernel(pos_ref, x0, x1, x2, x3, wq, wk, wv, *rest):
    out_refs, scratch = rest[:-3], rest[-3:]
    owners, message, _ = scratch[0].shape
    groups = message // (ROWS * SUB)
    everything = slice(0, owners * message)
    for w, a in zip((wq, wk, wv), scratch):
        a[...] = gathered((x0, x1, x2, x3), everything, w).reshape(a.shape)
    part = ROWS * SUB
    size = owners * part

    def row_and_class(dim):
        i = lax.broadcasted_iota(jnp.int32, (size, size), dim)
        return ((i // part) ^ pos_ref[0]) * ROWS + (i % part) // SUB, i % SUB

    (row_j, class_j), (row_i, class_i) = row_and_class(0), row_and_class(1)
    earlier = jnp.logical_and(class_i == class_j, row_i > row_j)
    stats = []
    for g in range(groups):
        at = slice(g * part, (g + 1) * part)
        lses = []
        for h in range(HEADS):
            cols = slice(h * DH, (h + 1) * DH)
            q, k, v = (a[:, at, cols].reshape(size, DH) for a in scratch)
            p, total, lse = softmax_columns(jnp.where(earlier, dot_t(k, q), -1e30))
            o = (dot_l(v, p.astype(BF16)) * (1.0 / total)).T.astype(BF16)
            rows = slice(h * message + g * part, h * message + (g + 1) * part)
            for n in range(owners):
                out_refs[n][rows, :] = o[n * part : (n + 1) * part]
            lses.append(lse)
        stats.append(jnp.concatenate(lses + lses, 0))
    upper = lax.broadcasted_iota(jnp.int32, (8, 128), 0) < HEADS
    blank = [jnp.zeros((8, 128 - message), F32)] if message < 128 else []
    for n in range(owners):
        x = jnp.concatenate([s[:, n * part : (n + 1) * part] for s in stats] + blank, 1)
        hi = x.astype(BF16).astype(F32)
        mid = (x - hi).astype(BF16).astype(F32)
        lo = x - hi - mid
        tail = jnp.concatenate([jnp.where(upper, hi, lo), jnp.where(upper, mid, 0.0)], 0)
        out_refs[n][HEADS * message : HEADS * message + 16, :] = tail.astype(BF16)


def column_part(pos, pieces, weights, owners, after):
    tokens, width = pieces[0].shape
    message = tokens // owners
    shapes = [shape((HEADS * message + 16, DH))] * owners
    scratch = [pltpu.VMEM((owners, message, width), BF16)] * 3
    return call(column_kernel, "column_part", 6, shapes, (pos, *pieces, *weights), after, scratch)


def mix_kernel(pos_ref, loc_ref, lse_ref, *rest):
    col_refs, (own_ref, send_ref, mixed) = rest[:-3], rest[-3:]
    owners, message, _ = loc_ref.shape
    groups = message // (ROWS * SUB)
    base = HEADS * message
    tiles = []
    for col_ref in col_refs:
        tail = col_ref[base : base + 16, :].astype(F32)
        tiles.append(tail[:8] + tail[8:])
    tiles.append(jnp.zeros((128 - 8 * owners, 128), F32))
    turned = jnp.concatenate(tiles, 0).T[:message]
    col_lse = turned + pltpu.roll(turned, 124, 1)
    loc_lse = lse_ref[...]
    top = jnp.maximum(col_lse, loc_lse)
    w_col = jnp.exp2(col_lse - top)
    w_loc = jnp.exp2(loc_lse - top)
    share = 1.0 / (w_col + w_loc)
    w_col = w_col * share
    w_loc = w_loc * share
    span = groups * SUB
    for k, col_ref in enumerate(col_refs):
        d = pos_ref[0] ^ k
        spot = pl.ds(pl.multiple_of(d * span, span), span)
        for h in range(HEADS):
            cols = slice(h * DH, (h + 1) * DH)
            at = slice(8 * k + h, 8 * k + h + 1)
            col = col_ref[h * message : (h + 1) * message, :].astype(F32)
            both = loc_ref[d, :, cols] * w_loc[:, at] + col * w_col[:, at]
            for r in range(ROWS):
                starts = [(g * ROWS + r) * SUB for g in range(groups)]
                piece = jnp.concatenate([both[s : s + SUB] for s in starts], 0)
                mixed[r, spot, cols] = piece.astype(BF16)
    core = pos_ref[1]
    for x in range(2):
        own_ref[x] = mixed[2 * x + core]
        send_ref[x] = mixed[2 * x + 1 - core]


def mix(pos, columns, local, lse, after):
    owners, message, width = local.shape
    tokens = owners * message // ROWS
    shapes = [shape((2, tokens, width))] * 2
    scratch = [pltpu.VMEM((ROWS, tokens, width), BF16)]
    return call(mix_kernel, "mix", 3, shapes, (pos, local, lse, *columns), after, scratch)


def out_kernel(pos_ref, a_ref, b_ref, wa_ref, wb_ref, send_ref, keep_ref):
    tokens, columns = send_ref.shape
    a = a_ref[...].reshape(2 * tokens, -1)
    b = b_ref[...].reshape(2 * tokens, -1)
    low_side = pos_ref[2] == 0
    tile = 512
    for n in range(0, columns, tile):
        at = slice(n, n + tile)
        total = dot(a, wa_ref[:, at]) + dot(b, wb_ref[:, at])
        send_ref[:, at] = jnp.where(low_side, total[tokens:], total[:tokens]).astype(BF16)
        keep_ref[:, at] = jnp.where(low_side, total[:tokens], total[tokens:])


def out_project(pos, own, other, w_own, w_other):
    dims = (own.shape[1], w_own.shape[1])
    shapes = [shape(dims), shape(dims, F32)]
    return call(out_kernel, "out_project", 3, shapes, (pos, own, other, w_own, w_other))


def join_kernel(*refs):
    out_ref = refs[-1]
    chunks = (len(refs) - 1) // 2
    tokens = refs[0].shape[0]
    span = 32 // chunks
    for i in range(chunks):
        keep, got = refs[2 * i], refs[2 * i + 1]
        for d in range(tokens // span):
            rows = slice(d * span, (d + 1) * span)
            at = (d * chunks + i) * span
            total = keep[rows, :] + got[rows, :].astype(F32)
            out_ref[at : at + span, :] = total.astype(BF16)


def join(pairs):
    columns = pairs[0][0].shape[1]
    args = [x for pair in pairs for x in pair]
    return call(join_kernel, "join", 2, shape((STRIDE, columns)), args)


def swap(value, distance):
    return lax.ppermute(value, "head", [(i, i ^ distance) for i in range(4)])


def exchange(messages):
    n = len(messages)
    return [messages[0]] + [
        lax.ppermute(messages[k], "seq", [(i, i ^ k) for i in range(n)]) for k in range(1, n)
    ]


def gather(own):
    far = swap(own, 2)
    return own, swap(own, 1), far, swap(far, 1)


def chunked(tokens, w_query, w_key, w_value, w_out):
    owners = lax.axis_size("seq")
    head = lax.axis_index("head")
    block = lax.axis_index("seq")
    order = jnp.bitwise_xor(jnp.arange(4, dtype=jnp.int32), head.astype(jnp.int32))
    pos = jnp.stack([block, head % 2, head // 2]).astype(jnp.int32)
    rows, width = tokens.shape

    pieces = gather(tokens)
    classes = [exchange(m) for m in pack(pos, tokens, owners)]
    weights = stage(order, (w_query, w_key, w_value), classes[0][1])
    w_other = swap(w_out, 1)
    own_halo = call(
        halo_kernel, "project_halo", 1.5, shape((2 * STRIDE, width)), (*pieces, *weights[1:])
    )
    halo = lax.ppermute(own_halo, "seq", [(i, i + 1) for i in range(owners - 1)])
    q, k, v = call(
        project_kernel,
        "project_block",
        7,
        [shape((rows, width))] * 3,
        (*pieces, *weights, own_halo),
    )
    columns, after = [], (q, halo)
    for i, messages in enumerate(classes):
        class_pieces = gather(jnp.concatenate(messages, 0))
        columns.append(column_part(pos, class_pieces, weights, owners, after))
        if i == 0:
            locals_ = local_part(pos, q, k, v, halo, owners, (columns[0][0],))
            after = (locals_[-1][-1],)
    pairs, after = [], (columns[-1][0],)
    for column, (local, lse) in zip(columns, locals_):
        own, send = mix(pos, exchange(column), local, lse, after)
        out, keep = out_project(pos, own, swap(send, 1), w_out, w_other)
        after = (keep,)
        pairs.append((keep, swap(out, 2)))
    return join(pairs)


def from_behind(value, axis, by):
    peers = lax.axis_size(axis)
    pairs = [(i, i + by) for i in range(peers) if 0 <= i + by < peers]
    return lax.ppermute(value, axis, pairs)


def general(tokens, w_query, w_key, w_value, w_out):
    tok_rows = tokens.shape[0]
    head_width = w_query.shape[1]
    head_count = head_width // DH
    score_scale = DH ** (-0.5)
    shard_piece = lax.all_gather(tokens, "head", axis=1, tiled=True)
    query_full, key_full, value_full = tuple(
        (
            jnp.dot(shard_piece, weight, preferred_element_type=jnp.float32)
            for weight in (w_query, w_key, w_value)
        )
    )
    query = query_full.astype(jnp.bfloat16).reshape(tok_rows, head_count, DH)
    key_heads = key_full.astype(jnp.bfloat16).reshape(tok_rows, head_count, DH)
    value_heads = value_full.astype(jnp.bfloat16).reshape(tok_rows, head_count, DH)
    prev_keys, prev_values = from_behind((key_heads[-STRIDE:], value_heads[-STRIDE:]), "seq", 1)
    blocks = tok_rows // STRIDE
    extended_keys = jnp.concatenate([prev_keys, key_heads], 0)
    extended_values = jnp.concatenate([prev_values, value_heads], 0)
    window_keys = jnp.concatenate(
        [
            extended_keys[:tok_rows].reshape(blocks, STRIDE, head_count, DH),
            extended_keys[STRIDE:].reshape(blocks, STRIDE, head_count, DH),
        ],
        1,
    )
    window_values = jnp.concatenate(
        [
            extended_values[:tok_rows].reshape(blocks, STRIDE, head_count, DH),
            extended_values[STRIDE:].reshape(blocks, STRIDE, head_count, DH),
        ],
        1,
    )
    query_blocks = query.reshape(blocks, STRIDE, head_count, DH)
    scores = (
        jnp.einsum("bthd,buhd->bhtu", query_blocks, window_keys, preferred_element_type=jnp.float32)
        * score_scale
    )
    first_position = lax.axis_index("seq") * tok_rows
    block_index = jnp.arange(blocks)[:, None, None, None]
    query_index = jnp.arange(STRIDE)[None, None, :, None]
    key_index = jnp.arange(2 * STRIDE)[None, None, None, :]
    allowed = (
        (key_index > query_index)
        & (key_index <= query_index + STRIDE)
        & (first_position + block_index * STRIDE + key_index - STRIDE >= 0)
    )
    local_top = jnp.max(jnp.where(allowed, scores, -1e30), axis=-1)
    local_weights = jnp.where(allowed, jnp.exp(scores - local_top[..., None]), 0.0)
    local_total = jnp.sum(local_weights, axis=-1)
    local_out = jnp.einsum(
        "bhtu,buhd->bthd",
        local_weights.astype(jnp.bfloat16),
        window_values,
        preferred_element_type=jnp.float32,
    )
    local_out = local_out.reshape(tok_rows, head_count, DH)
    local_top = local_top.transpose(0, 2, 1).reshape(tok_rows, head_count)
    local_total = local_total.transpose(0, 2, 1).reshape(tok_rows, head_count)
    row_count = tok_rows // STRIDE
    query_class = lax.all_to_all(
        query.reshape(row_count, STRIDE, head_count, DH),
        "seq",
        split_axis=1,
        concat_axis=0,
        tiled=True,
    )
    key_class = lax.all_to_all(
        key_heads.reshape(row_count, STRIDE, head_count, DH),
        "seq",
        split_axis=1,
        concat_axis=0,
        tiled=True,
    )
    value_class = lax.all_to_all(
        value_heads.reshape(row_count, STRIDE, head_count, DH),
        "seq",
        split_axis=1,
        concat_axis=0,
        tiled=True,
    )
    row_total = query_class.shape[0]
    class_scores = (
        jnp.einsum("rchd,schd->chrs", query_class, key_class, preferred_element_type=jnp.float32)
        * score_scale
    )
    earlier = (
        jnp.arange(row_total)[None, None, :, None] > jnp.arange(row_total)[None, None, None, :]
    )
    class_top = jnp.max(jnp.where(earlier, class_scores, -1e30), axis=-1)
    class_weights = jnp.where(earlier, jnp.exp(class_scores - class_top[..., None]), 0.0)
    class_total = jnp.sum(class_weights, axis=-1)
    summed = jnp.einsum(
        "chrs,schd->rchd",
        class_weights.astype(jnp.bfloat16),
        value_class,
        preferred_element_type=jnp.float32,
    )
    floor_total = jnp.maximum(class_total, 1.0).transpose(2, 0, 1)
    class_out = (summed / floor_total[..., None]).astype(jnp.bfloat16)
    class_top_rows = class_top.transpose(2, 0, 1)
    class_total_rows = class_total.transpose(2, 0, 1)
    column_out = class_out
    column_top = class_top_rows
    column_total = class_total_rows
    column_out, column_top, column_total = (
        lax.all_to_all(column_out, "seq", split_axis=0, concat_axis=1, tiled=True),
        lax.all_to_all(
            column_top.astype(jnp.bfloat16), "seq", split_axis=0, concat_axis=1, tiled=True
        ).astype(column_top.dtype),
        lax.all_to_all(
            column_total.astype(jnp.bfloat16), "seq", split_axis=0, concat_axis=1, tiled=True
        ).astype(column_total.dtype),
    )
    column_out = column_out.reshape(tok_rows, head_count, DH)
    column_top = column_top.reshape(tok_rows, head_count)
    column_total = column_total.reshape(tok_rows, head_count)
    top_score = jnp.maximum(local_top, column_top)
    local_weight = jnp.exp(local_top - top_score)
    column_weight = column_total * jnp.exp(column_top - top_score)
    denominator = local_total * local_weight + column_weight
    mixed = (
        local_out * local_weight[..., None]
        + column_out.astype(jnp.float32) * column_weight[..., None]
    ) / denominator[..., None]
    mixed = mixed.astype(jnp.bfloat16).reshape(tok_rows, head_width)
    return lax.psum_scatter(
        jnp.dot(mixed, w_out, preferred_element_type=jnp.float32).astype(jnp.bfloat16),
        "head",
        scatter_dimension=0,
        tiled=True,
    )


def shards(tokens, w_query, w_key, w_value, w_out):
    rows, width = w_query.shape
    fits = (
        lax.axis_size("seq") == STRIDE // 32
        and lax.axis_size("head") == 4
        and tokens.shape == (ROWS * STRIDE, HEADS * DH)
        and (rows, width) == (4 * HEADS * DH, HEADS * DH)
    )
    plan = chunked if fits else general
    return plan(tokens, w_query, w_key, w_value, w_out)


def solution(mesh):
    in_specs = (
        P("seq", "head"),
        P(None, "head"),
        P(None, "head"),
        P(None, "head"),
        P("head", None),
    )
    out_specs = P(("seq", "head"), None)
    return jax.shard_map(shards, mesh=mesh, in_specs=in_specs, out_specs=out_specs, check_vma=False)
```

```python
import jax
import jax.numpy as jnp
from jax import lax
from jax.experimental import pallas as pl
from jax.experimental.pallas import tpu as pltpu
from jax.sharding import PartitionSpec as P

DH = 128
STRIDE = 256
HEADS = 4
ROWS = 4
SUB = 8
CHUNKS = 2
SCALE2 = DH ** (-0.5) * 1.4426950408889634
FLOOR = -1e29
MIB = 1024 * 1024
F32 = jnp.float32
BF16 = jnp.bfloat16


ANYWHERE = pl.BlockSpec(memory_space=pl.ANY)
IN_VMEM = pl.BlockSpec(memory_space=pltpu.VMEM)
IN_SMEM = pl.BlockSpec(memory_space=pltpu.SMEM)


def call(body, name, micros, out_shape, args, after=(), scratch=(), mib=24):
    specs = [IN_SMEM if x.dtype == jnp.int32 else IN_VMEM for x in args]
    extra = len(after)

    def run(*refs):
        n = len(args)
        body(*refs[:n], *refs[n + extra :])

    return pl.pallas_call(
        run,
        in_specs=specs + [ANYWHERE] * extra,
        out_specs=jax.tree.map(lambda _: IN_VMEM, out_shape),
        out_shape=out_shape,
        scratch_shapes=list(scratch),
        compiler_params=pltpu.CompilerParams(vmem_limit_bytes=mib * MIB),
        cost_estimate=pl.CostEstimate(
            flops=int(micros * 1.1e9), bytes_accessed=MIB, transcendentals=0
        ),
        name=name,
    )(*args, *after)


def shape(dims, dtype=BF16):
    return jax.ShapeDtypeStruct(tuple(dims), dtype)


def dot(a, b):
    return jnp.dot(a, b, preferred_element_type=F32)


def dot_t(a, b):
    return lax.dot_general(a, b, (((1,), (1,)), ((), ())), preferred_element_type=F32)


def dot_l(a, b):
    return lax.dot_general(a, b, (((0,), (0,)), ((), ())), preferred_element_type=F32)


def pack_kernel(tok_hbm, *rest):
    out_refs, (tok_ref, sems) = rest[:-2], rest[-2:]
    owners = out_refs[0].shape[0]
    per_owner = STRIDE // owners
    groups = per_owner // SUB
    per_chunk = groups // CHUNKS
    spans = [slice(r * STRIDE, (r + 1) * STRIDE) for r in range(ROWS)]
    copies = [
        pltpu.make_async_copy(tok_hbm.at[at], tok_ref.at[at], sems.at[r])
        for r, at in enumerate(spans)
    ]
    for c in copies:
        c.start()
    for c in copies:
        c.wait()
    for d in range(owners):
        rows = [
            tok_ref[r * STRIDE + d * per_owner : r * STRIDE + (d + 1) * per_owner, :].astype(F32)
            for r in range(ROWS)
        ]
        for g in range(groups):
            piece = jnp.concatenate([x[g * SUB : (g + 1) * SUB] for x in rows], 0)
            at = (g % per_chunk) * ROWS * SUB
            out_refs[g // per_chunk][d, at : at + ROWS * SUB, :] = piece.astype(BF16)


def pack(tokens, owners):
    message = tokens.shape[0] // owners // CHUNKS
    return pl.pallas_call(
        pack_kernel,
        in_specs=[ANYWHERE],
        out_specs=[IN_VMEM] * CHUNKS,
        out_shape=[shape((owners, message, tokens.shape[1]))] * CHUNKS,
        scratch_shapes=[pltpu.VMEM(tokens.shape, BF16), pltpu.SemaphoreType.DMA((ROWS,))],
        compiler_params=pltpu.CompilerParams(vmem_limit_bytes=8 * MIB),
        cost_estimate=pl.CostEstimate(flops=0, bytes_accessed=2 * MIB, transcendentals=0),
        name="pack_tokens",
    )(tokens)


def stage_kernel(order_ref, wq, wk, wv, oq, ok, ov, sems):
    copies = []
    for n, (w, o) in enumerate(((wq, oq), (wk, ok), (wv, ov))):
        for p in range(4):
            rows = pl.ds(pl.multiple_of(order_ref[p] * 512, 512), 512)
            copies.append(
                pltpu.make_async_copy(w.at[rows], o.at[p * 512 : (p + 1) * 512], sems.at[4 * n + p])
            )
    for c in copies:
        c.start()
    for c in copies:
        c.wait()


def stage(order, weights, after):
    def body(order_ref, wq, wk, wv, *rest):
        stage_kernel(order_ref, wq, wk, wv, *rest[len(after) :])

    return pl.pallas_call(
        body,
        in_specs=[IN_SMEM] + [ANYWHERE] * (3 + len(after)),
        out_specs=[IN_VMEM] * 3,
        out_shape=[shape(w.shape) for w in weights],
        scratch_shapes=[pltpu.SemaphoreType.DMA((12,))],
        compiler_params=pltpu.CompilerParams(vmem_limit_bytes=16 * MIB),
        cost_estimate=pl.CostEstimate(flops=0, bytes_accessed=6 * MIB, transcendentals=0),
        name="stage_weights",
    )(order, *weights, *after)


def gathered(x_refs, at, w_ref):
    width = x_refs[0].shape[1]
    total = None
    for p, x_ref in enumerate(x_refs):
        term = dot(x_ref[at, :], w_ref[p * width : (p + 1) * width, :])
        total = term if total is None else total + term
    return total.astype(BF16)


def halo_kernel(x0, x1, x2, x3, wk, wv, out_ref):
    rows = x0.shape[0]
    at = slice(rows - STRIDE, rows)
    out_ref[:STRIDE, :] = gathered((x0, x1, x2, x3), at, wk)
    out_ref[STRIDE:, :] = gathered((x0, x1, x2, x3), at, wv)


def project_kernel(x0, x1, x2, x3, wq, wk, wv, halo, q_ref, k_ref, v_ref):
    rows = x0.shape[0]
    xs = (x0, x1, x2, x3)
    last = slice(rows - STRIDE, rows)
    k_ref[last, :] = halo[:STRIDE, :]
    v_ref[last, :] = halo[STRIDE:, :]
    for w, out, upto in ((wq, q_ref, rows), (wk, k_ref, rows - STRIDE), (wv, v_ref, rows - STRIDE)):
        out[:upto, :] = gathered(xs, slice(0, upto), w)


def softmax_columns(s):
    m = jnp.maximum(jnp.max(s, 0, keepdims=True), FLOOR)
    p = jnp.exp2((s - m) * SCALE2)
    total = jnp.maximum(jnp.sum(p, 0, keepdims=True), 1.0)
    return p, total, m * SCALE2 + jnp.log2(total)


def local_kernel(pos_ref, q_ref, k_ref, v_ref, halo_ref, *outs):
    out_refs, lse_refs = outs[:CHUNKS], outs[CHUNKS:]
    owners, message, _ = out_refs[0].shape
    groups = message // ROWS // SUB
    block = pos_ref[0]
    u = lax.broadcasted_iota(jnp.int32, (STRIDE, STRIDE), 0)
    t = lax.broadcasted_iota(jnp.int32, (STRIDE, STRIDE), 1)
    current = u <= t
    low = jnp.where(block == 0, -1e30, 0.0).astype(F32)
    for r in range(ROWS):
        lses = []
        here = slice(r * STRIDE, (r + 1) * STRIDE)
        back = slice((r - 1) * STRIDE, r * STRIDE)
        for h in range(HEADS):
            cols = slice(h * DH, (h + 1) * DH)
            q = q_ref[here, cols]
            k_prev = k_ref[back, cols] if r else halo_ref[:STRIDE, cols]
            v_prev = v_ref[back, cols] if r else halo_ref[STRIDE:, cols]
            s_prev = dot_t(k_prev, q)
            if r == 0:
                s_prev = s_prev + low
            p, total, lse = softmax_columns(jnp.where(current, dot_t(k_ref[here, cols], q), s_prev))
            p_now = jnp.where(current, p, 0.0).astype(BF16)
            p_prev = jnp.where(current, 0.0, p).astype(BF16)
            o = dot_l(v_ref[here, cols], p_now) + dot_l(v_prev, p_prev)
            o = (o * (1.0 / total)).T
            lses.append(lse)
            for d in range(owners):
                for i in range(CHUNKS):
                    for g in range(groups):
                        at = ((d * CHUNKS + i) * groups + g) * SUB
                        to = (g * ROWS + r) * SUB
                        out_refs[i][d, to : to + SUB, cols] = o[at : at + SUB]
        lses.append(jnp.zeros((128 - HEADS, STRIDE), F32))
        turned = jnp.concatenate(lses, 0).T
        for i in range(CHUNKS):
            for g in range(groups):
                total = None
                for d in range(owners):
                    at = ((d * CHUNKS + i) * groups + g) * SUB
                    moved = pltpu.roll(turned[at : at + SUB], 8 * d, 1)
                    total = moved if total is None else total + moved
                to = (g * ROWS + r) * SUB
                lse_refs[i][to : to + SUB, :] = total


def local_part(pos, q, k, v, halo, owners, after):
    rows, width = q.shape
    message = rows // owners // CHUNKS
    shapes = [shape((owners, message, width), F32)] * CHUNKS + [shape((message, 128), F32)] * CHUNKS
    outs = call(local_kernel, "local_part", 5, shapes, (pos, q, k, v, halo), after)
    return list(zip(outs[:CHUNKS], outs[CHUNKS:]))


def column_kernel(x0, x1, x2, x3, wq, wk, wv, out_ref, *scratch):
    owners, message, _ = scratch[0].shape
    groups = message // (ROWS * SUB)
    everything = slice(0, owners * message)
    for w, a in zip((wq, wk, wv), scratch):
        a[...] = gathered((x0, x1, x2, x3), everything, w).reshape(a.shape)
    part = ROWS * SUB
    size = owners * part

    j = lax.broadcasted_iota(jnp.int32, (size, size), 0)
    i = lax.broadcasted_iota(jnp.int32, (size, size), 1)
    earlier = jnp.logical_and(i % SUB == j % SUB, i > j)
    stats = []
    for g in range(groups):
        at = slice(g * part, (g + 1) * part)
        lses = []
        for h in range(HEADS):
            cols = slice(h * DH, (h + 1) * DH)
            q, k, v = (a[:, at, cols].reshape(size, DH) for a in scratch)
            p, total, lse = softmax_columns(jnp.where(earlier, dot_t(k, q), -1e30))
            o = (dot_l(v, p.astype(BF16)) * (1.0 / total)).T.astype(BF16)
            rows = slice(h * message + g * part, h * message + (g + 1) * part)
            out_ref[:, rows, :] = o.reshape(owners, part, DH)
            lses.append(lse)
        stats.append(jnp.concatenate(lses + lses, 0))
    upper = lax.broadcasted_iota(jnp.int32, (8, 128), 0) < HEADS
    blank = [jnp.zeros((8, 128 - message), F32)] if message < 128 else []
    for n in range(owners):
        x = jnp.concatenate([s[:, n * part : (n + 1) * part] for s in stats] + blank, 1)
        hi = x.astype(BF16).astype(F32)
        mid = (x - hi).astype(BF16).astype(F32)
        lo = x - hi - mid
        tail = jnp.concatenate([jnp.where(upper, hi, lo), jnp.where(upper, mid, 0.0)], 0)
        out_ref[n, HEADS * message : HEADS * message + 16, :] = tail.astype(BF16)


def column_part(pieces, weights, after):
    owners, message, width = pieces[0].shape
    dims = shape((owners, HEADS * message + 16, DH))
    scratch = [pltpu.VMEM((owners, message, width), BF16)] * 3
    pieces = [x.reshape(owners * message, width) for x in pieces]
    return call(column_kernel, "column_part", 6, dims, (*pieces, *weights), after, scratch)


def mix_kernel(pos_ref, loc_ref, lse_ref, col_ref, own_ref, send_ref, mixed):
    owners, message, _ = loc_ref.shape
    groups = message // (ROWS * SUB)
    base = HEADS * message
    tiles = []
    for d in range(owners):
        tail = col_ref[d, base : base + 16, :].astype(F32)
        tiles.append(tail[:8] + tail[8:])
    tiles.append(jnp.zeros((128 - 8 * owners, 128), F32))
    turned = jnp.concatenate(tiles, 0).T[:message]
    col_lse = turned + pltpu.roll(turned, 124, 1)
    loc_lse = lse_ref[...]
    top = jnp.maximum(col_lse, loc_lse)
    w_col = jnp.exp2(col_lse - top)
    w_loc = jnp.exp2(loc_lse - top)
    share = 1.0 / (w_col + w_loc)
    w_col = w_col * share
    w_loc = w_loc * share
    span = groups * SUB
    for d in range(owners):
        spot = slice(d * span, (d + 1) * span)
        for h in range(HEADS):
            cols = slice(h * DH, (h + 1) * DH)
            at = slice(8 * d + h, 8 * d + h + 1)
            col = col_ref[d, h * message : (h + 1) * message, :].astype(F32)
            both = loc_ref[d, :, cols] * w_loc[:, at] + col * w_col[:, at]
            for r in range(ROWS):
                starts = [(g * ROWS + r) * SUB for g in range(groups)]
                piece = jnp.concatenate([both[s : s + SUB] for s in starts], 0)
                mixed[r, spot, cols] = piece.astype(BF16)
    core = pos_ref[1]
    for x in range(2):
        own_ref[x] = mixed[2 * x + core]
        send_ref[x] = mixed[2 * x + 1 - core]


def mix(pos, column, local, lse, after):
    owners, message, width = local.shape
    tokens = owners * message // ROWS
    shapes = [shape((2, tokens, width))] * 2
    scratch = [pltpu.VMEM((ROWS, tokens, width), BF16)]
    return call(mix_kernel, "mix", 2, shapes, (pos, local, lse, column), after, scratch)


def out_kernel(pos_ref, a_ref, b_ref, wa_ref, wb_ref, send_ref, keep_ref):
    tokens, columns = send_ref.shape
    a = a_ref[...].reshape(2 * tokens, -1)
    b = b_ref[...].reshape(2 * tokens, -1)
    low_side = pos_ref[2] == 0
    tile = 512
    for n in range(0, columns, tile):
        at = slice(n, n + tile)
        total = dot(a, wa_ref[:, at]) + dot(b, wb_ref[:, at])
        send_ref[:, at] = jnp.where(low_side, total[tokens:], total[:tokens]).astype(BF16)
        keep_ref[:, at] = jnp.where(low_side, total[:tokens], total[tokens:])


def out_project(pos, own, other, w_own, w_other):
    dims = (own.shape[1], w_own.shape[1])
    shapes = [shape(dims), shape(dims, F32)]
    return call(out_kernel, "out_project", 3, shapes, (pos, own, other, w_own, w_other))


def join_kernel(*refs):
    out_ref = refs[-1]
    chunks = (len(refs) - 1) // 2
    tokens = refs[0].shape[0]
    span = 32 // chunks
    for i in range(chunks):
        keep, got = refs[2 * i], refs[2 * i + 1]
        for d in range(tokens // span):
            rows = slice(d * span, (d + 1) * span)
            at = (d * chunks + i) * span
            total = keep[rows, :] + got[rows, :].astype(F32)
            out_ref[at : at + span, :] = total.astype(BF16)


def join(pairs):
    columns = pairs[0][0].shape[1]
    args = [x for pair in pairs for x in pair]
    return call(join_kernel, "join", 2, shape((STRIDE, columns)), args)


def swap(value, distance):
    return lax.ppermute(value, "head", [(i, i ^ distance) for i in range(4)])


def exchange(messages):
    return lax.all_to_all(messages, "seq", split_axis=0, concat_axis=0, tiled=True)


def gather(own):
    far = swap(own, 2)
    return own, swap(own, 1), far, swap(far, 1)


def chunked(tokens, w_query, w_key, w_value, w_out):
    owners = lax.axis_size("seq")
    head = lax.axis_index("head")
    block = lax.axis_index("seq")
    order = jnp.bitwise_xor(jnp.arange(4, dtype=jnp.int32), head.astype(jnp.int32))
    pos = jnp.stack([block, head % 2, head // 2]).astype(jnp.int32)
    rows, width = tokens.shape

    pieces = gather(tokens)
    messages = pack(tokens, owners)
    classes = [exchange(m) for m in messages]
    weights = stage(order, (w_query, w_key, w_value), (messages[0], pieces[1]))
    w_other = swap(w_out, 1)
    own_halo = call(
        halo_kernel, "project_halo", 1.5, shape((2 * STRIDE, width)), (*pieces, *weights[1:])
    )
    halo = lax.ppermute(own_halo, "seq", [(i, i + 1) for i in range(owners - 1)])
    q, k, v = call(
        project_kernel,
        "project_block",
        7,
        [shape((rows, width))] * 3,
        (*pieces, *weights, own_halo),
    )
    columns, after = [], (q,)
    for i, c in enumerate(classes):
        columns.append(column_part(gather(c), weights, after))
        if i == 0:
            locals_ = local_part(pos, q, k, v, halo, owners, (columns[0],))
            after = (locals_[-1][-1],)
    pairs, after = [], (columns[-1],)
    for column, (local, lse) in zip(columns, locals_):
        own, send = mix(pos, exchange(column), local, lse, after)
        out, keep = out_project(pos, own, swap(send, 1), w_out, w_other)
        pairs.append((keep, swap(out, 2)))
        after = (pairs[-1][1],)
    return join(pairs)


def from_behind(value, axis, by):
    peers = lax.axis_size(axis)
    pairs = [(i, i + by) for i in range(peers) if 0 <= i + by < peers]
    return lax.ppermute(value, axis, pairs)


def general(tokens, w_query, w_key, w_value, w_out):
    tok_rows = tokens.shape[0]
    head_width = w_query.shape[1]
    head_count = head_width // DH
    score_scale = DH ** (-0.5)
    shard_piece = lax.all_gather(tokens, "head", axis=1, tiled=True)
    query_full, key_full, value_full = tuple(
        (
            jnp.dot(shard_piece, weight, preferred_element_type=jnp.float32)
            for weight in (w_query, w_key, w_value)
        )
    )
    query = query_full.astype(jnp.bfloat16).reshape(tok_rows, head_count, DH)
    key_heads = key_full.astype(jnp.bfloat16).reshape(tok_rows, head_count, DH)
    value_heads = value_full.astype(jnp.bfloat16).reshape(tok_rows, head_count, DH)
    prev_keys, prev_values = from_behind((key_heads[-STRIDE:], value_heads[-STRIDE:]), "seq", 1)
    blocks = tok_rows // STRIDE
    extended_keys = jnp.concatenate([prev_keys, key_heads], 0)
    extended_values = jnp.concatenate([prev_values, value_heads], 0)
    window_keys = jnp.concatenate(
        [
            extended_keys[:tok_rows].reshape(blocks, STRIDE, head_count, DH),
            extended_keys[STRIDE:].reshape(blocks, STRIDE, head_count, DH),
        ],
        1,
    )
    window_values = jnp.concatenate(
        [
            extended_values[:tok_rows].reshape(blocks, STRIDE, head_count, DH),
            extended_values[STRIDE:].reshape(blocks, STRIDE, head_count, DH),
        ],
        1,
    )
    query_blocks = query.reshape(blocks, STRIDE, head_count, DH)
    scores = (
        jnp.einsum("bthd,buhd->bhtu", query_blocks, window_keys, preferred_element_type=jnp.float32)
        * score_scale
    )
    first_position = lax.axis_index("seq") * tok_rows
    block_index = jnp.arange(blocks)[:, None, None, None]
    query_index = jnp.arange(STRIDE)[None, None, :, None]
    key_index = jnp.arange(2 * STRIDE)[None, None, None, :]
    allowed = (
        (key_index > query_index)
        & (key_index <= query_index + STRIDE)
        & (first_position + block_index * STRIDE + key_index - STRIDE >= 0)
    )
    local_top = jnp.max(jnp.where(allowed, scores, -1e30), axis=-1)
    local_weights = jnp.where(allowed, jnp.exp(scores - local_top[..., None]), 0.0)
    local_total = jnp.sum(local_weights, axis=-1)
    local_out = jnp.einsum(
        "bhtu,buhd->bthd",
        local_weights.astype(jnp.bfloat16),
        window_values,
        preferred_element_type=jnp.float32,
    )
    local_out = local_out.reshape(tok_rows, head_count, DH)
    local_top = local_top.transpose(0, 2, 1).reshape(tok_rows, head_count)
    local_total = local_total.transpose(0, 2, 1).reshape(tok_rows, head_count)
    row_count = tok_rows // STRIDE
    query_class = lax.all_to_all(
        query.reshape(row_count, STRIDE, head_count, DH),
        "seq",
        split_axis=1,
        concat_axis=0,
        tiled=True,
    )
    key_class = lax.all_to_all(
        key_heads.reshape(row_count, STRIDE, head_count, DH),
        "seq",
        split_axis=1,
        concat_axis=0,
        tiled=True,
    )
    value_class = lax.all_to_all(
        value_heads.reshape(row_count, STRIDE, head_count, DH),
        "seq",
        split_axis=1,
        concat_axis=0,
        tiled=True,
    )
    row_total = query_class.shape[0]
    class_scores = (
        jnp.einsum("rchd,schd->chrs", query_class, key_class, preferred_element_type=jnp.float32)
        * score_scale
    )
    earlier = (
        jnp.arange(row_total)[None, None, :, None] > jnp.arange(row_total)[None, None, None, :]
    )
    class_top = jnp.max(jnp.where(earlier, class_scores, -1e30), axis=-1)
    class_weights = jnp.where(earlier, jnp.exp(class_scores - class_top[..., None]), 0.0)
    class_total = jnp.sum(class_weights, axis=-1)
    summed = jnp.einsum(
        "chrs,schd->rchd",
        class_weights.astype(jnp.bfloat16),
        value_class,
        preferred_element_type=jnp.float32,
    )
    floor_total = jnp.maximum(class_total, 1.0).transpose(2, 0, 1)
    class_out = (summed / floor_total[..., None]).astype(jnp.bfloat16)
    class_top_rows = class_top.transpose(2, 0, 1)
    class_total_rows = class_total.transpose(2, 0, 1)
    column_out = class_out
    column_top = class_top_rows
    column_total = class_total_rows
    column_out, column_top, column_total = (
        lax.all_to_all(column_out, "seq", split_axis=0, concat_axis=1, tiled=True),
        lax.all_to_all(
            column_top.astype(jnp.bfloat16), "seq", split_axis=0, concat_axis=1, tiled=True
        ).astype(column_top.dtype),
        lax.all_to_all(
            column_total.astype(jnp.bfloat16), "seq", split_axis=0, concat_axis=1, tiled=True
        ).astype(column_total.dtype),
    )
    column_out = column_out.reshape(tok_rows, head_count, DH)
    column_top = column_top.reshape(tok_rows, head_count)
    column_total = column_total.reshape(tok_rows, head_count)
    top_score = jnp.maximum(local_top, column_top)
    local_weight = jnp.exp(local_top - top_score)
    column_weight = column_total * jnp.exp(column_top - top_score)
    denominator = local_total * local_weight + column_weight
    mixed = (
        local_out * local_weight[..., None]
        + column_out.astype(jnp.float32) * column_weight[..., None]
    ) / denominator[..., None]
    mixed = mixed.astype(jnp.bfloat16).reshape(tok_rows, head_width)
    return lax.psum_scatter(
        jnp.dot(mixed, w_out, preferred_element_type=jnp.float32).astype(jnp.bfloat16),
        "head",
        scatter_dimension=0,
        tiled=True,
    )


def shards(tokens, w_query, w_key, w_value, w_out):
    rows, width = w_query.shape
    fits = (
        lax.axis_size("seq") == STRIDE // 32
        and lax.axis_size("head") == 4
        and tokens.shape == (ROWS * STRIDE, HEADS * DH)
        and (rows, width) == (4 * HEADS * DH, HEADS * DH)
    )
    plan = chunked if fits else general
    return plan(tokens, w_query, w_key, w_value, w_out)


def solution(mesh):
    in_specs = (
        P("seq", "head"),
        P(None, "head"),
        P(None, "head"),
        P(None, "head"),
        P("head", None),
    )
    out_specs = P(("seq", "head"), None)
    return jax.shard_map(shards, mesh=mesh, in_specs=in_specs, out_specs=out_specs, check_vma=False)
```

```python
import jax
import jax.numpy as jnp
from jax import lax
from jax.experimental import pallas as pl
from jax.experimental.pallas import tpu as pltpu
from jax.sharding import PartitionSpec as P

DH = 128
STRIDE = 256
HEADS = 4
ROWS = 4
SUB = 8
CHUNKS = 2
SCALE2 = DH ** (-0.5) * 1.4426950408889634
FLOOR = -1e29
MIB = 1024 * 1024
F32 = jnp.float32
BF16 = jnp.bfloat16


ANYWHERE = pl.BlockSpec(memory_space=pl.ANY)
IN_VMEM = pl.BlockSpec(memory_space=pltpu.VMEM)
IN_SMEM = pl.BlockSpec(memory_space=pltpu.SMEM)


def call(body, name, micros, out_shape, args, after=(), scratch=(), mib=16):
    specs = [IN_SMEM if x.dtype == jnp.int32 else IN_VMEM for x in args]
    extra = len(after)

    def run(*refs):
        n = len(args)
        body(*refs[:n], *refs[n + extra :])

    return pl.pallas_call(
        run,
        in_specs=specs + [ANYWHERE] * extra,
        out_specs=jax.tree.map(lambda _: IN_VMEM, out_shape),
        out_shape=out_shape,
        scratch_shapes=list(scratch),
        compiler_params=pltpu.CompilerParams(vmem_limit_bytes=mib * MIB),
        cost_estimate=pl.CostEstimate(
            flops=int(micros * 1.1e9), bytes_accessed=MIB, transcendentals=0
        ),
        name=name,
    )(*args, *after)


def fence(value, *after):
    return pl.pallas_call(
        lambda *refs: None,
        in_specs=[ANYWHERE] * (1 + len(after)),
        out_specs=ANYWHERE,
        out_shape=jax.ShapeDtypeStruct(value.shape, value.dtype),
        input_output_aliases={0: 0},
        cost_estimate=pl.CostEstimate(flops=0, bytes_accessed=0, transcendentals=0),
        name="fence",
    )(value, *after)


def in_hbm(value):
    return pltpu.with_memory_space_constraint(value, pltpu.HBM)


def shape(dims, dtype=BF16):
    return jax.ShapeDtypeStruct(tuple(dims), dtype)


def dot(a, b):
    return jnp.dot(a, b, preferred_element_type=F32)


def dot_t(a, b):
    return lax.dot_general(a, b, (((1,), (1,)), ((), ())), preferred_element_type=F32)


def dot_l(a, b):
    return lax.dot_general(a, b, (((0,), (0,)), ((), ())), preferred_element_type=F32)


def pack_kernel(tok_hbm, *rest):
    out_refs, (tok_ref, sems) = rest[:-2], rest[-2:]
    owners = out_refs[0].shape[0]
    per_owner = STRIDE // owners
    groups = per_owner // SUB
    per_chunk = groups // CHUNKS
    spans = [slice(r * STRIDE, (r + 1) * STRIDE) for r in range(ROWS)]
    copies = [
        pltpu.make_async_copy(tok_hbm.at[at], tok_ref.at[at], sems.at[r])
        for r, at in enumerate(spans)
    ]
    for c in copies:
        c.start()
    for c in copies:
        c.wait()
    for d in range(owners):
        rows = [
            tok_ref[r * STRIDE + d * per_owner : r * STRIDE + (d + 1) * per_owner, :].astype(F32)
            for r in range(ROWS)
        ]
        for g in range(groups):
            piece = jnp.concatenate([x[g * SUB : (g + 1) * SUB] for x in rows], 0)
            at = (g % per_chunk) * ROWS * SUB
            out_refs[g // per_chunk][d, at : at + ROWS * SUB, :] = piece.astype(BF16)


def pack(tokens, owners):
    message = tokens.shape[0] // owners // CHUNKS
    return pl.pallas_call(
        pack_kernel,
        in_specs=[ANYWHERE],
        out_specs=[IN_VMEM] * CHUNKS,
        out_shape=[shape((owners, message, tokens.shape[1]))] * CHUNKS,
        scratch_shapes=[pltpu.VMEM(tokens.shape, BF16), pltpu.SemaphoreType.DMA((ROWS,))],
        compiler_params=pltpu.CompilerParams(vmem_limit_bytes=8 * MIB),
        cost_estimate=pl.CostEstimate(flops=0, bytes_accessed=2 * MIB, transcendentals=0),
        name="pack_tokens",
    )(in_hbm(tokens))


def stage_kernel(order_ref, wq, wk, wv, wo, *rest):
    oq, ok, ov, oo, sems = rest[-5:]
    copies = []
    for w, o, ordered in ((wq, oq, True), (wk, ok, True), (wv, ov, True), (wo, oo, False)):
        part = w.shape[0] // 4
        for p in range(4):
            source = pl.multiple_of(order_ref[p] * part, part) if ordered else p * part
            to = slice(p * part, (p + 1) * part)
            sem = sems.at[len(copies)]
            copies.append(pltpu.make_async_copy(w.at[pl.ds(source, part)], o.at[to], sem))
    for c in copies:
        c.start()
    for c in copies:
        c.wait()


def stage(order, weights, after):
    return pl.pallas_call(
        stage_kernel,
        in_specs=[IN_SMEM] + [ANYWHERE] * (4 + len(after)),
        out_specs=[IN_VMEM] * 4,
        out_shape=[pltpu.VMEM(w.shape, BF16) for w in weights],
        scratch_shapes=[pltpu.SemaphoreType.DMA((16,))],
        compiler_params=pltpu.CompilerParams(vmem_limit_bytes=16 * MIB),
        cost_estimate=pl.CostEstimate(flops=0, bytes_accessed=8 * MIB, transcendentals=0),
        name="stage_weights",
    )(order, *[in_hbm(w) for w in weights], *after)


def gathered(x_refs, at, w_ref):
    width = x_refs[0].shape[1]
    total = None
    for p, x_ref in enumerate(x_refs):
        term = dot(x_ref[at, :], w_ref[p * width : (p + 1) * width, :])
        total = term if total is None else total + term
    return total.astype(BF16)


def halo_kernel(x0, x1, x2, x3, wk, wv, out_ref):
    rows = x0.shape[0]
    at = slice(rows - STRIDE, rows)
    out_ref[:STRIDE, :] = gathered((x0, x1, x2, x3), at, wk)
    out_ref[STRIDE:, :] = gathered((x0, x1, x2, x3), at, wv)


def project_kernel(x0, x1, x2, x3, wq, wk, wv, halo, q_ref, k_ref, v_ref):
    rows = x0.shape[0]
    xs = (x0, x1, x2, x3)
    last = slice(rows - STRIDE, rows)
    k_ref[last, :] = halo[:STRIDE, :]
    v_ref[last, :] = halo[STRIDE:, :]
    for w, out, upto in ((wq, q_ref, rows), (wk, k_ref, rows - STRIDE), (wv, v_ref, rows - STRIDE)):
        out[:upto, :] = gathered(xs, slice(0, upto), w)


def softmax_columns(s):
    m = jnp.maximum(jnp.max(s, 0, keepdims=True), FLOOR)
    p = jnp.exp2((s - m) * SCALE2)
    total = jnp.maximum(jnp.sum(p, 0, keepdims=True), 1.0)
    return p, total, m * SCALE2 + jnp.log2(total)


def local_kernel(pos_ref, q_ref, k_ref, v_ref, halo_ref, *outs):
    out_refs, lse_refs = outs[:CHUNKS], outs[CHUNKS:]
    owners, message, _ = out_refs[0].shape
    groups = message // ROWS // SUB
    block = pos_ref[0]
    u = lax.broadcasted_iota(jnp.int32, (STRIDE, STRIDE), 0)
    t = lax.broadcasted_iota(jnp.int32, (STRIDE, STRIDE), 1)
    current = u <= t
    low = jnp.where(block == 0, -1e30, 0.0).astype(F32)
    for r in range(ROWS):
        lses = []
        here = slice(r * STRIDE, (r + 1) * STRIDE)
        back = slice((r - 1) * STRIDE, r * STRIDE)
        for h in range(HEADS):
            cols = slice(h * DH, (h + 1) * DH)
            q = q_ref[here, cols]
            k_prev = k_ref[back, cols] if r else halo_ref[:STRIDE, cols]
            v_prev = v_ref[back, cols] if r else halo_ref[STRIDE:, cols]
            s_prev = dot_t(k_prev, q)
            if r == 0:
                s_prev = s_prev + low
            p, total, lse = softmax_columns(jnp.where(current, dot_t(k_ref[here, cols], q), s_prev))
            p_now = jnp.where(current, p, 0.0).astype(BF16)
            p_prev = jnp.where(current, 0.0, p).astype(BF16)
            o = dot_l(v_ref[here, cols], p_now) + dot_l(v_prev, p_prev)
            o = (o * (1.0 / total)).T
            lses.append(lse)
            for d in range(owners):
                for i in range(CHUNKS):
                    for g in range(groups):
                        at = ((d * CHUNKS + i) * groups + g) * SUB
                        to = (g * ROWS + r) * SUB
                        out_refs[i][d, to : to + SUB, cols] = o[at : at + SUB]
        lses.append(jnp.zeros((128 - HEADS, STRIDE), F32))
        turned = jnp.concatenate(lses, 0).T
        for i in range(CHUNKS):
            for g in range(groups):
                total = None
                for d in range(owners):
                    at = ((d * CHUNKS + i) * groups + g) * SUB
                    moved = pltpu.roll(turned[at : at + SUB], 8 * d, 1)
                    total = moved if total is None else total + moved
                to = (g * ROWS + r) * SUB
                lse_refs[i][to : to + SUB, :] = total


def local_part(pos, q, k, v, halo, owners, after):
    rows, width = q.shape
    message = rows // owners // CHUNKS
    shapes = [shape((owners, message, width), F32)] * CHUNKS + [shape((message, 128), F32)] * CHUNKS
    outs = call(local_kernel, "local_part", 5, shapes, (pos, q, k, v, halo), after)
    return list(zip(outs[:CHUNKS], outs[CHUNKS:]))


def column_kernel(x0, x1, x2, x3, wq, wk, wv, out_ref, *scratch):
    owners, message, _ = scratch[0].shape
    groups = message // (ROWS * SUB)
    everything = slice(0, owners * message)
    for w, a in zip((wq, wk, wv), scratch):
        a[...] = gathered((x0, x1, x2, x3), everything, w).reshape(a.shape)
    part = ROWS * SUB
    size = owners * part

    j = lax.broadcasted_iota(jnp.int32, (size, size), 0)
    i = lax.broadcasted_iota(jnp.int32, (size, size), 1)
    earlier = jnp.logical_and(i % SUB == j % SUB, i > j)
    stats = []
    for g in range(groups):
        at = slice(g * part, (g + 1) * part)
        lses = []
        for h in range(HEADS):
            cols = slice(h * DH, (h + 1) * DH)
            q, k, v = (a[:, at, cols].reshape(size, DH) for a in scratch)
            p, total, lse = softmax_columns(jnp.where(earlier, dot_t(k, q), -1e30))
            o = (dot_l(v, p.astype(BF16)) * (1.0 / total)).T.astype(BF16)
            rows = slice(h * message + g * part, h * message + (g + 1) * part)
            out_ref[:, rows, :] = o.reshape(owners, part, DH)
            lses.append(lse)
        stats.append(jnp.concatenate(lses + lses, 0))
    upper = lax.broadcasted_iota(jnp.int32, (8, 128), 0) < HEADS
    blank = [jnp.zeros((8, 128 - message), F32)] if message < 128 else []
    for n in range(owners):
        x = jnp.concatenate([s[:, n * part : (n + 1) * part] for s in stats] + blank, 1)
        hi = x.astype(BF16).astype(F32)
        mid = (x - hi).astype(BF16).astype(F32)
        lo = x - hi - mid
        tail = jnp.concatenate([jnp.where(upper, hi, lo), jnp.where(upper, mid, 0.0)], 0)
        out_ref[n, HEADS * message : HEADS * message + 16, :] = tail.astype(BF16)


def column_part(pieces, weights, after):
    owners, message, width = pieces[0].shape
    dims = shape((owners, HEADS * message + 16, DH))
    scratch = [pltpu.VMEM((owners, message, width), BF16)] * 3
    pieces = [x.reshape(owners * message, width) for x in pieces]
    return call(column_kernel, "column_part", 6, dims, (*pieces, *weights), after, scratch)


def mix_kernel(pos_ref, loc_ref, lse_ref, col_ref, own_ref, send_ref, mixed):
    owners, message, _ = loc_ref.shape
    groups = message // (ROWS * SUB)
    base = HEADS * message
    tiles = []
    for d in range(owners):
        tail = col_ref[d, base : base + 16, :].astype(F32)
        tiles.append(tail[:8] + tail[8:])
    tiles.append(jnp.zeros((128 - 8 * owners, 128), F32))
    turned = jnp.concatenate(tiles, 0).T[:message]
    col_lse = turned + pltpu.roll(turned, 124, 1)
    loc_lse = lse_ref[...]
    top = jnp.maximum(col_lse, loc_lse)
    w_col = jnp.exp2(col_lse - top)
    w_loc = jnp.exp2(loc_lse - top)
    share = 1.0 / (w_col + w_loc)
    w_col = w_col * share
    w_loc = w_loc * share
    span = groups * SUB
    for d in range(owners):
        spot = slice(d * span, (d + 1) * span)
        for h in range(HEADS):
            cols = slice(h * DH, (h + 1) * DH)
            at = slice(8 * d + h, 8 * d + h + 1)
            col = col_ref[d, h * message : (h + 1) * message, :].astype(F32)
            both = loc_ref[d, :, cols] * w_loc[:, at] + col * w_col[:, at]
            for r in range(ROWS):
                starts = [(g * ROWS + r) * SUB for g in range(groups)]
                piece = jnp.concatenate([both[s : s + SUB] for s in starts], 0)
                mixed[r, spot, cols] = piece.astype(BF16)
    core = pos_ref[1]
    for x in range(2):
        own_ref[x] = mixed[2 * x + core]
        send_ref[x] = mixed[2 * x + 1 - core]


def mix(pos, column, local, lse, after):
    owners, message, width = local.shape
    tokens = owners * message // ROWS
    shapes = [shape((2, tokens, width))] * 2
    scratch = [pltpu.VMEM((ROWS, tokens, width), BF16)]
    return call(mix_kernel, "mix", 2, shapes, (pos, local, lse, column), after, scratch)


def out_kernel(pos_ref, a_ref, b_ref, wa_ref, wb_ref, send_ref, keep_ref):
    tokens, columns = send_ref.shape
    a = a_ref[...].reshape(2 * tokens, -1)
    b = b_ref[...].reshape(2 * tokens, -1)
    low_side = pos_ref[2] == 0
    tile = 512
    for n in range(0, columns, tile):
        at = slice(n, n + tile)
        total = dot(a, wa_ref[:, at]) + dot(b, wb_ref[:, at])
        send_ref[:, at] = jnp.where(low_side, total[tokens:], total[:tokens]).astype(BF16)
        keep_ref[:, at] = jnp.where(low_side, total[:tokens], total[tokens:])


def out_project(pos, own, other, w_own, w_other, after):
    dims = (own.shape[1], w_own.shape[1])
    shapes = [shape(dims), shape(dims, F32)]
    return call(out_kernel, "out_project", 2, shapes, (pos, own, other, w_own, w_other), after)


def join_kernel(*refs):
    out_ref = refs[-1]
    chunks = (len(refs) - 1) // 2
    tokens = refs[0].shape[0]
    span = 32 // chunks
    for i in range(chunks):
        keep, got = refs[2 * i], refs[2 * i + 1]
        for d in range(tokens // span):
            rows = slice(d * span, (d + 1) * span)
            at = (d * chunks + i) * span
            total = keep[rows, :] + got[rows, :].astype(F32)
            out_ref[at : at + span, :] = total.astype(BF16)


def join(pairs):
    columns = pairs[0][0].shape[1]
    args = [x for pair in pairs for x in pair]
    return call(join_kernel, "join", 2, shape((STRIDE, columns)), args)


def swap(value, distance):
    return lax.ppermute(value, "head", [(i, i ^ distance) for i in range(4)])


def exchange(messages):
    return lax.all_to_all(messages, "seq", split_axis=0, concat_axis=0, tiled=True)


def gather(own):
    far = swap(own, 2)
    return own, swap(own, 1), far, swap(far, 1)


def chunked(tokens, w_query, w_key, w_value, w_out):
    owners = lax.axis_size("seq")
    head = lax.axis_index("head")
    block = lax.axis_index("seq")
    order = jnp.bitwise_xor(jnp.arange(4, dtype=jnp.int32), head.astype(jnp.int32))
    pos = jnp.stack([block, head % 2, head // 2]).astype(jnp.int32)
    rows, width = tokens.shape

    pieces = gather(tokens)
    messages = pack(tokens, owners)
    classes = [exchange(m) for m in messages]
    *weights, w_own = stage(order, (w_query, w_key, w_value, w_out), (messages[0], pieces[1]))
    w_other = swap(w_out, 1)
    classes[0] = fence(classes[0], pieces[2], weights[0], w_other)
    own_halo = call(
        halo_kernel, "project_halo", 1.5, shape((2 * STRIDE, width)), (*pieces, *weights[1:])
    )
    halo = lax.ppermute(own_halo, "seq", [(i, i + 1) for i in range(owners - 1)])
    q, k, v = call(
        project_kernel,
        "project_block",
        7,
        [shape((rows, width))] * 3,
        (*pieces, *weights, own_halo),
        (classes[0],),
        mib=20,
    )
    columns, after = [], (q,)
    for i, c in enumerate(classes):
        columns.append(column_part(gather(c), weights, after))
        if i == 0:
            locals_ = local_part(pos, q, k, v, halo, owners, (columns[0],))
            after = (locals_[-1][-1],)
    pairs, after = [], ()
    for column, (local, lse) in zip(columns, locals_):
        own, send = mix(pos, exchange(column), local, lse, (columns[-1],))
        out, keep = out_project(pos, own, swap(send, 1), w_own, w_other, after)
        pairs.append((keep, swap(out, 2)))
        after = (pairs[-1][1],)
    return join(pairs)


def from_behind(value, axis, by):
    peers = lax.axis_size(axis)
    pairs = [(i, i + by) for i in range(peers) if 0 <= i + by < peers]
    return lax.ppermute(value, axis, pairs)


def general(tokens, w_query, w_key, w_value, w_out):
    tok_rows = tokens.shape[0]
    head_width = w_query.shape[1]
    head_count = head_width // DH
    score_scale = DH ** (-0.5)
    shard_piece = lax.all_gather(tokens, "head", axis=1, tiled=True)
    query_full, key_full, value_full = tuple(
        (
            jnp.dot(shard_piece, weight, preferred_element_type=jnp.float32)
            for weight in (w_query, w_key, w_value)
        )
    )
    query = query_full.astype(jnp.bfloat16).reshape(tok_rows, head_count, DH)
    key_heads = key_full.astype(jnp.bfloat16).reshape(tok_rows, head_count, DH)
    value_heads = value_full.astype(jnp.bfloat16).reshape(tok_rows, head_count, DH)
    prev_keys, prev_values = from_behind((key_heads[-STRIDE:], value_heads[-STRIDE:]), "seq", 1)
    blocks = tok_rows // STRIDE
    extended_keys = jnp.concatenate([prev_keys, key_heads], 0)
    extended_values = jnp.concatenate([prev_values, value_heads], 0)
    window_keys = jnp.concatenate(
        [
            extended_keys[:tok_rows].reshape(blocks, STRIDE, head_count, DH),
            extended_keys[STRIDE:].reshape(blocks, STRIDE, head_count, DH),
        ],
        1,
    )
    window_values = jnp.concatenate(
        [
            extended_values[:tok_rows].reshape(blocks, STRIDE, head_count, DH),
            extended_values[STRIDE:].reshape(blocks, STRIDE, head_count, DH),
        ],
        1,
    )
    query_blocks = query.reshape(blocks, STRIDE, head_count, DH)
    scores = (
        jnp.einsum("bthd,buhd->bhtu", query_blocks, window_keys, preferred_element_type=jnp.float32)
        * score_scale
    )
    first_position = lax.axis_index("seq") * tok_rows
    block_index = jnp.arange(blocks)[:, None, None, None]
    query_index = jnp.arange(STRIDE)[None, None, :, None]
    key_index = jnp.arange(2 * STRIDE)[None, None, None, :]
    allowed = (
        (key_index > query_index)
        & (key_index <= query_index + STRIDE)
        & (first_position + block_index * STRIDE + key_index - STRIDE >= 0)
    )
    local_top = jnp.max(jnp.where(allowed, scores, -1e30), axis=-1)
    local_weights = jnp.where(allowed, jnp.exp(scores - local_top[..., None]), 0.0)
    local_total = jnp.sum(local_weights, axis=-1)
    local_out = jnp.einsum(
        "bhtu,buhd->bthd",
        local_weights.astype(jnp.bfloat16),
        window_values,
        preferred_element_type=jnp.float32,
    )
    local_out = local_out.reshape(tok_rows, head_count, DH)
    local_top = local_top.transpose(0, 2, 1).reshape(tok_rows, head_count)
    local_total = local_total.transpose(0, 2, 1).reshape(tok_rows, head_count)
    row_count = tok_rows // STRIDE
    query_class = lax.all_to_all(
        query.reshape(row_count, STRIDE, head_count, DH),
        "seq",
        split_axis=1,
        concat_axis=0,
        tiled=True,
    )
    key_class = lax.all_to_all(
        key_heads.reshape(row_count, STRIDE, head_count, DH),
        "seq",
        split_axis=1,
        concat_axis=0,
        tiled=True,
    )
    value_class = lax.all_to_all(
        value_heads.reshape(row_count, STRIDE, head_count, DH),
        "seq",
        split_axis=1,
        concat_axis=0,
        tiled=True,
    )
    row_total = query_class.shape[0]
    class_scores = (
        jnp.einsum("rchd,schd->chrs", query_class, key_class, preferred_element_type=jnp.float32)
        * score_scale
    )
    earlier = (
        jnp.arange(row_total)[None, None, :, None] > jnp.arange(row_total)[None, None, None, :]
    )
    class_top = jnp.max(jnp.where(earlier, class_scores, -1e30), axis=-1)
    class_weights = jnp.where(earlier, jnp.exp(class_scores - class_top[..., None]), 0.0)
    class_total = jnp.sum(class_weights, axis=-1)
    summed = jnp.einsum(
        "chrs,schd->rchd",
        class_weights.astype(jnp.bfloat16),
        value_class,
        preferred_element_type=jnp.float32,
    )
    floor_total = jnp.maximum(class_total, 1.0).transpose(2, 0, 1)
    class_out = (summed / floor_total[..., None]).astype(jnp.bfloat16)
    class_top_rows = class_top.transpose(2, 0, 1)
    class_total_rows = class_total.transpose(2, 0, 1)
    column_out = class_out
    column_top = class_top_rows
    column_total = class_total_rows
    column_out, column_top, column_total = (
        lax.all_to_all(column_out, "seq", split_axis=0, concat_axis=1, tiled=True),
        lax.all_to_all(
            column_top.astype(jnp.bfloat16), "seq", split_axis=0, concat_axis=1, tiled=True
        ).astype(column_top.dtype),
        lax.all_to_all(
            column_total.astype(jnp.bfloat16), "seq", split_axis=0, concat_axis=1, tiled=True
        ).astype(column_total.dtype),
    )
    column_out = column_out.reshape(tok_rows, head_count, DH)
    column_top = column_top.reshape(tok_rows, head_count)
    column_total = column_total.reshape(tok_rows, head_count)
    top_score = jnp.maximum(local_top, column_top)
    local_weight = jnp.exp(local_top - top_score)
    column_weight = column_total * jnp.exp(column_top - top_score)
    denominator = local_total * local_weight + column_weight
    mixed = (
        local_out * local_weight[..., None]
        + column_out.astype(jnp.float32) * column_weight[..., None]
    ) / denominator[..., None]
    mixed = mixed.astype(jnp.bfloat16).reshape(tok_rows, head_width)
    return lax.psum_scatter(
        jnp.dot(mixed, w_out, preferred_element_type=jnp.float32).astype(jnp.bfloat16),
        "head",
        scatter_dimension=0,
        tiled=True,
    )


def shards(tokens, w_query, w_key, w_value, w_out):
    rows, width = w_query.shape
    fits = (
        lax.axis_size("seq") == STRIDE // 32
        and lax.axis_size("head") == 4
        and tokens.shape == (ROWS * STRIDE, HEADS * DH)
        and (rows, width) == (4 * HEADS * DH, HEADS * DH)
    )
    plan = chunked if fits else general
    return plan(tokens, w_query, w_key, w_value, w_out)


def solution(mesh):
    in_specs = (
        P("seq", "head"),
        P(None, "head"),
        P(None, "head"),
        P(None, "head"),
        P("head", None),
    )
    out_specs = P(("seq", "head"), None)
    return jax.shard_map(shards, mesh=mesh, in_specs=in_specs, out_specs=out_specs, check_vma=False)
```

```python
import functools

import jax
import jax.numpy as jnp
from jax import lax
from jax.experimental import pallas as pl
from jax.experimental.pallas import tpu as pltpu
from jax.sharding import PartitionSpec as P

DH = 128
STRIDE = 256
HEADS = 4
ROWS = 4
SUB = 8
NEAR = 4
SCALE2 = DH ** (-0.5) * 1.4426950408889634
FLOOR = -1e29
MIB = 1024 * 1024
F32 = jnp.float32
BF16 = jnp.bfloat16


ANYWHERE = pl.BlockSpec(memory_space=pl.ANY)
IN_VMEM = pl.BlockSpec(memory_space=pltpu.VMEM)
IN_SMEM = pl.BlockSpec(memory_space=pltpu.SMEM)


def call(body, name, micros, out_shape, args, after=(), scratch=(), mib=24):
    specs = [IN_SMEM if x.dtype == jnp.int32 else IN_VMEM for x in args]
    extra = len(after)

    def run(*refs):
        n = len(args)
        body(*refs[:n], *refs[n + extra :])

    return pl.pallas_call(
        run,
        in_specs=specs + [ANYWHERE] * extra,
        out_specs=jax.tree.map(lambda _: IN_VMEM, out_shape),
        out_shape=out_shape,
        scratch_shapes=list(scratch),
        compiler_params=pltpu.CompilerParams(vmem_limit_bytes=mib * MIB),
        cost_estimate=pl.CostEstimate(
            flops=int(micros * 1.1e9), bytes_accessed=MIB, transcendentals=0
        ),
        name=name,
    )(*args, *after)


def in_hbm(value):
    return pltpu.with_memory_space_constraint(value, pltpu.HBM)


def shape(dims, dtype=BF16):
    return jax.ShapeDtypeStruct(tuple(dims), dtype)


def dot(a, b):
    return jnp.dot(a, b, preferred_element_type=F32)


def dot_t(a, b):
    return lax.dot_general(a, b, (((1,), (1,)), ((), ())), preferred_element_type=F32)


def dot_l(a, b):
    return lax.dot_general(a, b, (((0,), (0,)), ((), ())), preferred_element_type=F32)


def pack_kernel(pos_ref, tok_hbm, *rest):
    out_refs, (tok_ref, sems) = rest[:-2], rest[-2:]
    per_owner = STRIDE // len(out_refs)
    part = ROWS * SUB
    spans = [slice(r * STRIDE, (r + 1) * STRIDE) for r in range(ROWS)]
    copies = [
        pltpu.make_async_copy(tok_hbm.at[at], tok_ref.at[at], sems.at[r])
        for r, at in enumerate(spans)
    ]
    for c in copies:
        c.start()
    for c in copies:
        c.wait()
    for k, out_ref in enumerate(out_refs):
        d = pos_ref[0] ^ k
        rows = [
            tok_ref[pl.ds(pl.multiple_of(r * STRIDE + d * per_owner, per_owner), per_owner), :]
            for r in range(ROWS)
        ]
        rows = [x.astype(F32) for x in rows]
        for g in range(per_owner // SUB):
            piece = jnp.concatenate([x[g * SUB : (g + 1) * SUB] for x in rows], 0)
            out_ref[g * part : (g + 1) * part, :] = piece.astype(BF16)


def pack(pos, tokens, owners):
    message = tokens.shape[0] // owners
    return pl.pallas_call(
        pack_kernel,
        in_specs=[IN_SMEM, ANYWHERE],
        out_specs=[IN_VMEM] * owners,
        out_shape=[shape((message, tokens.shape[1]))] * owners,
        scratch_shapes=[pltpu.VMEM(tokens.shape, BF16), pltpu.SemaphoreType.DMA((ROWS,))],
        compiler_params=pltpu.CompilerParams(vmem_limit_bytes=8 * MIB),
        cost_estimate=pl.CostEstimate(flops=0, bytes_accessed=2 * MIB, transcendentals=0),
        name="pack_tokens",
    )(pos, in_hbm(tokens))


def stage_kernel(order_ref, wq, wk, wv, wo, *rest):
    oq, ok, ov, oo, sems = rest[-5:]
    copies = []
    for w, o, ordered in ((wq, oq, True), (wk, ok, True), (wv, ov, True), (wo, oo, False)):
        part = w.shape[0] // 4
        for p in range(4):
            source = pl.multiple_of(order_ref[p] * part, part) if ordered else p * part
            to = slice(p * part, (p + 1) * part)
            sem = sems.at[len(copies)]
            copies.append(pltpu.make_async_copy(w.at[pl.ds(source, part)], o.at[to], sem))
    for c in copies:
        c.start()
    for c in copies:
        c.wait()


def stage(order, weights, after):
    return pl.pallas_call(
        stage_kernel,
        in_specs=[IN_SMEM] + [ANYWHERE] * (4 + len(after)),
        out_specs=[IN_VMEM] * 4,
        out_shape=[pltpu.VMEM(w.shape, BF16) for w in weights],
        scratch_shapes=[pltpu.SemaphoreType.DMA((16,))],
        compiler_params=pltpu.CompilerParams(vmem_limit_bytes=16 * MIB),
        cost_estimate=pl.CostEstimate(flops=0, bytes_accessed=8 * MIB, transcendentals=0),
        name="stage_weights",
    )(order, *[in_hbm(w) for w in weights], *after)


def gathered(x_refs, at, w_ref):
    width = x_refs[0].shape[1]
    total = None
    for p, x_ref in enumerate(x_refs):
        term = dot(x_ref[at, :], w_ref[p * width : (p + 1) * width, :])
        total = term if total is None else total + term
    return total.astype(BF16)


def halo_kernel(x0, x1, x2, x3, wk, wv, out_ref):
    rows = x0.shape[0]
    at = slice(rows - STRIDE, rows)
    out_ref[:STRIDE, :] = gathered((x0, x1, x2, x3), at, wk)
    out_ref[STRIDE:, :] = gathered((x0, x1, x2, x3), at, wv)


def project_kernel(x0, x1, x2, x3, wq, wk, wv, halo, q_ref, k_ref, v_ref):
    rows = x0.shape[0]
    xs = (x0, x1, x2, x3)
    last = slice(rows - STRIDE, rows)
    k_ref[last, :] = halo[:STRIDE, :]
    v_ref[last, :] = halo[STRIDE:, :]
    for w, out, upto in ((wq, q_ref, rows), (wk, k_ref, rows - STRIDE), (wv, v_ref, rows - STRIDE)):
        out[:upto, :] = gathered(xs, slice(0, upto), w)


def near_kernel(x0, x1, x2, x3, wq, wk, wv, q_ref, k_ref, v_ref):
    everything = slice(0, x0.shape[0])
    for w, out in ((wq, q_ref), (wk, k_ref), (wv, v_ref)):
        out[...] = gathered((x0, x1, x2, x3), everything, w)


def softmax_columns(s):
    m = jnp.maximum(jnp.max(s, 0, keepdims=True), FLOOR)
    p = jnp.exp2((s - m) * SCALE2)
    total = jnp.maximum(jnp.sum(p, 0, keepdims=True), 1.0)
    return p, total, m * SCALE2 + jnp.log2(total)


def local_kernel(pos_ref, q_ref, k_ref, v_ref, halo_ref, out_ref, lse_ref):
    owners, message, _ = out_ref.shape
    groups = message // ROWS // SUB
    block = pos_ref[0]
    u = lax.broadcasted_iota(jnp.int32, (STRIDE, STRIDE), 0)
    t = lax.broadcasted_iota(jnp.int32, (STRIDE, STRIDE), 1)
    current = u <= t
    low = jnp.where(block == 0, -1e30, 0.0).astype(F32)
    for r in range(ROWS):
        lses = []
        here = slice(r * STRIDE, (r + 1) * STRIDE)
        back = slice((r - 1) * STRIDE, r * STRIDE)
        for h in range(HEADS):
            cols = slice(h * DH, (h + 1) * DH)
            q = q_ref[here, cols]
            k_prev = k_ref[back, cols] if r else halo_ref[:STRIDE, cols]
            v_prev = v_ref[back, cols] if r else halo_ref[STRIDE:, cols]
            s_prev = dot_t(k_prev, q)
            if r == 0:
                s_prev = s_prev + low
            p, total, lse = softmax_columns(jnp.where(current, dot_t(k_ref[here, cols], q), s_prev))
            p_now = jnp.where(current, p, 0.0).astype(BF16)
            p_prev = jnp.where(current, 0.0, p).astype(BF16)
            o = dot_l(v_ref[here, cols], p_now) + dot_l(v_prev, p_prev)
            o = (o * (1.0 / total)).T
            lses.append(lse)
            for d in range(owners):
                for g in range(groups):
                    at = (d * groups + g) * SUB
                    to = (g * ROWS + r) * SUB
                    out_ref[d, to : to + SUB, cols] = o[at : at + SUB]
        lses.append(jnp.zeros((128 - HEADS, STRIDE), F32))
        turned = jnp.concatenate(lses, 0).T
        for g in range(groups):
            total = None
            for d in range(owners):
                at = (d * groups + g) * SUB
                moved = pltpu.roll(turned[at : at + SUB], 8 * (block ^ d), 1)
                total = moved if total is None else total + moved
            to = (g * ROWS + r) * SUB
            lse_ref[to : to + SUB, :] = total


def local_part(pos, q, k, v, halo, owners, after):
    rows, width = q.shape
    message = rows // owners
    shapes = [shape((owners, message, width), F32), shape((message, 128), F32)]
    return call(local_kernel, "local_part", 5, shapes, (pos, q, k, v, halo), after)


def column_kernel(pos_ref, x0, x1, x2, x3, wq, wk, wv, nq, nk, nv, *rest):
    out_refs, scratch = rest[:-3], rest[-3:]
    owners, message, width = scratch[0].shape
    groups = message // (ROWS * SUB)
    everything = slice(0, x0.shape[0])
    for w, near, a in zip((wq, wk, wv), (nq, nk, nv), scratch):
        a[:NEAR] = near[...].reshape(NEAR, message, width)
        far = gathered((x0, x1, x2, x3), everything, w)
        a[NEAR:] = far.reshape(owners - NEAR, message, width)
    part = ROWS * SUB
    size = owners * part

    def row_and_class(dim):
        i = lax.broadcasted_iota(jnp.int32, (size, size), dim)
        return ((i // part) ^ pos_ref[0]) * ROWS + (i % part) // SUB, i % SUB

    (row_j, class_j), (row_i, class_i) = row_and_class(0), row_and_class(1)
    earlier = jnp.logical_and(class_i == class_j, row_i > row_j)
    stats = []
    for g in range(groups):
        at = slice(g * part, (g + 1) * part)
        lses = []
        for h in range(HEADS):
            cols = slice(h * DH, (h + 1) * DH)
            q, k, v = (a[:, at, cols].reshape(size, DH) for a in scratch)
            p, total, lse = softmax_columns(jnp.where(earlier, dot_t(k, q), -1e30))
            o = (dot_l(v, p.astype(BF16)) * (1.0 / total)).T.astype(BF16)
            rows = slice(h * message + g * part, h * message + (g + 1) * part)
            for n in range(owners):
                out_refs[n][rows, :] = o[n * part : (n + 1) * part]
            lses.append(lse)
        stats.append(jnp.concatenate(lses + lses, 0))
    upper = lax.broadcasted_iota(jnp.int32, (8, 128), 0) < HEADS
    blank = [jnp.zeros((8, 128 - message), F32)] if message < 128 else []
    for n in range(owners):
        x = jnp.concatenate([s[:, n * part : (n + 1) * part] for s in stats] + blank, 1)
        hi = x.astype(BF16).astype(F32)
        mid = (x - hi).astype(BF16).astype(F32)
        lo = x - hi - mid
        tail = jnp.concatenate([jnp.where(upper, hi, lo), jnp.where(upper, mid, 0.0)], 0)
        out_refs[n][HEADS * message : HEADS * message + 16, :] = tail.astype(BF16)


def column_part(pos, pieces, weights, near, owners, after):
    tokens, width = pieces[0].shape
    message = tokens // (owners - NEAR)
    shapes = [shape((HEADS * message + 16, DH))] * owners
    scratch = [pltpu.VMEM((owners, message, width), BF16)] * 3
    args = (pos, *pieces, *weights, *near)
    return call(column_kernel, "column_part", 9, shapes, args, after, scratch)


def mix_kernel(first, pos_ref, loc_ref, lse_ref, *rest):
    col_refs, (own_ref, send_ref, mixed) = rest[:-3], rest[-3:]
    owners, message, _ = loc_ref.shape
    groups = message // (ROWS * SUB)
    base = HEADS * message
    tiles = [jnp.zeros((8, 128), F32)] * 16
    for n, col_ref in enumerate(col_refs):
        tail = col_ref[base : base + 16, :].astype(F32)
        tiles[first + n] = tail[:8] + tail[8:]
    turned = jnp.concatenate(tiles, 0).T[:message]
    col_lse = turned + pltpu.roll(turned, 124, 1)
    loc_lse = lse_ref[...]
    top = jnp.maximum(col_lse, loc_lse)
    w_col = jnp.exp2(col_lse - top)
    w_loc = jnp.exp2(loc_lse - top)
    share = 1.0 / (w_col + w_loc)
    w_col = w_col * share
    w_loc = w_loc * share
    span = groups * SUB
    for n, col_ref in enumerate(col_refs):
        k = first + n
        d = pos_ref[0] ^ k
        spot = slice(n * span, (n + 1) * span)
        for h in range(HEADS):
            cols = slice(h * DH, (h + 1) * DH)
            at = slice(8 * k + h, 8 * k + h + 1)
            col = col_ref[h * message : (h + 1) * message, :].astype(F32)
            both = loc_ref[d, :, cols] * w_loc[:, at] + col * w_col[:, at]
            for r in range(ROWS):
                starts = [(g * ROWS + r) * SUB for g in range(groups)]
                piece = jnp.concatenate([both[s : s + SUB] for s in starts], 0)
                mixed[r, spot, cols] = piece.astype(BF16)
    core = pos_ref[1]
    for x in range(2):
        own_ref[x] = mixed[2 * x + core]
        send_ref[x] = mixed[2 * x + 1 - core]


def mix(pos, first, columns, local, lse, after):
    _, message, width = local.shape
    tokens = len(columns) * message // ROWS
    shapes = [shape((2, tokens, width))] * 2
    scratch = [pltpu.VMEM((ROWS, tokens, width), BF16)]
    body = functools.partial(mix_kernel, first)
    return call(body, "mix", 2, shapes, (pos, local, lse, *columns), after, scratch)


def out_kernel(pos_ref, a_ref, b_ref, wa_ref, wb_ref, send_ref, keep_ref):
    tokens, columns = send_ref.shape
    a = a_ref[...].reshape(2 * tokens, -1)
    b = b_ref[...].reshape(2 * tokens, -1)
    low_side = pos_ref[2] == 0
    tile = 512
    for n in range(0, columns, tile):
        at = slice(n, n + tile)
        total = dot(a, wa_ref[:, at]) + dot(b, wb_ref[:, at])
        send_ref[:, at] = jnp.where(low_side, total[tokens:], total[:tokens]).astype(BF16)
        keep_ref[:, at] = jnp.where(low_side, total[:tokens], total[tokens:])


def out_project(pos, own, other, w_own, w_other, after):
    dims = (own.shape[1], w_own.shape[1])
    shapes = [shape(dims), shape(dims, F32)]
    return call(out_kernel, "out_project", 2, shapes, (pos, own, other, w_own, w_other), after)


def join_kernel(pos_ref, *refs):
    out_ref = refs[-1]
    span = STRIDE // 8
    k = 0
    for keep, got in zip(refs[0:-1:2], refs[1:-1:2]):
        for n in range(keep.shape[0] // span):
            rows = slice(n * span, (n + 1) * span)
            to = pl.ds(pl.multiple_of((pos_ref[0] ^ k) * span, span), span)
            out_ref[to, :] = (keep[rows, :] + got[rows, :].astype(F32)).astype(BF16)
            k += 1


def join(pos, pairs):
    columns = pairs[0][0].shape[1]
    args = [x for pair in pairs for x in pair]
    return call(join_kernel, "join", 2, shape((STRIDE, columns)), (pos, *args))


def swap(value, distance):
    return lax.ppermute(value, "head", [(i, i ^ distance) for i in range(4)])


def exchange(messages):
    n = len(messages)
    return [messages[0]] + [
        lax.ppermute(messages[k], "seq", [(i, i ^ k) for i in range(n)]) for k in range(1, n)
    ]


def gather(own):
    far = swap(own, 2)
    return own, swap(own, 1), far, swap(far, 1)


def chunked(tokens, w_query, w_key, w_value, w_out):
    owners = lax.axis_size("seq")
    head = lax.axis_index("head")
    block = lax.axis_index("seq")
    order = jnp.bitwise_xor(jnp.arange(4, dtype=jnp.int32), head.astype(jnp.int32))
    pos = jnp.stack([block, head % 2, head // 2]).astype(jnp.int32)
    rows, width = tokens.shape

    pieces = gather(tokens)
    sent = pack(pos, tokens, owners)
    messages = exchange(sent)
    *weights, w_own = stage(order, (w_query, w_key, w_value, w_out), (sent[0], pieces[1]))
    w_other = swap(w_out, 1)
    near_own = jnp.concatenate(messages[:NEAR], 0)
    far_own = jnp.concatenate(messages[NEAR:], 0)
    near_pieces, far_pieces = gather(near_own), gather(far_own)
    half = [shape((2 * STRIDE, width))]
    own_halo = call(
        halo_kernel, "project_halo", 1.5, half[0], (*pieces, *weights[1:]), (near_own,)
    )
    halo = lax.ppermute(own_halo, "seq", [(i, i + 1) for i in range(owners - 1)])
    q, k, v = call(
        project_kernel,
        "project_block",
        6,
        [shape((rows, width))] * 3,
        (*pieces, *weights, own_halo),
        (far_own,),
    )
    near = call(near_kernel, "project_near", 3, half * 3, (*near_pieces, *weights), (q,))
    local, lse = local_part(pos, q, k, v, halo, owners, (near[0],))
    columns = exchange(column_part(pos, far_pieces, weights, near, owners, (lse,)))
    pairs, after = [], ()
    for first, some in ((0, columns[:NEAR]), (NEAR, columns[NEAR:])):
        own, send = mix(pos, first, some, local, lse, tuple(x for x, _ in pairs))
        out, keep = out_project(pos, own, swap(send, 1), w_own, w_other, after)
        pairs.append((keep, swap(out, 2)))
        after = (pairs[0][1],)
    return join(pos, pairs)


def from_behind(value, axis, by):
    peers = lax.axis_size(axis)
    pairs = [(i, i + by) for i in range(peers) if 0 <= i + by < peers]
    return lax.ppermute(value, axis, pairs)


def general(tokens, w_query, w_key, w_value, w_out):
    tok_rows = tokens.shape[0]
    head_width = w_query.shape[1]
    head_count = head_width // DH
    score_scale = DH ** (-0.5)
    shard_piece = lax.all_gather(tokens, "head", axis=1, tiled=True)
    query_full, key_full, value_full = tuple(
        (
            jnp.dot(shard_piece, weight, preferred_element_type=jnp.float32)
            for weight in (w_query, w_key, w_value)
        )
    )
    query = query_full.astype(jnp.bfloat16).reshape(tok_rows, head_count, DH)
    key_heads = key_full.astype(jnp.bfloat16).reshape(tok_rows, head_count, DH)
    value_heads = value_full.astype(jnp.bfloat16).reshape(tok_rows, head_count, DH)
    prev_keys, prev_values = from_behind((key_heads[-STRIDE:], value_heads[-STRIDE:]), "seq", 1)
    blocks = tok_rows // STRIDE
    extended_keys = jnp.concatenate([prev_keys, key_heads], 0)
    extended_values = jnp.concatenate([prev_values, value_heads], 0)
    window_keys = jnp.concatenate(
        [
            extended_keys[:tok_rows].reshape(blocks, STRIDE, head_count, DH),
            extended_keys[STRIDE:].reshape(blocks, STRIDE, head_count, DH),
        ],
        1,
    )
    window_values = jnp.concatenate(
        [
            extended_values[:tok_rows].reshape(blocks, STRIDE, head_count, DH),
            extended_values[STRIDE:].reshape(blocks, STRIDE, head_count, DH),
        ],
        1,
    )
    query_blocks = query.reshape(blocks, STRIDE, head_count, DH)
    scores = (
        jnp.einsum("bthd,buhd->bhtu", query_blocks, window_keys, preferred_element_type=jnp.float32)
        * score_scale
    )
    first_position = lax.axis_index("seq") * tok_rows
    block_index = jnp.arange(blocks)[:, None, None, None]
    query_index = jnp.arange(STRIDE)[None, None, :, None]
    key_index = jnp.arange(2 * STRIDE)[None, None, None, :]
    allowed = (
        (key_index > query_index)
        & (key_index <= query_index + STRIDE)
        & (first_position + block_index * STRIDE + key_index - STRIDE >= 0)
    )
    local_top = jnp.max(jnp.where(allowed, scores, -1e30), axis=-1)
    local_weights = jnp.where(allowed, jnp.exp(scores - local_top[..., None]), 0.0)
    local_total = jnp.sum(local_weights, axis=-1)
    local_out = jnp.einsum(
        "bhtu,buhd->bthd",
        local_weights.astype(jnp.bfloat16),
        window_values,
        preferred_element_type=jnp.float32,
    )
    local_out = local_out.reshape(tok_rows, head_count, DH)
    local_top = local_top.transpose(0, 2, 1).reshape(tok_rows, head_count)
    local_total = local_total.transpose(0, 2, 1).reshape(tok_rows, head_count)
    row_count = tok_rows // STRIDE
    query_class = lax.all_to_all(
        query.reshape(row_count, STRIDE, head_count, DH),
        "seq",
        split_axis=1,
        concat_axis=0,
        tiled=True,
    )
    key_class = lax.all_to_all(
        key_heads.reshape(row_count, STRIDE, head_count, DH),
        "seq",
        split_axis=1,
        concat_axis=0,
        tiled=True,
    )
    value_class = lax.all_to_all(
        value_heads.reshape(row_count, STRIDE, head_count, DH),
        "seq",
        split_axis=1,
        concat_axis=0,
        tiled=True,
    )
    row_total = query_class.shape[0]
    class_scores = (
        jnp.einsum("rchd,schd->chrs", query_class, key_class, preferred_element_type=jnp.float32)
        * score_scale
    )
    earlier = (
        jnp.arange(row_total)[None, None, :, None] > jnp.arange(row_total)[None, None, None, :]
    )
    class_top = jnp.max(jnp.where(earlier, class_scores, -1e30), axis=-1)
    class_weights = jnp.where(earlier, jnp.exp(class_scores - class_top[..., None]), 0.0)
    class_total = jnp.sum(class_weights, axis=-1)
    summed = jnp.einsum(
        "chrs,schd->rchd",
        class_weights.astype(jnp.bfloat16),
        value_class,
        preferred_element_type=jnp.float32,
    )
    floor_total = jnp.maximum(class_total, 1.0).transpose(2, 0, 1)
    class_out = (summed / floor_total[..., None]).astype(jnp.bfloat16)
    class_top_rows = class_top.transpose(2, 0, 1)
    class_total_rows = class_total.transpose(2, 0, 1)
    column_out = class_out
    column_top = class_top_rows
    column_total = class_total_rows
    column_out, column_top, column_total = (
        lax.all_to_all(column_out, "seq", split_axis=0, concat_axis=1, tiled=True),
        lax.all_to_all(
            column_top.astype(jnp.bfloat16), "seq", split_axis=0, concat_axis=1, tiled=True
        ).astype(column_top.dtype),
        lax.all_to_all(
            column_total.astype(jnp.bfloat16), "seq", split_axis=0, concat_axis=1, tiled=True
        ).astype(column_total.dtype),
    )
    column_out = column_out.reshape(tok_rows, head_count, DH)
    column_top = column_top.reshape(tok_rows, head_count)
    column_total = column_total.reshape(tok_rows, head_count)
    top_score = jnp.maximum(local_top, column_top)
    local_weight = jnp.exp(local_top - top_score)
    column_weight = column_total * jnp.exp(column_top - top_score)
    denominator = local_total * local_weight + column_weight
    mixed = (
        local_out * local_weight[..., None]
        + column_out.astype(jnp.float32) * column_weight[..., None]
    ) / denominator[..., None]
    mixed = mixed.astype(jnp.bfloat16).reshape(tok_rows, head_width)
    return lax.psum_scatter(
        jnp.dot(mixed, w_out, preferred_element_type=jnp.float32).astype(jnp.bfloat16),
        "head",
        scatter_dimension=0,
        tiled=True,
    )


def shards(tokens, w_query, w_key, w_value, w_out):
    rows, width = w_query.shape
    fits = (
        lax.axis_size("seq") == 2 * NEAR
        and lax.axis_size("head") == 4
        and tokens.shape == (ROWS * STRIDE, HEADS * DH)
        and (rows, width) == (4 * HEADS * DH, HEADS * DH)
    )
    plan = chunked if fits else general
    return plan(tokens, w_query, w_key, w_value, w_out)


def solution(mesh):
    in_specs = (
        P("seq", "head"),
        P(None, "head"),
        P(None, "head"),
        P(None, "head"),
        P("head", None),
    )
    out_specs = P(("seq", "head"), None)
    return jax.shard_map(shards, mesh=mesh, in_specs=in_specs, out_specs=out_specs, check_vma=False)
```

```python
import jax
import jax.numpy as jnp
from jax import lax
from jax.experimental import pallas as pl
from jax.experimental.pallas import tpu as pltpu
from jax.sharding import PartitionSpec as P

DH = 128
STRIDE = 256
HEADS = 4
ROWS = 4
SUB = 8
CHUNKS = 2
SCALE2 = DH ** (-0.5) * 1.4426950408889634
FLOOR = -1e29
MIB = 1024 * 1024
F32 = jnp.float32
BF16 = jnp.bfloat16


ANYWHERE = pl.BlockSpec(memory_space=pl.ANY)
IN_VMEM = pl.BlockSpec(memory_space=pltpu.VMEM)
IN_SMEM = pl.BlockSpec(memory_space=pltpu.SMEM)


def call(body, name, micros, out_shape, args, after=(), scratch=(), mib=24):
    specs = [IN_SMEM if x.dtype == jnp.int32 else IN_VMEM for x in args]
    extra = len(after)

    def run(*refs):
        n = len(args)
        body(*refs[:n], *refs[n + extra :])

    return pl.pallas_call(
        run,
        in_specs=specs + [ANYWHERE] * extra,
        out_specs=jax.tree.map(lambda _: IN_VMEM, out_shape),
        out_shape=out_shape,
        scratch_shapes=list(scratch),
        compiler_params=pltpu.CompilerParams(vmem_limit_bytes=mib * MIB),
        cost_estimate=pl.CostEstimate(
            flops=int(micros * 1.1e9), bytes_accessed=MIB, transcendentals=0
        ),
        name=name,
    )(*args, *after)


def fence(value, *after):
    return pl.pallas_call(
        lambda *refs: None,
        in_specs=[ANYWHERE] * (1 + len(after)),
        out_specs=ANYWHERE,
        out_shape=jax.ShapeDtypeStruct(value.shape, value.dtype),
        input_output_aliases={0: 0},
        compiler_params=pltpu.CompilerParams(vmem_limit_bytes=MIB),
        cost_estimate=pl.CostEstimate(flops=0, bytes_accessed=0, transcendentals=0),
        name="fence",
    )(value, *after)


def in_hbm(value):
    return pltpu.with_memory_space_constraint(value, pltpu.HBM)


def shape(dims, dtype=BF16):
    return jax.ShapeDtypeStruct(tuple(dims), dtype)


def dot(a, b):
    return jnp.dot(a, b, preferred_element_type=F32)


def dot_t(a, b):
    return lax.dot_general(a, b, (((1,), (1,)), ((), ())), preferred_element_type=F32)


def dot_l(a, b):
    return lax.dot_general(a, b, (((0,), (0,)), ((), ())), preferred_element_type=F32)


def pack_kernel(pos_ref, tok_hbm, tok_ref, *rest):
    out_refs, sems = rest[:-1], rest[-1]
    spans = [slice(r * STRIDE, (r + 1) * STRIDE) for r in range(ROWS)]
    copies = [
        pltpu.make_async_copy(tok_hbm.at[at], tok_ref.at[at], sems.at[r])
        for r, at in enumerate(spans)
    ]
    for c in copies:
        c.start()
    for c in copies:
        c.wait()
    per_owner = STRIDE // len(out_refs)
    part = ROWS * SUB
    for k, out_ref in enumerate(out_refs):
        d = pos_ref[0] ^ k
        rows = [
            tok_ref[pl.ds(pl.multiple_of(r * STRIDE + d * per_owner, per_owner), per_owner), :]
            for r in range(ROWS)
        ]
        rows = [x.astype(F32) for x in rows]
        for g in range(per_owner // SUB):
            piece = jnp.concatenate([x[g * SUB : (g + 1) * SUB] for x in rows], 0)
            out_ref[g * part : (g + 1) * part, :] = piece.astype(BF16)


def pack(pos, tokens, owners):
    message = shape((tokens.shape[0] // owners, tokens.shape[1]))
    outs = pl.pallas_call(
        pack_kernel,
        in_specs=[IN_SMEM, ANYWHERE],
        out_specs=[IN_VMEM] * (1 + owners),
        out_shape=[shape(tokens.shape)] + [message] * owners,
        scratch_shapes=[pltpu.SemaphoreType.DMA((ROWS,))],
        compiler_params=pltpu.CompilerParams(vmem_limit_bytes=8 * MIB),
        cost_estimate=pl.CostEstimate(flops=0, bytes_accessed=2 * MIB, transcendentals=0),
        name="pack_tokens",
    )(pos, in_hbm(tokens))
    return outs[0], outs[1:]


def stage_kernel(order_ref, wq, wk, wv, oq, ok, ov, sems):
    copies = []
    for n, (w, o) in enumerate(((wq, oq), (wk, ok), (wv, ov))):
        for p in range(4):
            rows = pl.ds(pl.multiple_of(order_ref[p] * 512, 512), 512)
            copies.append(
                pltpu.make_async_copy(w.at[rows], o.at[p * 512 : (p + 1) * 512], sems.at[4 * n + p])
            )
    for c in copies:
        c.start()
    for c in copies:
        c.wait()


def stage(order, weights, after):
    def body(order_ref, wq, wk, wv, _, *rest):
        stage_kernel(order_ref, wq, wk, wv, *rest)

    return pl.pallas_call(
        body,
        in_specs=[IN_SMEM] + [ANYWHERE] * 4,
        out_specs=[IN_VMEM] * 3,
        out_shape=[shape(w.shape) for w in weights],
        scratch_shapes=[pltpu.SemaphoreType.DMA((12,))],
        compiler_params=pltpu.CompilerParams(vmem_limit_bytes=16 * MIB),
        cost_estimate=pl.CostEstimate(flops=0, bytes_accessed=6 * MIB, transcendentals=0),
        name="stage_weights",
    )(order, *weights, after)


def gathered(x_refs, at, w_ref):
    width = x_refs[0].shape[1]
    total = None
    for p, x_ref in enumerate(x_refs):
        term = dot(x_ref[at, :], w_ref[p * width : (p + 1) * width, :])
        total = term if total is None else total + term
    return total.astype(BF16)


def halo_kernel(x0, x1, x2, x3, wk, wv, out_ref):
    rows = x0.shape[0]
    at = slice(rows - STRIDE, rows)
    out_ref[:STRIDE, :] = gathered((x0, x1, x2, x3), at, wk)
    out_ref[STRIDE:, :] = gathered((x0, x1, x2, x3), at, wv)


def project_kernel(x0, x1, x2, x3, wq, wk, wv, halo, q_ref, k_ref, v_ref):
    rows = x0.shape[0]
    xs = (x0, x1, x2, x3)
    last = slice(rows - STRIDE, rows)
    k_ref[last, :] = halo[:STRIDE, :]
    v_ref[last, :] = halo[STRIDE:, :]
    for w, out, upto in ((wq, q_ref, rows), (wk, k_ref, rows - STRIDE), (wv, v_ref, rows - STRIDE)):
        out[:upto, :] = gathered(xs, slice(0, upto), w)


def softmax_columns(s):
    m = jnp.maximum(jnp.max(s, 0, keepdims=True), FLOOR)
    p = jnp.exp2((s - m) * SCALE2)
    total = jnp.maximum(jnp.sum(p, 0, keepdims=True), 1.0)
    return p, total, m * SCALE2 + jnp.log2(total)


def local_kernel(pos_ref, q_ref, k_ref, v_ref, halo_ref, *outs):
    out_refs, lse_refs = outs[:CHUNKS], outs[CHUNKS:]
    owners, message, _ = out_refs[0].shape
    groups = message // ROWS // SUB
    block = pos_ref[0]
    u = lax.broadcasted_iota(jnp.int32, (STRIDE, STRIDE), 0)
    t = lax.broadcasted_iota(jnp.int32, (STRIDE, STRIDE), 1)
    current = u <= t
    low = jnp.where(block == 0, -1e30, 0.0).astype(F32)
    for r in range(ROWS):
        lses = []
        here = slice(r * STRIDE, (r + 1) * STRIDE)
        back = slice((r - 1) * STRIDE, r * STRIDE)
        for h in range(HEADS):
            cols = slice(h * DH, (h + 1) * DH)
            q = q_ref[here, cols]
            k_prev = k_ref[back, cols] if r else halo_ref[:STRIDE, cols]
            v_prev = v_ref[back, cols] if r else halo_ref[STRIDE:, cols]
            s_prev = dot_t(k_prev, q)
            if r == 0:
                s_prev = s_prev + low
            p, total, lse = softmax_columns(jnp.where(current, dot_t(k_ref[here, cols], q), s_prev))
            p_now = jnp.where(current, p, 0.0).astype(BF16)
            p_prev = jnp.where(current, 0.0, p).astype(BF16)
            o = dot_l(v_ref[here, cols], p_now) + dot_l(v_prev, p_prev)
            o = (o * (1.0 / total)).T
            lses.append(lse)
            for d in range(owners):
                for i in range(CHUNKS):
                    for g in range(groups):
                        at = ((d * CHUNKS + i) * groups + g) * SUB
                        to = (g * ROWS + r) * SUB
                        out_refs[i][d, to : to + SUB, cols] = o[at : at + SUB]
        lses.append(jnp.zeros((128 - HEADS, STRIDE), F32))
        turned = jnp.concatenate(lses, 0).T
        for i in range(CHUNKS):
            for g in range(groups):
                total = None
                for d in range(owners):
                    at = ((d * CHUNKS + i) * groups + g) * SUB
                    moved = pltpu.roll(turned[at : at + SUB], 8 * (block ^ d), 1)
                    total = moved if total is None else total + moved
                to = (g * ROWS + r) * SUB
                lse_refs[i][to : to + SUB, :] = total


def local_part(pos, q, k, v, halo, owners, after):
    rows, width = q.shape
    message = rows // owners // CHUNKS
    shapes = [shape((owners, message, width), F32)] * CHUNKS + [shape((message, 128), F32)] * CHUNKS
    outs = call(local_kernel, "local_part", 5, shapes, (pos, q, k, v, halo), after)
    return list(zip(outs[:CHUNKS], outs[CHUNKS:]))


def column_kernel(pos_ref, x0, x1, x2, x3, wq, wk, wv, *rest):
    out_refs, scratch = rest[:-3], rest[-3:]
    owners, message, _ = scratch[0].shape
    groups = message // (ROWS * SUB)
    everything = slice(0, owners * message)
    for w, a in zip((wq, wk, wv), scratch):
        a[...] = gathered((x0, x1, x2, x3), everything, w).reshape(a.shape)
    part = ROWS * SUB
    size = owners * part

    def row_and_class(dim):
        i = lax.broadcasted_iota(jnp.int32, (size, size), dim)
        return ((i // part) ^ pos_ref[0]) * ROWS + (i % part) // SUB, i % SUB

    (row_j, class_j), (row_i, class_i) = row_and_class(0), row_and_class(1)
    earlier = jnp.logical_and(class_i == class_j, row_i > row_j)
    stats = []
    for g in range(groups):
        at = slice(g * part, (g + 1) * part)
        lses = []
        for h in range(HEADS):
            cols = slice(h * DH, (h + 1) * DH)
            q, k, v = (a[:, at, cols].reshape(size, DH) for a in scratch)
            p, total, lse = softmax_columns(jnp.where(earlier, dot_t(k, q), -1e30))
            o = (dot_l(v, p.astype(BF16)) * (1.0 / total)).T.astype(BF16)
            rows = slice(h * message + g * part, h * message + (g + 1) * part)
            for n in range(owners):
                out_refs[n][rows, :] = o[n * part : (n + 1) * part]
            lses.append(lse)
        stats.append(jnp.concatenate(lses + lses, 0))
    upper = lax.broadcasted_iota(jnp.int32, (8, 128), 0) < HEADS
    blank = [jnp.zeros((8, 128 - message), F32)] if message < 128 else []
    for n in range(owners):
        x = jnp.concatenate([s[:, n * part : (n + 1) * part] for s in stats] + blank, 1)
        hi = x.astype(BF16).astype(F32)
        mid = (x - hi).astype(BF16).astype(F32)
        lo = x - hi - mid
        tail = jnp.concatenate([jnp.where(upper, hi, lo), jnp.where(upper, mid, 0.0)], 0)
        out_refs[n][HEADS * message : HEADS * message + 16, :] = tail.astype(BF16)


def column_part(pos, pieces, weights, owners, after):
    tokens, width = pieces[0].shape
    message = tokens // owners
    shapes = [shape((HEADS * message + 16, DH))] * owners
    scratch = [pltpu.VMEM((owners, message, width), BF16)] * 3
    return call(column_kernel, "column_part", 6, shapes, (pos, *pieces, *weights), after, scratch)


def mix_kernel(pos_ref, loc_ref, lse_ref, *rest):
    col_refs, (own_ref, send_ref, mixed) = rest[:-3], rest[-3:]
    owners, message, _ = loc_ref.shape
    groups = message // (ROWS * SUB)
    base = HEADS * message
    tiles = []
    for col_ref in col_refs:
        tail = col_ref[base : base + 16, :].astype(F32)
        tiles.append(tail[:8] + tail[8:])
    tiles.append(jnp.zeros((128 - 8 * owners, 128), F32))
    turned = jnp.concatenate(tiles, 0).T[:message]
    col_lse = turned + pltpu.roll(turned, 124, 1)
    loc_lse = lse_ref[...]
    top = jnp.maximum(col_lse, loc_lse)
    w_col = jnp.exp2(col_lse - top)
    w_loc = jnp.exp2(loc_lse - top)
    share = 1.0 / (w_col + w_loc)
    w_col = w_col * share
    w_loc = w_loc * share
    span = groups * SUB
    for k, col_ref in enumerate(col_refs):
        d = pos_ref[0] ^ k
        spot = pl.ds(pl.multiple_of(d * span, span), span)
        for h in range(HEADS):
            cols = slice(h * DH, (h + 1) * DH)
            at = slice(8 * k + h, 8 * k + h + 1)
            col = col_ref[h * message : (h + 1) * message, :].astype(F32)
            both = loc_ref[d, :, cols] * w_loc[:, at] + col * w_col[:, at]
            for r in range(ROWS):
                starts = [(g * ROWS + r) * SUB for g in range(groups)]
                piece = jnp.concatenate([both[s : s + SUB] for s in starts], 0)
                mixed[r, spot, cols] = piece.astype(BF16)
    core = pos_ref[1]
    for x in range(2):
        own_ref[x] = mixed[2 * x + core]
        send_ref[x] = mixed[2 * x + 1 - core]


def mix(pos, columns, local, lse, after):
    owners, message, width = local.shape
    tokens = owners * message // ROWS
    shapes = [shape((2, tokens, width))] * 2
    scratch = [pltpu.VMEM((ROWS, tokens, width), BF16)]
    return call(mix_kernel, "mix", 3, shapes, (pos, local, lse, *columns), after, scratch)


def out_kernel(pos_ref, a_ref, b_ref, wa_ref, wb_ref, send_ref, keep_ref):
    tokens, columns = send_ref.shape
    a = a_ref[...].reshape(2 * tokens, -1)
    b = b_ref[...].reshape(2 * tokens, -1)
    low_side = pos_ref[2] == 0
    tile = 512
    for n in range(0, columns, tile):
        at = slice(n, n + tile)
        total = dot(a, wa_ref[:, at]) + dot(b, wb_ref[:, at])
        send_ref[:, at] = jnp.where(low_side, total[tokens:], total[:tokens]).astype(BF16)
        keep_ref[:, at] = jnp.where(low_side, total[:tokens], total[tokens:])


def out_project(pos, own, other, w_own, w_other, after):
    dims = (own.shape[1], w_own.shape[1])
    shapes = [shape(dims), shape(dims, F32)]
    return call(out_kernel, "out_project", 2, shapes, (pos, own, other, w_own, w_other), after)


def join_kernel(*refs):
    out_ref = refs[-1]
    chunks = (len(refs) - 1) // 2
    tokens = refs[0].shape[0]
    span = 32 // chunks
    for i in range(chunks):
        keep, got = refs[2 * i], refs[2 * i + 1]
        for d in range(tokens // span):
            rows = slice(d * span, (d + 1) * span)
            at = (d * chunks + i) * span
            total = keep[rows, :] + got[rows, :].astype(F32)
            out_ref[at : at + span, :] = total.astype(BF16)


def join(pairs):
    columns = pairs[0][0].shape[1]
    args = [x for pair in pairs for x in pair]
    return call(join_kernel, "join", 2, shape((STRIDE, columns)), args)


def swap(value, distance):
    return lax.ppermute(value, "head", [(i, i ^ distance) for i in range(4)])


def exchange(messages):
    n = len(messages)
    return [messages[0]] + [
        lax.ppermute(messages[k], "seq", [(i, i ^ k) for i in range(n)]) for k in range(1, n)
    ]


def gather(own):
    across = swap(own, 2)
    return own, swap(own, 1), across, swap(across, 1)


def chunked(tokens, w_query, w_key, w_value, w_out):
    owners = lax.axis_size("seq")
    head = lax.axis_index("head")
    block = lax.axis_index("seq")
    order = jnp.bitwise_xor(jnp.arange(4, dtype=jnp.int32), head.astype(jnp.int32))
    pos = jnp.stack([block, head % 2, head // 2]).astype(jnp.int32)
    rows, width = tokens.shape

    across = swap(tokens, 2)
    block_tokens, sent = pack(pos, tokens, owners)
    messages = exchange(sent)
    part = rows // owners // CHUNKS
    classes = [
        jnp.concatenate([m[i * part : (i + 1) * part] for m in messages], 0) for i in range(CHUNKS)
    ]
    across = fence(across, classes[0])
    pieces = (block_tokens, swap(fence(block_tokens, classes[0]), 1), across, swap(across, 1))
    class_pieces = []
    for c in classes:
        c = fence(c, class_pieces[-1][2]) if class_pieces else c
        class_pieces.append(gather(c))
    weights = stage(order, (w_query, w_key, w_value), messages[1])
    w_other = swap(w_out, 1)
    own_halo = call(
        halo_kernel, "project_halo", 1.5, shape((2 * STRIDE, width)), (*pieces, *weights[1:])
    )
    halo = lax.ppermute(own_halo, "seq", [(i, i + 1) for i in range(owners - 1)])
    q, k, v = call(
        project_kernel,
        "project_block",
        6,
        [shape((rows, width))] * 3,
        (*pieces, *weights, own_halo),
    )
    locals_ = local_part(pos, q, k, v, halo, owners, ())
    columns, after = [], (locals_[0][0],)
    for c in class_pieces:
        columns.append(column_part(pos, c, weights, owners, after))
        after = (columns[-1][0],)
    pairs, after, gate = [], (columns[-1][0],), ()
    for column, (local, lse) in zip(columns, locals_):
        own, send = mix(pos, exchange(column), local, lse, after)
        out, keep = out_project(pos, own, swap(send, 1), w_out, w_other, gate)
        pairs.append((keep, swap(out, 2)))
        after, gate = (keep,), (pairs[-1][1],)
    return join(pairs)


def from_behind(value, axis, by):
    peers = lax.axis_size(axis)
    pairs = [(i, i + by) for i in range(peers) if 0 <= i + by < peers]
    return lax.ppermute(value, axis, pairs)


def general(tokens, w_query, w_key, w_value, w_out):
    tok_rows = tokens.shape[0]
    head_width = w_query.shape[1]
    head_count = head_width // DH
    score_scale = DH ** (-0.5)
    shard_piece = lax.all_gather(tokens, "head", axis=1, tiled=True)
    query_full, key_full, value_full = tuple(
        (
            jnp.dot(shard_piece, weight, preferred_element_type=jnp.float32)
            for weight in (w_query, w_key, w_value)
        )
    )
    query = query_full.astype(jnp.bfloat16).reshape(tok_rows, head_count, DH)
    key_heads = key_full.astype(jnp.bfloat16).reshape(tok_rows, head_count, DH)
    value_heads = value_full.astype(jnp.bfloat16).reshape(tok_rows, head_count, DH)
    prev_keys, prev_values = from_behind((key_heads[-STRIDE:], value_heads[-STRIDE:]), "seq", 1)
    blocks = tok_rows // STRIDE
    extended_keys = jnp.concatenate([prev_keys, key_heads], 0)
    extended_values = jnp.concatenate([prev_values, value_heads], 0)
    window_keys = jnp.concatenate(
        [
            extended_keys[:tok_rows].reshape(blocks, STRIDE, head_count, DH),
            extended_keys[STRIDE:].reshape(blocks, STRIDE, head_count, DH),
        ],
        1,
    )
    window_values = jnp.concatenate(
        [
            extended_values[:tok_rows].reshape(blocks, STRIDE, head_count, DH),
            extended_values[STRIDE:].reshape(blocks, STRIDE, head_count, DH),
        ],
        1,
    )
    query_blocks = query.reshape(blocks, STRIDE, head_count, DH)
    scores = (
        jnp.einsum("bthd,buhd->bhtu", query_blocks, window_keys, preferred_element_type=jnp.float32)
        * score_scale
    )
    first_position = lax.axis_index("seq") * tok_rows
    block_index = jnp.arange(blocks)[:, None, None, None]
    query_index = jnp.arange(STRIDE)[None, None, :, None]
    key_index = jnp.arange(2 * STRIDE)[None, None, None, :]
    allowed = (
        (key_index > query_index)
        & (key_index <= query_index + STRIDE)
        & (first_position + block_index * STRIDE + key_index - STRIDE >= 0)
    )
    local_top = jnp.max(jnp.where(allowed, scores, -1e30), axis=-1)
    local_weights = jnp.where(allowed, jnp.exp(scores - local_top[..., None]), 0.0)
    local_total = jnp.sum(local_weights, axis=-1)
    local_out = jnp.einsum(
        "bhtu,buhd->bthd",
        local_weights.astype(jnp.bfloat16),
        window_values,
        preferred_element_type=jnp.float32,
    )
    local_out = local_out.reshape(tok_rows, head_count, DH)
    local_top = local_top.transpose(0, 2, 1).reshape(tok_rows, head_count)
    local_total = local_total.transpose(0, 2, 1).reshape(tok_rows, head_count)
    row_count = tok_rows // STRIDE
    query_class = lax.all_to_all(
        query.reshape(row_count, STRIDE, head_count, DH),
        "seq",
        split_axis=1,
        concat_axis=0,
        tiled=True,
    )
    key_class = lax.all_to_all(
        key_heads.reshape(row_count, STRIDE, head_count, DH),
        "seq",
        split_axis=1,
        concat_axis=0,
        tiled=True,
    )
    value_class = lax.all_to_all(
        value_heads.reshape(row_count, STRIDE, head_count, DH),
        "seq",
        split_axis=1,
        concat_axis=0,
        tiled=True,
    )
    row_total = query_class.shape[0]
    class_scores = (
        jnp.einsum("rchd,schd->chrs", query_class, key_class, preferred_element_type=jnp.float32)
        * score_scale
    )
    earlier = (
        jnp.arange(row_total)[None, None, :, None] > jnp.arange(row_total)[None, None, None, :]
    )
    class_top = jnp.max(jnp.where(earlier, class_scores, -1e30), axis=-1)
    class_weights = jnp.where(earlier, jnp.exp(class_scores - class_top[..., None]), 0.0)
    class_total = jnp.sum(class_weights, axis=-1)
    summed = jnp.einsum(
        "chrs,schd->rchd",
        class_weights.astype(jnp.bfloat16),
        value_class,
        preferred_element_type=jnp.float32,
    )
    floor_total = jnp.maximum(class_total, 1.0).transpose(2, 0, 1)
    class_out = (summed / floor_total[..., None]).astype(jnp.bfloat16)
    class_top_rows = class_top.transpose(2, 0, 1)
    class_total_rows = class_total.transpose(2, 0, 1)
    column_out = class_out
    column_top = class_top_rows
    column_total = class_total_rows
    column_out, column_top, column_total = (
        lax.all_to_all(column_out, "seq", split_axis=0, concat_axis=1, tiled=True),
        lax.all_to_all(
            column_top.astype(jnp.bfloat16), "seq", split_axis=0, concat_axis=1, tiled=True
        ).astype(column_top.dtype),
        lax.all_to_all(
            column_total.astype(jnp.bfloat16), "seq", split_axis=0, concat_axis=1, tiled=True
        ).astype(column_total.dtype),
    )
    column_out = column_out.reshape(tok_rows, head_count, DH)
    column_top = column_top.reshape(tok_rows, head_count)
    column_total = column_total.reshape(tok_rows, head_count)
    top_score = jnp.maximum(local_top, column_top)
    local_weight = jnp.exp(local_top - top_score)
    column_weight = column_total * jnp.exp(column_top - top_score)
    denominator = local_total * local_weight + column_weight
    mixed = (
        local_out * local_weight[..., None]
        + column_out.astype(jnp.float32) * column_weight[..., None]
    ) / denominator[..., None]
    mixed = mixed.astype(jnp.bfloat16).reshape(tok_rows, head_width)
    return lax.psum_scatter(
        jnp.dot(mixed, w_out, preferred_element_type=jnp.float32).astype(jnp.bfloat16),
        "head",
        scatter_dimension=0,
        tiled=True,
    )


def shards(tokens, w_query, w_key, w_value, w_out):
    rows, width = w_query.shape
    fits = (
        lax.axis_size("seq") == STRIDE // 32
        and lax.axis_size("head") == 4
        and tokens.shape == (ROWS * STRIDE, HEADS * DH)
        and (rows, width) == (4 * HEADS * DH, HEADS * DH)
    )
    plan = chunked if fits else general
    return plan(tokens, w_query, w_key, w_value, w_out)


def solution(mesh):
    in_specs = (
        P("seq", "head"),
        P(None, "head"),
        P(None, "head"),
        P(None, "head"),
        P("head", None),
    )
    out_specs = P(("seq", "head"), None)
    return jax.shard_map(shards, mesh=mesh, in_specs=in_specs, out_specs=out_specs, check_vma=False)
```

```python
import functools

import jax
import jax.numpy as jnp
from jax import lax
from jax.experimental import pallas as pl
from jax.experimental.pallas import tpu as pltpu
from jax.sharding import PartitionSpec as P

DH = 128
STRIDE = 256
HEADS = 4
ROWS = 4
SUB = 8
CHUNKS = 2
ORDER = (0, 4, 5, 6, 7, 1, 2, 3)
HALVES = ((0, 4, 5, 1), (6, 7, 2, 3))
SCALE2 = DH ** (-0.5) * 1.4426950408889634
FLOOR = -1e29
MIB = 1024 * 1024
F32 = jnp.float32
BF16 = jnp.bfloat16


ANYWHERE = pl.BlockSpec(memory_space=pl.ANY)
IN_VMEM = pl.BlockSpec(memory_space=pltpu.VMEM)
IN_SMEM = pl.BlockSpec(memory_space=pltpu.SMEM)


def call(body, name, micros, out_shape, args, after=(), scratch=(), mib=24):
    specs = [IN_SMEM if x.dtype == jnp.int32 else IN_VMEM for x in args]
    extra = len(after)

    def run(*refs):
        n = len(args)
        body(*refs[:n], *refs[n + extra :])

    return pl.pallas_call(
        run,
        in_specs=specs + [ANYWHERE] * extra,
        out_specs=jax.tree.map(lambda _: IN_VMEM, out_shape),
        out_shape=out_shape,
        scratch_shapes=list(scratch),
        compiler_params=pltpu.CompilerParams(vmem_limit_bytes=mib * MIB),
        cost_estimate=pl.CostEstimate(
            flops=int(micros * 1.1e9), bytes_accessed=MIB, transcendentals=0
        ),
        name=name,
    )(*args, *after)


def fence(value, *after):
    return pl.pallas_call(
        lambda *refs: None,
        in_specs=[ANYWHERE] * (1 + len(after)),
        out_specs=ANYWHERE,
        out_shape=jax.ShapeDtypeStruct(value.shape, value.dtype),
        input_output_aliases={0: 0},
        compiler_params=pltpu.CompilerParams(vmem_limit_bytes=MIB),
        cost_estimate=pl.CostEstimate(flops=0, bytes_accessed=0, transcendentals=0),
        name="fence",
    )(value, *after)


def in_hbm(value):
    return pltpu.with_memory_space_constraint(value, pltpu.HBM)


def shape(dims, dtype=BF16):
    return jax.ShapeDtypeStruct(tuple(dims), dtype)


def dot(a, b):
    return jnp.dot(a, b, preferred_element_type=F32)


def dot_t(a, b):
    return lax.dot_general(a, b, (((1,), (1,)), ((), ())), preferred_element_type=F32)


def dot_l(a, b):
    return lax.dot_general(a, b, (((0,), (0,)), ((), ())), preferred_element_type=F32)


def pack_kernel(pos_ref, tok_hbm, tok_ref, *rest):
    out_refs, sems = rest[:-1], rest[-1]
    spans = [slice(r * STRIDE, (r + 1) * STRIDE) for r in range(ROWS)]
    copies = [
        pltpu.make_async_copy(tok_hbm.at[at], tok_ref.at[at], sems.at[r])
        for r, at in enumerate(spans)
    ]
    for c in copies:
        c.start()
    for c in copies:
        c.wait()
    per_owner = STRIDE // len(out_refs)
    part = ROWS * SUB
    for k, out_ref in zip(ORDER, out_refs):
        d = pos_ref[0] ^ k
        rows = [
            tok_ref[pl.ds(pl.multiple_of(r * STRIDE + d * per_owner, per_owner), per_owner), :]
            for r in range(ROWS)
        ]
        rows = [x.astype(F32) for x in rows]
        for g in range(per_owner // SUB):
            piece = jnp.concatenate([x[g * SUB : (g + 1) * SUB] for x in rows], 0)
            out_ref[g * part : (g + 1) * part, :] = piece.astype(BF16)


def pack(pos, tokens, owners):
    message = shape((tokens.shape[0] // owners, tokens.shape[1]))
    outs = pl.pallas_call(
        pack_kernel,
        in_specs=[IN_SMEM, ANYWHERE],
        out_specs=[IN_VMEM] * (1 + owners),
        out_shape=[shape(tokens.shape)] + [message] * owners,
        scratch_shapes=[pltpu.SemaphoreType.DMA((ROWS,))],
        compiler_params=pltpu.CompilerParams(vmem_limit_bytes=8 * MIB),
        cost_estimate=pl.CostEstimate(flops=0, bytes_accessed=2 * MIB, transcendentals=0),
        name="pack_tokens",
    )(pos, in_hbm(tokens))
    return outs[0], outs[1:]


def stage_kernel(order_ref, wq, wk, wv, oq, ok, ov, sems):
    copies = []
    for n, (w, o) in enumerate(((wq, oq), (wk, ok), (wv, ov))):
        for p in range(4):
            rows = pl.ds(pl.multiple_of(order_ref[p] * 512, 512), 512)
            copies.append(
                pltpu.make_async_copy(w.at[rows], o.at[p * 512 : (p + 1) * 512], sems.at[4 * n + p])
            )
    for c in copies:
        c.start()
    for c in copies:
        c.wait()


def stage(order, weights, after):
    def body(order_ref, wq, wk, wv, _, *rest):
        stage_kernel(order_ref, wq, wk, wv, *rest)

    return pl.pallas_call(
        body,
        in_specs=[IN_SMEM] + [ANYWHERE] * 4,
        out_specs=[IN_VMEM] * 3,
        out_shape=[shape(w.shape) for w in weights],
        scratch_shapes=[pltpu.SemaphoreType.DMA((12,))],
        compiler_params=pltpu.CompilerParams(vmem_limit_bytes=16 * MIB),
        cost_estimate=pl.CostEstimate(flops=0, bytes_accessed=6 * MIB, transcendentals=0),
        name="stage_weights",
    )(order, *weights, after)


def gathered(x_refs, at, w_ref):
    width = x_refs[0].shape[1]
    total = None
    for p, x_ref in enumerate(x_refs):
        term = dot(x_ref[at, :], w_ref[p * width : (p + 1) * width, :])
        total = term if total is None else total + term
    return total.astype(BF16)


def halo_kernel(x0, x1, x2, x3, wk, wv, out_ref):
    rows = x0.shape[0]
    at = slice(rows - STRIDE, rows)
    out_ref[:STRIDE, :] = gathered((x0, x1, x2, x3), at, wk)
    out_ref[STRIDE:, :] = gathered((x0, x1, x2, x3), at, wv)


def project_kernel(x0, x1, x2, x3, wq, wk, wv, halo, q_ref, k_ref, v_ref):
    rows = x0.shape[0]
    xs = (x0, x1, x2, x3)
    last = slice(rows - STRIDE, rows)
    k_ref[last, :] = halo[:STRIDE, :]
    v_ref[last, :] = halo[STRIDE:, :]
    for w, out, upto in ((wq, q_ref, rows), (wk, k_ref, rows - STRIDE), (wv, v_ref, rows - STRIDE)):
        out[:upto, :] = gathered(xs, slice(0, upto), w)


def softmax_columns(s):
    m = jnp.maximum(jnp.max(s, 0, keepdims=True), FLOOR)
    p = jnp.exp2((s - m) * SCALE2)
    total = jnp.maximum(jnp.sum(p, 0, keepdims=True), 1.0)
    return p, total, m * SCALE2 + jnp.log2(total)


def local_kernel(pos_ref, q_ref, k_ref, v_ref, halo_ref, *outs):
    out_refs, lse_refs = outs[:CHUNKS], outs[CHUNKS:]
    owners, message, _ = out_refs[0].shape
    groups = message // ROWS // SUB
    block = pos_ref[0]
    u = lax.broadcasted_iota(jnp.int32, (STRIDE, STRIDE), 0)
    t = lax.broadcasted_iota(jnp.int32, (STRIDE, STRIDE), 1)
    current = u <= t
    low = jnp.where(block == 0, -1e30, 0.0).astype(F32)
    for r in range(ROWS):
        lses = []
        here = slice(r * STRIDE, (r + 1) * STRIDE)
        back = slice((r - 1) * STRIDE, r * STRIDE)
        for h in range(HEADS):
            cols = slice(h * DH, (h + 1) * DH)
            q = q_ref[here, cols]
            k_prev = k_ref[back, cols] if r else halo_ref[:STRIDE, cols]
            v_prev = v_ref[back, cols] if r else halo_ref[STRIDE:, cols]
            s_prev = dot_t(k_prev, q)
            if r == 0:
                s_prev = s_prev + low
            p, total, lse = softmax_columns(jnp.where(current, dot_t(k_ref[here, cols], q), s_prev))
            p_now = jnp.where(current, p, 0.0).astype(BF16)
            p_prev = jnp.where(current, 0.0, p).astype(BF16)
            o = dot_l(v_ref[here, cols], p_now) + dot_l(v_prev, p_prev)
            o = (o * (1.0 / total)).T
            lses.append(lse)
            for d in range(owners):
                for i in range(CHUNKS):
                    for g in range(groups):
                        at = ((d * CHUNKS + i) * groups + g) * SUB
                        to = (g * ROWS + r) * SUB
                        out_refs[i][d, to : to + SUB, cols] = o[at : at + SUB]
        lses.append(jnp.zeros((128 - HEADS, STRIDE), F32))
        turned = jnp.concatenate(lses, 0).T
        for i in range(CHUNKS):
            for g in range(groups):
                total = None
                for d in range(owners):
                    at = ((d * CHUNKS + i) * groups + g) * SUB
                    moved = pltpu.roll(turned[at : at + SUB], 8 * (block ^ d), 1)
                    total = moved if total is None else total + moved
                to = (g * ROWS + r) * SUB
                lse_refs[i][to : to + SUB, :] = total


def local_part(pos, q, k, v, halo, owners, after):
    rows, width = q.shape
    message = rows // owners // CHUNKS
    shapes = [shape((owners, message, width), F32)] * CHUNKS + [shape((message, 128), F32)] * CHUNKS
    outs = call(local_kernel, "local_part", 5, shapes, (pos, q, k, v, halo), after)
    return list(zip(outs[:CHUNKS], outs[CHUNKS:]))


def column_kernel(pos_ref, x0, x1, x2, x3, wq, wk, wv, *rest):
    refs, scratch = rest[:-3], rest[-3:]
    owners, message, _ = scratch[0].shape
    out_refs = refs[-owners:]
    size = HEADS * message + 16
    base = out_refs[0].shape[0] - size
    for old, new in zip(refs[:-owners], out_refs):
        new[:base, :] = old[...]
    groups = message // (ROWS * SUB)
    everything = slice(0, owners * message)
    for w, a in zip((wq, wk, wv), scratch):
        a[...] = gathered((x0, x1, x2, x3), everything, w).reshape(a.shape)
    part = ROWS * SUB
    size = owners * part

    def row_and_class(dim):
        i = lax.broadcasted_iota(jnp.int32, (size, size), dim)
        slot = i // part
        far = jnp.where(slot < 5, slot + 3, slot - 4)
        return (jnp.where(slot == 0, 0, far) ^ pos_ref[0]) * ROWS + (i % part) // SUB, i % SUB

    (row_j, class_j), (row_i, class_i) = row_and_class(0), row_and_class(1)
    earlier = jnp.logical_and(class_i == class_j, row_i > row_j)
    stats = []
    for g in range(groups):
        at = slice(g * part, (g + 1) * part)
        lses = []
        for h in range(HEADS):
            cols = slice(h * DH, (h + 1) * DH)
            q, k, v = (a[:, at, cols].reshape(size, DH) for a in scratch)
            p, total, lse = softmax_columns(jnp.where(earlier, dot_t(k, q), -1e30))
            o = (dot_l(v, p.astype(BF16)) * (1.0 / total)).T.astype(BF16)
            to = base + h * message + g * part
            rows = slice(to, to + part)
            for n in range(owners):
                out_refs[n][rows, :] = o[n * part : (n + 1) * part]
            lses.append(lse)
        stats.append(jnp.concatenate(lses + lses, 0))
    upper = lax.broadcasted_iota(jnp.int32, (8, 128), 0) < HEADS
    blank = [jnp.zeros((8, 128 - message), F32)] if message < 128 else []
    for n in range(owners):
        x = jnp.concatenate([s[:, n * part : (n + 1) * part] for s in stats] + blank, 1)
        hi = x.astype(BF16).astype(F32)
        mid = (x - hi).astype(BF16).astype(F32)
        lo = x - hi - mid
        tail = jnp.concatenate([jnp.where(upper, hi, lo), jnp.where(upper, mid, 0.0)], 0)
        to = base + HEADS * message
        out_refs[n][to : to + 16, :] = tail.astype(BF16)


def column_part(pos, pieces, weights, earlier, owners, after):
    tokens, width = pieces[0].shape
    message = tokens // owners
    rows = HEADS * message + 16 + (earlier[0].shape[0] if earlier else 0)
    scratch = [pltpu.VMEM((owners, message, width), BF16)] * 3
    args = (pos, *pieces, *weights, *earlier)
    return call(column_kernel, "column_part", 6, [shape((rows, DH))] * owners, args, after, scratch)


def mix_kernel(half, pos_ref, *refs):
    local_refs, refs = refs[: 2 * CHUNKS], refs[2 * CHUNKS :]
    col_refs, (own_ref, send_ref, mixed) = refs[:-3], refs[-3:]
    message = local_refs[0].shape[1]
    groups = message // (ROWS * SUB)
    size = HEADS * message + 16
    span = groups * SUB
    for i in range(CHUNKS):
        loc_ref, lse_ref = local_refs[2 * i : 2 * i + 2]
        tiles = [jnp.zeros((8, 128), F32)] * 16
        base = i * size
        for k, col_ref in zip(half, col_refs):
            tail = col_ref[base + HEADS * message : base + size, :].astype(F32)
            tiles[k] = tail[:8] + tail[8:]
        turned = jnp.concatenate(tiles, 0).T[:message]
        col_lse = turned + pltpu.roll(turned, 124, 1)
        loc_lse = lse_ref[...]
        top = jnp.maximum(col_lse, loc_lse)
        w_col = jnp.exp2(col_lse - top)
        w_loc = jnp.exp2(loc_lse - top)
        share = 1.0 / (w_col + w_loc)
        w_col = w_col * share
        w_loc = w_loc * share
        for n, (k, col_ref) in enumerate(zip(half, col_refs)):
            d = pos_ref[0] ^ k
            to = (n * CHUNKS + i) * span
            for h in range(HEADS):
                cols = slice(h * DH, (h + 1) * DH)
                at = slice(8 * k + h, 8 * k + h + 1)
                col = col_ref[base + h * message : base + (h + 1) * message, :].astype(F32)
                both = loc_ref[d, :, cols] * w_loc[:, at] + col * w_col[:, at]
                for r in range(ROWS):
                    starts = [(g * ROWS + r) * SUB for g in range(groups)]
                    piece = jnp.concatenate([both[s : s + SUB] for s in starts], 0)
                    mixed[r, to : to + span, cols] = piece.astype(BF16)
    core = pos_ref[1]
    for x in range(2):
        own_ref[x] = mixed[2 * x + core]
        send_ref[x] = mixed[2 * x + 1 - core]


def mix(pos, half, columns, locals_, after):
    owners, message, width = locals_[0][0].shape
    tokens = len(half) * CHUNKS * message // ROWS
    shapes = [shape((2, tokens, width))] * 2
    scratch = [pltpu.VMEM((ROWS, tokens, width), BF16)]
    args = (pos, *[x for pair in locals_ for x in pair], *columns)
    return call(functools.partial(mix_kernel, half), "mix", 2, shapes, args, after, scratch)


def out_kernel(pos_ref, a_ref, b_ref, wa_ref, wb_ref, send_ref, keep_ref):
    tokens, columns = send_ref.shape
    a = a_ref[...].reshape(2 * tokens, -1)
    b = b_ref[...].reshape(2 * tokens, -1)
    low_side = pos_ref[2] == 0
    tile = 512
    for n in range(0, columns, tile):
        at = slice(n, n + tile)
        total = dot(a, wa_ref[:, at]) + dot(b, wb_ref[:, at])
        send_ref[:, at] = jnp.where(low_side, total[tokens:], total[:tokens]).astype(BF16)
        keep_ref[:, at] = jnp.where(low_side, total[:tokens], total[tokens:])


def out_project(pos, own, other, w_own, w_other, after):
    dims = (own.shape[1], w_own.shape[1])
    shapes = [shape(dims), shape(dims, F32)]
    return call(out_kernel, "out_project", 2, shapes, (pos, own, other, w_own, w_other), after)


def join_kernel(pos_ref, *refs):
    out_ref = refs[-1]
    for half, keep, got in zip(HALVES, refs[0:-1:2], refs[1:-1:2]):
        span = keep.shape[0] // len(half)
        for n, k in enumerate(half):
            rows = slice(n * span, (n + 1) * span)
            to = pl.ds(pl.multiple_of((pos_ref[0] ^ k) * span, span), span)
            out_ref[to, :] = (keep[rows, :] + got[rows, :].astype(F32)).astype(BF16)


def join(pos, pairs):
    columns = pairs[0][0].shape[1]
    args = [x for pair in pairs for x in pair]
    return call(join_kernel, "join", 2, shape((STRIDE, columns)), (pos, *args))


def swap(value, distance):
    return lax.ppermute(value, "head", [(i, i ^ distance) for i in range(4)])


def exchange(messages):
    peers = lax.axis_size("seq")

    def move(value, k):
        return lax.ppermute(value, "seq", [(i, i ^ k) for i in range(peers)]) if k else value

    return [move(m, k) for m, k in zip(messages, ORDER)]


def gather(own):
    across = swap(own, 2)
    return own, swap(own, 1), across, swap(across, 1)


def chunked(tokens, w_query, w_key, w_value, w_out):
    owners = lax.axis_size("seq")
    head = lax.axis_index("head")
    block = lax.axis_index("seq")
    order = jnp.bitwise_xor(jnp.arange(4, dtype=jnp.int32), head.astype(jnp.int32))
    pos = jnp.stack([block, head % 2, head // 2]).astype(jnp.int32)
    rows, width = tokens.shape

    across = swap(tokens, 2)
    block_tokens, sent = pack(pos, tokens, owners)
    messages = exchange(sent)
    part = rows // owners // CHUNKS
    classes = [
        jnp.concatenate([m[i * part : (i + 1) * part] for m in messages], 0) for i in range(CHUNKS)
    ]
    across = fence(across, classes[0])
    pieces = (block_tokens, swap(fence(block_tokens, classes[0]), 1), across, swap(across, 1))
    first_pieces = gather(classes[0])
    weights = stage(order, (w_query, w_key, w_value), messages[1])
    w_other = swap(w_out, 1)
    own_halo = call(
        halo_kernel, "project_halo", 1.5, shape((2 * STRIDE, width)), (*pieces, *weights[1:])
    )
    halo = lax.ppermute(own_halo, "seq", [(i, i + 1) for i in range(owners - 1)])
    q, k, v = call(
        project_kernel,
        "project_block",
        6,
        [shape((rows, width))] * 3,
        (*pieces, *weights, own_halo),
    )
    class_pieces = (first_pieces, gather(fence(classes[1], first_pieces[2], q)))
    locals_ = local_part(pos, q, k, v, halo, owners, ())
    columns, after = [], (locals_[0][0],)
    for c in class_pieces:
        columns = column_part(pos, c, weights, columns, owners, after)
        after = ()
    columns = dict(zip(ORDER, exchange(columns)))
    pairs, after, gate = [], (), ()
    for half in HALVES:
        own, send = mix(pos, half, [columns[n] for n in half], locals_, after)
        out, keep = out_project(pos, own, swap(send, 1), w_out, w_other, gate)
        pairs.append((keep, swap(out, 2)))
        after, gate = (keep,), (pairs[-1][1],)
    return join(pos, pairs)


def from_behind(value, axis, by):
    peers = lax.axis_size(axis)
    pairs = [(i, i + by) for i in range(peers) if 0 <= i + by < peers]
    return lax.ppermute(value, axis, pairs)


def general(tokens, w_query, w_key, w_value, w_out):
    tok_rows = tokens.shape[0]
    head_width = w_query.shape[1]
    head_count = head_width // DH
    score_scale = DH ** (-0.5)
    shard_piece = lax.all_gather(tokens, "head", axis=1, tiled=True)
    query_full, key_full, value_full = tuple(
        (
            jnp.dot(shard_piece, weight, preferred_element_type=jnp.float32)
            for weight in (w_query, w_key, w_value)
        )
    )
    query = query_full.astype(jnp.bfloat16).reshape(tok_rows, head_count, DH)
    key_heads = key_full.astype(jnp.bfloat16).reshape(tok_rows, head_count, DH)
    value_heads = value_full.astype(jnp.bfloat16).reshape(tok_rows, head_count, DH)
    prev_keys, prev_values = from_behind((key_heads[-STRIDE:], value_heads[-STRIDE:]), "seq", 1)
    blocks = tok_rows // STRIDE
    extended_keys = jnp.concatenate([prev_keys, key_heads], 0)
    extended_values = jnp.concatenate([prev_values, value_heads], 0)
    window_keys = jnp.concatenate(
        [
            extended_keys[:tok_rows].reshape(blocks, STRIDE, head_count, DH),
            extended_keys[STRIDE:].reshape(blocks, STRIDE, head_count, DH),
        ],
        1,
    )
    window_values = jnp.concatenate(
        [
            extended_values[:tok_rows].reshape(blocks, STRIDE, head_count, DH),
            extended_values[STRIDE:].reshape(blocks, STRIDE, head_count, DH),
        ],
        1,
    )
    query_blocks = query.reshape(blocks, STRIDE, head_count, DH)
    scores = (
        jnp.einsum("bthd,buhd->bhtu", query_blocks, window_keys, preferred_element_type=jnp.float32)
        * score_scale
    )
    first_position = lax.axis_index("seq") * tok_rows
    block_index = jnp.arange(blocks)[:, None, None, None]
    query_index = jnp.arange(STRIDE)[None, None, :, None]
    key_index = jnp.arange(2 * STRIDE)[None, None, None, :]
    allowed = (
        (key_index > query_index)
        & (key_index <= query_index + STRIDE)
        & (first_position + block_index * STRIDE + key_index - STRIDE >= 0)
    )
    local_top = jnp.max(jnp.where(allowed, scores, -1e30), axis=-1)
    local_weights = jnp.where(allowed, jnp.exp(scores - local_top[..., None]), 0.0)
    local_total = jnp.sum(local_weights, axis=-1)
    local_out = jnp.einsum(
        "bhtu,buhd->bthd",
        local_weights.astype(jnp.bfloat16),
        window_values,
        preferred_element_type=jnp.float32,
    )
    local_out = local_out.reshape(tok_rows, head_count, DH)
    local_top = local_top.transpose(0, 2, 1).reshape(tok_rows, head_count)
    local_total = local_total.transpose(0, 2, 1).reshape(tok_rows, head_count)
    row_count = tok_rows // STRIDE
    query_class = lax.all_to_all(
        query.reshape(row_count, STRIDE, head_count, DH),
        "seq",
        split_axis=1,
        concat_axis=0,
        tiled=True,
    )
    key_class = lax.all_to_all(
        key_heads.reshape(row_count, STRIDE, head_count, DH),
        "seq",
        split_axis=1,
        concat_axis=0,
        tiled=True,
    )
    value_class = lax.all_to_all(
        value_heads.reshape(row_count, STRIDE, head_count, DH),
        "seq",
        split_axis=1,
        concat_axis=0,
        tiled=True,
    )
    row_total = query_class.shape[0]
    class_scores = (
        jnp.einsum("rchd,schd->chrs", query_class, key_class, preferred_element_type=jnp.float32)
        * score_scale
    )
    earlier = (
        jnp.arange(row_total)[None, None, :, None] > jnp.arange(row_total)[None, None, None, :]
    )
    class_top = jnp.max(jnp.where(earlier, class_scores, -1e30), axis=-1)
    class_weights = jnp.where(earlier, jnp.exp(class_scores - class_top[..., None]), 0.0)
    class_total = jnp.sum(class_weights, axis=-1)
    summed = jnp.einsum(
        "chrs,schd->rchd",
        class_weights.astype(jnp.bfloat16),
        value_class,
        preferred_element_type=jnp.float32,
    )
    floor_total = jnp.maximum(class_total, 1.0).transpose(2, 0, 1)
    class_out = (summed / floor_total[..., None]).astype(jnp.bfloat16)
    class_top_rows = class_top.transpose(2, 0, 1)
    class_total_rows = class_total.transpose(2, 0, 1)
    column_out = class_out
    column_top = class_top_rows
    column_total = class_total_rows
    column_out, column_top, column_total = (
        lax.all_to_all(column_out, "seq", split_axis=0, concat_axis=1, tiled=True),
        lax.all_to_all(
            column_top.astype(jnp.bfloat16), "seq", split_axis=0, concat_axis=1, tiled=True
        ).astype(column_top.dtype),
        lax.all_to_all(
            column_total.astype(jnp.bfloat16), "seq", split_axis=0, concat_axis=1, tiled=True
        ).astype(column_total.dtype),
    )
    column_out = column_out.reshape(tok_rows, head_count, DH)
    column_top = column_top.reshape(tok_rows, head_count)
    column_total = column_total.reshape(tok_rows, head_count)
    top_score = jnp.maximum(local_top, column_top)
    local_weight = jnp.exp(local_top - top_score)
    column_weight = column_total * jnp.exp(column_top - top_score)
    denominator = local_total * local_weight + column_weight
    mixed = (
        local_out * local_weight[..., None]
        + column_out.astype(jnp.float32) * column_weight[..., None]
    ) / denominator[..., None]
    mixed = mixed.astype(jnp.bfloat16).reshape(tok_rows, head_width)
    return lax.psum_scatter(
        jnp.dot(mixed, w_out, preferred_element_type=jnp.float32).astype(jnp.bfloat16),
        "head",
        scatter_dimension=0,
        tiled=True,
    )


def shards(tokens, w_query, w_key, w_value, w_out):
    rows, width = w_query.shape
    fits = (
        lax.axis_size("seq") == len(ORDER)
        and lax.axis_size("head") == 4
        and tokens.shape == (ROWS * STRIDE, HEADS * DH)
        and (rows, width) == (4 * HEADS * DH, HEADS * DH)
    )
    plan = chunked if fits else general
    return plan(tokens, w_query, w_key, w_value, w_out)


def solution(mesh):
    in_specs = (
        P("seq", "head"),
        P(None, "head"),
        P(None, "head"),
        P(None, "head"),
        P("head", None),
    )
    out_specs = P(("seq", "head"), None)
    return jax.shard_map(shards, mesh=mesh, in_specs=in_specs, out_specs=out_specs, check_vma=False)
```

```python
import functools

import jax
import jax.numpy as jnp
from jax import lax
from jax.experimental import pallas as pl
from jax.experimental.pallas import tpu as pltpu
from jax.sharding import PartitionSpec as P

DH = 128
STRIDE = 256
HEADS = 4
ROWS = 4
SUB = 8
CHUNKS = 2
PEERS = 8
SHARES = ((4, 5, 1, 2, 3, 0), (6, 7))
SCALE2 = DH ** (-0.5) * 1.4426950408889634
FLOOR = -1e29
MIB = 1024 * 1024
F32 = jnp.float32
BF16 = jnp.bfloat16


ANYWHERE = pl.BlockSpec(memory_space=pl.ANY)
IN_VMEM = pl.BlockSpec(memory_space=pltpu.VMEM)
IN_SMEM = pl.BlockSpec(memory_space=pltpu.SMEM)


def call(body, name, micros, out_shape, args, after=(), scratch=(), mib=24):
    specs = [IN_SMEM if x.dtype == jnp.int32 else IN_VMEM for x in args]
    extra = len(after)

    def run(*refs):
        n = len(args)
        body(*refs[:n], *refs[n + extra :])

    return pl.pallas_call(
        run,
        in_specs=specs + [ANYWHERE] * extra,
        out_specs=jax.tree.map(lambda _: IN_VMEM, out_shape),
        out_shape=out_shape,
        scratch_shapes=list(scratch),
        compiler_params=pltpu.CompilerParams(vmem_limit_bytes=mib * MIB),
        cost_estimate=pl.CostEstimate(
            flops=int(micros * 1.1e9), bytes_accessed=MIB, transcendentals=0
        ),
        name=name,
    )(*args, *after)


def fence(value, *after):
    return pl.pallas_call(
        lambda *refs: None,
        in_specs=[ANYWHERE] * (1 + len(after)),
        out_specs=ANYWHERE,
        out_shape=jax.ShapeDtypeStruct(value.shape, value.dtype),
        input_output_aliases={0: 0},
        compiler_params=pltpu.CompilerParams(vmem_limit_bytes=MIB),
        cost_estimate=pl.CostEstimate(flops=0, bytes_accessed=0, transcendentals=0),
        name="fence",
    )(value, *after)


def in_hbm(value):
    return pltpu.with_memory_space_constraint(value, pltpu.HBM)


def shape(dims, dtype=BF16):
    return jax.ShapeDtypeStruct(tuple(dims), dtype)


def dot(a, b):
    return jnp.dot(a, b, preferred_element_type=F32)


def dot_t(a, b):
    return lax.dot_general(a, b, (((1,), (1,)), ((), ())), preferred_element_type=F32)


def dot_l(a, b):
    return lax.dot_general(a, b, (((0,), (0,)), ((), ())), preferred_element_type=F32)


def pack_kernel(pos_ref, tok_hbm, tok_ref, *rest):
    out_refs, sems = rest[:-1], rest[-1]
    spans = [slice(r * STRIDE, (r + 1) * STRIDE) for r in range(ROWS)]
    copies = [
        pltpu.make_async_copy(tok_hbm.at[at], tok_ref.at[at], sems.at[r])
        for r, at in enumerate(spans)
    ]
    for c in copies:
        c.start()
    for c in copies:
        c.wait()
    per_owner = STRIDE // len(out_refs)
    part = ROWS * SUB
    for k, out_ref in enumerate(out_refs):
        d = pos_ref[0] ^ k
        rows = [
            tok_ref[pl.ds(pl.multiple_of(r * STRIDE + d * per_owner, per_owner), per_owner), :]
            for r in range(ROWS)
        ]
        rows = [x.astype(F32) for x in rows]
        for g in range(per_owner // SUB):
            piece = jnp.concatenate([x[g * SUB : (g + 1) * SUB] for x in rows], 0)
            out_ref[g * part : (g + 1) * part, :] = piece.astype(BF16)


def pack(pos, tokens, owners):
    message = shape((tokens.shape[0] // owners, tokens.shape[1]))
    outs = pl.pallas_call(
        pack_kernel,
        in_specs=[IN_SMEM, ANYWHERE],
        out_specs=[IN_VMEM] * (1 + owners),
        out_shape=[shape(tokens.shape)] + [message] * owners,
        scratch_shapes=[pltpu.SemaphoreType.DMA((ROWS,))],
        compiler_params=pltpu.CompilerParams(vmem_limit_bytes=8 * MIB),
        cost_estimate=pl.CostEstimate(flops=0, bytes_accessed=2 * MIB, transcendentals=0),
        name="pack_tokens",
    )(pos, in_hbm(tokens))
    return outs[0], outs[1:]


def stage_kernel(order_ref, wq, wk, wv, oq, ok, ov, sems):
    copies = []
    for n, (w, o) in enumerate(((wq, oq), (wk, ok), (wv, ov))):
        for p in range(4):
            rows = pl.ds(pl.multiple_of(order_ref[p] * 512, 512), 512)
            copies.append(
                pltpu.make_async_copy(w.at[rows], o.at[p * 512 : (p + 1) * 512], sems.at[4 * n + p])
            )
    for c in copies:
        c.start()
    for c in copies:
        c.wait()


def stage(order, weights, after):
    def body(order_ref, wq, wk, wv, _, *rest):
        stage_kernel(order_ref, wq, wk, wv, *rest)

    return pl.pallas_call(
        body,
        in_specs=[IN_SMEM] + [ANYWHERE] * 4,
        out_specs=[IN_VMEM] * 3,
        out_shape=[shape(w.shape) for w in weights],
        scratch_shapes=[pltpu.SemaphoreType.DMA((12,))],
        compiler_params=pltpu.CompilerParams(vmem_limit_bytes=16 * MIB),
        cost_estimate=pl.CostEstimate(flops=0, bytes_accessed=6 * MIB, transcendentals=0),
        name="stage_weights",
    )(order, *weights, after)


def gathered(x_refs, at, w_ref):
    width = x_refs[0].shape[1]
    total = None
    for p, x_ref in enumerate(x_refs):
        term = dot(x_ref[at, :], w_ref[p * width : (p + 1) * width, :])
        total = term if total is None else total + term
    return total.astype(BF16)


def halo_kernel(x0, x1, x2, x3, wk, wv, out_ref):
    rows = x0.shape[0]
    at = slice(rows - STRIDE, rows)
    out_ref[:STRIDE, :] = gathered((x0, x1, x2, x3), at, wk)
    out_ref[STRIDE:, :] = gathered((x0, x1, x2, x3), at, wv)


def project_kernel(x0, x1, x2, x3, wq, wk, wv, halo, q_ref, k_ref, v_ref):
    rows = x0.shape[0]
    xs = (x0, x1, x2, x3)
    last = slice(rows - STRIDE, rows)
    k_ref[last, :] = halo[:STRIDE, :]
    v_ref[last, :] = halo[STRIDE:, :]
    for w, out, upto in ((wq, q_ref, rows), (wk, k_ref, rows - STRIDE), (wv, v_ref, rows - STRIDE)):
        out[:upto, :] = gathered(xs, slice(0, upto), w)


def softmax_columns(s):
    m = jnp.maximum(jnp.max(s, 0, keepdims=True), FLOOR)
    p = jnp.exp2((s - m) * SCALE2)
    total = jnp.maximum(jnp.sum(p, 0, keepdims=True), 1.0)
    return p, total, m * SCALE2 + jnp.log2(total)


def local_kernel(pos_ref, q_ref, k_ref, v_ref, halo_ref, *outs):
    out_refs, lse_refs = outs[:CHUNKS], outs[CHUNKS:]
    owners, message, _ = out_refs[0].shape
    groups = message // ROWS // SUB
    block = pos_ref[0]
    u = lax.broadcasted_iota(jnp.int32, (STRIDE, STRIDE), 0)
    t = lax.broadcasted_iota(jnp.int32, (STRIDE, STRIDE), 1)
    current = u <= t
    low = jnp.where(block == 0, -1e30, 0.0).astype(F32)
    for r in range(ROWS):
        lses = []
        here = slice(r * STRIDE, (r + 1) * STRIDE)
        back = slice((r - 1) * STRIDE, r * STRIDE)
        for h in range(HEADS):
            cols = slice(h * DH, (h + 1) * DH)
            q = q_ref[here, cols]
            k_prev = k_ref[back, cols] if r else halo_ref[:STRIDE, cols]
            v_prev = v_ref[back, cols] if r else halo_ref[STRIDE:, cols]
            s_prev = dot_t(k_prev, q)
            if r == 0:
                s_prev = s_prev + low
            p, total, lse = softmax_columns(jnp.where(current, dot_t(k_ref[here, cols], q), s_prev))
            p_now = jnp.where(current, p, 0.0).astype(BF16)
            p_prev = jnp.where(current, 0.0, p).astype(BF16)
            o = dot_l(v_ref[here, cols], p_now) + dot_l(v_prev, p_prev)
            o = (o * (1.0 / total)).T
            lses.append(lse)
            for d in range(owners):
                for i in range(CHUNKS):
                    for g in range(groups):
                        at = ((d * CHUNKS + i) * groups + g) * SUB
                        to = (g * ROWS + r) * SUB
                        out_refs[i][d, to : to + SUB, cols] = o[at : at + SUB]
        lses.append(jnp.zeros((128 - HEADS, STRIDE), F32))
        turned = jnp.concatenate(lses, 0).T
        for i in range(CHUNKS):
            for g in range(groups):
                total = None
                for d in range(owners):
                    at = ((d * CHUNKS + i) * groups + g) * SUB
                    moved = pltpu.roll(turned[at : at + SUB], 8 * (block ^ d), 1)
                    total = moved if total is None else total + moved
                to = (g * ROWS + r) * SUB
                lse_refs[i][to : to + SUB, :] = total


def local_part(pos, q, k, v, halo, owners, after):
    rows, width = q.shape
    message = rows // owners // CHUNKS
    shapes = [shape((owners, message, width), F32)] * CHUNKS + [shape((message, 128), F32)] * CHUNKS
    outs = call(local_kernel, "local_part", 5, shapes, (pos, q, k, v, halo), after)
    return list(zip(outs[:CHUNKS], outs[CHUNKS:]))


def column_kernel(pos_ref, x0, x1, x2, x3, wq, wk, wv, *rest):
    refs, scratch = rest[:-3], rest[-3:]
    owners, message, _ = scratch[0].shape
    out_refs = refs[-owners:]
    size = HEADS * message + 16
    base = out_refs[0].shape[0] - size
    for old, new in zip(refs[:-owners], out_refs):
        new[:base, :] = old[...]
    groups = message // (ROWS * SUB)
    everything = slice(0, owners * message)
    for w, a in zip((wq, wk, wv), scratch):
        a[...] = gathered((x0, x1, x2, x3), everything, w).reshape(a.shape)
    part = ROWS * SUB
    size = owners * part

    def row_and_class(dim):
        i = lax.broadcasted_iota(jnp.int32, (size, size), dim)
        return ((i // part) ^ pos_ref[0]) * ROWS + (i % part) // SUB, i % SUB

    (row_j, class_j), (row_i, class_i) = row_and_class(0), row_and_class(1)
    earlier = jnp.logical_and(class_i == class_j, row_i > row_j)
    stats = []
    for g in range(groups):
        at = slice(g * part, (g + 1) * part)
        lses = []
        for h in range(HEADS):
            cols = slice(h * DH, (h + 1) * DH)
            q, k, v = (a[:, at, cols].reshape(size, DH) for a in scratch)
            p, total, lse = softmax_columns(jnp.where(earlier, dot_t(k, q), -1e30))
            o = (dot_l(v, p.astype(BF16)) * (1.0 / total)).T.astype(BF16)
            to = base + h * message + g * part
            rows = slice(to, to + part)
            for n in range(owners):
                out_refs[n][rows, :] = o[n * part : (n + 1) * part]
            lses.append(lse)
        stats.append(jnp.concatenate(lses + lses, 0))
    upper = lax.broadcasted_iota(jnp.int32, (8, 128), 0) < HEADS
    blank = [jnp.zeros((8, 128 - message), F32)] if message < 128 else []
    for n in range(owners):
        x = jnp.concatenate([s[:, n * part : (n + 1) * part] for s in stats] + blank, 1)
        hi = x.astype(BF16).astype(F32)
        mid = (x - hi).astype(BF16).astype(F32)
        lo = x - hi - mid
        tail = jnp.concatenate([jnp.where(upper, hi, lo), jnp.where(upper, mid, 0.0)], 0)
        to = base + HEADS * message
        out_refs[n][to : to + 16, :] = tail.astype(BF16)


def column_part(pos, pieces, weights, earlier, owners, after):
    tokens, width = pieces[0].shape
    message = tokens // owners
    rows = HEADS * message + 16 + (earlier[0].shape[0] if earlier else 0)
    scratch = [pltpu.VMEM((owners, message, width), BF16)] * 3
    args = (pos, *pieces, *weights, *earlier)
    return call(column_kernel, "column_part", 6, [shape((rows, DH))] * owners, args, after, scratch)


def mix_kernel(share, pos_ref, *refs):
    local_refs, refs = refs[: 2 * CHUNKS], refs[2 * CHUNKS :]
    col_refs, (own_ref, send_ref, mixed) = refs[:-3], refs[-3:]
    message = local_refs[0].shape[1]
    groups = message // (ROWS * SUB)
    size = HEADS * message + 16
    span = groups * SUB
    for i in range(CHUNKS):
        loc_ref, lse_ref = local_refs[2 * i : 2 * i + 2]
        tiles = [jnp.zeros((8, 128), F32)] * 16
        base = i * size
        for k, col_ref in zip(share, col_refs):
            tail = col_ref[base + HEADS * message : base + size, :].astype(F32)
            tiles[k] = tail[:8] + tail[8:]
        turned = jnp.concatenate(tiles, 0).T[:message]
        col_lse = turned + pltpu.roll(turned, 124, 1)
        loc_lse = lse_ref[...]
        top = jnp.maximum(col_lse, loc_lse)
        w_col = jnp.exp2(col_lse - top)
        w_loc = jnp.exp2(loc_lse - top)
        scale = 1.0 / (w_col + w_loc)
        w_col = w_col * scale
        w_loc = w_loc * scale
        for n, (k, col_ref) in enumerate(zip(share, col_refs)):
            d = pos_ref[0] ^ k
            to = (n * CHUNKS + i) * span
            for h in range(HEADS):
                cols = slice(h * DH, (h + 1) * DH)
                at = slice(8 * k + h, 8 * k + h + 1)
                col = col_ref[base + h * message : base + (h + 1) * message, :].astype(F32)
                both = loc_ref[d, :, cols] * w_loc[:, at] + col * w_col[:, at]
                for r in range(ROWS):
                    starts = [(g * ROWS + r) * SUB for g in range(groups)]
                    piece = jnp.concatenate([both[s : s + SUB] for s in starts], 0)
                    mixed[r, to : to + span, cols] = piece.astype(BF16)
    core = pos_ref[1]
    for x in range(2):
        own_ref[x] = mixed[2 * x + core]
        send_ref[x] = mixed[2 * x + 1 - core]


def mix(pos, share, columns, locals_, after):
    owners, message, width = locals_[0][0].shape
    tokens = len(share) * CHUNKS * message // ROWS
    shapes = [shape((2, tokens, width))] * 2
    scratch = [pltpu.VMEM((ROWS, tokens, width), BF16)]
    args = (pos, *[x for pair in locals_ for x in pair], *columns)
    return call(functools.partial(mix_kernel, share), "mix", 2, shapes, args, after, scratch)


def out_kernel(pos_ref, a_ref, b_ref, wa_ref, wb_ref, send_ref, keep_ref):
    tokens, columns = send_ref.shape
    a = a_ref[...].reshape(2 * tokens, -1)
    b = b_ref[...].reshape(2 * tokens, -1)
    low_side = pos_ref[2] == 0
    tile = 512
    for n in range(0, columns, tile):
        at = slice(n, n + tile)
        total = dot(a, wa_ref[:, at]) + dot(b, wb_ref[:, at])
        send_ref[:, at] = jnp.where(low_side, total[tokens:], total[:tokens]).astype(BF16)
        keep_ref[:, at] = jnp.where(low_side, total[:tokens], total[tokens:])


def out_project(pos, own, other, w_own, w_other):
    dims = (own.shape[1], w_own.shape[1])
    shapes = [shape(dims), shape(dims, F32)]
    return call(out_kernel, "out_project", 2, shapes, (pos, own, other, w_own, w_other))


def join_kernel(pos_ref, *refs):
    out_ref = refs[-1]
    for share, keep, got in zip(SHARES, refs[0:-1:2], refs[1:-1:2]):
        span = keep.shape[0] // len(share)
        for n, k in enumerate(share):
            rows = slice(n * span, (n + 1) * span)
            to = pl.ds(pl.multiple_of((pos_ref[0] ^ k) * span, span), span)
            out_ref[to, :] = (keep[rows, :] + got[rows, :].astype(F32)).astype(BF16)


def join(pos, pairs):
    columns = pairs[0][0].shape[1]
    args = [x for pair in pairs for x in pair]
    return call(join_kernel, "join", 2, shape((STRIDE, columns)), (pos, *args))


def swap(value, distance):
    return lax.ppermute(value, "head", [(i, i ^ distance) for i in range(4)])


def exchange(messages):
    peers = lax.axis_size("seq")

    def move(value, k):
        return lax.ppermute(value, "seq", [(i, i ^ k) for i in range(peers)]) if k else value

    return [move(m, k) for k, m in enumerate(messages)]


def chunked(tokens, w_query, w_key, w_value, w_out):
    owners = lax.axis_size("seq")
    head = lax.axis_index("head")
    block = lax.axis_index("seq")
    order = jnp.bitwise_xor(jnp.arange(4, dtype=jnp.int32), head.astype(jnp.int32))
    pos = jnp.stack([block, head % 2, head // 2]).astype(jnp.int32)
    rows, width = tokens.shape

    across = swap(tokens, 2)
    block_tokens, sent = pack(pos, tokens, owners)
    messages = exchange(sent)
    part = rows // owners // CHUNKS
    classes = [
        jnp.concatenate([m[i * part : (i + 1) * part] for m in messages], 0) for i in range(CHUNKS)
    ]
    across = fence(across, classes[0])
    pieces = (block_tokens, swap(fence(block_tokens, classes[0]), 1), across, swap(across, 1))
    first, first_core, first_across = classes[0], swap(classes[0], 1), swap(classes[0], 2)
    weights = stage(order, (w_query, w_key, w_value), messages[1])
    w_other = swap(w_out, 1)
    own_halo = call(
        halo_kernel, "project_halo", 1.5, shape((2 * STRIDE, width)), (*pieces, *weights[1:])
    )
    halo = lax.ppermute(own_halo, "seq", [(i, i + 1) for i in range(owners - 1)])
    q, k, v = call(
        project_kernel,
        "project_block",
        6,
        [shape((rows, width))] * 3,
        (*pieces, *weights, own_halo),
        (w_other,),
    )
    first_across = fence(first_across, q)
    first_pieces = (first, first_core, first_across, swap(first_across, 1))
    second = fence(classes[1], first_across)
    second_core, second_across = swap(second, 1), swap(second, 2)
    locals_ = local_part(pos, q, k, v, halo, owners, ())
    columns = column_part(pos, first_pieces, weights, (), owners, (locals_[0][0],))
    second_across = fence(second_across, columns[0])
    second_pieces = (second, second_core, second_across, swap(second_across, 1))
    columns = column_part(pos, second_pieces, weights, columns, owners, ())
    columns = exchange(columns)
    pairs, after = [], ()
    for share in SHARES:
        own, send = mix(pos, share, [columns[n] for n in share], locals_, after)
        out, keep = out_project(pos, own, swap(send, 1), w_out, w_other)
        pairs.append((keep, swap(out, 2)))
        after = (keep,)
    return join(pos, pairs)


def from_behind(value, axis, by):
    peers = lax.axis_size(axis)
    pairs = [(i, i + by) for i in range(peers) if 0 <= i + by < peers]
    return lax.ppermute(value, axis, pairs)


def general(tokens, w_query, w_key, w_value, w_out):
    tok_rows = tokens.shape[0]
    head_width = w_query.shape[1]
    head_count = head_width // DH
    score_scale = DH ** (-0.5)
    shard_piece = lax.all_gather(tokens, "head", axis=1, tiled=True)
    query_full, key_full, value_full = tuple(
        (
            jnp.dot(shard_piece, weight, preferred_element_type=jnp.float32)
            for weight in (w_query, w_key, w_value)
        )
    )
    query = query_full.astype(jnp.bfloat16).reshape(tok_rows, head_count, DH)
    key_heads = key_full.astype(jnp.bfloat16).reshape(tok_rows, head_count, DH)
    value_heads = value_full.astype(jnp.bfloat16).reshape(tok_rows, head_count, DH)
    prev_keys, prev_values = from_behind((key_heads[-STRIDE:], value_heads[-STRIDE:]), "seq", 1)
    blocks = tok_rows // STRIDE
    extended_keys = jnp.concatenate([prev_keys, key_heads], 0)
    extended_values = jnp.concatenate([prev_values, value_heads], 0)
    window_keys = jnp.concatenate(
        [
            extended_keys[:tok_rows].reshape(blocks, STRIDE, head_count, DH),
            extended_keys[STRIDE:].reshape(blocks, STRIDE, head_count, DH),
        ],
        1,
    )
    window_values = jnp.concatenate(
        [
            extended_values[:tok_rows].reshape(blocks, STRIDE, head_count, DH),
            extended_values[STRIDE:].reshape(blocks, STRIDE, head_count, DH),
        ],
        1,
    )
    query_blocks = query.reshape(blocks, STRIDE, head_count, DH)
    scores = (
        jnp.einsum("bthd,buhd->bhtu", query_blocks, window_keys, preferred_element_type=jnp.float32)
        * score_scale
    )
    first_position = lax.axis_index("seq") * tok_rows
    block_index = jnp.arange(blocks)[:, None, None, None]
    query_index = jnp.arange(STRIDE)[None, None, :, None]
    key_index = jnp.arange(2 * STRIDE)[None, None, None, :]
    allowed = (
        (key_index > query_index)
        & (key_index <= query_index + STRIDE)
        & (first_position + block_index * STRIDE + key_index - STRIDE >= 0)
    )
    local_top = jnp.max(jnp.where(allowed, scores, -1e30), axis=-1)
    local_weights = jnp.where(allowed, jnp.exp(scores - local_top[..., None]), 0.0)
    local_total = jnp.sum(local_weights, axis=-1)
    local_out = jnp.einsum(
        "bhtu,buhd->bthd",
        local_weights.astype(jnp.bfloat16),
        window_values,
        preferred_element_type=jnp.float32,
    )
    local_out = local_out.reshape(tok_rows, head_count, DH)
    local_top = local_top.transpose(0, 2, 1).reshape(tok_rows, head_count)
    local_total = local_total.transpose(0, 2, 1).reshape(tok_rows, head_count)
    row_count = tok_rows // STRIDE
    query_class = lax.all_to_all(
        query.reshape(row_count, STRIDE, head_count, DH),
        "seq",
        split_axis=1,
        concat_axis=0,
        tiled=True,
    )
    key_class = lax.all_to_all(
        key_heads.reshape(row_count, STRIDE, head_count, DH),
        "seq",
        split_axis=1,
        concat_axis=0,
        tiled=True,
    )
    value_class = lax.all_to_all(
        value_heads.reshape(row_count, STRIDE, head_count, DH),
        "seq",
        split_axis=1,
        concat_axis=0,
        tiled=True,
    )
    row_total = query_class.shape[0]
    class_scores = (
        jnp.einsum("rchd,schd->chrs", query_class, key_class, preferred_element_type=jnp.float32)
        * score_scale
    )
    earlier = (
        jnp.arange(row_total)[None, None, :, None] > jnp.arange(row_total)[None, None, None, :]
    )
    class_top = jnp.max(jnp.where(earlier, class_scores, -1e30), axis=-1)
    class_weights = jnp.where(earlier, jnp.exp(class_scores - class_top[..., None]), 0.0)
    class_total = jnp.sum(class_weights, axis=-1)
    summed = jnp.einsum(
        "chrs,schd->rchd",
        class_weights.astype(jnp.bfloat16),
        value_class,
        preferred_element_type=jnp.float32,
    )
    floor_total = jnp.maximum(class_total, 1.0).transpose(2, 0, 1)
    class_out = (summed / floor_total[..., None]).astype(jnp.bfloat16)
    class_top_rows = class_top.transpose(2, 0, 1)
    class_total_rows = class_total.transpose(2, 0, 1)
    column_out = class_out
    column_top = class_top_rows
    column_total = class_total_rows
    column_out, column_top, column_total = (
        lax.all_to_all(column_out, "seq", split_axis=0, concat_axis=1, tiled=True),
        lax.all_to_all(
            column_top.astype(jnp.bfloat16), "seq", split_axis=0, concat_axis=1, tiled=True
        ).astype(column_top.dtype),
        lax.all_to_all(
            column_total.astype(jnp.bfloat16), "seq", split_axis=0, concat_axis=1, tiled=True
        ).astype(column_total.dtype),
    )
    column_out = column_out.reshape(tok_rows, head_count, DH)
    column_top = column_top.reshape(tok_rows, head_count)
    column_total = column_total.reshape(tok_rows, head_count)
    top_score = jnp.maximum(local_top, column_top)
    local_weight = jnp.exp(local_top - top_score)
    column_weight = column_total * jnp.exp(column_top - top_score)
    denominator = local_total * local_weight + column_weight
    mixed = (
        local_out * local_weight[..., None]
        + column_out.astype(jnp.float32) * column_weight[..., None]
    ) / denominator[..., None]
    mixed = mixed.astype(jnp.bfloat16).reshape(tok_rows, head_width)
    return lax.psum_scatter(
        jnp.dot(mixed, w_out, preferred_element_type=jnp.float32).astype(jnp.bfloat16),
        "head",
        scatter_dimension=0,
        tiled=True,
    )


def shards(tokens, w_query, w_key, w_value, w_out):
    rows, width = w_query.shape
    fits = (
        lax.axis_size("seq") == PEERS
        and lax.axis_size("head") == 4
        and tokens.shape == (ROWS * STRIDE, HEADS * DH)
        and (rows, width) == (4 * HEADS * DH, HEADS * DH)
    )
    plan = chunked if fits else general
    return plan(tokens, w_query, w_key, w_value, w_out)


def solution(mesh):
    in_specs = (
        P("seq", "head"),
        P(None, "head"),
        P(None, "head"),
        P(None, "head"),
        P("head", None),
    )
    out_specs = P(("seq", "head"), None)
    return jax.shard_map(shards, mesh=mesh, in_specs=in_specs, out_specs=out_specs, check_vma=False)
```

```python
import functools

import jax
import jax.numpy as jnp
from jax import lax
from jax.experimental import pallas as pl
from jax.experimental.pallas import tpu as pltpu
from jax.sharding import PartitionSpec as P

DH = 128
STRIDE = 256
HEADS = 4
ROWS = 4
SUB = 8
CHUNKS = 2
PEERS = 8
SHARES = ((4, 5, 1, 2, 3, 0), (6, 7))
SCALE2 = DH ** (-0.5) * 1.4426950408889634
FLOOR = -1e29
MIB = 1024 * 1024
F32 = jnp.float32
BF16 = jnp.bfloat16


ANYWHERE = pl.BlockSpec(memory_space=pl.ANY)
IN_VMEM = pl.BlockSpec(memory_space=pltpu.VMEM)
IN_SMEM = pl.BlockSpec(memory_space=pltpu.SMEM)


def call(body, name, micros, out_shape, args, after=(), scratch=(), mib=24):
    specs = [IN_SMEM if x.dtype == jnp.int32 else IN_VMEM for x in args]
    extra = len(after)

    def run(*refs):
        n = len(args)
        body(*refs[:n], *refs[n + extra :])

    return pl.pallas_call(
        run,
        in_specs=specs + [ANYWHERE] * extra,
        out_specs=jax.tree.map(lambda _: IN_VMEM, out_shape),
        out_shape=out_shape,
        scratch_shapes=list(scratch),
        compiler_params=pltpu.CompilerParams(vmem_limit_bytes=mib * MIB),
        cost_estimate=pl.CostEstimate(
            flops=int(micros * 1.1e9), bytes_accessed=MIB, transcendentals=0
        ),
        name=name,
    )(*args, *after)


def fence(value, *after):
    return pl.pallas_call(
        lambda *refs: None,
        in_specs=[ANYWHERE] * (1 + len(after)),
        out_specs=ANYWHERE,
        out_shape=jax.ShapeDtypeStruct(value.shape, value.dtype),
        input_output_aliases={0: 0},
        compiler_params=pltpu.CompilerParams(vmem_limit_bytes=MIB),
        cost_estimate=pl.CostEstimate(flops=0, bytes_accessed=0, transcendentals=0),
        name="fence",
    )(value, *after)


def in_hbm(value):
    return pltpu.with_memory_space_constraint(value, pltpu.HBM)


def shape(dims, dtype=BF16):
    return jax.ShapeDtypeStruct(tuple(dims), dtype)


def dot(a, b):
    return jnp.dot(a, b, preferred_element_type=F32)


def dot_t(a, b):
    return lax.dot_general(a, b, (((1,), (1,)), ((), ())), preferred_element_type=F32)


def dot_l(a, b):
    return lax.dot_general(a, b, (((0,), (0,)), ((), ())), preferred_element_type=F32)


def pack_kernel(pos_ref, tok_hbm, tok_ref, *rest):
    out_refs, sems = rest[:-1], rest[-1]
    spans = [slice(r * STRIDE, (r + 1) * STRIDE) for r in range(ROWS)]
    copies = [
        pltpu.make_async_copy(tok_hbm.at[at], tok_ref.at[at], sems.at[r])
        for r, at in enumerate(spans)
    ]
    for c in copies:
        c.start()
    for c in copies:
        c.wait()
    per_owner = STRIDE // len(out_refs)
    part = ROWS * SUB
    for k, out_ref in enumerate(out_refs):
        d = pos_ref[0] ^ k
        rows = [
            tok_ref[pl.ds(pl.multiple_of(r * STRIDE + d * per_owner, per_owner), per_owner), :]
            for r in range(ROWS)
        ]
        rows = [x.astype(F32) for x in rows]
        for g in range(per_owner // SUB):
            piece = jnp.concatenate([x[g * SUB : (g + 1) * SUB] for x in rows], 0)
            out_ref[g * part : (g + 1) * part, :] = piece.astype(BF16)


def pack(pos, tokens, owners):
    message = shape((tokens.shape[0] // owners, tokens.shape[1]))
    outs = pl.pallas_call(
        pack_kernel,
        in_specs=[IN_SMEM, ANYWHERE],
        out_specs=[IN_VMEM] * (1 + owners),
        out_shape=[shape(tokens.shape)] + [message] * owners,
        scratch_shapes=[pltpu.SemaphoreType.DMA((ROWS,))],
        compiler_params=pltpu.CompilerParams(vmem_limit_bytes=8 * MIB),
        cost_estimate=pl.CostEstimate(flops=0, bytes_accessed=2 * MIB, transcendentals=0),
        name="pack_tokens",
    )(pos, in_hbm(tokens))
    return outs[0], outs[1:]


def stage_kernel(order_ref, wq, wk, wv, oq, ok, ov, sems):
    copies = []
    for n, (w, o) in enumerate(((wq, oq), (wk, ok), (wv, ov))):
        for p in range(4):
            rows = pl.ds(pl.multiple_of(order_ref[p] * 512, 512), 512)
            copies.append(
                pltpu.make_async_copy(w.at[rows], o.at[p * 512 : (p + 1) * 512], sems.at[4 * n + p])
            )
    for c in copies:
        c.start()
    for c in copies:
        c.wait()


def stage(order, weights, after):
    def body(order_ref, wq, wk, wv, _, *rest):
        stage_kernel(order_ref, wq, wk, wv, *rest)

    return pl.pallas_call(
        body,
        in_specs=[IN_SMEM] + [ANYWHERE] * 4,
        out_specs=[IN_VMEM] * 3,
        out_shape=[shape(w.shape) for w in weights],
        scratch_shapes=[pltpu.SemaphoreType.DMA((12,))],
        compiler_params=pltpu.CompilerParams(vmem_limit_bytes=16 * MIB),
        cost_estimate=pl.CostEstimate(flops=0, bytes_accessed=6 * MIB, transcendentals=0),
        name="stage_weights",
    )(order, *weights, after)


def gathered(x_refs, at, w_ref):
    width = x_refs[0].shape[1]
    total = None
    for p, x_ref in enumerate(x_refs):
        term = dot(x_ref[at, :], w_ref[p * width : (p + 1) * width, :])
        total = term if total is None else total + term
    return total.astype(BF16)


def halo_kernel(x0, x1, x2, x3, wk, wv, out_ref):
    rows = x0.shape[0]
    at = slice(rows - STRIDE, rows)
    out_ref[:STRIDE, :] = gathered((x0, x1, x2, x3), at, wk)
    out_ref[STRIDE:, :] = gathered((x0, x1, x2, x3), at, wv)


def project_kernel(x0, x1, x2, x3, wq, wk, wv, halo, q_ref, k_ref, v_ref):
    rows = x0.shape[0]
    xs = (x0, x1, x2, x3)
    last = slice(rows - STRIDE, rows)
    k_ref[last, :] = halo[:STRIDE, :]
    v_ref[last, :] = halo[STRIDE:, :]
    for w, out, upto in ((wq, q_ref, rows), (wk, k_ref, rows - STRIDE), (wv, v_ref, rows - STRIDE)):
        out[:upto, :] = gathered(xs, slice(0, upto), w)


def softmax_columns(s):
    m = jnp.maximum(jnp.max(s, 0, keepdims=True), FLOOR)
    p = jnp.exp2((s - m) * SCALE2)
    total = jnp.maximum(jnp.sum(p, 0, keepdims=True), 1.0)
    return p, total, m * SCALE2 + jnp.log2(total)


def local_kernel(pos_ref, q_ref, k_ref, v_ref, halo_ref, *outs):
    out_refs, lse_refs = outs[:CHUNKS], outs[CHUNKS:]
    owners, message, _ = out_refs[0].shape
    groups = message // ROWS // SUB
    block = pos_ref[0]
    u = lax.broadcasted_iota(jnp.int32, (STRIDE, STRIDE), 0)
    t = lax.broadcasted_iota(jnp.int32, (STRIDE, STRIDE), 1)
    current = u <= t
    low = jnp.where(block == 0, -1e30, 0.0).astype(F32)
    for r in range(ROWS):
        lses = []
        here = slice(r * STRIDE, (r + 1) * STRIDE)
        back = slice((r - 1) * STRIDE, r * STRIDE)
        for h in range(HEADS):
            cols = slice(h * DH, (h + 1) * DH)
            q = q_ref[here, cols]
            k_prev = k_ref[back, cols] if r else halo_ref[:STRIDE, cols]
            v_prev = v_ref[back, cols] if r else halo_ref[STRIDE:, cols]
            s_prev = dot_t(k_prev, q)
            if r == 0:
                s_prev = s_prev + low
            p, total, lse = softmax_columns(jnp.where(current, dot_t(k_ref[here, cols], q), s_prev))
            p_now = jnp.where(current, p, 0.0).astype(BF16)
            p_prev = jnp.where(current, 0.0, p).astype(BF16)
            o = dot_l(v_ref[here, cols], p_now) + dot_l(v_prev, p_prev)
            o = (o * (1.0 / total)).T
            lses.append(lse)
            for d in range(owners):
                for i in range(CHUNKS):
                    for g in range(groups):
                        at = ((d * CHUNKS + i) * groups + g) * SUB
                        to = (g * ROWS + r) * SUB
                        out_refs[i][d, to : to + SUB, cols] = o[at : at + SUB]
        lses.append(jnp.zeros((128 - HEADS, STRIDE), F32))
        turned = jnp.concatenate(lses, 0).T
        for i in range(CHUNKS):
            for g in range(groups):
                total = None
                for d in range(owners):
                    at = ((d * CHUNKS + i) * groups + g) * SUB
                    moved = pltpu.roll(turned[at : at + SUB], 8 * (block ^ d), 1)
                    total = moved if total is None else total + moved
                to = (g * ROWS + r) * SUB
                lse_refs[i][to : to + SUB, :] = total


def local_part(pos, q, k, v, halo, owners, after):
    rows, width = q.shape
    message = rows // owners // CHUNKS
    shapes = [shape((owners, message, width), F32)] * CHUNKS + [shape((message, 128), F32)] * CHUNKS
    outs = call(local_kernel, "local_part", 5, shapes, (pos, q, k, v, halo), after)
    return list(zip(outs[:CHUNKS], outs[CHUNKS:]))


def column_kernel(pos_ref, x0, x1, x2, x3, wq, wk, wv, *rest):
    refs, scratch = rest[:-3], rest[-3:]
    owners, message, _ = scratch[0].shape
    out_refs = refs[-owners:]
    size = HEADS * message + 16
    base = out_refs[0].shape[0] - size
    for old, new in zip(refs[:-owners], out_refs):
        new[:base, :] = old[...]
    groups = message // (ROWS * SUB)
    everything = slice(0, owners * message)
    for w, a in zip((wq, wk, wv), scratch):
        a[...] = gathered((x0, x1, x2, x3), everything, w).reshape(a.shape)
    part = ROWS * SUB
    size = owners * part

    def row_and_class(dim):
        i = lax.broadcasted_iota(jnp.int32, (size, size), dim)
        return ((i // part) ^ pos_ref[0]) * ROWS + (i % part) // SUB, i % SUB

    (row_j, class_j), (row_i, class_i) = row_and_class(0), row_and_class(1)
    earlier = jnp.logical_and(class_i == class_j, row_i > row_j)
    stats = []
    for g in range(groups):
        at = slice(g * part, (g + 1) * part)
        lses = []
        for h in range(HEADS):
            cols = slice(h * DH, (h + 1) * DH)
            q, k, v = (a[:, at, cols].reshape(size, DH) for a in scratch)
            p, total, lse = softmax_columns(jnp.where(earlier, dot_t(k, q), -1e30))
            o = (dot_l(v, p.astype(BF16)) * (1.0 / total)).T.astype(BF16)
            to = base + h * message + g * part
            rows = slice(to, to + part)
            for n in range(owners):
                out_refs[n][rows, :] = o[n * part : (n + 1) * part]
            lses.append(lse)
        stats.append(jnp.concatenate(lses + lses, 0))
    upper = lax.broadcasted_iota(jnp.int32, (8, 128), 0) < HEADS
    blank = [jnp.zeros((8, 128 - message), F32)] if message < 128 else []
    for n in range(owners):
        x = jnp.concatenate([s[:, n * part : (n + 1) * part] for s in stats] + blank, 1)
        hi = x.astype(BF16).astype(F32)
        mid = (x - hi).astype(BF16).astype(F32)
        lo = x - hi - mid
        tail = jnp.concatenate([jnp.where(upper, hi, lo), jnp.where(upper, mid, 0.0)], 0)
        to = base + HEADS * message
        out_refs[n][to : to + 16, :] = tail.astype(BF16)


def column_part(pos, pieces, weights, earlier, owners, after):
    tokens, width = pieces[0].shape
    message = tokens // owners
    rows = HEADS * message + 16 + (earlier[0].shape[0] if earlier else 0)
    scratch = [pltpu.VMEM((owners, message, width), BF16)] * 3
    args = (pos, *pieces, *weights, *earlier)
    return call(column_kernel, "column_part", 6, [shape((rows, DH))] * owners, args, after, scratch)


def mix_kernel(share, pos_ref, *refs):
    local_refs, refs = refs[: 2 * CHUNKS], refs[2 * CHUNKS :]
    col_refs, (own_ref, send_ref, mixed) = refs[:-3], refs[-3:]
    message = local_refs[0].shape[1]
    groups = message // (ROWS * SUB)
    size = HEADS * message + 16
    span = groups * SUB
    for i in range(CHUNKS):
        loc_ref, lse_ref = local_refs[2 * i : 2 * i + 2]
        tiles = [jnp.zeros((8, 128), F32)] * 16
        base = i * size
        for k, col_ref in zip(share, col_refs):
            tail = col_ref[base + HEADS * message : base + size, :].astype(F32)
            tiles[k] = tail[:8] + tail[8:]
        turned = jnp.concatenate(tiles, 0).T[:message]
        col_lse = turned + pltpu.roll(turned, 124, 1)
        loc_lse = lse_ref[...]
        top = jnp.maximum(col_lse, loc_lse)
        w_col = jnp.exp2(col_lse - top)
        w_loc = jnp.exp2(loc_lse - top)
        scale = 1.0 / (w_col + w_loc)
        w_col = w_col * scale
        w_loc = w_loc * scale
        for n, (k, col_ref) in enumerate(zip(share, col_refs)):
            d = pos_ref[0] ^ k
            to = (n * CHUNKS + i) * span
            for h in range(HEADS):
                cols = slice(h * DH, (h + 1) * DH)
                at = slice(8 * k + h, 8 * k + h + 1)
                col = col_ref[base + h * message : base + (h + 1) * message, :].astype(F32)
                both = loc_ref[d, :, cols] * w_loc[:, at] + col * w_col[:, at]
                for r in range(ROWS):
                    starts = [(g * ROWS + r) * SUB for g in range(groups)]
                    piece = jnp.concatenate([both[s : s + SUB] for s in starts], 0)
                    mixed[r, to : to + span, cols] = piece.astype(BF16)
    core = pos_ref[1]
    for x in range(2):
        own_ref[x] = mixed[2 * x + core]
        send_ref[x] = mixed[2 * x + 1 - core]


def mix(pos, share, columns, locals_, after):
    owners, message, width = locals_[0][0].shape
    tokens = len(share) * CHUNKS * message // ROWS
    shapes = [shape((2, tokens, width))] * 2
    scratch = [pltpu.VMEM((ROWS, tokens, width), BF16)]
    args = (pos, *[x for pair in locals_ for x in pair], *columns)
    return call(functools.partial(mix_kernel, share), "mix", 2, shapes, args, after, scratch)


def out_kernel(pos_ref, a_ref, b_ref, wa_ref, wb_ref, send_ref, keep_ref):
    tokens, columns = send_ref.shape
    a = a_ref[...].reshape(2 * tokens, -1)
    b = b_ref[...].reshape(2 * tokens, -1)
    low_side = pos_ref[2] == 0
    tile = 512
    for n in range(0, columns, tile):
        at = slice(n, n + tile)
        total = dot(a, wa_ref[:, at]) + dot(b, wb_ref[:, at])
        send_ref[:, at] = jnp.where(low_side, total[tokens:], total[:tokens]).astype(BF16)
        keep_ref[:, at] = jnp.where(low_side, total[:tokens], total[tokens:])


def out_project(pos, own, other, w_own, w_other):
    dims = (own.shape[1], w_own.shape[1])
    shapes = [shape(dims), shape(dims, F32)]
    return call(out_kernel, "out_project", 2, shapes, (pos, own, other, w_own, w_other))


def join_kernel(pos_ref, *refs):
    out_ref = refs[-1]
    for share, keep, got in zip(SHARES, refs[0:-1:2], refs[1:-1:2]):
        span = keep.shape[0] // len(share)
        for n, k in enumerate(share):
            rows = slice(n * span, (n + 1) * span)
            to = pl.ds(pl.multiple_of((pos_ref[0] ^ k) * span, span), span)
            out_ref[to, :] = (keep[rows, :] + got[rows, :].astype(F32)).astype(BF16)


def join(pos, pairs):
    columns = pairs[0][0].shape[1]
    args = [x for pair in pairs for x in pair]
    return call(join_kernel, "join", 2, shape((STRIDE, columns)), (pos, *args))


def swap(value, distance):
    return lax.ppermute(value, "head", [(i, i ^ distance) for i in range(4)])


def exchange(messages):
    peers = lax.axis_size("seq")

    def move(value, k):
        return lax.ppermute(value, "seq", [(i, i ^ k) for i in range(peers)]) if k else value

    return [move(m, k) for k, m in enumerate(messages)]


def chunked(tokens, w_query, w_key, w_value, w_out):
    owners = lax.axis_size("seq")
    head = lax.axis_index("head")
    block = lax.axis_index("seq")
    order = jnp.bitwise_xor(jnp.arange(4, dtype=jnp.int32), head.astype(jnp.int32))
    pos = jnp.stack([block, head % 2, head // 2]).astype(jnp.int32)
    rows, width = tokens.shape

    across = swap(tokens, 2)
    block_tokens, sent = pack(pos, tokens, owners)
    messages = exchange(sent)
    part = rows // owners // CHUNKS
    classes = [
        jnp.concatenate([m[i * part : (i + 1) * part] for m in messages], 0) for i in range(CHUNKS)
    ]
    across = fence(across, classes[0])
    pieces = (block_tokens, swap(fence(block_tokens, classes[0]), 1), across, swap(across, 1))
    first, first_core, first_across = classes[0], swap(classes[0], 1), swap(classes[0], 2)
    weights = stage(order, (w_query, w_key, w_value), messages[1])
    w_other = swap(w_out, 1)
    own_halo = call(
        halo_kernel, "project_halo", 1.5, shape((2 * STRIDE, width)), (*pieces, *weights[1:])
    )
    halo = lax.ppermute(own_halo, "seq", [(i, i + 1) for i in range(owners - 1)])
    q, k, v = call(
        project_kernel,
        "project_block",
        6,
        [shape((rows, width))] * 3,
        (*pieces, *weights, own_halo),
        (w_other,),
    )
    first_across = fence(first_across, q)
    first_pieces = (first, first_core, first_across, swap(first_across, 1))
    second = fence(classes[1], first_across)
    second_core, second_across = swap(second, 1), swap(second, 2)
    columns = column_part(pos, first_pieces, weights, (), owners, ())
    locals_ = local_part(pos, q, k, v, halo, owners, (columns[0],))
    second_across = fence(second_across, locals_[0][0])
    second_pieces = (second, second_core, second_across, swap(second_across, 1))
    columns = column_part(pos, second_pieces, weights, columns, owners, ())
    columns = exchange(columns)
    pairs, after = [], ()
    for share in SHARES:
        own, send = mix(pos, share, [columns[n] for n in share], locals_, after)
        out, keep = out_project(pos, own, swap(send, 1), w_out, w_other)
        pairs.append((keep, swap(out, 2)))
        after = (keep,)
    return join(pos, pairs)


def from_behind(value, axis, by):
    peers = lax.axis_size(axis)
    pairs = [(i, i + by) for i in range(peers) if 0 <= i + by < peers]
    return lax.ppermute(value, axis, pairs)


def general(tokens, w_query, w_key, w_value, w_out):
    tok_rows = tokens.shape[0]
    head_width = w_query.shape[1]
    head_count = head_width // DH
    score_scale = DH ** (-0.5)
    shard_piece = lax.all_gather(tokens, "head", axis=1, tiled=True)
    query_full, key_full, value_full = tuple(
        (
            jnp.dot(shard_piece, weight, preferred_element_type=jnp.float32)
            for weight in (w_query, w_key, w_value)
        )
    )
    query = query_full.astype(jnp.bfloat16).reshape(tok_rows, head_count, DH)
    key_heads = key_full.astype(jnp.bfloat16).reshape(tok_rows, head_count, DH)
    value_heads = value_full.astype(jnp.bfloat16).reshape(tok_rows, head_count, DH)
    prev_keys, prev_values = from_behind((key_heads[-STRIDE:], value_heads[-STRIDE:]), "seq", 1)
    blocks = tok_rows // STRIDE
    extended_keys = jnp.concatenate([prev_keys, key_heads], 0)
    extended_values = jnp.concatenate([prev_values, value_heads], 0)
    window_keys = jnp.concatenate(
        [
            extended_keys[:tok_rows].reshape(blocks, STRIDE, head_count, DH),
            extended_keys[STRIDE:].reshape(blocks, STRIDE, head_count, DH),
        ],
        1,
    )
    window_values = jnp.concatenate(
        [
            extended_values[:tok_rows].reshape(blocks, STRIDE, head_count, DH),
            extended_values[STRIDE:].reshape(blocks, STRIDE, head_count, DH),
        ],
        1,
    )
    query_blocks = query.reshape(blocks, STRIDE, head_count, DH)
    scores = (
        jnp.einsum("bthd,buhd->bhtu", query_blocks, window_keys, preferred_element_type=jnp.float32)
        * score_scale
    )
    first_position = lax.axis_index("seq") * tok_rows
    block_index = jnp.arange(blocks)[:, None, None, None]
    query_index = jnp.arange(STRIDE)[None, None, :, None]
    key_index = jnp.arange(2 * STRIDE)[None, None, None, :]
    allowed = (
        (key_index > query_index)
        & (key_index <= query_index + STRIDE)
        & (first_position + block_index * STRIDE + key_index - STRIDE >= 0)
    )
    local_top = jnp.max(jnp.where(allowed, scores, -1e30), axis=-1)
    local_weights = jnp.where(allowed, jnp.exp(scores - local_top[..., None]), 0.0)
    local_total = jnp.sum(local_weights, axis=-1)
    local_out = jnp.einsum(
        "bhtu,buhd->bthd",
        local_weights.astype(jnp.bfloat16),
        window_values,
        preferred_element_type=jnp.float32,
    )
    local_out = local_out.reshape(tok_rows, head_count, DH)
    local_top = local_top.transpose(0, 2, 1).reshape(tok_rows, head_count)
    local_total = local_total.transpose(0, 2, 1).reshape(tok_rows, head_count)
    row_count = tok_rows // STRIDE
    query_class = lax.all_to_all(
        query.reshape(row_count, STRIDE, head_count, DH),
        "seq",
        split_axis=1,
        concat_axis=0,
        tiled=True,
    )
    key_class = lax.all_to_all(
        key_heads.reshape(row_count, STRIDE, head_count, DH),
        "seq",
        split_axis=1,
        concat_axis=0,
        tiled=True,
    )
    value_class = lax.all_to_all(
        value_heads.reshape(row_count, STRIDE, head_count, DH),
        "seq",
        split_axis=1,
        concat_axis=0,
        tiled=True,
    )
    row_total = query_class.shape[0]
    class_scores = (
        jnp.einsum("rchd,schd->chrs", query_class, key_class, preferred_element_type=jnp.float32)
        * score_scale
    )
    earlier = (
        jnp.arange(row_total)[None, None, :, None] > jnp.arange(row_total)[None, None, None, :]
    )
    class_top = jnp.max(jnp.where(earlier, class_scores, -1e30), axis=-1)
    class_weights = jnp.where(earlier, jnp.exp(class_scores - class_top[..., None]), 0.0)
    class_total = jnp.sum(class_weights, axis=-1)
    summed = jnp.einsum(
        "chrs,schd->rchd",
        class_weights.astype(jnp.bfloat16),
        value_class,
        preferred_element_type=jnp.float32,
    )
    floor_total = jnp.maximum(class_total, 1.0).transpose(2, 0, 1)
    class_out = (summed / floor_total[..., None]).astype(jnp.bfloat16)
    class_top_rows = class_top.transpose(2, 0, 1)
    class_total_rows = class_total.transpose(2, 0, 1)
    column_out = class_out
    column_top = class_top_rows
    column_total = class_total_rows
    column_out, column_top, column_total = (
        lax.all_to_all(column_out, "seq", split_axis=0, concat_axis=1, tiled=True),
        lax.all_to_all(
            column_top.astype(jnp.bfloat16), "seq", split_axis=0, concat_axis=1, tiled=True
        ).astype(column_top.dtype),
        lax.all_to_all(
            column_total.astype(jnp.bfloat16), "seq", split_axis=0, concat_axis=1, tiled=True
        ).astype(column_total.dtype),
    )
    column_out = column_out.reshape(tok_rows, head_count, DH)
    column_top = column_top.reshape(tok_rows, head_count)
    column_total = column_total.reshape(tok_rows, head_count)
    top_score = jnp.maximum(local_top, column_top)
    local_weight = jnp.exp(local_top - top_score)
    column_weight = column_total * jnp.exp(column_top - top_score)
    denominator = local_total * local_weight + column_weight
    mixed = (
        local_out * local_weight[..., None]
        + column_out.astype(jnp.float32) * column_weight[..., None]
    ) / denominator[..., None]
    mixed = mixed.astype(jnp.bfloat16).reshape(tok_rows, head_width)
    return lax.psum_scatter(
        jnp.dot(mixed, w_out, preferred_element_type=jnp.float32).astype(jnp.bfloat16),
        "head",
        scatter_dimension=0,
        tiled=True,
    )


def shards(tokens, w_query, w_key, w_value, w_out):
    rows, width = w_query.shape
    fits = (
        lax.axis_size("seq") == PEERS
        and lax.axis_size("head") == 4
        and tokens.shape == (ROWS * STRIDE, HEADS * DH)
        and (rows, width) == (4 * HEADS * DH, HEADS * DH)
    )
    plan = chunked if fits else general
    return plan(tokens, w_query, w_key, w_value, w_out)


def solution(mesh):
    in_specs = (
        P("seq", "head"),
        P(None, "head"),
        P(None, "head"),
        P(None, "head"),
        P("head", None),
    )
    out_specs = P(("seq", "head"), None)
    return jax.shard_map(shards, mesh=mesh, in_specs=in_specs, out_specs=out_specs, check_vma=False)
```

```python
import functools

import jax
import jax.numpy as jnp
from jax import lax
from jax.experimental import pallas as pl
from jax.experimental.pallas import tpu as pltpu
from jax.sharding import PartitionSpec as P

DH = 128
STRIDE = 256
HEADS = 4
ROWS = 4
SUB = 8
CHUNKS = ((0, 1, 2), (3,))
PEERS = 8
SHARES = ((4, 5, 1, 2, 3, 0), (6, 7))
SCALE2 = DH ** (-0.5) * 1.4426950408889634
FLOOR = -1e29
MIB = 1024 * 1024
F32 = jnp.float32
BF16 = jnp.bfloat16


ANYWHERE = pl.BlockSpec(memory_space=pl.ANY)
IN_VMEM = pl.BlockSpec(memory_space=pltpu.VMEM)
IN_SMEM = pl.BlockSpec(memory_space=pltpu.SMEM)


def call(body, name, micros, out_shape, args, after=(), scratch=(), mib=24):
    specs = [IN_SMEM if x.dtype == jnp.int32 else IN_VMEM for x in args]
    extra = len(after)

    def run(*refs):
        n = len(args)
        body(*refs[:n], *refs[n + extra :])

    return pl.pallas_call(
        run,
        in_specs=specs + [ANYWHERE] * extra,
        out_specs=jax.tree.map(lambda _: IN_VMEM, out_shape),
        out_shape=out_shape,
        scratch_shapes=list(scratch),
        compiler_params=pltpu.CompilerParams(vmem_limit_bytes=mib * MIB),
        cost_estimate=pl.CostEstimate(
            flops=int(micros * 1.1e9), bytes_accessed=MIB, transcendentals=0
        ),
        name=name,
    )(*args, *after)


def fence(value, *after):
    return pl.pallas_call(
        lambda *refs: None,
        in_specs=[ANYWHERE] * (1 + len(after)),
        out_specs=ANYWHERE,
        out_shape=jax.ShapeDtypeStruct(value.shape, value.dtype),
        input_output_aliases={0: 0},
        compiler_params=pltpu.CompilerParams(vmem_limit_bytes=MIB),
        cost_estimate=pl.CostEstimate(flops=0, bytes_accessed=0, transcendentals=0),
        name="fence",
    )(value, *after)


def in_hbm(value):
    return pltpu.with_memory_space_constraint(value, pltpu.HBM)


def shape(dims, dtype=BF16):
    return jax.ShapeDtypeStruct(tuple(dims), dtype)


def dot(a, b):
    return jnp.dot(a, b, preferred_element_type=F32)


def dot_t(a, b):
    return lax.dot_general(a, b, (((1,), (1,)), ((), ())), preferred_element_type=F32)


def dot_l(a, b):
    return lax.dot_general(a, b, (((0,), (0,)), ((), ())), preferred_element_type=F32)


def pack_kernel(pos_ref, tok_hbm, tok_ref, *rest):
    out_refs, sems = rest[:-1], rest[-1]
    spans = [slice(r * STRIDE, (r + 1) * STRIDE) for r in range(ROWS)]
    copies = [
        pltpu.make_async_copy(tok_hbm.at[at], tok_ref.at[at], sems.at[r])
        for r, at in enumerate(spans)
    ]
    for c in copies:
        c.start()
    for c in copies:
        c.wait()
    per_owner = STRIDE // len(out_refs)
    part = ROWS * SUB
    for k, out_ref in enumerate(out_refs):
        d = pos_ref[0] ^ k
        rows = [
            tok_ref[pl.ds(pl.multiple_of(r * STRIDE + d * per_owner, per_owner), per_owner), :]
            for r in range(ROWS)
        ]
        rows = [x.astype(F32) for x in rows]
        for g in range(per_owner // SUB):
            piece = jnp.concatenate([x[g * SUB : (g + 1) * SUB] for x in rows], 0)
            out_ref[g * part : (g + 1) * part, :] = piece.astype(BF16)


def pack(pos, tokens, owners):
    message = shape((tokens.shape[0] // owners, tokens.shape[1]))
    outs = pl.pallas_call(
        pack_kernel,
        in_specs=[IN_SMEM, ANYWHERE],
        out_specs=[IN_VMEM] * (1 + owners),
        out_shape=[shape(tokens.shape)] + [message] * owners,
        scratch_shapes=[pltpu.SemaphoreType.DMA((ROWS,))],
        compiler_params=pltpu.CompilerParams(vmem_limit_bytes=8 * MIB),
        cost_estimate=pl.CostEstimate(flops=0, bytes_accessed=2 * MIB, transcendentals=0),
        name="pack_tokens",
    )(pos, in_hbm(tokens))
    return outs[0], outs[1:]


def stage_kernel(order_ref, wq, wk, wv, oq, ok, ov, sems):
    copies = []
    for n, (w, o) in enumerate(((wq, oq), (wk, ok), (wv, ov))):
        for p in range(4):
            rows = pl.ds(pl.multiple_of(order_ref[p] * 512, 512), 512)
            copies.append(
                pltpu.make_async_copy(w.at[rows], o.at[p * 512 : (p + 1) * 512], sems.at[4 * n + p])
            )
    for c in copies:
        c.start()
    for c in copies:
        c.wait()


def stage(order, weights, after):
    def body(order_ref, wq, wk, wv, _, *rest):
        stage_kernel(order_ref, wq, wk, wv, *rest)

    return pl.pallas_call(
        body,
        in_specs=[IN_SMEM] + [ANYWHERE] * 4,
        out_specs=[IN_VMEM] * 3,
        out_shape=[shape(w.shape) for w in weights],
        scratch_shapes=[pltpu.SemaphoreType.DMA((12,))],
        compiler_params=pltpu.CompilerParams(vmem_limit_bytes=16 * MIB),
        cost_estimate=pl.CostEstimate(flops=0, bytes_accessed=6 * MIB, transcendentals=0),
        name="stage_weights",
    )(order, *weights, after)


def gathered(x_refs, at, w_ref):
    width = x_refs[0].shape[1]
    total = None
    for p, x_ref in enumerate(x_refs):
        term = dot(x_ref[at, :], w_ref[p * width : (p + 1) * width, :])
        total = term if total is None else total + term
    return total.astype(BF16)


def halo_kernel(x0, x1, x2, x3, wk, wv, out_ref):
    rows = x0.shape[0]
    at = slice(rows - STRIDE, rows)
    out_ref[:STRIDE, :] = gathered((x0, x1, x2, x3), at, wk)
    out_ref[STRIDE:, :] = gathered((x0, x1, x2, x3), at, wv)


def project_kernel(x0, x1, x2, x3, wq, wk, wv, halo, q_ref, k_ref, v_ref):
    rows = x0.shape[0]
    xs = (x0, x1, x2, x3)
    last = slice(rows - STRIDE, rows)
    k_ref[last, :] = halo[:STRIDE, :]
    v_ref[last, :] = halo[STRIDE:, :]
    for w, out, upto in ((wq, q_ref, rows), (wk, k_ref, rows - STRIDE), (wv, v_ref, rows - STRIDE)):
        out[:upto, :] = gathered(xs, slice(0, upto), w)


def softmax_columns(s):
    m = jnp.maximum(jnp.max(s, 0, keepdims=True), FLOOR)
    p = jnp.exp2((s - m) * SCALE2)
    total = jnp.maximum(jnp.sum(p, 0, keepdims=True), 1.0)
    return p, total, m * SCALE2 + jnp.log2(total)


def local_kernel(pos_ref, q_ref, k_ref, v_ref, halo_ref, *outs):
    out_refs, lse_refs = outs[: len(CHUNKS)], outs[len(CHUNKS) :]
    owners = out_refs[0].shape[0]
    groups = STRIDE // owners // SUB
    block = pos_ref[0]
    u = lax.broadcasted_iota(jnp.int32, (STRIDE, STRIDE), 0)
    t = lax.broadcasted_iota(jnp.int32, (STRIDE, STRIDE), 1)
    current = u <= t
    low = jnp.where(block == 0, -1e30, 0.0).astype(F32)
    for r in range(ROWS):
        lses = []
        here = slice(r * STRIDE, (r + 1) * STRIDE)
        back = slice((r - 1) * STRIDE, r * STRIDE)
        for h in range(HEADS):
            cols = slice(h * DH, (h + 1) * DH)
            q = q_ref[here, cols]
            k_prev = k_ref[back, cols] if r else halo_ref[:STRIDE, cols]
            v_prev = v_ref[back, cols] if r else halo_ref[STRIDE:, cols]
            s_prev = dot_t(k_prev, q)
            if r == 0:
                s_prev = s_prev + low
            p, total, lse = softmax_columns(jnp.where(current, dot_t(k_ref[here, cols], q), s_prev))
            p_now = jnp.where(current, p, 0.0).astype(BF16)
            p_prev = jnp.where(current, 0.0, p).astype(BF16)
            o = dot_l(v_ref[here, cols], p_now) + dot_l(v_prev, p_prev)
            o = (o * (1.0 / total)).T
            lses.append(lse)
            for d in range(owners):
                for chunk, out_ref in zip(CHUNKS, out_refs):
                    for n, g in enumerate(chunk):
                        at = (d * groups + g) * SUB
                        to = (n * ROWS + r) * SUB
                        out_ref[d, to : to + SUB, cols] = o[at : at + SUB]
        lses.append(jnp.zeros((128 - HEADS, STRIDE), F32))
        turned = jnp.concatenate(lses, 0).T
        for chunk, lse_ref in zip(CHUNKS, lse_refs):
            for n, g in enumerate(chunk):
                total = None
                for d in range(owners):
                    at = (d * groups + g) * SUB
                    moved = pltpu.roll(turned[at : at + SUB], 8 * (block ^ d), 1)
                    total = moved if total is None else total + moved
                to = (n * ROWS + r) * SUB
                lse_ref[to : to + SUB, :] = total


def local_part(pos, q, k, v, halo, owners, after):
    rows, width = q.shape
    sizes = [len(chunk) * ROWS * SUB for chunk in CHUNKS]
    shapes = [shape((owners, m, width), F32) for m in sizes] + [shape((m, 128), F32) for m in sizes]
    outs = call(local_kernel, "local_part", 5, shapes, (pos, q, k, v, halo), after)
    return list(zip(outs[: len(sizes)], outs[len(sizes) :]))


def column_kernel(pos_ref, x0, x1, x2, x3, wq, wk, wv, *rest):
    refs, scratch = rest[:-3], rest[-3:]
    owners, message, _ = scratch[0].shape
    out_refs = refs[-owners:]
    size = HEADS * message + 16
    base = out_refs[0].shape[0] - size
    for old, new in zip(refs[:-owners], out_refs):
        new[:base, :] = old[...]
    groups = message // (ROWS * SUB)
    everything = slice(0, owners * message)
    for w, a in zip((wq, wk, wv), scratch):
        a[...] = gathered((x0, x1, x2, x3), everything, w).reshape(a.shape)
    part = ROWS * SUB
    size = owners * part

    def row_and_class(dim):
        i = lax.broadcasted_iota(jnp.int32, (size, size), dim)
        return ((i // part) ^ pos_ref[0]) * ROWS + (i % part) // SUB, i % SUB

    (row_j, class_j), (row_i, class_i) = row_and_class(0), row_and_class(1)
    earlier = jnp.logical_and(class_i == class_j, row_i > row_j)
    stats = []
    for g in range(groups):
        at = slice(g * part, (g + 1) * part)
        lses = []
        for h in range(HEADS):
            cols = slice(h * DH, (h + 1) * DH)
            q, k, v = (a[:, at, cols].reshape(size, DH) for a in scratch)
            p, total, lse = softmax_columns(jnp.where(earlier, dot_t(k, q), -1e30))
            o = (dot_l(v, p.astype(BF16)) * (1.0 / total)).T.astype(BF16)
            to = base + h * message + g * part
            rows = slice(to, to + part)
            for n in range(owners):
                out_refs[n][rows, :] = o[n * part : (n + 1) * part]
            lses.append(lse)
        stats.append(jnp.concatenate(lses + lses, 0))
    upper = lax.broadcasted_iota(jnp.int32, (8, 128), 0) < HEADS
    blank = [jnp.zeros((8, 128 - message), F32)] if message < 128 else []
    for n in range(owners):
        x = jnp.concatenate([s[:, n * part : (n + 1) * part] for s in stats] + blank, 1)
        hi = x.astype(BF16).astype(F32)
        mid = (x - hi).astype(BF16).astype(F32)
        lo = x - hi - mid
        tail = jnp.concatenate([jnp.where(upper, hi, lo), jnp.where(upper, mid, 0.0)], 0)
        to = base + HEADS * message
        out_refs[n][to : to + 16, :] = tail.astype(BF16)


def column_part(pos, pieces, weights, earlier, owners, after):
    tokens, width = pieces[0].shape
    message = tokens // owners
    rows = HEADS * message + 16 + (earlier[0].shape[0] if earlier else 0)
    scratch = [pltpu.VMEM((owners, message, width), BF16)] * 3
    args = (pos, *pieces, *weights, *earlier)
    return call(column_kernel, "column_part", 0, [shape((rows, DH))] * owners, args, after, scratch)


def mix_kernel(share, pos_ref, *refs):
    count = 2 * len(CHUNKS)
    local_refs, col_refs, (own_ref, send_ref, mixed) = refs[:count], refs[count:-3], refs[-3:]
    per_owner = mixed.shape[1] // len(share)
    base = 0
    for chunk, loc_ref, lse_ref in zip(CHUNKS, local_refs[::2], local_refs[1::2]):
        message = loc_ref.shape[1]
        size = HEADS * message + 16
        tiles = [jnp.zeros((8, 128), F32)] * 16
        for k, col_ref in zip(share, col_refs):
            tail = col_ref[base + HEADS * message : base + size, :].astype(F32)
            tiles[k] = tail[:8] + tail[8:]
        turned = jnp.concatenate(tiles, 0).T[:message]
        col_lse = turned + pltpu.roll(turned, 124, 1)
        loc_lse = lse_ref[...]
        top = jnp.maximum(col_lse, loc_lse)
        w_col = jnp.exp2(col_lse - top)
        w_loc = jnp.exp2(loc_lse - top)
        scale = 1.0 / (w_col + w_loc)
        w_col = w_col * scale
        w_loc = w_loc * scale
        for n, (k, col_ref) in enumerate(zip(share, col_refs)):
            d = pos_ref[0] ^ k
            for h in range(HEADS):
                cols = slice(h * DH, (h + 1) * DH)
                at = slice(8 * k + h, 8 * k + h + 1)
                col = col_ref[base + h * message : base + (h + 1) * message, :].astype(F32)
                both = loc_ref[d, :, cols] * w_loc[:, at] + col * w_col[:, at]
                for r in range(ROWS):
                    for m, g in enumerate(chunk):
                        start = (m * ROWS + r) * SUB
                        to = n * per_owner + g * SUB
                        mixed[r, to : to + SUB, cols] = both[start : start + SUB]
        base += size
    core = pos_ref[1]
    for x in range(2):
        own_ref[x] = mixed[2 * x + core].astype(BF16)
        send_ref[x] = mixed[2 * x + 1 - core].astype(BF16)


def mix(pos, share, columns, locals_, after):
    owners, _, width = locals_[0][0].shape
    tokens = len(share) * STRIDE // owners
    shapes = [shape((2, tokens, width))] * 2
    scratch = [pltpu.VMEM((ROWS, tokens, width), F32)]
    args = (pos, *[x for pair in locals_ for x in pair], *columns)
    return call(functools.partial(mix_kernel, share), "mix", 2, shapes, args, after, scratch)


def out_kernel(pos_ref, a_ref, b_ref, wa_ref, wb_ref, send_ref, keep_ref):
    tokens, columns = send_ref.shape
    a = a_ref[...].reshape(2 * tokens, -1)
    b = b_ref[...].reshape(2 * tokens, -1)
    low_side = pos_ref[2] == 0
    tile = 512
    for n in range(0, columns, tile):
        at = slice(n, n + tile)
        total = dot(a, wa_ref[:, at]) + dot(b, wb_ref[:, at])
        send_ref[:, at] = jnp.where(low_side, total[tokens:], total[:tokens]).astype(BF16)
        keep_ref[:, at] = jnp.where(low_side, total[:tokens], total[tokens:])


def out_project(pos, own, other, w_own, w_other):
    dims = (own.shape[1], w_own.shape[1])
    shapes = [shape(dims), shape(dims, F32)]
    return call(out_kernel, "out_project", 2, shapes, (pos, own, other, w_own, w_other))


def join_kernel(pos_ref, *refs):
    out_ref = refs[-1]
    for share, keep, got in zip(SHARES, refs[0:-1:2], refs[1:-1:2]):
        span = keep.shape[0] // len(share)
        for n, k in enumerate(share):
            rows = slice(n * span, (n + 1) * span)
            to = pl.ds(pl.multiple_of((pos_ref[0] ^ k) * span, span), span)
            out_ref[to, :] = (keep[rows, :] + got[rows, :].astype(F32)).astype(BF16)


def join(pos, pairs):
    columns = pairs[0][0].shape[1]
    args = [x for pair in pairs for x in pair]
    return call(join_kernel, "join", 2, shape((STRIDE, columns)), (pos, *args))


def swap(value, distance):
    return lax.ppermute(value, "head", [(i, i ^ distance) for i in range(4)])


def exchange(messages):
    peers = lax.axis_size("seq")

    def move(value, k):
        return lax.ppermute(value, "seq", [(i, i ^ k) for i in range(peers)]) if k else value

    return [move(m, k) for k, m in enumerate(messages)]


def chunked(tokens, w_query, w_key, w_value, w_out):
    owners = lax.axis_size("seq")
    head = lax.axis_index("head")
    block = lax.axis_index("seq")
    order = jnp.bitwise_xor(jnp.arange(4, dtype=jnp.int32), head.astype(jnp.int32))
    pos = jnp.stack([block, head % 2, head // 2]).astype(jnp.int32)
    rows, width = tokens.shape

    across = swap(tokens, 2)
    block_tokens, sent = pack(pos, tokens, owners)
    messages = exchange(sent)
    part = ROWS * SUB
    classes = [
        jnp.concatenate([m[chunk[0] * part : (chunk[-1] + 1) * part] for m in messages], 0)
        for chunk in CHUNKS
    ]
    across = fence(across, classes[0])
    pieces = (block_tokens, swap(fence(block_tokens, classes[0]), 1), across, swap(across, 1))
    weights = stage(order, (w_query, w_key, w_value), messages[1])
    w_other = swap(w_out, 1)
    own_halo = call(
        halo_kernel, "project_halo", 1.5, shape((2 * STRIDE, width)), (*pieces, *weights[1:])
    )
    first = classes[0]
    first_core, first_across = swap(first, 1), swap(first, 2)
    halo = lax.ppermute(own_halo, "seq", [(i, i + 1) for i in range(owners - 1)])
    q, k, v = call(
        project_kernel,
        "project_block",
        6,
        [shape((rows, width))] * 3,
        (*pieces, *weights, own_halo),
        (w_other,),
    )
    first_across = fence(first_across, q)
    first_pieces = (first, first_core, first_across, swap(first_across, 1))
    second = fence(classes[1], first_across)
    second_core, second_across = swap(second, 1), swap(second, 2)
    columns = column_part(pos, first_pieces, weights, (), owners, ())
    second_across = fence(second_across, columns[0])
    second_pieces = (second, second_core, second_across, swap(second_across, 1))
    columns = column_part(pos, second_pieces, weights, columns, owners, (halo,))
    locals_ = local_part(pos, q, k, v, halo, owners, (columns[0],))
    columns = exchange(columns)
    pairs, after = [], ()
    for share in SHARES:
        own, send = mix(pos, share, [columns[n] for n in share], locals_, after)
        out, keep = out_project(pos, own, swap(send, 1), w_out, w_other)
        pairs.append((keep, swap(out, 2)))
        after = (keep,)
    return join(pos, pairs)


def from_behind(value, axis, by):
    peers = lax.axis_size(axis)
    pairs = [(i, i + by) for i in range(peers) if 0 <= i + by < peers]
    return lax.ppermute(value, axis, pairs)


def general(tokens, w_query, w_key, w_value, w_out):
    tok_rows = tokens.shape[0]
    head_width = w_query.shape[1]
    head_count = head_width // DH
    score_scale = DH ** (-0.5)
    shard_piece = lax.all_gather(tokens, "head", axis=1, tiled=True)
    query_full, key_full, value_full = tuple(
        (
            jnp.dot(shard_piece, weight, preferred_element_type=jnp.float32)
            for weight in (w_query, w_key, w_value)
        )
    )
    query = query_full.astype(jnp.bfloat16).reshape(tok_rows, head_count, DH)
    key_heads = key_full.astype(jnp.bfloat16).reshape(tok_rows, head_count, DH)
    value_heads = value_full.astype(jnp.bfloat16).reshape(tok_rows, head_count, DH)
    prev_keys, prev_values = from_behind((key_heads[-STRIDE:], value_heads[-STRIDE:]), "seq", 1)
    blocks = tok_rows // STRIDE
    extended_keys = jnp.concatenate([prev_keys, key_heads], 0)
    extended_values = jnp.concatenate([prev_values, value_heads], 0)
    window_keys = jnp.concatenate(
        [
            extended_keys[:tok_rows].reshape(blocks, STRIDE, head_count, DH),
            extended_keys[STRIDE:].reshape(blocks, STRIDE, head_count, DH),
        ],
        1,
    )
    window_values = jnp.concatenate(
        [
            extended_values[:tok_rows].reshape(blocks, STRIDE, head_count, DH),
            extended_values[STRIDE:].reshape(blocks, STRIDE, head_count, DH),
        ],
        1,
    )
    query_blocks = query.reshape(blocks, STRIDE, head_count, DH)
    scores = (
        jnp.einsum("bthd,buhd->bhtu", query_blocks, window_keys, preferred_element_type=jnp.float32)
        * score_scale
    )
    first_position = lax.axis_index("seq") * tok_rows
    block_index = jnp.arange(blocks)[:, None, None, None]
    query_index = jnp.arange(STRIDE)[None, None, :, None]
    key_index = jnp.arange(2 * STRIDE)[None, None, None, :]
    allowed = (
        (key_index > query_index)
        & (key_index <= query_index + STRIDE)
        & (first_position + block_index * STRIDE + key_index - STRIDE >= 0)
    )
    local_top = jnp.max(jnp.where(allowed, scores, -1e30), axis=-1)
    local_weights = jnp.where(allowed, jnp.exp(scores - local_top[..., None]), 0.0)
    local_total = jnp.sum(local_weights, axis=-1)
    local_out = jnp.einsum(
        "bhtu,buhd->bthd",
        local_weights.astype(jnp.bfloat16),
        window_values,
        preferred_element_type=jnp.float32,
    )
    local_out = local_out.reshape(tok_rows, head_count, DH)
    local_top = local_top.transpose(0, 2, 1).reshape(tok_rows, head_count)
    local_total = local_total.transpose(0, 2, 1).reshape(tok_rows, head_count)
    row_count = tok_rows // STRIDE
    query_class = lax.all_to_all(
        query.reshape(row_count, STRIDE, head_count, DH),
        "seq",
        split_axis=1,
        concat_axis=0,
        tiled=True,
    )
    key_class = lax.all_to_all(
        key_heads.reshape(row_count, STRIDE, head_count, DH),
        "seq",
        split_axis=1,
        concat_axis=0,
        tiled=True,
    )
    value_class = lax.all_to_all(
        value_heads.reshape(row_count, STRIDE, head_count, DH),
        "seq",
        split_axis=1,
        concat_axis=0,
        tiled=True,
    )
    row_total = query_class.shape[0]
    class_scores = (
        jnp.einsum("rchd,schd->chrs", query_class, key_class, preferred_element_type=jnp.float32)
        * score_scale
    )
    earlier = (
        jnp.arange(row_total)[None, None, :, None] > jnp.arange(row_total)[None, None, None, :]
    )
    class_top = jnp.max(jnp.where(earlier, class_scores, -1e30), axis=-1)
    class_weights = jnp.where(earlier, jnp.exp(class_scores - class_top[..., None]), 0.0)
    class_total = jnp.sum(class_weights, axis=-1)
    summed = jnp.einsum(
        "chrs,schd->rchd",
        class_weights.astype(jnp.bfloat16),
        value_class,
        preferred_element_type=jnp.float32,
    )
    floor_total = jnp.maximum(class_total, 1.0).transpose(2, 0, 1)
    class_out = (summed / floor_total[..., None]).astype(jnp.bfloat16)
    class_top_rows = class_top.transpose(2, 0, 1)
    class_total_rows = class_total.transpose(2, 0, 1)
    column_out = class_out
    column_top = class_top_rows
    column_total = class_total_rows
    column_out, column_top, column_total = (
        lax.all_to_all(column_out, "seq", split_axis=0, concat_axis=1, tiled=True),
        lax.all_to_all(
            column_top.astype(jnp.bfloat16), "seq", split_axis=0, concat_axis=1, tiled=True
        ).astype(column_top.dtype),
        lax.all_to_all(
            column_total.astype(jnp.bfloat16), "seq", split_axis=0, concat_axis=1, tiled=True
        ).astype(column_total.dtype),
    )
    column_out = column_out.reshape(tok_rows, head_count, DH)
    column_top = column_top.reshape(tok_rows, head_count)
    column_total = column_total.reshape(tok_rows, head_count)
    top_score = jnp.maximum(local_top, column_top)
    local_weight = jnp.exp(local_top - top_score)
    column_weight = column_total * jnp.exp(column_top - top_score)
    denominator = local_total * local_weight + column_weight
    mixed = (
        local_out * local_weight[..., None]
        + column_out.astype(jnp.float32) * column_weight[..., None]
    ) / denominator[..., None]
    mixed = mixed.astype(jnp.bfloat16).reshape(tok_rows, head_width)
    return lax.psum_scatter(
        jnp.dot(mixed, w_out, preferred_element_type=jnp.float32).astype(jnp.bfloat16),
        "head",
        scatter_dimension=0,
        tiled=True,
    )


def shards(tokens, w_query, w_key, w_value, w_out):
    rows, width = w_query.shape
    fits = (
        lax.axis_size("seq") == PEERS
        and lax.axis_size("head") == 4
        and tokens.shape == (ROWS * STRIDE, HEADS * DH)
        and (rows, width) == (4 * HEADS * DH, HEADS * DH)
    )
    plan = chunked if fits else general
    return plan(tokens, w_query, w_key, w_value, w_out)


def solution(mesh):
    in_specs = (
        P("seq", "head"),
        P(None, "head"),
        P(None, "head"),
        P(None, "head"),
        P("head", None),
    )
    out_specs = P(("seq", "head"), None)
    return jax.shard_map(shards, mesh=mesh, in_specs=in_specs, out_specs=out_specs, check_vma=False)
```

```python
import functools

import jax
import jax.numpy as jnp
from jax import lax
from jax.experimental import pallas as pl
from jax.experimental.pallas import tpu as pltpu
from jax.sharding import PartitionSpec as P

DH = 128
STRIDE = 256
HEADS = 4
ROWS = 4
SUB = 8
CHUNKS = ((0, 1, 2), (3,))
PEERS = 8
SHARES = ((4, 5, 1, 2, 3, 0), (6, 7))
SCALE2 = DH ** (-0.5) * 1.4426950408889634
FLOOR = -1e29
MIB = 1024 * 1024
F32 = jnp.float32
BF16 = jnp.bfloat16


ANYWHERE = pl.BlockSpec(memory_space=pl.ANY)
IN_VMEM = pl.BlockSpec(memory_space=pltpu.VMEM)
IN_SMEM = pl.BlockSpec(memory_space=pltpu.SMEM)


def call(body, name, micros, out_shape, args, after=(), scratch=(), mib=24):
    specs = [IN_SMEM if x.dtype == jnp.int32 else IN_VMEM for x in args]
    extra = len(after)

    def run(*refs):
        n = len(args)
        body(*refs[:n], *refs[n + extra :])

    return pl.pallas_call(
        run,
        in_specs=specs + [ANYWHERE] * extra,
        out_specs=jax.tree.map(lambda _: IN_VMEM, out_shape),
        out_shape=out_shape,
        scratch_shapes=list(scratch),
        compiler_params=pltpu.CompilerParams(vmem_limit_bytes=mib * MIB),
        cost_estimate=pl.CostEstimate(
            flops=int(micros * 1.1e9), bytes_accessed=MIB, transcendentals=0
        ),
        name=name,
    )(*args, *after)


def fence(value, *after):
    return pl.pallas_call(
        lambda *refs: None,
        in_specs=[ANYWHERE] * (1 + len(after)),
        out_specs=ANYWHERE,
        out_shape=jax.ShapeDtypeStruct(value.shape, value.dtype),
        input_output_aliases={0: 0},
        compiler_params=pltpu.CompilerParams(vmem_limit_bytes=MIB),
        cost_estimate=pl.CostEstimate(flops=0, bytes_accessed=0, transcendentals=0),
        name="fence",
    )(value, *after)


def in_hbm(value):
    return pltpu.with_memory_space_constraint(value, pltpu.HBM)


def shape(dims, dtype=BF16):
    return jax.ShapeDtypeStruct(tuple(dims), dtype)


def dot(a, b):
    return jnp.dot(a, b, preferred_element_type=F32)


def dot_t(a, b):
    return lax.dot_general(a, b, (((1,), (1,)), ((), ())), preferred_element_type=F32)


def dot_l(a, b):
    return lax.dot_general(a, b, (((0,), (0,)), ((), ())), preferred_element_type=F32)


def pack_kernel(pos_ref, tok_hbm, tok_ref, *rest):
    out_refs, sems = rest[:-1], rest[-1]
    spans = [slice(r * STRIDE, (r + 1) * STRIDE) for r in range(ROWS)]
    copies = [
        pltpu.make_async_copy(tok_hbm.at[at], tok_ref.at[at], sems.at[r])
        for r, at in enumerate(spans)
    ]
    for c in copies:
        c.start()
    for c in copies:
        c.wait()
    per_owner = STRIDE // len(out_refs)
    part = ROWS * SUB
    for k, out_ref in enumerate(out_refs):
        d = pos_ref[0] ^ k
        rows = [
            tok_ref[pl.ds(pl.multiple_of(r * STRIDE + d * per_owner, per_owner), per_owner), :]
            for r in range(ROWS)
        ]
        rows = [x.astype(F32) for x in rows]
        for g in range(per_owner // SUB):
            piece = jnp.concatenate([x[g * SUB : (g + 1) * SUB] for x in rows], 0)
            out_ref[g * part : (g + 1) * part, :] = piece.astype(BF16)


def pack(pos, tokens, owners):
    message = shape((tokens.shape[0] // owners, tokens.shape[1]))
    outs = pl.pallas_call(
        pack_kernel,
        in_specs=[IN_SMEM, ANYWHERE],
        out_specs=[IN_VMEM] * (1 + owners),
        out_shape=[shape(tokens.shape)] + [message] * owners,
        scratch_shapes=[pltpu.SemaphoreType.DMA((ROWS,))],
        compiler_params=pltpu.CompilerParams(vmem_limit_bytes=8 * MIB),
        cost_estimate=pl.CostEstimate(flops=0, bytes_accessed=2 * MIB, transcendentals=0),
        name="pack_tokens",
    )(pos, in_hbm(tokens))
    return outs[0], outs[1:]


def stage_kernel(order_ref, wq, wk, wv, oq, ok, ov, sems):
    copies = []
    for n, (w, o) in enumerate(((wq, oq), (wk, ok), (wv, ov))):
        for p in range(4):
            rows = pl.ds(pl.multiple_of(order_ref[p] * 512, 512), 512)
            copies.append(
                pltpu.make_async_copy(w.at[rows], o.at[p * 512 : (p + 1) * 512], sems.at[4 * n + p])
            )
    for c in copies:
        c.start()
    for c in copies:
        c.wait()


def stage(order, weights, after):
    def body(order_ref, wq, wk, wv, _, *rest):
        stage_kernel(order_ref, wq, wk, wv, *rest)

    return pl.pallas_call(
        body,
        in_specs=[IN_SMEM] + [ANYWHERE] * 4,
        out_specs=[IN_VMEM] * 3,
        out_shape=[shape(w.shape) for w in weights],
        scratch_shapes=[pltpu.SemaphoreType.DMA((12,))],
        compiler_params=pltpu.CompilerParams(vmem_limit_bytes=16 * MIB),
        cost_estimate=pl.CostEstimate(flops=0, bytes_accessed=6 * MIB, transcendentals=0),
        name="stage_weights",
    )(order, *weights, after)


def gathered(x_refs, at, w_ref):
    width = x_refs[0].shape[1]
    total = None
    for p, x_ref in enumerate(x_refs):
        term = dot(x_ref[at, :], w_ref[p * width : (p + 1) * width, :])
        total = term if total is None else total + term
    return total.astype(BF16)


def half_kernel(x0, x1, wq, wk, wv, *outs):
    width = x0.shape[1]
    for w, out in zip((wq, wk, wv), outs):
        out[...] = dot(x0[...], w[:width, :]) + dot(x1[...], w[width : 2 * width, :])


def half_sums(own, core, weights, after):
    shapes = [shape(own.shape, F32)] * 3
    return call(half_kernel, "half_sums", 3, shapes, (own, core, *weights), after)


def halo_kernel(x0, x1, x2, x3, wk, wv, out_ref):
    rows = x0.shape[0]
    at = slice(rows - STRIDE, rows)
    out_ref[:STRIDE, :] = gathered((x0, x1, x2, x3), at, wk)
    out_ref[STRIDE:, :] = gathered((x0, x1, x2, x3), at, wv)


def project_kernel(x0, x1, x2, x3, wq, wk, wv, halo, q_ref, k_ref, v_ref):
    rows = x0.shape[0]
    xs = (x0, x1, x2, x3)
    last = slice(rows - STRIDE, rows)
    k_ref[last, :] = halo[:STRIDE, :]
    v_ref[last, :] = halo[STRIDE:, :]
    for w, out, upto in ((wq, q_ref, rows), (wk, k_ref, rows - STRIDE), (wv, v_ref, rows - STRIDE)):
        out[:upto, :] = gathered(xs, slice(0, upto), w)


def softmax_columns(s):
    m = jnp.maximum(jnp.max(s, 0, keepdims=True), FLOOR)
    p = jnp.exp2((s - m) * SCALE2)
    total = jnp.maximum(jnp.sum(p, 0, keepdims=True), 1.0)
    return p, total, m * SCALE2 + jnp.log2(total)


def local_kernel(pos_ref, q_ref, k_ref, v_ref, halo_ref, *outs):
    out_refs, lse_refs = outs[: len(CHUNKS)], outs[len(CHUNKS) :]
    owners = out_refs[0].shape[0]
    groups = STRIDE // owners // SUB
    block = pos_ref[0]
    u = lax.broadcasted_iota(jnp.int32, (STRIDE, STRIDE), 0)
    t = lax.broadcasted_iota(jnp.int32, (STRIDE, STRIDE), 1)
    current = u <= t
    low = jnp.where(block == 0, -1e30, 0.0).astype(F32)
    for r in range(ROWS):
        lses = []
        here = slice(r * STRIDE, (r + 1) * STRIDE)
        back = slice((r - 1) * STRIDE, r * STRIDE)
        for h in range(HEADS):
            cols = slice(h * DH, (h + 1) * DH)
            q = q_ref[here, cols]
            k_prev = k_ref[back, cols] if r else halo_ref[:STRIDE, cols]
            v_prev = v_ref[back, cols] if r else halo_ref[STRIDE:, cols]
            s_prev = dot_t(k_prev, q)
            if r == 0:
                s_prev = s_prev + low
            p, total, lse = softmax_columns(jnp.where(current, dot_t(k_ref[here, cols], q), s_prev))
            p_now = jnp.where(current, p, 0.0).astype(BF16)
            p_prev = jnp.where(current, 0.0, p).astype(BF16)
            o = dot_l(v_ref[here, cols], p_now) + dot_l(v_prev, p_prev)
            o = (o * (1.0 / total)).T
            lses.append(lse)
            for d in range(owners):
                for chunk, out_ref in zip(CHUNKS, out_refs):
                    for n, g in enumerate(chunk):
                        at = (d * groups + g) * SUB
                        to = (n * ROWS + r) * SUB
                        out_ref[d, to : to + SUB, cols] = o[at : at + SUB]
        lses.append(jnp.zeros((128 - HEADS, STRIDE), F32))
        turned = jnp.concatenate(lses, 0).T
        for chunk, lse_ref in zip(CHUNKS, lse_refs):
            for n, g in enumerate(chunk):
                total = None
                for d in range(owners):
                    at = (d * groups + g) * SUB
                    moved = pltpu.roll(turned[at : at + SUB], 8 * (block ^ d), 1)
                    total = moved if total is None else total + moved
                to = (n * ROWS + r) * SUB
                lse_ref[to : to + SUB, :] = total


def local_part(pos, q, k, v, halo, owners, after):
    rows, width = q.shape
    sizes = [len(chunk) * ROWS * SUB for chunk in CHUNKS]
    shapes = [shape((owners, m, width), F32) for m in sizes] + [shape((m, 128), F32) for m in sizes]
    outs = call(local_kernel, "local_part", 5, shapes, (pos, q, k, v, halo), after)
    return list(zip(outs[: len(sizes)], outs[len(sizes) :]))


def column_kernel(pos_ref, x2, x3, hq, hk, hv, wq, wk, wv, *rest):
    refs, scratch = rest[:-3], rest[-3:]
    owners, message, _ = scratch[0].shape
    out_refs = refs[-owners:]
    size = HEADS * message + 16
    base = out_refs[0].shape[0] - size
    for old, new in zip(refs[:-owners], out_refs):
        new[:base, :] = old[...]
    groups = message // (ROWS * SUB)
    width = x2.shape[1]
    for h, w, a in zip((hq, hk, hv), (wq, wk, wv), scratch):
        total = h[...] + dot(x2[...], w[2 * width : 3 * width, :])
        total = total + dot(x3[...], w[3 * width :, :])
        a[...] = total.astype(BF16).reshape(a.shape)
    part = ROWS * SUB
    size = owners * part

    def row_and_class(dim):
        i = lax.broadcasted_iota(jnp.int32, (size, size), dim)
        return ((i // part) ^ pos_ref[0]) * ROWS + (i % part) // SUB, i % SUB

    (row_j, class_j), (row_i, class_i) = row_and_class(0), row_and_class(1)
    earlier = jnp.logical_and(class_i == class_j, row_i > row_j)
    stats = []
    for g in range(groups):
        at = slice(g * part, (g + 1) * part)
        lses = []
        for h in range(HEADS):
            cols = slice(h * DH, (h + 1) * DH)
            q, k, v = (a[:, at, cols].reshape(size, DH) for a in scratch)
            p, total, lse = softmax_columns(jnp.where(earlier, dot_t(k, q), -1e30))
            o = (dot_l(v, p.astype(BF16)) * (1.0 / total)).T.astype(BF16)
            to = base + h * message + g * part
            rows = slice(to, to + part)
            for n in range(owners):
                out_refs[n][rows, :] = o[n * part : (n + 1) * part]
            lses.append(lse)
        stats.append(jnp.concatenate(lses + lses, 0))
    upper = lax.broadcasted_iota(jnp.int32, (8, 128), 0) < HEADS
    blank = [jnp.zeros((8, 128 - message), F32)] if message < 128 else []
    for n in range(owners):
        x = jnp.concatenate([s[:, n * part : (n + 1) * part] for s in stats] + blank, 1)
        hi = x.astype(BF16).astype(F32)
        mid = (x - hi).astype(BF16).astype(F32)
        lo = x - hi - mid
        tail = jnp.concatenate([jnp.where(upper, hi, lo), jnp.where(upper, mid, 0.0)], 0)
        to = base + HEADS * message
        out_refs[n][to : to + 16, :] = tail.astype(BF16)


def column_part(pos, across, halves, weights, earlier, owners):
    tokens, width = across.shape
    message = tokens // owners
    rows = HEADS * message + 16 + (earlier[0].shape[0] if earlier else 0)
    scratch = [pltpu.VMEM((owners, message, width), BF16)] * 3
    args = (pos, across, swap(across, 1), *halves, *weights, *earlier)
    return call(column_kernel, "column_part", 0, [shape((rows, DH))] * owners, args, (), scratch)


def mix_kernel(share, pos_ref, *refs):
    count = 2 * len(CHUNKS)
    local_refs, col_refs, (own_ref, send_ref, mixed) = refs[:count], refs[count:-3], refs[-3:]
    per_owner = mixed.shape[1] // len(share)
    base = 0
    for chunk, loc_ref, lse_ref in zip(CHUNKS, local_refs[::2], local_refs[1::2]):
        message = loc_ref.shape[1]
        size = HEADS * message + 16
        tiles = [jnp.zeros((8, 128), F32)] * 16
        for k, col_ref in zip(share, col_refs):
            tail = col_ref[base + HEADS * message : base + size, :].astype(F32)
            tiles[k] = tail[:8] + tail[8:]
        turned = jnp.concatenate(tiles, 0).T[:message]
        col_lse = turned + pltpu.roll(turned, 124, 1)
        loc_lse = lse_ref[...]
        top = jnp.maximum(col_lse, loc_lse)
        w_col = jnp.exp2(col_lse - top)
        w_loc = jnp.exp2(loc_lse - top)
        scale = 1.0 / (w_col + w_loc)
        w_col = w_col * scale
        w_loc = w_loc * scale
        for n, (k, col_ref) in enumerate(zip(share, col_refs)):
            d = pos_ref[0] ^ k
            for h in range(HEADS):
                cols = slice(h * DH, (h + 1) * DH)
                at = slice(8 * k + h, 8 * k + h + 1)
                col = col_ref[base + h * message : base + (h + 1) * message, :].astype(F32)
                both = loc_ref[d, :, cols] * w_loc[:, at] + col * w_col[:, at]
                for r in range(ROWS):
                    for m, g in enumerate(chunk):
                        start = (m * ROWS + r) * SUB
                        to = n * per_owner + g * SUB
                        mixed[r, to : to + SUB, cols] = both[start : start + SUB]
        base += size
    core = pos_ref[1]
    for x in range(2):
        own_ref[x] = mixed[2 * x + core].astype(BF16)
        send_ref[x] = mixed[2 * x + 1 - core].astype(BF16)


def mix(pos, share, columns, locals_, after):
    owners, _, width = locals_[0][0].shape
    tokens = len(share) * STRIDE // owners
    shapes = [shape((2, tokens, width))] * 2
    scratch = [pltpu.VMEM((ROWS, tokens, width), F32)]
    args = (pos, *[x for pair in locals_ for x in pair], *columns)
    return call(functools.partial(mix_kernel, share), "mix", 2, shapes, args, after, scratch)


def out_kernel(pos_ref, a_ref, b_ref, wa_ref, wb_ref, send_ref, keep_ref):
    tokens, columns = send_ref.shape
    a = a_ref[...].reshape(2 * tokens, -1)
    b = b_ref[...].reshape(2 * tokens, -1)
    low_side = pos_ref[2] == 0
    tile = 512
    for n in range(0, columns, tile):
        at = slice(n, n + tile)
        total = dot(a, wa_ref[:, at]) + dot(b, wb_ref[:, at])
        send_ref[:, at] = jnp.where(low_side, total[tokens:], total[:tokens]).astype(BF16)
        keep_ref[:, at] = jnp.where(low_side, total[:tokens], total[tokens:])


def out_project(pos, own, other, w_own, w_other):
    dims = (own.shape[1], w_own.shape[1])
    shapes = [shape(dims), shape(dims, F32)]
    return call(out_kernel, "out_project", 2, shapes, (pos, own, other, w_own, w_other))


def join_kernel(share, pos_ref, keep, got, *rest):
    out_hbm, joined, sems = rest[-3:]
    span = keep.shape[0] // len(share)
    joined[...] = (keep[...] + got[...].astype(F32)).astype(BF16)
    copies = []
    for n, k in enumerate(share):
        to = pl.ds(pl.multiple_of((pos_ref[0] ^ k) * span, span), span)
        rows = slice(n * span, (n + 1) * span)
        copies.append(pltpu.make_async_copy(joined.at[rows], out_hbm.at[to], sems.at[n]))
    for c in copies:
        c.start()
    for c in copies:
        c.wait()


def join(pos, share, keep, got, earlier):
    return pl.pallas_call(
        functools.partial(join_kernel, share),
        in_specs=[IN_SMEM, IN_VMEM, IN_VMEM] + [ANYWHERE] * len(earlier),
        out_specs=ANYWHERE,
        out_shape=shape((STRIDE, keep.shape[1])),
        input_output_aliases={3: 0} if earlier else {},
        scratch_shapes=[pltpu.VMEM(keep.shape, BF16), pltpu.SemaphoreType.DMA((len(share),))],
        compiler_params=pltpu.CompilerParams(vmem_limit_bytes=16 * MIB),
        cost_estimate=pl.CostEstimate(flops=int(1.1e9), bytes_accessed=MIB, transcendentals=0),
        name="join",
    )(pos, keep, got, *earlier)


def swap(value, distance):
    return lax.ppermute(value, "head", [(i, i ^ distance) for i in range(4)])


def exchange(messages):
    peers = lax.axis_size("seq")

    def move(value, k):
        return lax.ppermute(value, "seq", [(i, i ^ k) for i in range(peers)]) if k else value

    return [move(m, k) for k, m in enumerate(messages)]


def chunked(tokens, w_query, w_key, w_value, w_out):
    owners = lax.axis_size("seq")
    head = lax.axis_index("head")
    block = lax.axis_index("seq")
    order = jnp.bitwise_xor(jnp.arange(4, dtype=jnp.int32), head.astype(jnp.int32))
    pos = jnp.stack([block, head % 2, head // 2]).astype(jnp.int32)
    rows, width = tokens.shape

    across = swap(tokens, 2)
    block_tokens, sent = pack(pos, tokens, owners)
    messages = exchange(sent)
    part = ROWS * SUB
    classes = [
        jnp.concatenate([m[chunk[0] * part : (chunk[-1] + 1) * part] for m in messages], 0)
        for chunk in CHUNKS
    ]
    across = fence(across, classes[0])
    pieces = (block_tokens, swap(fence(block_tokens, classes[0]), 1), across, swap(across, 1))
    weights = stage(order, (w_query, w_key, w_value), messages[1])
    w_other = swap(w_out, 1)
    own_halo = call(
        halo_kernel, "project_halo", 1.5, shape((2 * STRIDE, width)), (*pieces, *weights[1:])
    )
    first = classes[0]
    first_core, first_across = swap(first, 1), swap(first, 2)
    halo = lax.ppermute(own_halo, "seq", [(i, i + 1) for i in range(owners - 1)])
    q, k, v = call(
        project_kernel,
        "project_block",
        6,
        [shape((rows, width))] * 3,
        (*pieces, *weights, own_halo),
        (w_other,),
    )
    second_core = swap(classes[1], 1)
    first_half = half_sums(first, first_core, weights, (q,))
    second_half = half_sums(classes[1], second_core, weights, (first_half[0],))
    first_across = fence(first_across, halo, second_half[0])
    second_across = swap(fence(classes[1], first_across), 2)
    columns = column_part(pos, first_across, first_half, weights, (), owners)
    second_across = fence(second_across, columns[0])
    columns = column_part(pos, second_across, second_half, weights, columns, owners)
    locals_ = local_part(pos, q, k, v, halo, owners, (columns[0],))
    columns = exchange(columns)
    sums, after = [], ()
    for share in SHARES:
        own, send = mix(pos, share, [columns[n] for n in share], locals_, after)
        out, keep = out_project(pos, own, swap(send, 1), w_out, w_other)
        sums.append((keep, swap(out, 2)))
        after = (keep,)
    result = ()
    for share, (keep, got) in zip(SHARES, sums):
        result = (join(pos, share, keep, got, result),)
    return result[0]


def from_behind(value, axis, by):
    peers = lax.axis_size(axis)
    pairs = [(i, i + by) for i in range(peers) if 0 <= i + by < peers]
    return lax.ppermute(value, axis, pairs)


def general(tokens, w_query, w_key, w_value, w_out):
    tok_rows = tokens.shape[0]
    head_width = w_query.shape[1]
    head_count = head_width // DH
    score_scale = DH ** (-0.5)
    shard_piece = lax.all_gather(tokens, "head", axis=1, tiled=True)
    query_full, key_full, value_full = tuple(
        (
            jnp.dot(shard_piece, weight, preferred_element_type=jnp.float32)
            for weight in (w_query, w_key, w_value)
        )
    )
    query = query_full.astype(jnp.bfloat16).reshape(tok_rows, head_count, DH)
    key_heads = key_full.astype(jnp.bfloat16).reshape(tok_rows, head_count, DH)
    value_heads = value_full.astype(jnp.bfloat16).reshape(tok_rows, head_count, DH)
    prev_keys, prev_values = from_behind((key_heads[-STRIDE:], value_heads[-STRIDE:]), "seq", 1)
    blocks = tok_rows // STRIDE
    extended_keys = jnp.concatenate([prev_keys, key_heads], 0)
    extended_values = jnp.concatenate([prev_values, value_heads], 0)
    window_keys = jnp.concatenate(
        [
            extended_keys[:tok_rows].reshape(blocks, STRIDE, head_count, DH),
            extended_keys[STRIDE:].reshape(blocks, STRIDE, head_count, DH),
        ],
        1,
    )
    window_values = jnp.concatenate(
        [
            extended_values[:tok_rows].reshape(blocks, STRIDE, head_count, DH),
            extended_values[STRIDE:].reshape(blocks, STRIDE, head_count, DH),
        ],
        1,
    )
    query_blocks = query.reshape(blocks, STRIDE, head_count, DH)
    scores = (
        jnp.einsum("bthd,buhd->bhtu", query_blocks, window_keys, preferred_element_type=jnp.float32)
        * score_scale
    )
    first_position = lax.axis_index("seq") * tok_rows
    block_index = jnp.arange(blocks)[:, None, None, None]
    query_index = jnp.arange(STRIDE)[None, None, :, None]
    key_index = jnp.arange(2 * STRIDE)[None, None, None, :]
    allowed = (
        (key_index > query_index)
        & (key_index <= query_index + STRIDE)
        & (first_position + block_index * STRIDE + key_index - STRIDE >= 0)
    )
    local_top = jnp.max(jnp.where(allowed, scores, -1e30), axis=-1)
    local_weights = jnp.where(allowed, jnp.exp(scores - local_top[..., None]), 0.0)
    local_total = jnp.sum(local_weights, axis=-1)
    local_out = jnp.einsum(
        "bhtu,buhd->bthd",
        local_weights.astype(jnp.bfloat16),
        window_values,
        preferred_element_type=jnp.float32,
    )
    local_out = local_out.reshape(tok_rows, head_count, DH)
    local_top = local_top.transpose(0, 2, 1).reshape(tok_rows, head_count)
    local_total = local_total.transpose(0, 2, 1).reshape(tok_rows, head_count)
    row_count = tok_rows // STRIDE
    query_class = lax.all_to_all(
        query.reshape(row_count, STRIDE, head_count, DH),
        "seq",
        split_axis=1,
        concat_axis=0,
        tiled=True,
    )
    key_class = lax.all_to_all(
        key_heads.reshape(row_count, STRIDE, head_count, DH),
        "seq",
        split_axis=1,
        concat_axis=0,
        tiled=True,
    )
    value_class = lax.all_to_all(
        value_heads.reshape(row_count, STRIDE, head_count, DH),
        "seq",
        split_axis=1,
        concat_axis=0,
        tiled=True,
    )
    row_total = query_class.shape[0]
    class_scores = (
        jnp.einsum("rchd,schd->chrs", query_class, key_class, preferred_element_type=jnp.float32)
        * score_scale
    )
    earlier = (
        jnp.arange(row_total)[None, None, :, None] > jnp.arange(row_total)[None, None, None, :]
    )
    class_top = jnp.max(jnp.where(earlier, class_scores, -1e30), axis=-1)
    class_weights = jnp.where(earlier, jnp.exp(class_scores - class_top[..., None]), 0.0)
    class_total = jnp.sum(class_weights, axis=-1)
    summed = jnp.einsum(
        "chrs,schd->rchd",
        class_weights.astype(jnp.bfloat16),
        value_class,
        preferred_element_type=jnp.float32,
    )
    floor_total = jnp.maximum(class_total, 1.0).transpose(2, 0, 1)
    class_out = (summed / floor_total[..., None]).astype(jnp.bfloat16)
    class_top_rows = class_top.transpose(2, 0, 1)
    class_total_rows = class_total.transpose(2, 0, 1)
    column_out = class_out
    column_top = class_top_rows
    column_total = class_total_rows
    column_out, column_top, column_total = (
        lax.all_to_all(column_out, "seq", split_axis=0, concat_axis=1, tiled=True),
        lax.all_to_all(
            column_top.astype(jnp.bfloat16), "seq", split_axis=0, concat_axis=1, tiled=True
        ).astype(column_top.dtype),
        lax.all_to_all(
            column_total.astype(jnp.bfloat16), "seq", split_axis=0, concat_axis=1, tiled=True
        ).astype(column_total.dtype),
    )
    column_out = column_out.reshape(tok_rows, head_count, DH)
    column_top = column_top.reshape(tok_rows, head_count)
    column_total = column_total.reshape(tok_rows, head_count)
    top_score = jnp.maximum(local_top, column_top)
    local_weight = jnp.exp(local_top - top_score)
    column_weight = column_total * jnp.exp(column_top - top_score)
    denominator = local_total * local_weight + column_weight
    mixed = (
        local_out * local_weight[..., None]
        + column_out.astype(jnp.float32) * column_weight[..., None]
    ) / denominator[..., None]
    mixed = mixed.astype(jnp.bfloat16).reshape(tok_rows, head_width)
    return lax.psum_scatter(
        jnp.dot(mixed, w_out, preferred_element_type=jnp.float32).astype(jnp.bfloat16),
        "head",
        scatter_dimension=0,
        tiled=True,
    )


def shards(tokens, w_query, w_key, w_value, w_out):
    rows, width = w_query.shape
    fits = (
        lax.axis_size("seq") == PEERS
        and lax.axis_size("head") == 4
        and tokens.shape == (ROWS * STRIDE, HEADS * DH)
        and (rows, width) == (4 * HEADS * DH, HEADS * DH)
    )
    plan = chunked if fits else general
    return plan(tokens, w_query, w_key, w_value, w_out)


def solution(mesh):
    in_specs = (
        P("seq", "head"),
        P(None, "head"),
        P(None, "head"),
        P(None, "head"),
        P("head", None),
    )
    out_specs = P(("seq", "head"), None)
    return jax.shard_map(shards, mesh=mesh, in_specs=in_specs, out_specs=out_specs, check_vma=False)
```

```python
import functools

import jax
import jax.numpy as jnp
from jax import lax
from jax.experimental import pallas as pl
from jax.experimental.pallas import tpu as pltpu
from jax.sharding import PartitionSpec as P

DH = 128
STRIDE = 256
HEADS = 4
ROWS = 4
SUB = 8
CHUNKS = ((0, 1, 2, 3),)
NEAR = 4
PEERS = 8
SHARES = ((4, 5, 1, 2, 3, 0), (6, 7))
SCALE2 = DH ** (-0.5) * 1.4426950408889634
FLOOR = -1e29
MIB = 1024 * 1024
F32 = jnp.float32
BF16 = jnp.bfloat16


ANYWHERE = pl.BlockSpec(memory_space=pl.ANY)
IN_VMEM = pl.BlockSpec(memory_space=pltpu.VMEM)
IN_SMEM = pl.BlockSpec(memory_space=pltpu.SMEM)


def call(body, name, micros, out_shape, args, after=(), scratch=(), mib=24):
    specs = [IN_SMEM if x.dtype == jnp.int32 else IN_VMEM for x in args]
    extra = len(after)

    def run(*refs):
        n = len(args)
        body(*refs[:n], *refs[n + extra :])

    return pl.pallas_call(
        run,
        in_specs=specs + [ANYWHERE] * extra,
        out_specs=jax.tree.map(lambda _: IN_VMEM, out_shape),
        out_shape=out_shape,
        scratch_shapes=list(scratch),
        compiler_params=pltpu.CompilerParams(vmem_limit_bytes=mib * MIB),
        cost_estimate=pl.CostEstimate(
            flops=int(micros * 1.1e9), bytes_accessed=0, transcendentals=0
        ),
        name=name,
    )(*args, *after)


def fence(value, *after):
    return pl.pallas_call(
        lambda *refs: None,
        in_specs=[ANYWHERE] * (1 + len(after)),
        out_specs=ANYWHERE,
        out_shape=jax.ShapeDtypeStruct(value.shape, value.dtype),
        input_output_aliases={0: 0},
        compiler_params=pltpu.CompilerParams(vmem_limit_bytes=MIB),
        cost_estimate=pl.CostEstimate(flops=0, bytes_accessed=0, transcendentals=0),
        name="fence",
    )(value, *after)


def in_hbm(value):
    return pltpu.with_memory_space_constraint(value, pltpu.HBM)


def shape(dims, dtype=BF16):
    return jax.ShapeDtypeStruct(tuple(dims), dtype)


def dot(a, b):
    return jnp.dot(a, b, preferred_element_type=F32)


def dot_t(a, b):
    return lax.dot_general(a, b, (((1,), (1,)), ((), ())), preferred_element_type=F32)


def dot_l(a, b):
    return lax.dot_general(a, b, (((0,), (0,)), ((), ())), preferred_element_type=F32)


def pack_kernel(pos_ref, tok_hbm, tok_ref, *rest):
    out_refs, sems = rest[:-1], rest[-1]
    spans = [slice(r * STRIDE, (r + 1) * STRIDE) for r in range(ROWS)]
    copies = [
        pltpu.make_async_copy(tok_hbm.at[at], tok_ref.at[at], sems.at[r])
        for r, at in enumerate(spans)
    ]
    for c in copies:
        c.start()
    for c in copies:
        c.wait()
    per_owner = STRIDE // len(out_refs)
    part = ROWS * SUB
    for k, out_ref in enumerate(out_refs):
        d = pos_ref[0] ^ k
        rows = [
            tok_ref[pl.ds(pl.multiple_of(r * STRIDE + d * per_owner, per_owner), per_owner), :]
            for r in range(ROWS)
        ]
        rows = [x.astype(F32) for x in rows]
        for g in range(per_owner // SUB):
            piece = jnp.concatenate([x[g * SUB : (g + 1) * SUB] for x in rows], 0)
            out_ref[g * part : (g + 1) * part, :] = piece.astype(BF16)


def pack(pos, tokens, owners):
    message = shape((tokens.shape[0] // owners, tokens.shape[1]))
    outs = pl.pallas_call(
        pack_kernel,
        in_specs=[IN_SMEM, ANYWHERE],
        out_specs=[IN_VMEM] * (1 + owners),
        out_shape=[shape(tokens.shape)] + [message] * owners,
        scratch_shapes=[pltpu.SemaphoreType.DMA((ROWS,))],
        compiler_params=pltpu.CompilerParams(vmem_limit_bytes=8 * MIB),
        cost_estimate=pl.CostEstimate(flops=0, bytes_accessed=2 * MIB, transcendentals=0),
        name="pack_tokens",
    )(pos, in_hbm(tokens))
    return outs[0], outs[1:]


def stage_kernel(order_ref, wq, wk, wv, oq, ok, ov, sems):
    copies = []
    for n, (w, o) in enumerate(((wq, oq), (wk, ok), (wv, ov))):
        for p in range(4):
            rows = pl.ds(pl.multiple_of(order_ref[p] * 512, 512), 512)
            copies.append(
                pltpu.make_async_copy(w.at[rows], o.at[p * 512 : (p + 1) * 512], sems.at[4 * n + p])
            )
    for c in copies:
        c.start()
    for c in copies:
        c.wait()


def stage(order, weights, after):
    def body(order_ref, wq, wk, wv, _, *rest):
        stage_kernel(order_ref, wq, wk, wv, *rest)

    return pl.pallas_call(
        body,
        in_specs=[IN_SMEM] + [ANYWHERE] * 4,
        out_specs=[IN_VMEM] * 3,
        out_shape=[shape(w.shape) for w in weights],
        scratch_shapes=[pltpu.SemaphoreType.DMA((12,))],
        compiler_params=pltpu.CompilerParams(vmem_limit_bytes=16 * MIB),
        cost_estimate=pl.CostEstimate(flops=0, bytes_accessed=0, transcendentals=0),
        name="stage_weights",
    )(order, *weights, after)


def gathered(x_refs, at, w_ref):
    width = x_refs[0].shape[1]
    total = None
    for p, x_ref in enumerate(x_refs):
        term = dot(x_ref[at, :], w_ref[p * width : (p + 1) * width, :])
        total = term if total is None else total + term
    return total.astype(BF16)


def half_kernel(x0, x1, wq, wk, wv, *outs):
    width = x0.shape[1]
    for w, out in zip((wq, wk, wv), outs):
        out[...] = dot(x0[...], w[:width, :]) + dot(x1[...], w[width : 2 * width, :])


def half_sums(own, core, weights, after):
    shapes = [shape(own.shape, F32)] * 3
    return call(half_kernel, "half_sums", 0, shapes, (own, core, *weights), after)


def near_kernel(x0, x1, x2, x3, wq, wk, wv, *outs):
    everything = slice(0, x0.shape[0])
    for w, out in zip((wq, wk, wv), outs):
        out[...] = gathered((x0, x1, x2, x3), everything, w)


def halo_kernel(x0, x1, x2, x3, wk, wv, out_ref):
    rows = x0.shape[0]
    at = slice(rows - STRIDE, rows)
    out_ref[:STRIDE, :] = gathered((x0, x1, x2, x3), at, wk)
    out_ref[STRIDE:, :] = gathered((x0, x1, x2, x3), at, wv)


def project_kernel(x0, x1, x2, x3, wq, wk, wv, halo, q_ref, k_ref, v_ref):
    rows = x0.shape[0]
    xs = (x0, x1, x2, x3)
    last = slice(rows - STRIDE, rows)
    k_ref[last, :] = halo[:STRIDE, :]
    v_ref[last, :] = halo[STRIDE:, :]
    for w, out, upto in ((wq, q_ref, rows), (wk, k_ref, rows - STRIDE), (wv, v_ref, rows - STRIDE)):
        out[:upto, :] = gathered(xs, slice(0, upto), w)


def softmax_columns(s):
    m = jnp.maximum(jnp.max(s, 0, keepdims=True), FLOOR)
    p = jnp.exp2((s - m) * SCALE2)
    total = jnp.maximum(jnp.sum(p, 0, keepdims=True), 1.0)
    return p, total, m * SCALE2 + jnp.log2(total)


def local_kernel(pos_ref, q_ref, k_ref, v_ref, halo_ref, *outs):
    out_refs, lse_refs = outs[: len(CHUNKS)], outs[len(CHUNKS) :]
    owners = out_refs[0].shape[0]
    groups = STRIDE // owners // SUB
    block = pos_ref[0]
    u = lax.broadcasted_iota(jnp.int32, (STRIDE, STRIDE), 0)
    t = lax.broadcasted_iota(jnp.int32, (STRIDE, STRIDE), 1)
    current = u <= t
    low = jnp.where(block == 0, -1e30, 0.0).astype(F32)
    for r in range(ROWS):
        lses = []
        here = slice(r * STRIDE, (r + 1) * STRIDE)
        back = slice((r - 1) * STRIDE, r * STRIDE)
        for h in range(HEADS):
            cols = slice(h * DH, (h + 1) * DH)
            q = q_ref[here, cols]
            k_prev = k_ref[back, cols] if r else halo_ref[:STRIDE, cols]
            v_prev = v_ref[back, cols] if r else halo_ref[STRIDE:, cols]
            s_prev = dot_t(k_prev, q)
            if r == 0:
                s_prev = s_prev + low
            p, total, lse = softmax_columns(jnp.where(current, dot_t(k_ref[here, cols], q), s_prev))
            p_now = jnp.where(current, p, 0.0).astype(BF16)
            p_prev = jnp.where(current, 0.0, p).astype(BF16)
            o = dot_l(v_ref[here, cols], p_now) + dot_l(v_prev, p_prev)
            o = (o * (1.0 / total)).T
            lses.append(lse)
            for d in range(owners):
                for chunk, out_ref in zip(CHUNKS, out_refs):
                    for n, g in enumerate(chunk):
                        at = (d * groups + g) * SUB
                        to = (n * ROWS + r) * SUB
                        out_ref[d, to : to + SUB, cols] = o[at : at + SUB]
        lses.append(jnp.zeros((128 - HEADS, STRIDE), F32))
        turned = jnp.concatenate(lses, 0).T
        for chunk, lse_ref in zip(CHUNKS, lse_refs):
            for n, g in enumerate(chunk):
                total = None
                for d in range(owners):
                    at = (d * groups + g) * SUB
                    moved = pltpu.roll(turned[at : at + SUB], 8 * (block ^ d), 1)
                    total = moved if total is None else total + moved
                to = (n * ROWS + r) * SUB
                lse_ref[to : to + SUB, :] = total


def local_part(pos, q, k, v, halo, owners, after):
    rows, width = q.shape
    sizes = [len(chunk) * ROWS * SUB for chunk in CHUNKS]
    shapes = [shape((owners, m, width), F32) for m in sizes] + [shape((m, 128), F32) for m in sizes]
    outs = call(local_kernel, "local_part", 5, shapes, (pos, q, k, v, halo), after)
    return list(zip(outs[: len(sizes)], outs[len(sizes) :]))


def column_kernel(pos_ref, x2, x3, hq, hk, hv, wq, wk, wv, nq, nk, nv, *rest):
    out_refs, scratch = rest[:-3], rest[-3:]
    owners, message, width = scratch[0].shape
    groups = message // (ROWS * SUB)
    for h, w, near, a in zip((hq, hk, hv), (wq, wk, wv), (nq, nk, nv), scratch):
        total = h[...] + dot(x2[...], w[2 * width : 3 * width, :])
        total = total + dot(x3[...], w[3 * width :, :])
        a[:NEAR] = near[...].reshape(NEAR, message, width)
        a[NEAR:] = total.astype(BF16).reshape(owners - NEAR, message, width)
    part = ROWS * SUB
    size = owners * part

    def row_and_class(dim):
        i = lax.broadcasted_iota(jnp.int32, (size, size), dim)
        return ((i // part) ^ pos_ref[0]) * ROWS + (i % part) // SUB, i % SUB

    (row_j, class_j), (row_i, class_i) = row_and_class(0), row_and_class(1)
    earlier = jnp.logical_and(class_i == class_j, row_i > row_j)
    stats = []
    for g in range(groups):
        at = slice(g * part, (g + 1) * part)
        lses = []
        for h in range(HEADS):
            cols = slice(h * DH, (h + 1) * DH)
            q, k, v = (a[:, at, cols].reshape(size, DH) for a in scratch)
            p, total, lse = softmax_columns(jnp.where(earlier, dot_t(k, q), -1e30))
            o = (dot_l(v, p.astype(BF16)) * (1.0 / total)).T.astype(BF16)
            to = h * message + g * part
            rows = slice(to, to + part)
            for n in range(owners):
                out_refs[n][rows, :] = o[n * part : (n + 1) * part]
            lses.append(lse)
        stats.append(jnp.concatenate(lses + lses, 0))
    upper = lax.broadcasted_iota(jnp.int32, (8, 128), 0) < HEADS
    blank = [jnp.zeros((8, 128 - message), F32)] if message < 128 else []
    for n in range(owners):
        x = jnp.concatenate([s[:, n * part : (n + 1) * part] for s in stats] + blank, 1)
        hi = x.astype(BF16).astype(F32)
        mid = (x - hi).astype(BF16).astype(F32)
        lo = x - hi - mid
        tail = jnp.concatenate([jnp.where(upper, hi, lo), jnp.where(upper, mid, 0.0)], 0)
        to = HEADS * message
        out_refs[n][to : to + 16, :] = tail.astype(BF16)


def column_part(pos, across, halves, weights, near, owners, after):
    tokens, width = across.shape
    message = tokens // (owners - NEAR)
    shapes = [shape((HEADS * message + 16, DH))] * owners
    scratch = [pltpu.VMEM((owners, message, width), BF16)] * 3
    args = (pos, across, swap(across, 1), *halves, *weights, *near)
    return call(column_kernel, "column_part", 0, shapes, args, after, scratch)


def mix_kernel(share, pos_ref, *refs):
    count = 2 * len(CHUNKS)
    local_refs, col_refs, (own_ref, send_ref, mixed) = refs[:count], refs[count:-3], refs[-3:]
    per_owner = mixed.shape[1] // len(share)
    base = 0
    for chunk, loc_ref, lse_ref in zip(CHUNKS, local_refs[::2], local_refs[1::2]):
        message = loc_ref.shape[1]
        size = HEADS * message + 16
        tiles = [jnp.zeros((8, 128), F32)] * 16
        for k, col_ref in zip(share, col_refs):
            tail = col_ref[base + HEADS * message : base + size, :].astype(F32)
            tiles[k] = tail[:8] + tail[8:]
        turned = jnp.concatenate(tiles, 0).T[:message]
        col_lse = turned + pltpu.roll(turned, 124, 1)
        loc_lse = lse_ref[...]
        top = jnp.maximum(col_lse, loc_lse)
        w_col = jnp.exp2(col_lse - top)
        w_loc = jnp.exp2(loc_lse - top)
        scale = 1.0 / (w_col + w_loc)
        w_col = w_col * scale
        w_loc = w_loc * scale
        for n, (k, col_ref) in enumerate(zip(share, col_refs)):
            d = pos_ref[0] ^ k
            for h in range(HEADS):
                cols = slice(h * DH, (h + 1) * DH)
                at = slice(8 * k + h, 8 * k + h + 1)
                col = col_ref[base + h * message : base + (h + 1) * message, :].astype(F32)
                both = loc_ref[d, :, cols] * w_loc[:, at] + col * w_col[:, at]
                for r in range(ROWS):
                    for m, g in enumerate(chunk):
                        start = (m * ROWS + r) * SUB
                        to = n * per_owner + g * SUB
                        mixed[r, to : to + SUB, cols] = both[start : start + SUB]
        base += size
    core = pos_ref[1]
    for x in range(2):
        own_ref[x] = mixed[2 * x + core].astype(BF16)
        send_ref[x] = mixed[2 * x + 1 - core].astype(BF16)


def mix(pos, share, columns, locals_, after):
    owners, _, width = locals_[0][0].shape
    tokens = len(share) * STRIDE // owners
    shapes = [shape((2, tokens, width))] * 2
    scratch = [pltpu.VMEM((ROWS, tokens, width), F32)]
    args = (pos, *[x for pair in locals_ for x in pair], *columns)
    return call(functools.partial(mix_kernel, share), "mix", 2, shapes, args, after, scratch)


def out_kernel(pos_ref, a_ref, b_ref, wa_ref, wb_ref, send_ref, keep_ref):
    tokens, columns = send_ref.shape
    a = a_ref[...].reshape(2 * tokens, -1)
    b = b_ref[...].reshape(2 * tokens, -1)
    low_side = pos_ref[2] == 0
    tile = 512
    for n in range(0, columns, tile):
        at = slice(n, n + tile)
        total = dot(a, wa_ref[:, at]) + dot(b, wb_ref[:, at])
        send_ref[:, at] = jnp.where(low_side, total[tokens:], total[:tokens]).astype(BF16)
        keep_ref[:, at] = jnp.where(low_side, total[:tokens], total[tokens:])


def out_project(pos, own, other, w_own, w_other):
    dims = (own.shape[1], w_own.shape[1])
    shapes = [shape(dims), shape(dims, F32)]
    return call(out_kernel, "out_project", 2, shapes, (pos, own, other, w_own, w_other))


def join_kernel(share, pos_ref, keep, got, *rest):
    out_hbm, joined, sems = rest[-3:]
    span = keep.shape[0] // len(share)
    joined[...] = (keep[...] + got[...].astype(F32)).astype(BF16)
    copies = []
    for n, k in enumerate(share):
        to = pl.ds(pl.multiple_of((pos_ref[0] ^ k) * span, span), span)
        rows = slice(n * span, (n + 1) * span)
        copies.append(pltpu.make_async_copy(joined.at[rows], out_hbm.at[to], sems.at[n]))
    for c in copies:
        c.start()
    for c in copies:
        c.wait()


def join(pos, share, keep, got, earlier):
    return pl.pallas_call(
        functools.partial(join_kernel, share),
        in_specs=[IN_SMEM, IN_VMEM, IN_VMEM] + [ANYWHERE] * len(earlier),
        out_specs=ANYWHERE,
        out_shape=shape((STRIDE, keep.shape[1])),
        input_output_aliases={3: 0} if earlier else {},
        scratch_shapes=[pltpu.VMEM(keep.shape, BF16), pltpu.SemaphoreType.DMA((len(share),))],
        compiler_params=pltpu.CompilerParams(vmem_limit_bytes=16 * MIB),
        cost_estimate=pl.CostEstimate(flops=int(1.1e9), bytes_accessed=0, transcendentals=0),
        name="join",
    )(pos, keep, got, *earlier)


def swap(value, distance):
    return lax.ppermute(value, "head", [(i, i ^ distance) for i in range(4)])


def exchange(messages):
    peers = lax.axis_size("seq")

    def move(value, k):
        return lax.ppermute(value, "seq", [(i, i ^ k) for i in range(peers)]) if k else value

    return [move(m, k) for k, m in enumerate(messages)]


def chunked(tokens, w_query, w_key, w_value, w_out):
    owners = lax.axis_size("seq")
    head = lax.axis_index("head")
    block = lax.axis_index("seq")
    order = jnp.bitwise_xor(jnp.arange(4, dtype=jnp.int32), head.astype(jnp.int32))
    pos = jnp.stack([block, head % 2, head // 2]).astype(jnp.int32)
    rows, width = tokens.shape

    across = swap(tokens, 2)
    block_tokens, sent = pack(pos, tokens, owners)
    messages = exchange(sent)
    near_own = jnp.concatenate(messages[:NEAR], 0)
    near_core, near_across = swap(near_own, 1), swap(near_own, 2)
    w_other = swap(w_out, 1)
    far_own = jnp.concatenate(messages[NEAR:], 0)
    far_core, far_across = swap(far_own, 1), swap(far_own, 2)
    weights = stage(order, (w_query, w_key, w_value), messages[1])
    block_core = swap(fence(block_tokens, near_own, far_own), 1)
    across = fence(across, near_across, far_own)
    pieces = (block_tokens, block_core, across, swap(across, 1))
    own_halo = call(
        halo_kernel, "project_halo", 1.5, shape((2 * STRIDE, width)), (*pieces, *weights[1:])
    )
    halo = lax.ppermute(own_halo, "seq", [(i, i + 1) for i in range(owners - 1)])
    q, k, v = call(
        project_kernel,
        "project_block",
        0,
        [shape((rows, width))] * 3,
        (*pieces, *weights, own_halo),
        (far_own,),
    )
    near = call(
        near_kernel,
        "project_near",
        0,
        [shape(near_own.shape)] * 3,
        (near_own, near_core, near_across, swap(near_across, 1), *weights),
        (q,),
    )
    far_half = half_sums(far_own, far_core, weights, (near[0],))
    far_across = fence(far_across, near[0], halo)
    columns = column_part(pos, far_across, far_half, weights, near, owners, (w_other,))
    locals_ = local_part(pos, q, k, v, halo, owners, (columns[0],))
    columns = exchange(columns)
    sums, after = [], ()
    for share in SHARES:
        own, send = mix(pos, share, [columns[n] for n in share], locals_, after)
        out, keep = out_project(pos, own, swap(send, 1), w_out, w_other)
        sums.append((keep, swap(out, 2)))
        after = (keep,)
    result = ()
    for share, (keep, got) in zip(SHARES, sums):
        result = (join(pos, share, keep, got, result),)
    return result[0]


def from_behind(value, axis, by):
    peers = lax.axis_size(axis)
    pairs = [(i, i + by) for i in range(peers) if 0 <= i + by < peers]
    return lax.ppermute(value, axis, pairs)


def general(tokens, w_query, w_key, w_value, w_out):
    tok_rows = tokens.shape[0]
    head_width = w_query.shape[1]
    head_count = head_width // DH
    score_scale = DH ** (-0.5)
    shard_piece = lax.all_gather(tokens, "head", axis=1, tiled=True)
    query_full, key_full, value_full = tuple(
        (
            jnp.dot(shard_piece, weight, preferred_element_type=jnp.float32)
            for weight in (w_query, w_key, w_value)
        )
    )
    query = query_full.astype(jnp.bfloat16).reshape(tok_rows, head_count, DH)
    key_heads = key_full.astype(jnp.bfloat16).reshape(tok_rows, head_count, DH)
    value_heads = value_full.astype(jnp.bfloat16).reshape(tok_rows, head_count, DH)
    prev_keys, prev_values = from_behind((key_heads[-STRIDE:], value_heads[-STRIDE:]), "seq", 1)
    blocks = tok_rows // STRIDE
    extended_keys = jnp.concatenate([prev_keys, key_heads], 0)
    extended_values = jnp.concatenate([prev_values, value_heads], 0)
    window_keys = jnp.concatenate(
        [
            extended_keys[:tok_rows].reshape(blocks, STRIDE, head_count, DH),
            extended_keys[STRIDE:].reshape(blocks, STRIDE, head_count, DH),
        ],
        1,
    )
    window_values = jnp.concatenate(
        [
            extended_values[:tok_rows].reshape(blocks, STRIDE, head_count, DH),
            extended_values[STRIDE:].reshape(blocks, STRIDE, head_count, DH),
        ],
        1,
    )
    query_blocks = query.reshape(blocks, STRIDE, head_count, DH)
    scores = (
        jnp.einsum("bthd,buhd->bhtu", query_blocks, window_keys, preferred_element_type=jnp.float32)
        * score_scale
    )
    first_position = lax.axis_index("seq") * tok_rows
    block_index = jnp.arange(blocks)[:, None, None, None]
    query_index = jnp.arange(STRIDE)[None, None, :, None]
    key_index = jnp.arange(2 * STRIDE)[None, None, None, :]
    allowed = (
        (key_index > query_index)
        & (key_index <= query_index + STRIDE)
        & (first_position + block_index * STRIDE + key_index - STRIDE >= 0)
    )
    local_top = jnp.max(jnp.where(allowed, scores, -1e30), axis=-1)
    local_weights = jnp.where(allowed, jnp.exp(scores - local_top[..., None]), 0.0)
    local_total = jnp.sum(local_weights, axis=-1)
    local_out = jnp.einsum(
        "bhtu,buhd->bthd",
        local_weights.astype(jnp.bfloat16),
        window_values,
        preferred_element_type=jnp.float32,
    )
    local_out = local_out.reshape(tok_rows, head_count, DH)
    local_top = local_top.transpose(0, 2, 1).reshape(tok_rows, head_count)
    local_total = local_total.transpose(0, 2, 1).reshape(tok_rows, head_count)
    row_count = tok_rows // STRIDE
    query_class = lax.all_to_all(
        query.reshape(row_count, STRIDE, head_count, DH),
        "seq",
        split_axis=1,
        concat_axis=0,
        tiled=True,
    )
    key_class = lax.all_to_all(
        key_heads.reshape(row_count, STRIDE, head_count, DH),
        "seq",
        split_axis=1,
        concat_axis=0,
        tiled=True,
    )
    value_class = lax.all_to_all(
        value_heads.reshape(row_count, STRIDE, head_count, DH),
        "seq",
        split_axis=1,
        concat_axis=0,
        tiled=True,
    )
    row_total = query_class.shape[0]
    class_scores = (
        jnp.einsum("rchd,schd->chrs", query_class, key_class, preferred_element_type=jnp.float32)
        * score_scale
    )
    earlier = (
        jnp.arange(row_total)[None, None, :, None] > jnp.arange(row_total)[None, None, None, :]
    )
    class_top = jnp.max(jnp.where(earlier, class_scores, -1e30), axis=-1)
    class_weights = jnp.where(earlier, jnp.exp(class_scores - class_top[..., None]), 0.0)
    class_total = jnp.sum(class_weights, axis=-1)
    summed = jnp.einsum(
        "chrs,schd->rchd",
        class_weights.astype(jnp.bfloat16),
        value_class,
        preferred_element_type=jnp.float32,
    )
    floor_total = jnp.maximum(class_total, 1.0).transpose(2, 0, 1)
    class_out = (summed / floor_total[..., None]).astype(jnp.bfloat16)
    class_top_rows = class_top.transpose(2, 0, 1)
    class_total_rows = class_total.transpose(2, 0, 1)
    column_out = class_out
    column_top = class_top_rows
    column_total = class_total_rows
    column_out, column_top, column_total = (
        lax.all_to_all(column_out, "seq", split_axis=0, concat_axis=1, tiled=True),
        lax.all_to_all(
            column_top.astype(jnp.bfloat16), "seq", split_axis=0, concat_axis=1, tiled=True
        ).astype(column_top.dtype),
        lax.all_to_all(
            column_total.astype(jnp.bfloat16), "seq", split_axis=0, concat_axis=1, tiled=True
        ).astype(column_total.dtype),
    )
    column_out = column_out.reshape(tok_rows, head_count, DH)
    column_top = column_top.reshape(tok_rows, head_count)
    column_total = column_total.reshape(tok_rows, head_count)
    top_score = jnp.maximum(local_top, column_top)
    local_weight = jnp.exp(local_top - top_score)
    column_weight = column_total * jnp.exp(column_top - top_score)
    denominator = local_total * local_weight + column_weight
    mixed = (
        local_out * local_weight[..., None]
        + column_out.astype(jnp.float32) * column_weight[..., None]
    ) / denominator[..., None]
    mixed = mixed.astype(jnp.bfloat16).reshape(tok_rows, head_width)
    return lax.psum_scatter(
        jnp.dot(mixed, w_out, preferred_element_type=jnp.float32).astype(jnp.bfloat16),
        "head",
        scatter_dimension=0,
        tiled=True,
    )


def shards(tokens, w_query, w_key, w_value, w_out):
    rows, width = w_query.shape
    fits = (
        lax.axis_size("seq") == PEERS
        and lax.axis_size("head") == 4
        and tokens.shape == (ROWS * STRIDE, HEADS * DH)
        and (rows, width) == (4 * HEADS * DH, HEADS * DH)
    )
    plan = chunked if fits else general
    return plan(tokens, w_query, w_key, w_value, w_out)


def solution(mesh):
    in_specs = (
        P("seq", "head"),
        P(None, "head"),
        P(None, "head"),
        P(None, "head"),
        P("head", None),
    )
    out_specs = P(("seq", "head"), None)
    return jax.shard_map(shards, mesh=mesh, in_specs=in_specs, out_specs=out_specs, check_vma=False)
```

```python
import functools

import jax
import jax.numpy as jnp
from jax import lax
from jax.experimental import pallas as pl
from jax.experimental.pallas import tpu as pltpu
from jax.sharding import PartitionSpec as P

DH = 128
STRIDE = 256
HEADS = 4
ROWS = 4
SUB = 8
CHUNKS = ((0, 1, 2, 3),)
NEAR = 4
PEERS = 8
SHARES = ((4, 5, 1, 2, 3, 0), (6, 7))
SCALE2 = DH ** (-0.5) * 1.4426950408889634
FLOOR = -1e29
MIB = 1024 * 1024
F32 = jnp.float32
BF16 = jnp.bfloat16


ANYWHERE = pl.BlockSpec(memory_space=pl.ANY)
IN_VMEM = pl.BlockSpec(memory_space=pltpu.VMEM)
IN_SMEM = pl.BlockSpec(memory_space=pltpu.SMEM)


def call(body, name, micros, out_shape, args, after=(), scratch=(), mib=24):
    specs = [IN_SMEM if x.dtype == jnp.int32 else IN_VMEM for x in args]
    extra = len(after)

    def run(*refs):
        n = len(args)
        body(*refs[:n], *refs[n + extra :])

    return pl.pallas_call(
        run,
        in_specs=specs + [ANYWHERE] * extra,
        out_specs=jax.tree.map(lambda _: IN_VMEM, out_shape),
        out_shape=out_shape,
        scratch_shapes=list(scratch),
        compiler_params=pltpu.CompilerParams(vmem_limit_bytes=mib * MIB),
        cost_estimate=pl.CostEstimate(
            flops=int(micros * 1.1e9), bytes_accessed=0, transcendentals=0
        ),
        name=name,
    )(*args, *after)


def fence(value, *after):
    return pl.pallas_call(
        lambda *refs: None,
        in_specs=[ANYWHERE] * (1 + len(after)),
        out_specs=ANYWHERE,
        out_shape=jax.ShapeDtypeStruct(value.shape, value.dtype),
        input_output_aliases={0: 0},
        compiler_params=pltpu.CompilerParams(vmem_limit_bytes=MIB),
        cost_estimate=pl.CostEstimate(flops=0, bytes_accessed=0, transcendentals=0),
        name="fence",
    )(value, *after)


def in_hbm(value):
    return pltpu.with_memory_space_constraint(value, pltpu.HBM)


def shape(dims, dtype=BF16):
    return jax.ShapeDtypeStruct(tuple(dims), dtype)


def dot(a, b):
    return jnp.dot(a, b, preferred_element_type=F32)


def dot_t(a, b):
    return lax.dot_general(a, b, (((1,), (1,)), ((), ())), preferred_element_type=F32)


def dot_l(a, b):
    return lax.dot_general(a, b, (((0,), (0,)), ((), ())), preferred_element_type=F32)


def pack_kernel(pos_ref, tok_hbm, tok_ref, *rest):
    out_refs, sems = rest[:-1], rest[-1]
    spans = [slice(r * STRIDE, (r + 1) * STRIDE) for r in range(ROWS)]
    copies = [
        pltpu.make_async_copy(tok_hbm.at[at], tok_ref.at[at], sems.at[r])
        for r, at in enumerate(spans)
    ]
    for c in copies:
        c.start()
    for c in copies:
        c.wait()
    per_owner = STRIDE // len(out_refs)
    part = ROWS * SUB
    for k, out_ref in enumerate(out_refs):
        d = pos_ref[0] ^ k
        rows = [
            tok_ref[pl.ds(pl.multiple_of(r * STRIDE + d * per_owner, per_owner), per_owner), :]
            for r in range(ROWS)
        ]
        rows = [x.astype(F32) for x in rows]
        for g in range(per_owner // SUB):
            piece = jnp.concatenate([x[g * SUB : (g + 1) * SUB] for x in rows], 0)
            out_ref[g * part : (g + 1) * part, :] = piece.astype(BF16)


def pack(pos, tokens, owners):
    message = shape((tokens.shape[0] // owners, tokens.shape[1]))
    outs = pl.pallas_call(
        pack_kernel,
        in_specs=[IN_SMEM, ANYWHERE],
        out_specs=[IN_VMEM] * (1 + owners),
        out_shape=[shape(tokens.shape)] + [message] * owners,
        scratch_shapes=[pltpu.SemaphoreType.DMA((ROWS,))],
        compiler_params=pltpu.CompilerParams(vmem_limit_bytes=8 * MIB),
        cost_estimate=pl.CostEstimate(flops=0, bytes_accessed=2 * MIB, transcendentals=0),
        name="pack_tokens",
    )(pos, in_hbm(tokens))
    return outs[0], outs[1:]


def stage_kernel(order_ref, wq, wk, wv, oq, ok, ov, sems):
    copies = []
    for n, (w, o) in enumerate(((wq, oq), (wk, ok), (wv, ov))):
        for p in range(4):
            rows = pl.ds(pl.multiple_of(order_ref[p] * 512, 512), 512)
            copies.append(
                pltpu.make_async_copy(w.at[rows], o.at[p * 512 : (p + 1) * 512], sems.at[4 * n + p])
            )
    for c in copies:
        c.start()
    for c in copies:
        c.wait()


def stage(order, weights, after):
    def body(order_ref, wq, wk, wv, _, *rest):
        stage_kernel(order_ref, wq, wk, wv, *rest)

    return pl.pallas_call(
        body,
        in_specs=[IN_SMEM] + [ANYWHERE] * 4,
        out_specs=[IN_VMEM] * 3,
        out_shape=[shape(w.shape) for w in weights],
        scratch_shapes=[pltpu.SemaphoreType.DMA((12,))],
        compiler_params=pltpu.CompilerParams(vmem_limit_bytes=16 * MIB),
        cost_estimate=pl.CostEstimate(flops=0, bytes_accessed=0, transcendentals=0),
        name="stage_weights",
    )(order, *weights, after)


def gathered(x_refs, at, w_ref):
    width = x_refs[0].shape[1]
    total = None
    for p, x_ref in enumerate(x_refs):
        term = dot(x_ref[at, :], w_ref[p * width : (p + 1) * width, :])
        total = term if total is None else total + term
    return total.astype(BF16)


def half_kernel(x0, x1, wq, wk, wv, *outs):
    width = x0.shape[1]
    for w, out in zip((wq, wk, wv), outs):
        out[...] = dot(x0[...], w[:width, :]) + dot(x1[...], w[width : 2 * width, :])


def half_sums(own, core, weights, after):
    shapes = [shape(own.shape, F32)] * 3
    return call(half_kernel, "half_sums", 0, shapes, (own, core, *weights), after)


def near_kernel(x0, x1, x2, x3, wq, wk, wv, *outs):
    everything = slice(0, x0.shape[0])
    for w, out in zip((wq, wk, wv), outs):
        out[...] = gathered((x0, x1, x2, x3), everything, w)


def halo_kernel(x0, x1, x2, x3, wk, wv, out_ref):
    rows = x0.shape[0]
    at = slice(rows - STRIDE, rows)
    out_ref[:STRIDE, :] = gathered((x0, x1, x2, x3), at, wk)
    out_ref[STRIDE:, :] = gathered((x0, x1, x2, x3), at, wv)


def project_kernel(x0, x1, x2, x3, wq, wk, wv, halo, q_ref, k_ref, v_ref):
    rows = x0.shape[0]
    xs = (x0, x1, x2, x3)
    last = slice(rows - STRIDE, rows)
    k_ref[last, :] = halo[:STRIDE, :]
    v_ref[last, :] = halo[STRIDE:, :]
    for w, out, upto in ((wq, q_ref, rows), (wk, k_ref, rows - STRIDE), (wv, v_ref, rows - STRIDE)):
        out[:upto, :] = gathered(xs, slice(0, upto), w)


def softmax_columns(s):
    m = jnp.maximum(jnp.max(s, 0, keepdims=True), FLOOR)
    p = jnp.exp2((s - m) * SCALE2)
    total = jnp.maximum(jnp.sum(p, 0, keepdims=True), 1.0)
    return p, total, m * SCALE2 + jnp.log2(total)


def local_kernel(pos_ref, q_ref, k_ref, v_ref, halo_ref, *outs):
    out_refs, lse_refs = outs[: len(CHUNKS)], outs[len(CHUNKS) :]
    owners = out_refs[0].shape[0]
    groups = STRIDE // owners // SUB
    block = pos_ref[0]
    u = lax.broadcasted_iota(jnp.int32, (STRIDE, STRIDE), 0)
    t = lax.broadcasted_iota(jnp.int32, (STRIDE, STRIDE), 1)
    current = u <= t
    low = jnp.where(block == 0, -1e30, 0.0).astype(F32)
    for r in range(ROWS):
        lses = []
        here = slice(r * STRIDE, (r + 1) * STRIDE)
        back = slice((r - 1) * STRIDE, r * STRIDE)
        heads = [slice(h * DH, (h + 1) * DH) for h in range(HEADS)]
        scores = []
        for cols in heads:
            q = q_ref[here, cols]
            s_prev = dot_t(k_ref[back, cols] if r else halo_ref[:STRIDE, cols], q)
            if r == 0:
                s_prev = s_prev + low
            scores.append(jnp.where(current, dot_t(k_ref[here, cols], q), s_prev))
        parts = []
        for p, total, lse in [softmax_columns(s) for s in scores]:
            now = jnp.where(current, p, 0.0).astype(BF16)
            before = jnp.where(current, 0.0, p).astype(BF16)
            parts.append((now, before, 1.0 / total))
            lses.append(lse)
        results = []
        for cols, (now, before, share) in zip(heads, parts):
            v_prev = v_ref[back, cols] if r else halo_ref[STRIDE:, cols]
            results.append((dot_l(v_ref[here, cols], now) + dot_l(v_prev, before)) * share)
        for cols, o in zip(heads, results):
            o = o.T
            for d in range(owners):
                for chunk, out_ref in zip(CHUNKS, out_refs):
                    for n, g in enumerate(chunk):
                        at = (d * groups + g) * SUB
                        to = (n * ROWS + r) * SUB
                        out_ref[d, to : to + SUB, cols] = o[at : at + SUB]
        lses.append(jnp.zeros((128 - HEADS, STRIDE), F32))
        turned = jnp.concatenate(lses, 0).T
        for chunk, lse_ref in zip(CHUNKS, lse_refs):
            for n, g in enumerate(chunk):
                total = None
                for d in range(owners):
                    at = (d * groups + g) * SUB
                    moved = pltpu.roll(turned[at : at + SUB], 8 * (block ^ d), 1)
                    total = moved if total is None else total + moved
                to = (n * ROWS + r) * SUB
                lse_ref[to : to + SUB, :] = total


def local_part(pos, q, k, v, halo, owners, after):
    rows, width = q.shape
    sizes = [len(chunk) * ROWS * SUB for chunk in CHUNKS]
    shapes = [shape((owners, m, width), F32) for m in sizes] + [shape((m, 128), F32) for m in sizes]
    outs = call(local_kernel, "local_part", 5, shapes, (pos, q, k, v, halo), after)
    return list(zip(outs[: len(sizes)], outs[len(sizes) :]))


def column_kernel(pos_ref, x2, x3, hq, hk, hv, wq, wk, wv, nq, nk, nv, *rest):
    out_refs, scratch = rest[:-3], rest[-3:]
    owners, message, width = scratch[0].shape
    groups = message // (ROWS * SUB)
    for h, w, near, a in zip((hq, hk, hv), (wq, wk, wv), (nq, nk, nv), scratch):
        total = h[...] + dot(x2[...], w[2 * width : 3 * width, :])
        total = total + dot(x3[...], w[3 * width :, :])
        a[:NEAR] = near[...].reshape(NEAR, message, width)
        a[NEAR:] = total.astype(BF16).reshape(owners - NEAR, message, width)
    part = ROWS * SUB
    size = owners * part

    def row_and_class(dim):
        i = lax.broadcasted_iota(jnp.int32, (size, size), dim)
        return ((i // part) ^ pos_ref[0]) * ROWS + (i % part) // SUB, i % SUB

    (row_j, class_j), (row_i, class_i) = row_and_class(0), row_and_class(1)
    earlier = jnp.logical_and(class_i == class_j, row_i > row_j)
    stats = []
    for g in range(groups):
        at = slice(g * part, (g + 1) * part)
        heads = [slice(h * DH, (h + 1) * DH) for h in range(HEADS)]
        operands = [[a[:, at, cols].reshape(size, DH) for a in scratch] for cols in heads]
        scores = [jnp.where(earlier, dot_t(k, q), -1e30) for q, k, _ in operands]
        parts = [softmax_columns(s) for s in scores]
        results = [
            dot_l(v, p.astype(BF16)) * (1.0 / total)
            for (_, _, v), (p, total, _) in zip(operands, parts)
        ]
        lses = [lse for _, _, lse in parts]
        for h, o in enumerate(results):
            o = o.T.astype(BF16)
            to = h * message + g * part
            for n in range(owners):
                out_refs[n][to : to + part, :] = o[n * part : (n + 1) * part]
        stats.append(jnp.concatenate(lses + lses, 0))
    upper = lax.broadcasted_iota(jnp.int32, (8, 128), 0) < HEADS
    blank = [jnp.zeros((8, 128 - message), F32)] if message < 128 else []
    for n in range(owners):
        x = jnp.concatenate([s[:, n * part : (n + 1) * part] for s in stats] + blank, 1)
        hi = x.astype(BF16).astype(F32)
        mid = (x - hi).astype(BF16).astype(F32)
        lo = x - hi - mid
        tail = jnp.concatenate([jnp.where(upper, hi, lo), jnp.where(upper, mid, 0.0)], 0)
        to = HEADS * message
        out_refs[n][to : to + 16, :] = tail.astype(BF16)


def column_part(pos, across, halves, weights, near, owners, after):
    tokens, width = across.shape
    message = tokens // (owners - NEAR)
    shapes = [shape((HEADS * message + 16, DH))] * owners
    scratch = [pltpu.VMEM((owners, message, width), BF16)] * 3
    args = (pos, across, swap(across, 1), *halves, *weights, *near)
    return call(column_kernel, "column_part", 0, shapes, args, after, scratch)


def mix_kernel(share, pos_ref, *refs):
    count = 2 * len(CHUNKS)
    local_refs, col_refs, (own_ref, send_ref, mixed) = refs[:count], refs[count:-3], refs[-3:]
    per_owner = mixed.shape[1] // len(share)
    base = 0
    for chunk, loc_ref, lse_ref in zip(CHUNKS, local_refs[::2], local_refs[1::2]):
        message = loc_ref.shape[1]
        size = HEADS * message + 16
        tiles = [jnp.zeros((8, 128), F32)] * 16
        for k, col_ref in zip(share, col_refs):
            tail = col_ref[base + HEADS * message : base + size, :].astype(F32)
            tiles[k] = tail[:8] + tail[8:]
        turned = jnp.concatenate(tiles, 0).T[:message]
        col_lse = turned + pltpu.roll(turned, 124, 1)
        loc_lse = lse_ref[...]
        top = jnp.maximum(col_lse, loc_lse)
        w_col = jnp.exp2(col_lse - top)
        w_loc = jnp.exp2(loc_lse - top)
        scale = 1.0 / (w_col + w_loc)
        w_col = w_col * scale
        w_loc = w_loc * scale
        for n, (k, col_ref) in enumerate(zip(share, col_refs)):
            d = pos_ref[0] ^ k
            for h in range(HEADS):
                cols = slice(h * DH, (h + 1) * DH)
                at = slice(8 * k + h, 8 * k + h + 1)
                col = col_ref[base + h * message : base + (h + 1) * message, :].astype(F32)
                both = loc_ref[d, :, cols] * w_loc[:, at] + col * w_col[:, at]
                for r in range(ROWS):
                    for m, g in enumerate(chunk):
                        start = (m * ROWS + r) * SUB
                        to = n * per_owner + g * SUB
                        mixed[r, to : to + SUB, cols] = both[start : start + SUB]
        base += size
    core = pos_ref[1]
    for x in range(2):
        own_ref[x] = mixed[2 * x + core].astype(BF16)
        send_ref[x] = mixed[2 * x + 1 - core].astype(BF16)


def mix(pos, share, columns, locals_, after):
    owners, _, width = locals_[0][0].shape
    tokens = len(share) * STRIDE // owners
    shapes = [shape((2, tokens, width))] * 2
    scratch = [pltpu.VMEM((ROWS, tokens, width), F32)]
    args = (pos, *[x for pair in locals_ for x in pair], *columns)
    return call(functools.partial(mix_kernel, share), "mix", 2, shapes, args, after, scratch)


def out_kernel(here, pos_ref, a_ref, b_ref, wa_ref, wb_ref, out_ref):
    side = pos_ref[2] if here else 1 - pos_ref[2]
    a, b = a_ref[side], b_ref[side]
    tile = 512
    for n in range(0, out_ref.shape[1], tile):
        at = slice(n, n + tile)
        total = dot(a, wa_ref[:, at]) + dot(b, wb_ref[:, at])
        out_ref[:, at] = total.astype(out_ref.dtype)


def out_project(pos, here, own, other, w_own, w_other):
    dims = shape((own.shape[1], w_own.shape[1]), F32 if here else BF16)
    body = functools.partial(out_kernel, here)
    return call(body, "out_project", 2, dims, (pos, own, other, w_own, w_other))


def join_kernel(share, pos_ref, keep, got, *rest):
    out_hbm, joined, sems = rest[-3:]
    span = keep.shape[0] // len(share)
    joined[...] = (keep[...] + got[...].astype(F32)).astype(BF16)
    copies = []
    for n, k in enumerate(share):
        to = pl.ds(pl.multiple_of((pos_ref[0] ^ k) * span, span), span)
        rows = slice(n * span, (n + 1) * span)
        copies.append(pltpu.make_async_copy(joined.at[rows], out_hbm.at[to], sems.at[n]))
    for c in copies:
        c.start()
    for c in copies:
        c.wait()


def join(pos, share, keep, got, earlier):
    return pl.pallas_call(
        functools.partial(join_kernel, share),
        in_specs=[IN_SMEM, IN_VMEM, IN_VMEM] + [ANYWHERE] * len(earlier),
        out_specs=ANYWHERE,
        out_shape=shape((STRIDE, keep.shape[1])),
        input_output_aliases={3: 0} if earlier else {},
        scratch_shapes=[pltpu.VMEM(keep.shape, BF16), pltpu.SemaphoreType.DMA((len(share),))],
        compiler_params=pltpu.CompilerParams(vmem_limit_bytes=16 * MIB),
        cost_estimate=pl.CostEstimate(flops=int(1.1e9), bytes_accessed=0, transcendentals=0),
        name="join",
    )(pos, keep, got, *earlier)


def swap(value, distance):
    return lax.ppermute(value, "head", [(i, i ^ distance) for i in range(4)])


def exchange(messages):
    peers = lax.axis_size("seq")

    def move(value, k):
        return lax.ppermute(value, "seq", [(i, i ^ k) for i in range(peers)]) if k else value

    return [move(m, k) for k, m in enumerate(messages)]


def chunked(tokens, w_query, w_key, w_value, w_out):
    owners = lax.axis_size("seq")
    head = lax.axis_index("head")
    block = lax.axis_index("seq")
    order = jnp.bitwise_xor(jnp.arange(4, dtype=jnp.int32), head.astype(jnp.int32))
    pos = jnp.stack([block, head % 2, head // 2]).astype(jnp.int32)
    rows, width = tokens.shape

    across = swap(tokens, 2)
    block_tokens, sent = pack(pos, tokens, owners)
    messages = exchange(sent)
    near_own = jnp.concatenate(messages[:NEAR], 0)
    near_core, near_across = swap(near_own, 1), swap(near_own, 2)
    w_other = swap(w_out, 1)
    far_own = jnp.concatenate(messages[NEAR:], 0)
    far_core, far_across = swap(far_own, 1), swap(far_own, 2)
    weights = stage(order, (w_query, w_key, w_value), messages[1])
    block_core = swap(fence(block_tokens, near_own, far_own), 1)
    across = fence(across, near_across, far_own)
    pieces = (block_tokens, block_core, across, swap(across, 1))
    own_halo = call(
        halo_kernel, "project_halo", 1.5, shape((2 * STRIDE, width)), (*pieces, *weights[1:])
    )
    halo = lax.ppermute(own_halo, "seq", [(i, i + 1) for i in range(owners - 1)])
    q, k, v = call(
        project_kernel,
        "project_block",
        0,
        [shape((rows, width))] * 3,
        (*pieces, *weights, own_halo),
        (far_own,),
    )
    near = call(
        near_kernel,
        "project_near",
        0,
        [shape(near_own.shape)] * 3,
        (near_own, near_core, near_across, swap(near_across, 1), *weights),
        (q,),
    )
    far_half = half_sums(far_own, far_core, weights, (near[0],))
    far_across = fence(far_across, near[0], halo)
    columns = column_part(pos, far_across, far_half, weights, near, owners, (w_other,))
    locals_ = local_part(pos, q, k, v, halo, owners, (columns[0],))
    columns = exchange(columns)
    sums, after = [], ()
    for share in SHARES:
        own, send = mix(pos, share, [columns[n] for n in share], locals_, after)
        other = swap(send, 1)
        out = out_project(pos, False, own, other, w_out, w_other)
        keep = out_project(pos, True, own, other, w_out, w_other)
        sums.append((keep, swap(out, 2)))
        after = (out,)
    result = ()
    for share, (keep, got) in zip(SHARES, sums):
        result = (join(pos, share, keep, got, result),)
    return result[0]


def from_behind(value, axis, by):
    peers = lax.axis_size(axis)
    pairs = [(i, i + by) for i in range(peers) if 0 <= i + by < peers]
    return lax.ppermute(value, axis, pairs)


def general(tokens, w_query, w_key, w_value, w_out):
    tok_rows = tokens.shape[0]
    head_width = w_query.shape[1]
    head_count = head_width // DH
    score_scale = DH ** (-0.5)
    shard_piece = lax.all_gather(tokens, "head", axis=1, tiled=True)
    query_full, key_full, value_full = tuple(
        (
            jnp.dot(shard_piece, weight, preferred_element_type=jnp.float32)
            for weight in (w_query, w_key, w_value)
        )
    )
    query = query_full.astype(jnp.bfloat16).reshape(tok_rows, head_count, DH)
    key_heads = key_full.astype(jnp.bfloat16).reshape(tok_rows, head_count, DH)
    value_heads = value_full.astype(jnp.bfloat16).reshape(tok_rows, head_count, DH)
    prev_keys, prev_values = from_behind((key_heads[-STRIDE:], value_heads[-STRIDE:]), "seq", 1)
    blocks = tok_rows // STRIDE
    extended_keys = jnp.concatenate([prev_keys, key_heads], 0)
    extended_values = jnp.concatenate([prev_values, value_heads], 0)
    window_keys = jnp.concatenate(
        [
            extended_keys[:tok_rows].reshape(blocks, STRIDE, head_count, DH),
            extended_keys[STRIDE:].reshape(blocks, STRIDE, head_count, DH),
        ],
        1,
    )
    window_values = jnp.concatenate(
        [
            extended_values[:tok_rows].reshape(blocks, STRIDE, head_count, DH),
            extended_values[STRIDE:].reshape(blocks, STRIDE, head_count, DH),
        ],
        1,
    )
    query_blocks = query.reshape(blocks, STRIDE, head_count, DH)
    scores = (
        jnp.einsum("bthd,buhd->bhtu", query_blocks, window_keys, preferred_element_type=jnp.float32)
        * score_scale
    )
    first_position = lax.axis_index("seq") * tok_rows
    block_index = jnp.arange(blocks)[:, None, None, None]
    query_index = jnp.arange(STRIDE)[None, None, :, None]
    key_index = jnp.arange(2 * STRIDE)[None, None, None, :]
    allowed = (
        (key_index > query_index)
        & (key_index <= query_index + STRIDE)
        & (first_position + block_index * STRIDE + key_index - STRIDE >= 0)
    )
    local_top = jnp.max(jnp.where(allowed, scores, -1e30), axis=-1)
    local_weights = jnp.where(allowed, jnp.exp(scores - local_top[..., None]), 0.0)
    local_total = jnp.sum(local_weights, axis=-1)
    local_out = jnp.einsum(
        "bhtu,buhd->bthd",
        local_weights.astype(jnp.bfloat16),
        window_values,
        preferred_element_type=jnp.float32,
    )
    local_out = local_out.reshape(tok_rows, head_count, DH)
    local_top = local_top.transpose(0, 2, 1).reshape(tok_rows, head_count)
    local_total = local_total.transpose(0, 2, 1).reshape(tok_rows, head_count)
    row_count = tok_rows // STRIDE
    query_class = lax.all_to_all(
        query.reshape(row_count, STRIDE, head_count, DH),
        "seq",
        split_axis=1,
        concat_axis=0,
        tiled=True,
    )
    key_class = lax.all_to_all(
        key_heads.reshape(row_count, STRIDE, head_count, DH),
        "seq",
        split_axis=1,
        concat_axis=0,
        tiled=True,
    )
    value_class = lax.all_to_all(
        value_heads.reshape(row_count, STRIDE, head_count, DH),
        "seq",
        split_axis=1,
        concat_axis=0,
        tiled=True,
    )
    row_total = query_class.shape[0]
    class_scores = (
        jnp.einsum("rchd,schd->chrs", query_class, key_class, preferred_element_type=jnp.float32)
        * score_scale
    )
    earlier = (
        jnp.arange(row_total)[None, None, :, None] > jnp.arange(row_total)[None, None, None, :]
    )
    class_top = jnp.max(jnp.where(earlier, class_scores, -1e30), axis=-1)
    class_weights = jnp.where(earlier, jnp.exp(class_scores - class_top[..., None]), 0.0)
    class_total = jnp.sum(class_weights, axis=-1)
    summed = jnp.einsum(
        "chrs,schd->rchd",
        class_weights.astype(jnp.bfloat16),
        value_class,
        preferred_element_type=jnp.float32,
    )
    floor_total = jnp.maximum(class_total, 1.0).transpose(2, 0, 1)
    class_out = (summed / floor_total[..., None]).astype(jnp.bfloat16)
    class_top_rows = class_top.transpose(2, 0, 1)
    class_total_rows = class_total.transpose(2, 0, 1)
    column_out = class_out
    column_top = class_top_rows
    column_total = class_total_rows
    column_out, column_top, column_total = (
        lax.all_to_all(column_out, "seq", split_axis=0, concat_axis=1, tiled=True),
        lax.all_to_all(
            column_top.astype(jnp.bfloat16), "seq", split_axis=0, concat_axis=1, tiled=True
        ).astype(column_top.dtype),
        lax.all_to_all(
            column_total.astype(jnp.bfloat16), "seq", split_axis=0, concat_axis=1, tiled=True
        ).astype(column_total.dtype),
    )
    column_out = column_out.reshape(tok_rows, head_count, DH)
    column_top = column_top.reshape(tok_rows, head_count)
    column_total = column_total.reshape(tok_rows, head_count)
    top_score = jnp.maximum(local_top, column_top)
    local_weight = jnp.exp(local_top - top_score)
    column_weight = column_total * jnp.exp(column_top - top_score)
    denominator = local_total * local_weight + column_weight
    mixed = (
        local_out * local_weight[..., None]
        + column_out.astype(jnp.float32) * column_weight[..., None]
    ) / denominator[..., None]
    mixed = mixed.astype(jnp.bfloat16).reshape(tok_rows, head_width)
    return lax.psum_scatter(
        jnp.dot(mixed, w_out, preferred_element_type=jnp.float32).astype(jnp.bfloat16),
        "head",
        scatter_dimension=0,
        tiled=True,
    )


def shards(tokens, w_query, w_key, w_value, w_out):
    rows, width = w_query.shape
    fits = (
        lax.axis_size("seq") == PEERS
        and lax.axis_size("head") == 4
        and tokens.shape == (ROWS * STRIDE, HEADS * DH)
        and (rows, width) == (4 * HEADS * DH, HEADS * DH)
    )
    plan = chunked if fits else general
    return plan(tokens, w_query, w_key, w_value, w_out)


def solution(mesh):
    in_specs = (
        P("seq", "head"),
        P(None, "head"),
        P(None, "head"),
        P(None, "head"),
        P("head", None),
    )
    out_specs = P(("seq", "head"), None)
    return jax.shard_map(shards, mesh=mesh, in_specs=in_specs, out_specs=out_specs, check_vma=False)
```

```python
import functools

import jax
import jax.numpy as jnp
from jax import lax
from jax.experimental import pallas as pl
from jax.experimental.pallas import tpu as pltpu
from jax.sharding import PartitionSpec as P

DH = 128
STRIDE = 256
HEADS = 4
ROWS = 4
SUB = 8
CHUNKS = ((0, 1, 2, 3),)
NEAR = 4
PEERS = 8
SHARES = ((4, 5, 1, 2, 3, 0), (6, 7))
SCALE2 = DH ** (-0.5) * 1.4426950408889634
FLOOR = -1e29
MIB = 1024 * 1024
F32 = jnp.float32
BF16 = jnp.bfloat16


ANYWHERE = pl.BlockSpec(memory_space=pl.ANY)
IN_VMEM = pl.BlockSpec(memory_space=pltpu.VMEM)
IN_SMEM = pl.BlockSpec(memory_space=pltpu.SMEM)


def call(body, name, micros, out_shape, args, after=(), scratch=(), mib=24):
    specs = [IN_SMEM if x.dtype == jnp.int32 else IN_VMEM for x in args]
    extra = len(after)

    def run(*refs):
        n = len(args)
        body(*refs[:n], *refs[n + extra :])

    return pl.pallas_call(
        run,
        in_specs=specs + [ANYWHERE] * extra,
        out_specs=jax.tree.map(lambda _: IN_VMEM, out_shape),
        out_shape=out_shape,
        scratch_shapes=list(scratch),
        compiler_params=pltpu.CompilerParams(vmem_limit_bytes=mib * MIB),
        cost_estimate=pl.CostEstimate(
            flops=int(micros * 1.1e9), bytes_accessed=0, transcendentals=0
        ),
        name=name,
    )(*args, *after)


def fence(value, *after):
    return pl.pallas_call(
        lambda *refs: None,
        in_specs=[ANYWHERE] * (1 + len(after)),
        out_specs=ANYWHERE,
        out_shape=jax.ShapeDtypeStruct(value.shape, value.dtype),
        input_output_aliases={0: 0},
        compiler_params=pltpu.CompilerParams(vmem_limit_bytes=MIB),
        cost_estimate=pl.CostEstimate(flops=0, bytes_accessed=0, transcendentals=0),
        name="fence",
    )(value, *after)


def in_hbm(value):
    return pltpu.with_memory_space_constraint(value, pltpu.HBM)


def shape(dims, dtype=BF16):
    return jax.ShapeDtypeStruct(tuple(dims), dtype)


def dot(a, b):
    return jnp.dot(a, b, preferred_element_type=F32)


def dot_t(a, b):
    return lax.dot_general(a, b, (((1,), (1,)), ((), ())), preferred_element_type=F32)


def dot_l(a, b):
    return lax.dot_general(a, b, (((0,), (0,)), ((), ())), preferred_element_type=F32)


def pack_kernel(pos_ref, tok_hbm, tok_ref, *rest):
    out_refs, sems = rest[:-1], rest[-1]
    spans = [slice(r * STRIDE, (r + 1) * STRIDE) for r in range(ROWS)]
    copies = [
        pltpu.make_async_copy(tok_hbm.at[at], tok_ref.at[at], sems.at[r])
        for r, at in enumerate(spans)
    ]
    for c in copies:
        c.start()
    for c in copies:
        c.wait()
    per_owner = STRIDE // len(out_refs)
    part = ROWS * SUB
    for k, out_ref in enumerate(out_refs):
        d = pos_ref[0] ^ k
        rows = [
            tok_ref[pl.ds(pl.multiple_of(r * STRIDE + d * per_owner, per_owner), per_owner), :]
            for r in range(ROWS)
        ]
        rows = [x.astype(F32) for x in rows]
        for g in range(per_owner // SUB):
            piece = jnp.concatenate([x[g * SUB : (g + 1) * SUB] for x in rows], 0)
            out_ref[g * part : (g + 1) * part, :] = piece.astype(BF16)


def pack(pos, tokens, owners):
    message = shape((tokens.shape[0] // owners, tokens.shape[1]))
    outs = pl.pallas_call(
        pack_kernel,
        in_specs=[IN_SMEM, ANYWHERE],
        out_specs=[IN_VMEM] * (1 + owners),
        out_shape=[shape(tokens.shape)] + [message] * owners,
        scratch_shapes=[pltpu.SemaphoreType.DMA((ROWS,))],
        compiler_params=pltpu.CompilerParams(vmem_limit_bytes=8 * MIB),
        cost_estimate=pl.CostEstimate(flops=0, bytes_accessed=2 * MIB, transcendentals=0),
        name="pack_tokens",
    )(pos, in_hbm(tokens))
    return outs[0], outs[1:]


def stage_kernel(order_ref, wq, wk, wv, wo, after, oq, ok, ov, oo, sems):
    copies = []
    for w, o in ((wq, oq), (wk, ok), (wv, ov), (wo, oo)):
        part = w.shape[0] // 4
        for p in range(4):
            place = p if w is wo else order_ref[p]
            rows = pl.ds(pl.multiple_of(place * part, part), part)
            to = slice(p * part, (p + 1) * part)
            sem = sems.at[len(copies)]
            copies.append(pltpu.make_async_copy(w.at[rows], o.at[to], sem))
    for c in copies:
        c.start()
    for c in copies:
        c.wait()


def stage(order, weights, after):
    return pl.pallas_call(
        stage_kernel,
        in_specs=[IN_SMEM] + [ANYWHERE] * 5,
        out_specs=[IN_VMEM] * 4,
        out_shape=[shape(w.shape) for w in weights],
        scratch_shapes=[pltpu.SemaphoreType.DMA((16,))],
        compiler_params=pltpu.CompilerParams(vmem_limit_bytes=16 * MIB),
        cost_estimate=pl.CostEstimate(flops=0, bytes_accessed=0, transcendentals=0),
        name="stage_weights",
    )(order, *weights, after)


def gathered(x_refs, at, w_ref):
    width = x_refs[0].shape[1]
    total = None
    for p, x_ref in enumerate(x_refs):
        term = dot(x_ref[at, :], w_ref[p * width : (p + 1) * width, :])
        total = term if total is None else total + term
    return total.astype(BF16)


def half_kernel(x0, x1, wq, wk, wv, *outs):
    width = x0.shape[1]
    for w, out in zip((wq, wk, wv), outs):
        out[...] = dot(x0[...], w[:width, :]) + dot(x1[...], w[width : 2 * width, :])


def half_sums(own, core, weights, after):
    shapes = [shape(own.shape, F32)] * 3
    return call(half_kernel, "half_sums", 0, shapes, (own, core, *weights), after)


def near_kernel(x0, x1, x2, x3, wq, wk, wv, *outs):
    everything = slice(0, x0.shape[0])
    for w, out in zip((wq, wk, wv), outs):
        out[...] = gathered((x0, x1, x2, x3), everything, w)


def halo_kernel(x0, x1, x2, x3, wk, wv, out_ref):
    rows = x0.shape[0]
    at = slice(rows - STRIDE, rows)
    out_ref[:STRIDE, :] = gathered((x0, x1, x2, x3), at, wk)
    out_ref[STRIDE:, :] = gathered((x0, x1, x2, x3), at, wv)


def query_kernel(x0, x1, x2, x3, wq, q_ref):
    q_ref[...] = gathered((x0, x1, x2, x3), slice(0, x0.shape[0]), wq)


def key_kernel(x0, x1, x2, x3, wk, wv, halo, k_ref, v_ref):
    upto = x0.shape[0] - STRIDE
    k_ref[upto:, :] = halo[:STRIDE, :]
    v_ref[upto:, :] = halo[STRIDE:, :]
    for w, out in ((wk, k_ref), (wv, v_ref)):
        out[:upto, :] = gathered((x0, x1, x2, x3), slice(0, upto), w)


def softmax_columns(s):
    m = jnp.maximum(jnp.max(s, 0, keepdims=True), FLOOR)
    p = jnp.exp2((s - m) * SCALE2)
    total = jnp.maximum(jnp.sum(p, 0, keepdims=True), 1.0)
    return p, total, m * SCALE2 + jnp.log2(total)


def local_kernel(pos_ref, q_ref, k_ref, v_ref, halo_ref, *outs):
    out_refs, lse_refs = outs[: len(CHUNKS)], outs[len(CHUNKS) :]
    owners = out_refs[0].shape[0]
    groups = STRIDE // owners // SUB
    block = pos_ref[0]
    u = lax.broadcasted_iota(jnp.int32, (STRIDE, STRIDE), 0)
    t = lax.broadcasted_iota(jnp.int32, (STRIDE, STRIDE), 1)
    current = u <= t
    low = jnp.where(block == 0, -1e30, 0.0).astype(F32)
    for r in range(ROWS):
        lses = []
        here = slice(r * STRIDE, (r + 1) * STRIDE)
        back = slice((r - 1) * STRIDE, r * STRIDE)
        heads = [slice(h * DH, (h + 1) * DH) for h in range(HEADS)]
        scores = []
        for cols in heads:
            q = q_ref[here, cols]
            s_prev = dot_t(k_ref[back, cols] if r else halo_ref[:STRIDE, cols], q)
            if r == 0:
                s_prev = s_prev + low
            scores.append(jnp.where(current, dot_t(k_ref[here, cols], q), s_prev))
        parts = []
        for p, total, lse in [softmax_columns(s) for s in scores]:
            now = jnp.where(current, p, 0.0).astype(BF16)
            before = jnp.where(current, 0.0, p).astype(BF16)
            parts.append((now, before, 1.0 / total))
            lses.append(lse)
        results = []
        for cols, (now, before, share) in zip(heads, parts):
            v_prev = v_ref[back, cols] if r else halo_ref[STRIDE:, cols]
            results.append((dot_l(v_ref[here, cols], now) + dot_l(v_prev, before)) * share)
        for cols, o in zip(heads, results):
            o = o.T
            for d in range(owners):
                for chunk, out_ref in zip(CHUNKS, out_refs):
                    for n, g in enumerate(chunk):
                        at = (d * groups + g) * SUB
                        to = (n * ROWS + r) * SUB
                        out_ref[d, to : to + SUB, cols] = o[at : at + SUB]
        lses.append(jnp.zeros((128 - HEADS, STRIDE), F32))
        turned = jnp.concatenate(lses, 0).T
        for chunk, lse_ref in zip(CHUNKS, lse_refs):
            for n, g in enumerate(chunk):
                total = None
                for d in range(owners):
                    at = (d * groups + g) * SUB
                    moved = pltpu.roll(turned[at : at + SUB], 8 * (block ^ d), 1)
                    total = moved if total is None else total + moved
                to = (n * ROWS + r) * SUB
                lse_ref[to : to + SUB, :] = total


def local_part(pos, q, k, v, halo, owners, after):
    rows, width = q.shape
    sizes = [len(chunk) * ROWS * SUB for chunk in CHUNKS]
    shapes = [shape((owners, m, width), F32) for m in sizes] + [shape((m, 128), F32) for m in sizes]
    outs = call(local_kernel, "local_part", 5, shapes, (pos, q, k, v, halo), after)
    return list(zip(outs[: len(sizes)], outs[len(sizes) :]))


def column_kernel(pos_ref, x2, x3a, x3b, hq, hk, hv, wq, wk, wv, nq, nk, nv, *rest):
    out_refs, scratch = rest[:-3], rest[-3:]
    owners, message, width = scratch[0].shape
    groups = message // (ROWS * SUB)
    for h, w, near, a in zip((hq, hk, hv), (wq, wk, wv), (nq, nk, nv), scratch):
        total = h[...] + dot(x2[...], w[2 * width : 3 * width, :])
        diagonal = [dot(x[...], w[3 * width :, :]) for x in (x3a, x3b)]
        total = total + jnp.concatenate(diagonal, 0)
        a[:NEAR] = near[...].reshape(NEAR, message, width)
        a[NEAR:] = total.astype(BF16).reshape(owners - NEAR, message, width)
    part = ROWS * SUB
    size = owners * part

    def row_and_class(dim):
        i = lax.broadcasted_iota(jnp.int32, (size, size), dim)
        return ((i // part) ^ pos_ref[0]) * ROWS + (i % part) // SUB, i % SUB

    (row_j, class_j), (row_i, class_i) = row_and_class(0), row_and_class(1)
    earlier = jnp.logical_and(class_i == class_j, row_i > row_j)
    stats = []
    for g in range(groups):
        at = slice(g * part, (g + 1) * part)
        heads = [slice(h * DH, (h + 1) * DH) for h in range(HEADS)]
        operands = [[a[:, at, cols].reshape(size, DH) for a in scratch] for cols in heads]
        scores = [jnp.where(earlier, dot_t(k, q), -1e30) for q, k, _ in operands]
        parts = [softmax_columns(s) for s in scores]
        results = [
            dot_l(v, p.astype(BF16)) * (1.0 / total)
            for (_, _, v), (p, total, _) in zip(operands, parts)
        ]
        lses = [lse for _, _, lse in parts]
        for h, o in enumerate(results):
            o = o.T.astype(BF16)
            to = h * message + g * part
            for n in range(owners):
                out_refs[n][to : to + part, :] = o[n * part : (n + 1) * part]
        stats.append(jnp.concatenate(lses + lses, 0))
    upper = lax.broadcasted_iota(jnp.int32, (8, 128), 0) < HEADS
    blank = [jnp.zeros((8, 128 - message), F32)] if message < 128 else []
    for n in range(owners):
        x = jnp.concatenate([s[:, n * part : (n + 1) * part] for s in stats] + blank, 1)
        hi = x.astype(BF16).astype(F32)
        mid = (x - hi).astype(BF16).astype(F32)
        lo = x - hi - mid
        tail = jnp.concatenate([jnp.where(upper, hi, lo), jnp.where(upper, mid, 0.0)], 0)
        to = HEADS * message
        out_refs[n][to : to + 16, :] = tail.astype(BF16)


def column_part(pos, across, halves, weights, near, owners, after):
    tokens, width = across.shape
    message = tokens // (owners - NEAR)
    shapes = [shape((HEADS * message + 16, DH))] * owners
    scratch = [pltpu.VMEM((owners, message, width), BF16)] * 3
    middle = tokens // 2
    diagonal = [swap(x, 1) for x in (across[:middle], across[middle:])]
    args = (pos, across, *diagonal, *halves, *weights, *near)
    return call(column_kernel, "column_part", 0, shapes, args, after, scratch)


def mix_kernel(share, pos_ref, *refs):
    count = 2 * len(CHUNKS)
    local_refs, col_refs, (own_ref, send_ref, mixed) = refs[:count], refs[count:-3], refs[-3:]
    per_owner = mixed.shape[1] // len(share)
    base = 0
    for chunk, loc_ref, lse_ref in zip(CHUNKS, local_refs[::2], local_refs[1::2]):
        message = loc_ref.shape[1]
        size = HEADS * message + 16
        tiles = [jnp.zeros((8, 128), F32)] * 16
        for k, col_ref in zip(share, col_refs):
            tail = col_ref[base + HEADS * message : base + size, :].astype(F32)
            tiles[k] = tail[:8] + tail[8:]
        turned = jnp.concatenate(tiles, 0).T[:message]
        col_lse = turned + pltpu.roll(turned, 124, 1)
        loc_lse = lse_ref[...]
        top = jnp.maximum(col_lse, loc_lse)
        w_col = jnp.exp2(col_lse - top)
        w_loc = jnp.exp2(loc_lse - top)
        scale = 1.0 / (w_col + w_loc)
        w_col = w_col * scale
        w_loc = w_loc * scale
        for n, (k, col_ref) in enumerate(zip(share, col_refs)):
            d = pos_ref[0] ^ k
            for h in range(HEADS):
                cols = slice(h * DH, (h + 1) * DH)
                at = slice(8 * k + h, 8 * k + h + 1)
                col = col_ref[base + h * message : base + (h + 1) * message, :].astype(F32)
                both = loc_ref[d, :, cols] * w_loc[:, at] + col * w_col[:, at]
                for r in range(ROWS):
                    for m, g in enumerate(chunk):
                        start = (m * ROWS + r) * SUB
                        to = n * per_owner + g * SUB
                        mixed[r, to : to + SUB, cols] = both[start : start + SUB]
        base += size
    core = pos_ref[1]
    for x in range(2):
        own_ref[x] = mixed[2 * x + core].astype(BF16)
        send_ref[x] = mixed[2 * x + 1 - core].astype(BF16)


def mix(pos, share, columns, locals_, after):
    owners, _, width = locals_[0][0].shape
    tokens = len(share) * STRIDE // owners
    shapes = [shape((2, tokens, width))] * 2
    scratch = [pltpu.VMEM((ROWS, tokens, width), F32)]
    args = (pos, *[x for pair in locals_ for x in pair], *columns)
    return call(functools.partial(mix_kernel, share), "mix", 2, shapes, args, after, scratch)


def out_kernel(here, pos_ref, a_ref, b_ref, wa_ref, wb_ref, out_ref):
    side = pos_ref[2] if here else 1 - pos_ref[2]
    a, b = a_ref[side], b_ref[side]
    tile = 512
    for n in range(0, out_ref.shape[1], tile):
        at = slice(n, n + tile)
        total = dot(a, wa_ref[:, at]) + dot(b, wb_ref[:, at])
        out_ref[:, at] = total.astype(out_ref.dtype)


def out_project(pos, here, own, other, w_own, w_other):
    dims = shape((own.shape[1], w_own.shape[1]), F32 if here else BF16)
    body = functools.partial(out_kernel, here)
    return call(body, "out_project", 2, dims, (pos, own, other, w_own, w_other))


def join_kernel(share, pos_ref, keep, got, *rest):
    out_hbm, joined, sems = rest[-3:]
    span = keep.shape[0] // len(share)
    joined[...] = (keep[...] + got[...].astype(F32)).astype(BF16)
    copies = []
    for n, k in enumerate(share):
        to = pl.ds(pl.multiple_of((pos_ref[0] ^ k) * span, span), span)
        rows = slice(n * span, (n + 1) * span)
        copies.append(pltpu.make_async_copy(joined.at[rows], out_hbm.at[to], sems.at[n]))
    for c in copies:
        c.start()
    for c in copies:
        c.wait()


def join(pos, share, keep, got, earlier):
    return pl.pallas_call(
        functools.partial(join_kernel, share),
        in_specs=[IN_SMEM, IN_VMEM, IN_VMEM] + [ANYWHERE] * len(earlier),
        out_specs=ANYWHERE,
        out_shape=shape((STRIDE, keep.shape[1])),
        input_output_aliases={3: 0} if earlier else {},
        scratch_shapes=[pltpu.VMEM(keep.shape, BF16), pltpu.SemaphoreType.DMA((len(share),))],
        compiler_params=pltpu.CompilerParams(vmem_limit_bytes=16 * MIB),
        cost_estimate=pl.CostEstimate(flops=int(1.1e9), bytes_accessed=0, transcendentals=0),
        name="join",
    )(pos, keep, got, *earlier)


def swap(value, distance):
    return lax.ppermute(value, "head", [(i, i ^ distance) for i in range(4)])


def exchange(messages):
    peers = lax.axis_size("seq")

    def move(value, k):
        return lax.ppermute(value, "seq", [(i, i ^ k) for i in range(peers)]) if k else value

    return [move(m, k) for k, m in enumerate(messages)]


def chunked(tokens, w_query, w_key, w_value, w_out):
    owners = lax.axis_size("seq")
    head = lax.axis_index("head")
    block = lax.axis_index("seq")
    order = jnp.bitwise_xor(jnp.arange(4, dtype=jnp.int32), head.astype(jnp.int32))
    pos = jnp.stack([block, head % 2, head // 2]).astype(jnp.int32)
    rows, width = tokens.shape

    across = swap(tokens, 2)
    block_tokens, sent = pack(pos, tokens, owners)
    messages = exchange(sent)
    near_own = jnp.concatenate(messages[:NEAR], 0)
    near_core, near_across = swap(near_own, 1), swap(near_own, 2)
    far_own = jnp.concatenate(messages[NEAR:], 0)
    far_core, far_across = swap(far_own, 1), swap(far_own, 2)
    *weights, w_own = stage(order, (w_query, w_key, w_value, w_out), messages[1])
    w_other = swap(w_own, 1)
    block_core = swap(fence(block_tokens, near_own, far_own), 1)
    across = fence(across, near_across, far_own)
    pieces = (block_tokens, block_core, across, swap(across, 1))
    own_halo = call(
        halo_kernel, "project_halo", 1.5, shape((2 * STRIDE, width)), (*pieces, *weights[1:])
    )
    halo = lax.ppermute(own_halo, "seq", [(i, i + 1) for i in range(owners - 1)])
    q = call(
        query_kernel,
        "project_query",
        0,
        shape((rows, width)),
        (*pieces, weights[0]),
        (far_own,),
    )
    near = call(
        near_kernel,
        "project_near",
        0,
        [shape(near_own.shape)] * 3,
        (near_own, near_core, near_across, swap(near_across, 1), *weights),
        (q,),
    )
    far_half = half_sums(far_own, far_core, weights, (near[0],))
    far_across = fence(far_across, near[0])
    columns = column_part(pos, far_across, far_half, weights, near, owners, (w_other,))
    k, v = call(
        key_kernel,
        "project_key",
        0,
        [shape((rows, width))] * 2,
        (*pieces, *weights[1:], own_halo),
        (columns[0],),
    )
    locals_ = local_part(pos, q, k, v, halo, owners, (columns[0],))
    columns = list(columns)
    columns[1] = fence(columns[1], halo)
    columns = exchange(columns)
    sums, after = [], ()
    for share in SHARES:
        own, send = mix(pos, share, [columns[n] for n in share], locals_, after)
        other = swap(send, 1)
        out = out_project(pos, False, own, other, w_own, w_other)
        keep = out_project(pos, True, own, other, w_own, w_other)
        sums.append((keep, swap(out, 2)))
        after = (out,)
    result = ()
    for share, (keep, got) in zip(SHARES, sums):
        result = (join(pos, share, keep, got, result),)
    return result[0]


def from_behind(value, axis, by):
    peers = lax.axis_size(axis)
    pairs = [(i, i + by) for i in range(peers) if 0 <= i + by < peers]
    return lax.ppermute(value, axis, pairs)


def general(tokens, w_query, w_key, w_value, w_out):
    tok_rows = tokens.shape[0]
    head_width = w_query.shape[1]
    head_count = head_width // DH
    score_scale = DH ** (-0.5)
    shard_piece = lax.all_gather(tokens, "head", axis=1, tiled=True)
    query_full, key_full, value_full = tuple(
        (
            jnp.dot(shard_piece, weight, preferred_element_type=jnp.float32)
            for weight in (w_query, w_key, w_value)
        )
    )
    query = query_full.astype(jnp.bfloat16).reshape(tok_rows, head_count, DH)
    key_heads = key_full.astype(jnp.bfloat16).reshape(tok_rows, head_count, DH)
    value_heads = value_full.astype(jnp.bfloat16).reshape(tok_rows, head_count, DH)
    prev_keys, prev_values = from_behind((key_heads[-STRIDE:], value_heads[-STRIDE:]), "seq", 1)
    blocks = tok_rows // STRIDE
    extended_keys = jnp.concatenate([prev_keys, key_heads], 0)
    extended_values = jnp.concatenate([prev_values, value_heads], 0)
    window_keys = jnp.concatenate(
        [
            extended_keys[:tok_rows].reshape(blocks, STRIDE, head_count, DH),
            extended_keys[STRIDE:].reshape(blocks, STRIDE, head_count, DH),
        ],
        1,
    )
    window_values = jnp.concatenate(
        [
            extended_values[:tok_rows].reshape(blocks, STRIDE, head_count, DH),
            extended_values[STRIDE:].reshape(blocks, STRIDE, head_count, DH),
        ],
        1,
    )
    query_blocks = query.reshape(blocks, STRIDE, head_count, DH)
    scores = (
        jnp.einsum("bthd,buhd->bhtu", query_blocks, window_keys, preferred_element_type=jnp.float32)
        * score_scale
    )
    first_position = lax.axis_index("seq") * tok_rows
    block_index = jnp.arange(blocks)[:, None, None, None]
    query_index = jnp.arange(STRIDE)[None, None, :, None]
    key_index = jnp.arange(2 * STRIDE)[None, None, None, :]
    allowed = (
        (key_index > query_index)
        & (key_index <= query_index + STRIDE)
        & (first_position + block_index * STRIDE + key_index - STRIDE >= 0)
    )
    local_top = jnp.max(jnp.where(allowed, scores, -1e30), axis=-1)
    local_weights = jnp.where(allowed, jnp.exp(scores - local_top[..., None]), 0.0)
    local_total = jnp.sum(local_weights, axis=-1)
    local_out = jnp.einsum(
        "bhtu,buhd->bthd",
        local_weights.astype(jnp.bfloat16),
        window_values,
        preferred_element_type=jnp.float32,
    )
    local_out = local_out.reshape(tok_rows, head_count, DH)
    local_top = local_top.transpose(0, 2, 1).reshape(tok_rows, head_count)
    local_total = local_total.transpose(0, 2, 1).reshape(tok_rows, head_count)
    row_count = tok_rows // STRIDE
    query_class = lax.all_to_all(
        query.reshape(row_count, STRIDE, head_count, DH),
        "seq",
        split_axis=1,
        concat_axis=0,
        tiled=True,
    )
    key_class = lax.all_to_all(
        key_heads.reshape(row_count, STRIDE, head_count, DH),
        "seq",
        split_axis=1,
        concat_axis=0,
        tiled=True,
    )
    value_class = lax.all_to_all(
        value_heads.reshape(row_count, STRIDE, head_count, DH),
        "seq",
        split_axis=1,
        concat_axis=0,
        tiled=True,
    )
    row_total = query_class.shape[0]
    class_scores = (
        jnp.einsum("rchd,schd->chrs", query_class, key_class, preferred_element_type=jnp.float32)
        * score_scale
    )
    earlier = (
        jnp.arange(row_total)[None, None, :, None] > jnp.arange(row_total)[None, None, None, :]
    )
    class_top = jnp.max(jnp.where(earlier, class_scores, -1e30), axis=-1)
    class_weights = jnp.where(earlier, jnp.exp(class_scores - class_top[..., None]), 0.0)
    class_total = jnp.sum(class_weights, axis=-1)
    summed = jnp.einsum(
        "chrs,schd->rchd",
        class_weights.astype(jnp.bfloat16),
        value_class,
        preferred_element_type=jnp.float32,
    )
    floor_total = jnp.maximum(class_total, 1.0).transpose(2, 0, 1)
    class_out = (summed / floor_total[..., None]).astype(jnp.bfloat16)
    class_top_rows = class_top.transpose(2, 0, 1)
    class_total_rows = class_total.transpose(2, 0, 1)
    column_out = class_out
    column_top = class_top_rows
    column_total = class_total_rows
    column_out, column_top, column_total = (
        lax.all_to_all(column_out, "seq", split_axis=0, concat_axis=1, tiled=True),
        lax.all_to_all(
            column_top.astype(jnp.bfloat16), "seq", split_axis=0, concat_axis=1, tiled=True
        ).astype(column_top.dtype),
        lax.all_to_all(
            column_total.astype(jnp.bfloat16), "seq", split_axis=0, concat_axis=1, tiled=True
        ).astype(column_total.dtype),
    )
    column_out = column_out.reshape(tok_rows, head_count, DH)
    column_top = column_top.reshape(tok_rows, head_count)
    column_total = column_total.reshape(tok_rows, head_count)
    top_score = jnp.maximum(local_top, column_top)
    local_weight = jnp.exp(local_top - top_score)
    column_weight = column_total * jnp.exp(column_top - top_score)
    denominator = local_total * local_weight + column_weight
    mixed = (
        local_out * local_weight[..., None]
        + column_out.astype(jnp.float32) * column_weight[..., None]
    ) / denominator[..., None]
    mixed = mixed.astype(jnp.bfloat16).reshape(tok_rows, head_width)
    return lax.psum_scatter(
        jnp.dot(mixed, w_out, preferred_element_type=jnp.float32).astype(jnp.bfloat16),
        "head",
        scatter_dimension=0,
        tiled=True,
    )


def shards(tokens, w_query, w_key, w_value, w_out):
    rows, width = w_query.shape
    fits = (
        lax.axis_size("seq") == PEERS
        and lax.axis_size("head") == 4
        and tokens.shape == (ROWS * STRIDE, HEADS * DH)
        and (rows, width) == (4 * HEADS * DH, HEADS * DH)
    )
    plan = chunked if fits else general
    return plan(tokens, w_query, w_key, w_value, w_out)


def solution(mesh):
    in_specs = (
        P("seq", "head"),
        P(None, "head"),
        P(None, "head"),
        P(None, "head"),
        P("head", None),
    )
    out_specs = P(("seq", "head"), None)
    return jax.shard_map(shards, mesh=mesh, in_specs=in_specs, out_specs=out_specs, check_vma=False)
```

```python
import functools

import jax
import jax.numpy as jnp
from jax import lax
from jax.experimental import pallas as pl
from jax.experimental.pallas import tpu as pltpu
from jax.sharding import PartitionSpec as P

DH = 128
STRIDE = 256
HEADS = 4
ROWS = 4
SUB = 8
CHUNKS = ((0, 1, 2, 3),)
NEAR = 4
PEERS = 8
SHARES = ((4, 5, 1, 2, 3, 0), (6, 7))
SCALE2 = DH ** (-0.5) * 1.4426950408889634
FLOOR = -1e29
MIB = 1024 * 1024
F32 = jnp.float32
BF16 = jnp.bfloat16


ANYWHERE = pl.BlockSpec(memory_space=pl.ANY)
IN_VMEM = pl.BlockSpec(memory_space=pltpu.VMEM)
IN_SMEM = pl.BlockSpec(memory_space=pltpu.SMEM)


def call(body, name, micros, out_shape, args, after=(), scratch=(), mib=24):
    specs = [IN_SMEM if x.dtype == jnp.int32 else IN_VMEM for x in args]
    extra = len(after)

    def run(*refs):
        n = len(args)
        body(*refs[:n], *refs[n + extra :])

    return pl.pallas_call(
        run,
        in_specs=specs + [ANYWHERE] * extra,
        out_specs=jax.tree.map(lambda _: IN_VMEM, out_shape),
        out_shape=out_shape,
        scratch_shapes=list(scratch),
        compiler_params=pltpu.CompilerParams(vmem_limit_bytes=mib * MIB),
        cost_estimate=pl.CostEstimate(
            flops=int(micros * 1.1e9), bytes_accessed=0, transcendentals=0
        ),
        name=name,
    )(*args, *after)


def fence(value, *after):
    return pl.pallas_call(
        lambda *refs: None,
        in_specs=[ANYWHERE] * (1 + len(after)),
        out_specs=ANYWHERE,
        out_shape=jax.ShapeDtypeStruct(value.shape, value.dtype),
        input_output_aliases={0: 0},
        compiler_params=pltpu.CompilerParams(vmem_limit_bytes=MIB),
        cost_estimate=pl.CostEstimate(flops=0, bytes_accessed=0, transcendentals=0),
        name="fence",
    )(value, *after)


def in_hbm(value):
    return pltpu.with_memory_space_constraint(value, pltpu.HBM)


def shape(dims, dtype=BF16):
    return jax.ShapeDtypeStruct(tuple(dims), dtype)


def dot(a, b):
    return jnp.dot(a, b, preferred_element_type=F32)


def dot_t(a, b):
    return lax.dot_general(a, b, (((1,), (1,)), ((), ())), preferred_element_type=F32)


def dot_l(a, b):
    return lax.dot_general(a, b, (((0,), (0,)), ((), ())), preferred_element_type=F32)


def pack_kernel(pos_ref, tok_hbm, tok_ref, *rest):
    out_refs, sems = rest[:-1], rest[-1]
    spans = [slice(r * STRIDE, (r + 1) * STRIDE) for r in range(ROWS)]
    copies = [
        pltpu.make_async_copy(tok_hbm.at[at], tok_ref.at[at], sems.at[r])
        for r, at in enumerate(spans)
    ]
    for c in copies:
        c.start()
    for c in copies:
        c.wait()
    per_owner = STRIDE // len(out_refs)
    part = ROWS * SUB
    for k, out_ref in enumerate(out_refs):
        d = pos_ref[0] ^ k
        rows = [
            tok_ref[pl.ds(pl.multiple_of(r * STRIDE + d * per_owner, per_owner), per_owner), :]
            for r in range(ROWS)
        ]
        rows = [x.astype(F32) for x in rows]
        for g in range(per_owner // SUB):
            piece = jnp.concatenate([x[g * SUB : (g + 1) * SUB] for x in rows], 0)
            out_ref[g * part : (g + 1) * part, :] = piece.astype(BF16)


def pack(pos, tokens, owners):
    message = shape((tokens.shape[0] // owners, tokens.shape[1]))
    outs = pl.pallas_call(
        pack_kernel,
        in_specs=[IN_SMEM, ANYWHERE],
        out_specs=[IN_VMEM] * (1 + owners),
        out_shape=[shape(tokens.shape)] + [message] * owners,
        scratch_shapes=[pltpu.SemaphoreType.DMA((ROWS,))],
        compiler_params=pltpu.CompilerParams(vmem_limit_bytes=8 * MIB),
        cost_estimate=pl.CostEstimate(flops=0, bytes_accessed=2 * MIB, transcendentals=0),
        name="pack_tokens",
    )(pos, in_hbm(tokens))
    return outs[0], outs[1:]


def stage_kernel(order_ref, wq, wk, wv, wo, after, oq, ok, ov, oo, sems):
    copies = []
    for w, o in ((wq, oq), (wk, ok), (wv, ov), (wo, oo)):
        part = w.shape[0] // 4
        for p in range(4):
            place = p if w is wo else order_ref[p]
            rows = pl.ds(pl.multiple_of(place * part, part), part)
            to = slice(p * part, (p + 1) * part)
            sem = sems.at[len(copies)]
            copies.append(pltpu.make_async_copy(w.at[rows], o.at[to], sem))
    for c in copies:
        c.start()
    for c in copies:
        c.wait()


def stage(order, weights, after):
    return pl.pallas_call(
        stage_kernel,
        in_specs=[IN_SMEM] + [ANYWHERE] * 5,
        out_specs=[IN_VMEM] * 4,
        out_shape=[shape(w.shape) for w in weights],
        scratch_shapes=[pltpu.SemaphoreType.DMA((16,))],
        compiler_params=pltpu.CompilerParams(vmem_limit_bytes=16 * MIB),
        cost_estimate=pl.CostEstimate(flops=0, bytes_accessed=0, transcendentals=0),
        name="stage_weights",
    )(order, *weights, after)


def gathered(x_refs, at, w_ref):
    width = x_refs[0].shape[1]
    total = None
    for p, x_ref in enumerate(x_refs):
        term = dot(x_ref[at, :], w_ref[p * width : (p + 1) * width, :])
        total = term if total is None else total + term
    return total.astype(BF16)


def half_kernel(x0, x1, wq, wk, wv, *outs):
    width = x0.shape[1]
    for w, out in zip((wq, wk, wv), outs):
        out[...] = dot(x0[...], w[:width, :]) + dot(x1[...], w[width : 2 * width, :])


def half_sums(own, core, weights, after):
    shapes = [shape(own.shape, F32)] * 3
    return call(half_kernel, "half_sums", 0, shapes, (own, core, *weights), after)


def near_kernel(x0, x1, x2, x3, wq, wk, wv, *outs):
    everything = slice(0, x0.shape[0])
    for w, out in zip((wq, wk, wv), outs):
        out[...] = gathered((x0, x1, x2, x3), everything, w)


def halo_kernel(x0, x1, x2, x3, wk, wv, out_ref):
    rows = x0.shape[0]
    at = slice(rows - STRIDE, rows)
    out_ref[:STRIDE, :] = gathered((x0, x1, x2, x3), at, wk)
    out_ref[STRIDE:, :] = gathered((x0, x1, x2, x3), at, wv)


def query_kernel(x0, x1, x2, x3, wq, q_ref):
    q_ref[...] = gathered((x0, x1, x2, x3), slice(0, x0.shape[0]), wq)


def key_kernel(x0, x1, x2, x3, wk, wv, halo, k_ref, v_ref):
    upto = x0.shape[0] - STRIDE
    k_ref[upto:, :] = halo[:STRIDE, :]
    v_ref[upto:, :] = halo[STRIDE:, :]
    for w, out in ((wk, k_ref), (wv, v_ref)):
        out[:upto, :] = gathered((x0, x1, x2, x3), slice(0, upto), w)


def softmax_columns(s):
    m = jnp.maximum(jnp.max(s, 0, keepdims=True), FLOOR)
    p = jnp.exp2((s - m) * SCALE2)
    total = jnp.maximum(jnp.sum(p, 0, keepdims=True), 1.0)
    return p, total, m * SCALE2 + jnp.log2(total)


def local_kernel(pos_ref, q_ref, k_ref, v_ref, halo_ref, *outs):
    out_refs, lse_refs = outs[: len(CHUNKS)], outs[len(CHUNKS) :]
    owners = out_refs[0].shape[0]
    groups = STRIDE // owners // SUB
    block = pos_ref[0]
    u = lax.broadcasted_iota(jnp.int32, (STRIDE, STRIDE), 0)
    t = lax.broadcasted_iota(jnp.int32, (STRIDE, STRIDE), 1)
    current = u <= t
    low = jnp.where(block == 0, -1e30, 0.0).astype(F32)
    for r in range(ROWS):
        lses = []
        here = slice(r * STRIDE, (r + 1) * STRIDE)
        back = slice((r - 1) * STRIDE, r * STRIDE)
        heads = [slice(h * DH, (h + 1) * DH) for h in range(HEADS)]
        scores = []
        for cols in heads:
            q = q_ref[here, cols]
            s_prev = dot_t(k_ref[back, cols] if r else halo_ref[:STRIDE, cols], q)
            if r == 0:
                s_prev = s_prev + low
            scores.append(jnp.where(current, dot_t(k_ref[here, cols], q), s_prev))
        parts = []
        for p, total, lse in [softmax_columns(s) for s in scores]:
            now = jnp.where(current, p, 0.0).astype(BF16)
            before = jnp.where(current, 0.0, p).astype(BF16)
            parts.append((now, before, 1.0 / total))
            lses.append(lse)
        results = []
        for cols, (now, before, share) in zip(heads, parts):
            v_prev = v_ref[back, cols] if r else halo_ref[STRIDE:, cols]
            results.append((dot_l(v_ref[here, cols], now) + dot_l(v_prev, before)) * share)
        for cols, o in zip(heads, results):
            o = o.T
            for d in range(owners):
                for chunk, out_ref in zip(CHUNKS, out_refs):
                    for n, g in enumerate(chunk):
                        at = (d * groups + g) * SUB
                        to = (n * ROWS + r) * SUB
                        out_ref[d, to : to + SUB, cols] = o[at : at + SUB]
        lses.append(jnp.zeros((128 - HEADS, STRIDE), F32))
        turned = jnp.concatenate(lses, 0).T
        for chunk, lse_ref in zip(CHUNKS, lse_refs):
            for n, g in enumerate(chunk):
                total = None
                for d in range(owners):
                    at = (d * groups + g) * SUB
                    moved = pltpu.roll(turned[at : at + SUB], 8 * (block ^ d), 1)
                    total = moved if total is None else total + moved
                to = (n * ROWS + r) * SUB
                lse_ref[to : to + SUB, :] = total


def local_part(pos, q, k, v, halo, owners, after):
    rows, width = q.shape
    sizes = [len(chunk) * ROWS * SUB for chunk in CHUNKS]
    shapes = [shape((owners, m, width), F32) for m in sizes] + [shape((m, 128), F32) for m in sizes]
    outs = call(local_kernel, "local_part", 5, shapes, (pos, q, k, v, halo), after)
    return list(zip(outs[: len(sizes)], outs[len(sizes) :]))


def column_kernel(pos_ref, x2, x3a, x3b, hq, hk, hv, wq, wk, wv, nq, nk, nv, *rest):
    out_refs, scratch = rest[:-3], rest[-3:]
    owners, message, width = scratch[0].shape
    groups = message // (ROWS * SUB)
    for h, w, near, a in zip((hq, hk, hv), (wq, wk, wv), (nq, nk, nv), scratch):
        total = h[...] + dot(x2[...], w[2 * width : 3 * width, :])
        diagonal = [dot(x[...], w[3 * width :, :]) for x in (x3a, x3b)]
        total = total + jnp.concatenate(diagonal, 0)
        a[:NEAR] = near[...].reshape(NEAR, message, width)
        a[NEAR:] = total.astype(BF16).reshape(owners - NEAR, message, width)
    part = ROWS * SUB
    size = owners * part

    def row_and_class(dim):
        i = lax.broadcasted_iota(jnp.int32, (size, size), dim)
        return ((i // part) ^ pos_ref[0]) * ROWS + (i % part) // SUB, i % SUB

    (row_j, class_j), (row_i, class_i) = row_and_class(0), row_and_class(1)
    earlier = jnp.logical_and(class_i == class_j, row_i > row_j)
    stats = []
    for g in range(groups):
        at = slice(g * part, (g + 1) * part)
        heads = [slice(h * DH, (h + 1) * DH) for h in range(HEADS)]
        operands = [[a[:, at, cols].reshape(size, DH) for a in scratch] for cols in heads]
        scores = [jnp.where(earlier, dot_t(k, q), -1e30) for q, k, _ in operands]
        parts = [softmax_columns(s) for s in scores]
        results = [
            dot_l(v, p.astype(BF16)) * (1.0 / total)
            for (_, _, v), (p, total, _) in zip(operands, parts)
        ]
        lses = [lse for _, _, lse in parts]
        for h, o in enumerate(results):
            o = o.T.astype(BF16)
            to = h * message + g * part
            for n in range(owners):
                out_refs[n][to : to + part, :] = o[n * part : (n + 1) * part]
        stats.append(jnp.concatenate(lses + lses, 0))
    upper = lax.broadcasted_iota(jnp.int32, (8, 128), 0) < HEADS
    blank = [jnp.zeros((8, 128 - message), F32)] if message < 128 else []
    for n in range(owners):
        x = jnp.concatenate([s[:, n * part : (n + 1) * part] for s in stats] + blank, 1)
        hi = x.astype(BF16).astype(F32)
        mid = (x - hi).astype(BF16).astype(F32)
        lo = x - hi - mid
        tail = jnp.concatenate([jnp.where(upper, hi, lo), jnp.where(upper, mid, 0.0)], 0)
        to = HEADS * message
        out_refs[n][to : to + 16, :] = tail.astype(BF16)


def column_part(pos, across, halves, weights, near, owners, after):
    tokens, width = across.shape
    message = tokens // (owners - NEAR)
    shapes = [shape((HEADS * message + 16, DH))] * owners
    scratch = [pltpu.VMEM((owners, message, width), BF16)] * 3
    middle = tokens // 2
    diagonal = [swap(x, 1) for x in (across[:middle], across[middle:])]
    args = (pos, across, *diagonal, *halves, *weights, *near)
    return call(column_kernel, "column_part", 0, shapes, args, after, scratch)


def mix_kernel(share, pos_ref, *refs):
    count = 2 * len(CHUNKS)
    local_refs, col_refs, (own_ref, send_ref, mixed) = refs[:count], refs[count:-3], refs[-3:]
    per_owner = mixed.shape[1] // len(share)
    base = 0
    for chunk, loc_ref, lse_ref in zip(CHUNKS, local_refs[::2], local_refs[1::2]):
        message = loc_ref.shape[1]
        size = HEADS * message + 16
        tiles = [jnp.zeros((8, 128), F32)] * 16
        for k, col_ref in zip(share, col_refs):
            tail = col_ref[base + HEADS * message : base + size, :].astype(F32)
            tiles[k] = tail[:8] + tail[8:]
        turned = jnp.concatenate(tiles, 0).T[:message]
        col_lse = turned + pltpu.roll(turned, 124, 1)
        loc_lse = lse_ref[...]
        top = jnp.maximum(col_lse, loc_lse)
        w_col = jnp.exp2(col_lse - top)
        w_loc = jnp.exp2(loc_lse - top)
        scale = 1.0 / (w_col + w_loc)
        w_col = w_col * scale
        w_loc = w_loc * scale
        for n, (k, col_ref) in enumerate(zip(share, col_refs)):
            d = pos_ref[0] ^ k
            for h in range(HEADS):
                cols = slice(h * DH, (h + 1) * DH)
                at = slice(8 * k + h, 8 * k + h + 1)
                col = col_ref[base + h * message : base + (h + 1) * message, :].astype(F32)
                both = loc_ref[d, :, cols] * w_loc[:, at] + col * w_col[:, at]
                for r in range(ROWS):
                    for m, g in enumerate(chunk):
                        start = (m * ROWS + r) * SUB
                        to = n * per_owner + g * SUB
                        mixed[r, to : to + SUB, cols] = both[start : start + SUB]
        base += size
    core = pos_ref[1]
    for x in range(2):
        own_ref[x] = mixed[2 * x + core].astype(BF16)
        send_ref[x] = mixed[2 * x + 1 - core].astype(BF16)


def mix(pos, share, columns, locals_, after):
    owners, _, width = locals_[0][0].shape
    tokens = len(share) * STRIDE // owners
    shapes = [shape((2, tokens, width))] * 2
    scratch = [pltpu.VMEM((ROWS, tokens, width), F32)]
    args = (pos, *[x for pair in locals_ for x in pair], *columns)
    return call(functools.partial(mix_kernel, share), "mix", 2, shapes, args, after, scratch)


def out_kernel(here, pos_ref, a_ref, b_ref, wa_ref, wb_ref, out_ref):
    side = pos_ref[2] if here else 1 - pos_ref[2]
    a, b = a_ref[side], b_ref[side]
    tile = 512
    for n in range(0, out_ref.shape[1], tile):
        at = slice(n, n + tile)
        total = dot(a, wa_ref[:, at]) + dot(b, wb_ref[:, at])
        out_ref[:, at] = total.astype(out_ref.dtype)


def out_project(pos, here, own, other, w_own, w_other):
    dims = shape((own.shape[1], w_own.shape[1]), F32 if here else BF16)
    body = functools.partial(out_kernel, here)
    return call(body, "out_project", 2, dims, (pos, own, other, w_own, w_other))


def join_kernel(share, pos_ref, keep, got, *rest):
    out_hbm, joined, sems = rest[-3:]
    span = keep.shape[0] // len(share)
    joined[...] = (keep[...] + got[...].astype(F32)).astype(BF16)
    copies = []
    for n, k in enumerate(share):
        to = pl.ds(pl.multiple_of((pos_ref[0] ^ k) * span, span), span)
        rows = slice(n * span, (n + 1) * span)
        copies.append(pltpu.make_async_copy(joined.at[rows], out_hbm.at[to], sems.at[n]))
    for c in copies:
        c.start()
    for c in copies:
        c.wait()


def join(pos, share, keep, got, earlier):
    return pl.pallas_call(
        functools.partial(join_kernel, share),
        in_specs=[IN_SMEM, IN_VMEM, IN_VMEM] + [ANYWHERE] * len(earlier),
        out_specs=ANYWHERE,
        out_shape=shape((STRIDE, keep.shape[1])),
        input_output_aliases={3: 0} if earlier else {},
        scratch_shapes=[pltpu.VMEM(keep.shape, BF16), pltpu.SemaphoreType.DMA((len(share),))],
        compiler_params=pltpu.CompilerParams(vmem_limit_bytes=16 * MIB),
        cost_estimate=pl.CostEstimate(flops=int(1.1e9), bytes_accessed=0, transcendentals=0),
        name="join",
    )(pos, keep, got, *earlier)


def swap(value, distance):
    return lax.ppermute(value, "head", [(i, i ^ distance) for i in range(4)])


def exchange(messages):
    peers = lax.axis_size("seq")

    def move(value, k):
        return lax.ppermute(value, "seq", [(i, i ^ k) for i in range(peers)]) if k else value

    return [move(m, k) for k, m in enumerate(messages)]


def chunked(tokens, w_query, w_key, w_value, w_out):
    owners = lax.axis_size("seq")
    head = lax.axis_index("head")
    block = lax.axis_index("seq")
    order = jnp.bitwise_xor(jnp.arange(4, dtype=jnp.int32), head.astype(jnp.int32))
    pos = jnp.stack([block, head % 2, head // 2]).astype(jnp.int32)
    rows, width = tokens.shape

    across = swap(tokens, 2)
    block_tokens, sent = pack(pos, tokens, owners)
    messages = exchange(sent)
    near_own = jnp.concatenate(messages[:NEAR], 0)
    near_core, near_across = swap(near_own, 1), swap(near_own, 2)
    far_own = jnp.concatenate(messages[NEAR:], 0)
    far_core, far_across = swap(far_own, 1), swap(far_own, 2)
    *weights, w_own = stage(order, (w_query, w_key, w_value, w_out), messages[1])
    w_other = swap(w_own, 1)
    block_core = swap(fence(block_tokens, near_own, far_own), 1)
    across = fence(across, near_across, far_own)
    pieces = (block_tokens, block_core, across, swap(across, 1))
    own_halo = call(
        halo_kernel, "project_halo", 1.5, shape((2 * STRIDE, width)), (*pieces, *weights[1:])
    )
    halo = lax.ppermute(own_halo, "seq", [(i, i + 1) for i in range(owners - 1)])
    q = call(
        query_kernel,
        "project_query",
        0,
        shape((rows, width)),
        (*pieces, weights[0]),
        (far_own,),
    )
    near = call(
        near_kernel,
        "project_near",
        0,
        [shape(near_own.shape)] * 3,
        (near_own, near_core, near_across, swap(near_across, 1), *weights),
        (q,),
    )
    far_half = half_sums(far_own, far_core, weights, (near[0],))
    far_across = fence(far_across, near[0])
    columns = column_part(pos, far_across, far_half, weights, near, owners, (w_other,))
    k, v = call(
        key_kernel,
        "project_key",
        0,
        [shape((rows, width))] * 2,
        (*pieces, *weights[1:], own_halo),
        (columns[0], halo),
    )
    locals_ = local_part(pos, q, k, v, halo, owners, (columns[0],))
    columns = list(columns)
    columns = exchange(columns)
    sums, after = [], ()
    for share in SHARES:
        own, send = mix(pos, share, [columns[n] for n in share], locals_, after)
        other = swap(send, 1)
        out = out_project(pos, False, own, other, w_own, w_other)
        keep = out_project(pos, True, own, other, w_own, w_other)
        sums.append((keep, swap(out, 2)))
        after = (out,)
    result = ()
    for share, (keep, got) in zip(SHARES, sums):
        result = (join(pos, share, keep, got, result),)
    return result[0]


def from_behind(value, axis, by):
    peers = lax.axis_size(axis)
    pairs = [(i, i + by) for i in range(peers) if 0 <= i + by < peers]
    return lax.ppermute(value, axis, pairs)


def general(tokens, w_query, w_key, w_value, w_out):
    tok_rows = tokens.shape[0]
    head_width = w_query.shape[1]
    head_count = head_width // DH
    score_scale = DH ** (-0.5)
    shard_piece = lax.all_gather(tokens, "head", axis=1, tiled=True)
    query_full, key_full, value_full = tuple(
        (
            jnp.dot(shard_piece, weight, preferred_element_type=jnp.float32)
            for weight in (w_query, w_key, w_value)
        )
    )
    query = query_full.astype(jnp.bfloat16).reshape(tok_rows, head_count, DH)
    key_heads = key_full.astype(jnp.bfloat16).reshape(tok_rows, head_count, DH)
    value_heads = value_full.astype(jnp.bfloat16).reshape(tok_rows, head_count, DH)
    prev_keys, prev_values = from_behind((key_heads[-STRIDE:], value_heads[-STRIDE:]), "seq", 1)
    blocks = tok_rows // STRIDE
    extended_keys = jnp.concatenate([prev_keys, key_heads], 0)
    extended_values = jnp.concatenate([prev_values, value_heads], 0)
    window_keys = jnp.concatenate(
        [
            extended_keys[:tok_rows].reshape(blocks, STRIDE, head_count, DH),
            extended_keys[STRIDE:].reshape(blocks, STRIDE, head_count, DH),
        ],
        1,
    )
    window_values = jnp.concatenate(
        [
            extended_values[:tok_rows].reshape(blocks, STRIDE, head_count, DH),
            extended_values[STRIDE:].reshape(blocks, STRIDE, head_count, DH),
        ],
        1,
    )
    query_blocks = query.reshape(blocks, STRIDE, head_count, DH)
    scores = (
        jnp.einsum("bthd,buhd->bhtu", query_blocks, window_keys, preferred_element_type=jnp.float32)
        * score_scale
    )
    first_position = lax.axis_index("seq") * tok_rows
    block_index = jnp.arange(blocks)[:, None, None, None]
    query_index = jnp.arange(STRIDE)[None, None, :, None]
    key_index = jnp.arange(2 * STRIDE)[None, None, None, :]
    allowed = (
        (key_index > query_index)
        & (key_index <= query_index + STRIDE)
        & (first_position + block_index * STRIDE + key_index - STRIDE >= 0)
    )
    local_top = jnp.max(jnp.where(allowed, scores, -1e30), axis=-1)
    local_weights = jnp.where(allowed, jnp.exp(scores - local_top[..., None]), 0.0)
    local_total = jnp.sum(local_weights, axis=-1)
    local_out = jnp.einsum(
        "bhtu,buhd->bthd",
        local_weights.astype(jnp.bfloat16),
        window_values,
        preferred_element_type=jnp.float32,
    )
    local_out = local_out.reshape(tok_rows, head_count, DH)
    local_top = local_top.transpose(0, 2, 1).reshape(tok_rows, head_count)
    local_total = local_total.transpose(0, 2, 1).reshape(tok_rows, head_count)
    row_count = tok_rows // STRIDE
    query_class = lax.all_to_all(
        query.reshape(row_count, STRIDE, head_count, DH),
        "seq",
        split_axis=1,
        concat_axis=0,
        tiled=True,
    )
    key_class = lax.all_to_all(
        key_heads.reshape(row_count, STRIDE, head_count, DH),
        "seq",
        split_axis=1,
        concat_axis=0,
        tiled=True,
    )
    value_class = lax.all_to_all(
        value_heads.reshape(row_count, STRIDE, head_count, DH),
        "seq",
        split_axis=1,
        concat_axis=0,
        tiled=True,
    )
    row_total = query_class.shape[0]
    class_scores = (
        jnp.einsum("rchd,schd->chrs", query_class, key_class, preferred_element_type=jnp.float32)
        * score_scale
    )
    earlier = (
        jnp.arange(row_total)[None, None, :, None] > jnp.arange(row_total)[None, None, None, :]
    )
    class_top = jnp.max(jnp.where(earlier, class_scores, -1e30), axis=-1)
    class_weights = jnp.where(earlier, jnp.exp(class_scores - class_top[..., None]), 0.0)
    class_total = jnp.sum(class_weights, axis=-1)
    summed = jnp.einsum(
        "chrs,schd->rchd",
        class_weights.astype(jnp.bfloat16),
        value_class,
        preferred_element_type=jnp.float32,
    )
    floor_total = jnp.maximum(class_total, 1.0).transpose(2, 0, 1)
    class_out = (summed / floor_total[..., None]).astype(jnp.bfloat16)
    class_top_rows = class_top.transpose(2, 0, 1)
    class_total_rows = class_total.transpose(2, 0, 1)
    column_out = class_out
    column_top = class_top_rows
    column_total = class_total_rows
    column_out, column_top, column_total = (
        lax.all_to_all(column_out, "seq", split_axis=0, concat_axis=1, tiled=True),
        lax.all_to_all(
            column_top.astype(jnp.bfloat16), "seq", split_axis=0, concat_axis=1, tiled=True
        ).astype(column_top.dtype),
        lax.all_to_all(
            column_total.astype(jnp.bfloat16), "seq", split_axis=0, concat_axis=1, tiled=True
        ).astype(column_total.dtype),
    )
    column_out = column_out.reshape(tok_rows, head_count, DH)
    column_top = column_top.reshape(tok_rows, head_count)
    column_total = column_total.reshape(tok_rows, head_count)
    top_score = jnp.maximum(local_top, column_top)
    local_weight = jnp.exp(local_top - top_score)
    column_weight = column_total * jnp.exp(column_top - top_score)
    denominator = local_total * local_weight + column_weight
    mixed = (
        local_out * local_weight[..., None]
        + column_out.astype(jnp.float32) * column_weight[..., None]
    ) / denominator[..., None]
    mixed = mixed.astype(jnp.bfloat16).reshape(tok_rows, head_width)
    return lax.psum_scatter(
        jnp.dot(mixed, w_out, preferred_element_type=jnp.float32).astype(jnp.bfloat16),
        "head",
        scatter_dimension=0,
        tiled=True,
    )


def shards(tokens, w_query, w_key, w_value, w_out):
    rows, width = w_query.shape
    fits = (
        lax.axis_size("seq") == PEERS
        and lax.axis_size("head") == 4
        and tokens.shape == (ROWS * STRIDE, HEADS * DH)
        and (rows, width) == (4 * HEADS * DH, HEADS * DH)
    )
    plan = chunked if fits else general
    return plan(tokens, w_query, w_key, w_value, w_out)


def solution(mesh):
    in_specs = (
        P("seq", "head"),
        P(None, "head"),
        P(None, "head"),
        P(None, "head"),
        P("head", None),
    )
    out_specs = P(("seq", "head"), None)
    return jax.shard_map(shards, mesh=mesh, in_specs=in_specs, out_specs=out_specs, check_vma=False)
```

```python
import functools

import jax
import jax.numpy as jnp
from jax import lax
from jax.experimental import pallas as pl
from jax.experimental.pallas import tpu as pltpu
from jax.sharding import PartitionSpec as P

DH = 128
STRIDE = 256
HEADS = 4
ROWS = 4
SUB = 8
CHUNKS = ((0, 1, 2, 3),)
NEAR = 4
PEERS = 8
SHARES = ((4, 5, 1, 2, 3, 0), (6, 7))
SCALE2 = DH ** (-0.5) * 1.4426950408889634
FLOOR = -1e29
MIB = 1024 * 1024
F32 = jnp.float32
BF16 = jnp.bfloat16


ANYWHERE = pl.BlockSpec(memory_space=pl.ANY)
IN_VMEM = pl.BlockSpec(memory_space=pltpu.VMEM)
IN_SMEM = pl.BlockSpec(memory_space=pltpu.SMEM)


def call(body, name, micros, out_shape, args, after=(), scratch=(), mib=24):
    specs = [IN_SMEM if x.dtype == jnp.int32 else IN_VMEM for x in args]
    extra = len(after)

    def run(*refs):
        n = len(args)
        body(*refs[:n], *refs[n + extra :])

    return pl.pallas_call(
        run,
        in_specs=specs + [ANYWHERE] * extra,
        out_specs=jax.tree.map(lambda _: IN_VMEM, out_shape),
        out_shape=out_shape,
        scratch_shapes=list(scratch),
        compiler_params=pltpu.CompilerParams(vmem_limit_bytes=mib * MIB),
        cost_estimate=pl.CostEstimate(
            flops=int(micros * 1.1e9), bytes_accessed=0, transcendentals=0
        ),
        name=name,
    )(*args, *after)


def fence(value, *after):
    return pl.pallas_call(
        lambda *refs: None,
        in_specs=[ANYWHERE] * (1 + len(after)),
        out_specs=ANYWHERE,
        out_shape=jax.ShapeDtypeStruct(value.shape, value.dtype),
        input_output_aliases={0: 0},
        compiler_params=pltpu.CompilerParams(vmem_limit_bytes=MIB),
        cost_estimate=pl.CostEstimate(flops=0, bytes_accessed=0, transcendentals=0),
        name="fence",
    )(value, *after)


def in_hbm(value):
    return pltpu.with_memory_space_constraint(value, pltpu.HBM)


def shape(dims, dtype=BF16):
    return jax.ShapeDtypeStruct(tuple(dims), dtype)


def dot(a, b):
    return jnp.dot(a, b, preferred_element_type=F32)


def dot_t(a, b):
    return lax.dot_general(a, b, (((1,), (1,)), ((), ())), preferred_element_type=F32)


def dot_l(a, b):
    return lax.dot_general(a, b, (((0,), (0,)), ((), ())), preferred_element_type=F32)


def pack_kernel(pos_ref, tok_hbm, tok_ref, *rest):
    out_refs, sems = rest[:-1], rest[-1]
    spans = [slice(r * STRIDE, (r + 1) * STRIDE) for r in range(ROWS)]
    copies = [
        pltpu.make_async_copy(tok_hbm.at[at], tok_ref.at[at], sems.at[r])
        for r, at in enumerate(spans)
    ]
    for c in copies:
        c.start()
    for c in copies:
        c.wait()
    per_owner = STRIDE // len(out_refs)
    part = ROWS * SUB
    for k, out_ref in enumerate(out_refs):
        d = pos_ref[0] ^ k
        rows = [
            tok_ref[pl.ds(pl.multiple_of(r * STRIDE + d * per_owner, per_owner), per_owner), :]
            for r in range(ROWS)
        ]
        rows = [x.astype(F32) for x in rows]
        for g in range(per_owner // SUB):
            piece = jnp.concatenate([x[g * SUB : (g + 1) * SUB] for x in rows], 0)
            out_ref[g * part : (g + 1) * part, :] = piece.astype(BF16)


def pack(pos, tokens, owners):
    message = shape((tokens.shape[0] // owners, tokens.shape[1]))
    outs = pl.pallas_call(
        pack_kernel,
        in_specs=[IN_SMEM, ANYWHERE],
        out_specs=[IN_VMEM] * (1 + owners),
        out_shape=[shape(tokens.shape)] + [message] * owners,
        scratch_shapes=[pltpu.SemaphoreType.DMA((ROWS,))],
        compiler_params=pltpu.CompilerParams(vmem_limit_bytes=8 * MIB),
        cost_estimate=pl.CostEstimate(flops=0, bytes_accessed=2 * MIB, transcendentals=0),
        name="pack_tokens",
    )(pos, in_hbm(tokens))
    return outs[0], outs[1:]


def stage_kernel(order_ref, wq, wk, wv, wo, after, oq, ok, ov, oo, sems):
    copies = []
    for w, o in ((wq, oq), (wk, ok), (wv, ov), (wo, oo)):
        part = w.shape[0] // 4
        for p in range(4):
            place = p if w is wo else order_ref[p]
            rows = pl.ds(pl.multiple_of(place * part, part), part)
            to = slice(p * part, (p + 1) * part)
            sem = sems.at[len(copies)]
            copies.append(pltpu.make_async_copy(w.at[rows], o.at[to], sem))
    for c in copies:
        c.start()
    for c in copies:
        c.wait()


def stage(order, weights, after):
    return pl.pallas_call(
        stage_kernel,
        in_specs=[IN_SMEM] + [ANYWHERE] * 5,
        out_specs=[IN_VMEM] * 4,
        out_shape=[shape(w.shape) for w in weights],
        scratch_shapes=[pltpu.SemaphoreType.DMA((16,))],
        compiler_params=pltpu.CompilerParams(vmem_limit_bytes=16 * MIB),
        cost_estimate=pl.CostEstimate(flops=0, bytes_accessed=0, transcendentals=0),
        name="stage_weights",
    )(order, *weights, after)


def gathered(x_refs, at, w_ref):
    width = x_refs[0].shape[1]
    total = None
    for p, x_ref in enumerate(x_refs):
        term = dot(x_ref[at, :], w_ref[p * width : (p + 1) * width, :])
        total = term if total is None else total + term
    return total.astype(BF16)


def half_kernel(x0, x1, wq, wk, wv, *outs):
    width = x0.shape[1]
    for w, out in zip((wq, wk, wv), outs):
        out[...] = dot(x0[...], w[:width, :]) + dot(x1[...], w[width : 2 * width, :])


def half_sums(own, core, weights, after):
    shapes = [shape(own.shape, F32)] * 3
    return call(half_kernel, "half_sums", 0, shapes, (own, core, *weights), after)


def near_kernel(x0, x1, x2, x3, wq, wk, wv, *outs):
    everything = slice(0, x0.shape[0])
    for w, out in zip((wq, wk, wv), outs):
        out[...] = gathered((x0, x1, x2, x3), everything, w)


def halo_kernel(x0, x1, x2, x3, wk, wv, out_ref):
    rows = x0.shape[0]
    at = slice(rows - STRIDE, rows)
    out_ref[:STRIDE, :] = gathered((x0, x1, x2, x3), at, wk)
    out_ref[STRIDE:, :] = gathered((x0, x1, x2, x3), at, wv)


def query_kernel(x0, x1, x2, x3, wq, q_ref):
    q_ref[...] = gathered((x0, x1, x2, x3), slice(0, x0.shape[0]), wq)


def key_kernel(x0, x1, x2, x3, wk, wv, halo, k_ref, v_ref):
    upto = x0.shape[0] - STRIDE
    k_ref[upto:, :] = halo[:STRIDE, :]
    v_ref[upto:, :] = halo[STRIDE:, :]
    for w, out in ((wk, k_ref), (wv, v_ref)):
        out[:upto, :] = gathered((x0, x1, x2, x3), slice(0, upto), w)


def softmax_columns(s):
    m = jnp.maximum(jnp.max(s, 0, keepdims=True), FLOOR)
    p = jnp.exp2((s - m) * SCALE2)
    total = jnp.maximum(jnp.sum(p, 0, keepdims=True), 1.0)
    return p, total, m * SCALE2 + jnp.log2(total)


def local_kernel(pos_ref, q_ref, k_ref, v_ref, halo_ref, *outs):
    out_refs, lse_refs = outs[: len(CHUNKS)], outs[len(CHUNKS) :]
    owners = out_refs[0].shape[0]
    groups = STRIDE // owners // SUB
    block = pos_ref[0]
    u = lax.broadcasted_iota(jnp.int32, (STRIDE, STRIDE), 0)
    t = lax.broadcasted_iota(jnp.int32, (STRIDE, STRIDE), 1)
    current = u <= t
    low = jnp.where(block == 0, -1e30, 0.0).astype(F32)
    for r in range(ROWS):
        lses = []
        here = slice(r * STRIDE, (r + 1) * STRIDE)
        back = slice((r - 1) * STRIDE, r * STRIDE)
        heads = [slice(h * DH, (h + 1) * DH) for h in range(HEADS)]
        scores = []
        for cols in heads:
            q = q_ref[here, cols]
            s_prev = dot_t(k_ref[back, cols] if r else halo_ref[:STRIDE, cols], q)
            if r == 0:
                s_prev = s_prev + low
            scores.append(jnp.where(current, dot_t(k_ref[here, cols], q), s_prev))
        parts = []
        for p, total, lse in [softmax_columns(s) for s in scores]:
            now = jnp.where(current, p, 0.0).astype(BF16)
            before = jnp.where(current, 0.0, p).astype(BF16)
            parts.append((now, before, 1.0 / total))
            lses.append(lse)
        results = []
        for cols, (now, before, share) in zip(heads, parts):
            v_prev = v_ref[back, cols] if r else halo_ref[STRIDE:, cols]
            results.append((dot_l(v_ref[here, cols], now) + dot_l(v_prev, before)) * share)
        for cols, o in zip(heads, results):
            o = o.T
            for d in range(owners):
                for chunk, out_ref in zip(CHUNKS, out_refs):
                    for n, g in enumerate(chunk):
                        at = (d * groups + g) * SUB
                        to = (n * ROWS + r) * SUB
                        out_ref[d, to : to + SUB, cols] = o[at : at + SUB]
        lses.append(jnp.zeros((128 - HEADS, STRIDE), F32))
        turned = jnp.concatenate(lses, 0).T
        for chunk, lse_ref in zip(CHUNKS, lse_refs):
            for n, g in enumerate(chunk):
                total = None
                for d in range(owners):
                    at = (d * groups + g) * SUB
                    moved = pltpu.roll(turned[at : at + SUB], 8 * (block ^ d), 1)
                    total = moved if total is None else total + moved
                to = (n * ROWS + r) * SUB
                lse_ref[to : to + SUB, :] = total


def local_part(pos, q, k, v, halo, owners, after):
    rows, width = q.shape
    sizes = [len(chunk) * ROWS * SUB for chunk in CHUNKS]
    shapes = [shape((owners, m, width), F32) for m in sizes] + [shape((m, 128), F32) for m in sizes]
    outs = call(local_kernel, "local_part", 5, shapes, (pos, q, k, v, halo), after)
    return list(zip(outs[: len(sizes)], outs[len(sizes) :]))


def column_kernel(pos_ref, x2, x3a, x3b, hq, hk, hv, wq, wk, wv, nq, nk, nv, *rest):
    out_refs, scratch = rest[:-3], rest[-3:]
    owners, message, width = scratch[0].shape
    groups = message // (ROWS * SUB)
    for h, w, near, a in zip((hq, hk, hv), (wq, wk, wv), (nq, nk, nv), scratch):
        total = h[...] + dot(x2[...], w[2 * width : 3 * width, :])
        diagonal = [dot(x[...], w[3 * width :, :]) for x in (x3a, x3b)]
        total = total + jnp.concatenate(diagonal, 0)
        a[:NEAR] = near[...].reshape(NEAR, message, width)
        a[NEAR:] = total.astype(BF16).reshape(owners - NEAR, message, width)
    part = ROWS * SUB
    size = owners * part

    def row_and_class(dim):
        i = lax.broadcasted_iota(jnp.int32, (size, size), dim)
        return ((i // part) ^ pos_ref[0]) * ROWS + (i % part) // SUB, i % SUB

    (row_j, class_j), (row_i, class_i) = row_and_class(0), row_and_class(1)
    earlier = jnp.logical_and(class_i == class_j, row_i > row_j)
    stats = []
    heads = [slice(h * DH, (h + 1) * DH) for h in range(HEADS)]
    for pair in range(0, groups, 2):
        tiles = [(g, h) for g in range(pair, pair + 2) for h in range(HEADS)]
        operands = [
            [a[:, g * part : (g + 1) * part, heads[h]].reshape(size, DH) for a in scratch]
            for g, h in tiles
        ]
        scores = [jnp.where(earlier, dot_t(k, q), -1e30) for q, k, _ in operands]
        parts = [softmax_columns(s) for s in scores]
        results = [
            dot_l(v, p.astype(BF16)) * (1.0 / total)
            for (_, _, v), (p, total, _) in zip(operands, parts)
        ]
        lses = [lse for _, _, lse in parts]
        for (g, h), o in zip(tiles, results):
            o = o.T.astype(BF16)
            to = h * message + g * part
            for n in range(owners):
                out_refs[n][to : to + part, :] = o[n * part : (n + 1) * part]
        for some in (lses[:HEADS], lses[HEADS:]):
            stats.append(jnp.concatenate(some + some, 0))
    upper = lax.broadcasted_iota(jnp.int32, (8, 128), 0) < HEADS
    blank = [jnp.zeros((8, 128 - message), F32)] if message < 128 else []
    for n in range(owners):
        x = jnp.concatenate([s[:, n * part : (n + 1) * part] for s in stats] + blank, 1)
        hi = x.astype(BF16).astype(F32)
        mid = (x - hi).astype(BF16).astype(F32)
        lo = x - hi - mid
        tail = jnp.concatenate([jnp.where(upper, hi, lo), jnp.where(upper, mid, 0.0)], 0)
        to = HEADS * message
        out_refs[n][to : to + 16, :] = tail.astype(BF16)


def column_part(pos, across, halves, weights, near, owners, after):
    tokens, width = across.shape
    message = tokens // (owners - NEAR)
    shapes = [shape((HEADS * message + 16, DH))] * owners
    scratch = [pltpu.VMEM((owners, message, width), BF16)] * 3
    middle = tokens // 2
    diagonal = [swap(x, 1) for x in (across[:middle], across[middle:])]
    args = (pos, across, *diagonal, *halves, *weights, *near)
    return call(column_kernel, "column_part", 0, shapes, args, after, scratch)


def mix_kernel(share, pos_ref, *refs):
    count = 2 * len(CHUNKS)
    local_refs, col_refs, (own_ref, send_ref) = refs[:count], refs[count:-2], refs[-2:]
    per_owner = own_ref.shape[1] // len(share)
    first_core = pos_ref[1] == 0
    base = 0
    for chunk, loc_ref, lse_ref in zip(CHUNKS, local_refs[::2], local_refs[1::2]):
        message = loc_ref.shape[1]
        size = HEADS * message + 16
        tiles = [jnp.zeros((8, 128), F32)] * 16
        for k, col_ref in zip(share, col_refs):
            tail = col_ref[base + HEADS * message : base + size, :].astype(F32)
            tiles[k] = tail[:8] + tail[8:]
        turned = jnp.concatenate(tiles, 0).T[:message]
        col_lse = turned + pltpu.roll(turned, 124, 1)
        loc_lse = lse_ref[...]
        top = jnp.maximum(col_lse, loc_lse)
        w_col = jnp.exp2(col_lse - top)
        w_loc = jnp.exp2(loc_lse - top)
        scale = 1.0 / (w_col + w_loc)
        w_col = w_col * scale
        w_loc = w_loc * scale
        for n, (k, col_ref) in enumerate(zip(share, col_refs)):
            d = pos_ref[0] ^ k
            for h in range(HEADS):
                cols = slice(h * DH, (h + 1) * DH)
                at = slice(8 * k + h, 8 * k + h + 1)
                col = col_ref[base + h * message : base + (h + 1) * message, :].astype(F32)
                both = loc_ref[d, :, cols] * w_loc[:, at] + col * w_col[:, at]
                rows = []
                for r in range(ROWS):
                    starts = [(m * ROWS + r) * SUB for m in range(len(chunk))]
                    rows.append(jnp.concatenate([both[t : t + SUB] for t in starts], 0))
                to = n * per_owner + chunk[0] * SUB
                spot = slice(to, to + len(chunk) * SUB)
                for x in range(2):
                    even, odd = rows[2 * x], rows[2 * x + 1]
                    own_ref[x, spot, cols] = jnp.where(first_core, even, odd).astype(BF16)
                    send_ref[x, spot, cols] = jnp.where(first_core, odd, even).astype(BF16)
        base += size


def mix(pos, share, columns, locals_, after):
    owners, _, width = locals_[0][0].shape
    tokens = len(share) * STRIDE // owners
    shapes = [shape((2, tokens, width))] * 2
    args = (pos, *[x for pair in locals_ for x in pair], *columns)
    return call(functools.partial(mix_kernel, share), "mix", 2, shapes, args, after)


def out_kernel(here, pos_ref, a_ref, b_ref, wa_ref, wb_ref, out_ref):
    side = pos_ref[2] if here else 1 - pos_ref[2]
    a, b = a_ref[side], b_ref[side]
    tile = 512
    for n in range(0, out_ref.shape[1], tile):
        at = slice(n, n + tile)
        total = dot(a, wa_ref[:, at]) + dot(b, wb_ref[:, at])
        out_ref[:, at] = total.astype(out_ref.dtype)


def out_project(pos, here, own, other, w_own, w_other):
    dims = shape((own.shape[1], w_own.shape[1]), F32 if here else BF16)
    body = functools.partial(out_kernel, here)
    return call(body, "out_project", 2, dims, (pos, own, other, w_own, w_other))


def join_kernel(share, pos_ref, keep, got, *rest):
    out_hbm, joined, sems = rest[-3:]
    span = keep.shape[0] // len(share)
    joined[...] = (keep[...] + got[...].astype(F32)).astype(BF16)
    copies = []
    for n, k in enumerate(share):
        to = pl.ds(pl.multiple_of((pos_ref[0] ^ k) * span, span), span)
        rows = slice(n * span, (n + 1) * span)
        copies.append(pltpu.make_async_copy(joined.at[rows], out_hbm.at[to], sems.at[n]))
    for c in copies:
        c.start()
    for c in copies:
        c.wait()


def join(pos, share, keep, got, earlier):
    return pl.pallas_call(
        functools.partial(join_kernel, share),
        in_specs=[IN_SMEM, IN_VMEM, IN_VMEM] + [ANYWHERE] * len(earlier),
        out_specs=ANYWHERE,
        out_shape=shape((STRIDE, keep.shape[1])),
        input_output_aliases={3: 0} if earlier else {},
        scratch_shapes=[pltpu.VMEM(keep.shape, BF16), pltpu.SemaphoreType.DMA((len(share),))],
        compiler_params=pltpu.CompilerParams(vmem_limit_bytes=16 * MIB),
        cost_estimate=pl.CostEstimate(flops=int(1.1e9), bytes_accessed=0, transcendentals=0),
        name="join",
    )(pos, keep, got, *earlier)


def swap(value, distance):
    return lax.ppermute(value, "head", [(i, i ^ distance) for i in range(4)])


def exchange(messages):
    peers = lax.axis_size("seq")

    def move(value, k):
        return lax.ppermute(value, "seq", [(i, i ^ k) for i in range(peers)]) if k else value

    return [move(m, k) for k, m in enumerate(messages)]


def chunked(tokens, w_query, w_key, w_value, w_out):
    owners = lax.axis_size("seq")
    head = lax.axis_index("head")
    block = lax.axis_index("seq")
    order = jnp.bitwise_xor(jnp.arange(4, dtype=jnp.int32), head.astype(jnp.int32))
    pos = jnp.stack([block, head % 2, head // 2]).astype(jnp.int32)
    rows, width = tokens.shape

    across = swap(tokens, 2)
    block_tokens, sent = pack(pos, tokens, owners)
    messages = exchange(sent)
    near_own = jnp.concatenate(messages[:NEAR], 0)
    near_core, near_across = swap(near_own, 1), swap(near_own, 2)
    far_own = jnp.concatenate(messages[NEAR:], 0)
    far_core, far_across = swap(far_own, 1), swap(far_own, 2)
    *weights, w_own = stage(order, (w_query, w_key, w_value, w_out), messages[1])
    w_other = swap(w_own, 1)
    block_core = swap(fence(block_tokens, near_own, far_own), 1)
    across = fence(across, near_across, far_own)
    pieces = (block_tokens, block_core, across, swap(across, 1))
    own_halo = call(
        halo_kernel, "project_halo", 1.5, shape((2 * STRIDE, width)), (*pieces, *weights[1:])
    )
    halo = lax.ppermute(own_halo, "seq", [(i, i + 1) for i in range(owners - 1)])
    q = call(
        query_kernel,
        "project_query",
        0,
        shape((rows, width)),
        (*pieces, weights[0]),
        (far_own,),
    )
    near = call(
        near_kernel,
        "project_near",
        0,
        [shape(near_own.shape)] * 3,
        (near_own, near_core, near_across, swap(near_across, 1), *weights),
        (q,),
    )
    far_half = half_sums(far_own, far_core, weights, (near[0],))
    far_across = fence(far_across, near[0])
    columns = column_part(pos, far_across, far_half, weights, near, owners, (w_other,))
    k, v = call(
        key_kernel,
        "project_key",
        0,
        [shape((rows, width))] * 2,
        (*pieces, *weights[1:], own_halo),
        (columns[0], halo),
    )
    locals_ = local_part(pos, q, k, v, halo, owners, (columns[0],))
    columns = list(columns)
    columns = exchange(columns)
    sums, after = [], ()
    for share in SHARES:
        own, send = mix(pos, share, [columns[n] for n in share], locals_, after)
        other = swap(send, 1)
        out = out_project(pos, False, own, other, w_own, w_other)
        keep = out_project(pos, True, own, other, w_own, w_other)
        sums.append((keep, swap(out, 2)))
        after = (out,)
    result = ()
    for share, (keep, got) in zip(SHARES, sums):
        result = (join(pos, share, keep, got, result),)
    return result[0]


def from_behind(value, axis, by):
    peers = lax.axis_size(axis)
    pairs = [(i, i + by) for i in range(peers) if 0 <= i + by < peers]
    return lax.ppermute(value, axis, pairs)


def general(tokens, w_query, w_key, w_value, w_out):
    tok_rows = tokens.shape[0]
    head_width = w_query.shape[1]
    head_count = head_width // DH
    score_scale = DH ** (-0.5)
    shard_piece = lax.all_gather(tokens, "head", axis=1, tiled=True)
    query_full, key_full, value_full = tuple(
        (
            jnp.dot(shard_piece, weight, preferred_element_type=jnp.float32)
            for weight in (w_query, w_key, w_value)
        )
    )
    query = query_full.astype(jnp.bfloat16).reshape(tok_rows, head_count, DH)
    key_heads = key_full.astype(jnp.bfloat16).reshape(tok_rows, head_count, DH)
    value_heads = value_full.astype(jnp.bfloat16).reshape(tok_rows, head_count, DH)
    prev_keys, prev_values = from_behind((key_heads[-STRIDE:], value_heads[-STRIDE:]), "seq", 1)
    blocks = tok_rows // STRIDE
    extended_keys = jnp.concatenate([prev_keys, key_heads], 0)
    extended_values = jnp.concatenate([prev_values, value_heads], 0)
    window_keys = jnp.concatenate(
        [
            extended_keys[:tok_rows].reshape(blocks, STRIDE, head_count, DH),
            extended_keys[STRIDE:].reshape(blocks, STRIDE, head_count, DH),
        ],
        1,
    )
    window_values = jnp.concatenate(
        [
            extended_values[:tok_rows].reshape(blocks, STRIDE, head_count, DH),
            extended_values[STRIDE:].reshape(blocks, STRIDE, head_count, DH),
        ],
        1,
    )
    query_blocks = query.reshape(blocks, STRIDE, head_count, DH)
    scores = (
        jnp.einsum("bthd,buhd->bhtu", query_blocks, window_keys, preferred_element_type=jnp.float32)
        * score_scale
    )
    first_position = lax.axis_index("seq") * tok_rows
    block_index = jnp.arange(blocks)[:, None, None, None]
    query_index = jnp.arange(STRIDE)[None, None, :, None]
    key_index = jnp.arange(2 * STRIDE)[None, None, None, :]
    allowed = (
        (key_index > query_index)
        & (key_index <= query_index + STRIDE)
        & (first_position + block_index * STRIDE + key_index - STRIDE >= 0)
    )
    local_top = jnp.max(jnp.where(allowed, scores, -1e30), axis=-1)
    local_weights = jnp.where(allowed, jnp.exp(scores - local_top[..., None]), 0.0)
    local_total = jnp.sum(local_weights, axis=-1)
    local_out = jnp.einsum(
        "bhtu,buhd->bthd",
        local_weights.astype(jnp.bfloat16),
        window_values,
        preferred_element_type=jnp.float32,
    )
    local_out = local_out.reshape(tok_rows, head_count, DH)
    local_top = local_top.transpose(0, 2, 1).reshape(tok_rows, head_count)
    local_total = local_total.transpose(0, 2, 1).reshape(tok_rows, head_count)
    row_count = tok_rows // STRIDE
    query_class = lax.all_to_all(
        query.reshape(row_count, STRIDE, head_count, DH),
        "seq",
        split_axis=1,
        concat_axis=0,
        tiled=True,
    )
    key_class = lax.all_to_all(
        key_heads.reshape(row_count, STRIDE, head_count, DH),
        "seq",
        split_axis=1,
        concat_axis=0,
        tiled=True,
    )
    value_class = lax.all_to_all(
        value_heads.reshape(row_count, STRIDE, head_count, DH),
        "seq",
        split_axis=1,
        concat_axis=0,
        tiled=True,
    )
    row_total = query_class.shape[0]
    class_scores = (
        jnp.einsum("rchd,schd->chrs", query_class, key_class, preferred_element_type=jnp.float32)
        * score_scale
    )
    earlier = (
        jnp.arange(row_total)[None, None, :, None] > jnp.arange(row_total)[None, None, None, :]
    )
    class_top = jnp.max(jnp.where(earlier, class_scores, -1e30), axis=-1)
    class_weights = jnp.where(earlier, jnp.exp(class_scores - class_top[..., None]), 0.0)
    class_total = jnp.sum(class_weights, axis=-1)
    summed = jnp.einsum(
        "chrs,schd->rchd",
        class_weights.astype(jnp.bfloat16),
        value_class,
        preferred_element_type=jnp.float32,
    )
    floor_total = jnp.maximum(class_total, 1.0).transpose(2, 0, 1)
    class_out = (summed / floor_total[..., None]).astype(jnp.bfloat16)
    class_top_rows = class_top.transpose(2, 0, 1)
    class_total_rows = class_total.transpose(2, 0, 1)
    column_out = class_out
    column_top = class_top_rows
    column_total = class_total_rows
    column_out, column_top, column_total = (
        lax.all_to_all(column_out, "seq", split_axis=0, concat_axis=1, tiled=True),
        lax.all_to_all(
            column_top.astype(jnp.bfloat16), "seq", split_axis=0, concat_axis=1, tiled=True
        ).astype(column_top.dtype),
        lax.all_to_all(
            column_total.astype(jnp.bfloat16), "seq", split_axis=0, concat_axis=1, tiled=True
        ).astype(column_total.dtype),
    )
    column_out = column_out.reshape(tok_rows, head_count, DH)
    column_top = column_top.reshape(tok_rows, head_count)
    column_total = column_total.reshape(tok_rows, head_count)
    top_score = jnp.maximum(local_top, column_top)
    local_weight = jnp.exp(local_top - top_score)
    column_weight = column_total * jnp.exp(column_top - top_score)
    denominator = local_total * local_weight + column_weight
    mixed = (
        local_out * local_weight[..., None]
        + column_out.astype(jnp.float32) * column_weight[..., None]
    ) / denominator[..., None]
    mixed = mixed.astype(jnp.bfloat16).reshape(tok_rows, head_width)
    return lax.psum_scatter(
        jnp.dot(mixed, w_out, preferred_element_type=jnp.float32).astype(jnp.bfloat16),
        "head",
        scatter_dimension=0,
        tiled=True,
    )


def shards(tokens, w_query, w_key, w_value, w_out):
    rows, width = w_query.shape
    fits = (
        lax.axis_size("seq") == PEERS
        and lax.axis_size("head") == 4
        and tokens.shape == (ROWS * STRIDE, HEADS * DH)
        and (rows, width) == (4 * HEADS * DH, HEADS * DH)
    )
    plan = chunked if fits else general
    return plan(tokens, w_query, w_key, w_value, w_out)


def solution(mesh):
    in_specs = (
        P("seq", "head"),
        P(None, "head"),
        P(None, "head"),
        P(None, "head"),
        P("head", None),
    )
    out_specs = P(("seq", "head"), None)
    return jax.shard_map(shards, mesh=mesh, in_specs=in_specs, out_specs=out_specs, check_vma=False)
```

```python
import functools

import jax
import jax.numpy as jnp
from jax import lax
from jax.experimental import pallas as pl
from jax.experimental.pallas import tpu as pltpu
from jax.sharding import PartitionSpec as P

DH = 128
STRIDE = 256
HEADS = 4
ROWS = 4
SUB = 8
CHUNKS = ((0, 1, 2, 3),)
NEAR = 4
PEERS = 8
SHARES = ((4, 5, 1, 2, 0), (6, 7, 3))
SCALE2 = DH ** (-0.5) * 1.4426950408889634
FLOOR = -1e29
MIB = 1024 * 1024
F32 = jnp.float32
BF16 = jnp.bfloat16


ANYWHERE = pl.BlockSpec(memory_space=pl.ANY)
IN_VMEM = pl.BlockSpec(memory_space=pltpu.VMEM)
IN_SMEM = pl.BlockSpec(memory_space=pltpu.SMEM)


def call(body, name, micros, out_shape, args, after=(), scratch=(), mib=24):
    specs = [IN_SMEM if x.dtype == jnp.int32 else IN_VMEM for x in args]
    extra = len(after)

    def run(*refs):
        n = len(args)
        body(*refs[:n], *refs[n + extra :])

    return pl.pallas_call(
        run,
        in_specs=specs + [ANYWHERE] * extra,
        out_specs=jax.tree.map(lambda _: IN_VMEM, out_shape),
        out_shape=out_shape,
        scratch_shapes=list(scratch),
        compiler_params=pltpu.CompilerParams(vmem_limit_bytes=mib * MIB),
        cost_estimate=pl.CostEstimate(
            flops=int(micros * 1.1e9), bytes_accessed=0, transcendentals=0
        ),
        name=name,
    )(*args, *after)


def fence(value, *after):
    return pl.pallas_call(
        lambda *refs: None,
        in_specs=[ANYWHERE] * (1 + len(after)),
        out_specs=ANYWHERE,
        out_shape=jax.ShapeDtypeStruct(value.shape, value.dtype),
        input_output_aliases={0: 0},
        compiler_params=pltpu.CompilerParams(vmem_limit_bytes=MIB),
        cost_estimate=pl.CostEstimate(flops=0, bytes_accessed=0, transcendentals=0),
        name="fence",
    )(value, *after)


def in_hbm(value):
    return pltpu.with_memory_space_constraint(value, pltpu.HBM)


def shape(dims, dtype=BF16):
    return jax.ShapeDtypeStruct(tuple(dims), dtype)


def dot(a, b):
    return jnp.dot(a, b, preferred_element_type=F32)


def dot_t(a, b):
    return lax.dot_general(a, b, (((1,), (1,)), ((), ())), preferred_element_type=F32)


def dot_l(a, b):
    return lax.dot_general(a, b, (((0,), (0,)), ((), ())), preferred_element_type=F32)


def pack_kernel(pos_ref, tok_hbm, tok_ref, *rest):
    out_refs, sems = rest[:-1], rest[-1]
    spans = [slice(r * STRIDE, (r + 1) * STRIDE) for r in range(ROWS)]
    copies = [
        pltpu.make_async_copy(tok_hbm.at[at], tok_ref.at[at], sems.at[r])
        for r, at in enumerate(spans)
    ]
    for c in copies:
        c.start()
    for c in copies:
        c.wait()
    per_owner = STRIDE // len(out_refs)
    part = ROWS * SUB
    for k, out_ref in enumerate(out_refs):
        d = pos_ref[0] ^ k
        rows = [
            tok_ref[pl.ds(pl.multiple_of(r * STRIDE + d * per_owner, per_owner), per_owner), :]
            for r in range(ROWS)
        ]
        rows = [x.astype(F32) for x in rows]
        for g in range(per_owner // SUB):
            piece = jnp.concatenate([x[g * SUB : (g + 1) * SUB] for x in rows], 0)
            out_ref[g * part : (g + 1) * part, :] = piece.astype(BF16)


def pack(pos, tokens, owners):
    message = shape((tokens.shape[0] // owners, tokens.shape[1]))
    outs = pl.pallas_call(
        pack_kernel,
        in_specs=[IN_SMEM, ANYWHERE],
        out_specs=[IN_VMEM] * (1 + owners),
        out_shape=[shape(tokens.shape)] + [message] * owners,
        scratch_shapes=[pltpu.SemaphoreType.DMA((ROWS,))],
        compiler_params=pltpu.CompilerParams(vmem_limit_bytes=8 * MIB),
        cost_estimate=pl.CostEstimate(flops=0, bytes_accessed=2 * MIB, transcendentals=0),
        name="pack_tokens",
    )(pos, in_hbm(tokens))
    return outs[0], outs[1:]


def stage_kernel(order_ref, wq, wk, wv, wo, after, oq, ok, ov, oo, sems):
    copies = []
    for w, o in ((wq, oq), (wk, ok), (wv, ov), (wo, oo)):
        part = w.shape[0] // 4
        for p in range(4):
            place = p if w is wo else order_ref[p]
            rows = pl.ds(pl.multiple_of(place * part, part), part)
            to = slice(p * part, (p + 1) * part)
            sem = sems.at[len(copies)]
            copies.append(pltpu.make_async_copy(w.at[rows], o.at[to], sem))
    for c in copies:
        c.start()
    for c in copies:
        c.wait()


def stage(order, weights, after):
    return pl.pallas_call(
        stage_kernel,
        in_specs=[IN_SMEM] + [ANYWHERE] * 5,
        out_specs=[IN_VMEM] * 4,
        out_shape=[shape(w.shape) for w in weights],
        scratch_shapes=[pltpu.SemaphoreType.DMA((16,))],
        compiler_params=pltpu.CompilerParams(vmem_limit_bytes=16 * MIB),
        cost_estimate=pl.CostEstimate(flops=0, bytes_accessed=0, transcendentals=0),
        name="stage_weights",
    )(order, *weights, after)


def gathered(x_refs, at, w_ref):
    width = x_refs[0].shape[1]
    total = None
    for p, x_ref in enumerate(x_refs):
        term = dot(x_ref[at, :], w_ref[p * width : (p + 1) * width, :])
        total = term if total is None else total + term
    return total.astype(BF16)


def half_kernel(x0, x1, wq, wk, wv, *outs):
    width = x0.shape[1]
    for w, out in zip((wq, wk, wv), outs):
        out[...] = dot(x0[...], w[:width, :]) + dot(x1[...], w[width : 2 * width, :])


def half_sums(own, core, weights, after):
    shapes = [shape(own.shape, F32)] * 3
    return call(half_kernel, "half_sums", 0, shapes, (own, core, *weights), after)


def near_kernel(x0, x1, x2, x3, wq, wk, wv, *outs):
    everything = slice(0, x0.shape[0])
    for w, out in zip((wq, wk, wv), outs):
        out[...] = gathered((x0, x1, x2, x3), everything, w)


def halo_kernel(x0, x1, x2, x3, wk, wv, out_ref):
    rows = x0.shape[0]
    at = slice(rows - STRIDE, rows)
    out_ref[:STRIDE, :] = gathered((x0, x1, x2, x3), at, wk)
    out_ref[STRIDE:, :] = gathered((x0, x1, x2, x3), at, wv)


def query_kernel(x0, x1, x2, x3, wq, q_ref):
    q_ref[...] = gathered((x0, x1, x2, x3), slice(0, x0.shape[0]), wq)


def key_kernel(x0, x1, x2, x3, wk, wv, halo, k_ref, v_ref):
    upto = x0.shape[0] - STRIDE
    k_ref[upto:, :] = halo[:STRIDE, :]
    v_ref[upto:, :] = halo[STRIDE:, :]
    for w, out in ((wk, k_ref), (wv, v_ref)):
        out[:upto, :] = gathered((x0, x1, x2, x3), slice(0, upto), w)


def softmax_columns(s):
    m = jnp.maximum(jnp.max(s, 0, keepdims=True), FLOOR)
    p = jnp.exp2((s - m) * SCALE2)
    total = jnp.maximum(jnp.sum(p, 0, keepdims=True), 1.0)
    return p, total, m * SCALE2 + jnp.log2(total)


def local_kernel(pos_ref, q_ref, k_ref, v_ref, halo_ref, *outs):
    out_refs, lse_refs = outs[: len(CHUNKS)], outs[len(CHUNKS) :]
    owners = out_refs[0].shape[0]
    groups = STRIDE // owners // SUB
    block = pos_ref[0]
    u = lax.broadcasted_iota(jnp.int32, (STRIDE, STRIDE), 0)
    t = lax.broadcasted_iota(jnp.int32, (STRIDE, STRIDE), 1)
    current = u <= t
    low = jnp.where(block == 0, -1e30, 0.0).astype(F32)
    for r in range(ROWS):
        lses = []
        here = slice(r * STRIDE, (r + 1) * STRIDE)
        back = slice((r - 1) * STRIDE, r * STRIDE)
        heads = [slice(h * DH, (h + 1) * DH) for h in range(HEADS)]
        scores = []
        for cols in heads:
            q = q_ref[here, cols]
            s_prev = dot_t(k_ref[back, cols] if r else halo_ref[:STRIDE, cols], q)
            if r == 0:
                s_prev = s_prev + low
            scores.append(jnp.where(current, dot_t(k_ref[here, cols], q), s_prev))
        parts = []
        for p, total, lse in [softmax_columns(s) for s in scores]:
            now = jnp.where(current, p, 0.0).astype(BF16)
            before = jnp.where(current, 0.0, p).astype(BF16)
            parts.append((now, before, 1.0 / total))
            lses.append(lse)
        results = []
        for cols, (now, before, share) in zip(heads, parts):
            v_prev = v_ref[back, cols] if r else halo_ref[STRIDE:, cols]
            results.append((dot_l(v_ref[here, cols], now) + dot_l(v_prev, before)) * share)
        for cols, o in zip(heads, results):
            o = o.T
            for d in range(owners):
                for chunk, out_ref in zip(CHUNKS, out_refs):
                    for n, g in enumerate(chunk):
                        at = (d * groups + g) * SUB
                        to = (n * ROWS + r) * SUB
                        out_ref[d, to : to + SUB, cols] = o[at : at + SUB]
        lses.append(jnp.zeros((128 - HEADS, STRIDE), F32))
        turned = jnp.concatenate(lses, 0).T
        for chunk, lse_ref in zip(CHUNKS, lse_refs):
            for n, g in enumerate(chunk):
                total = None
                for d in range(owners):
                    at = (d * groups + g) * SUB
                    moved = pltpu.roll(turned[at : at + SUB], 8 * (block ^ d), 1)
                    total = moved if total is None else total + moved
                to = (n * ROWS + r) * SUB
                lse_ref[to : to + SUB, :] = total


def local_part(pos, q, k, v, halo, owners, after):
    rows, width = q.shape
    sizes = [len(chunk) * ROWS * SUB for chunk in CHUNKS]
    shapes = [shape((owners, m, width), F32) for m in sizes] + [shape((m, 128), F32) for m in sizes]
    outs = call(local_kernel, "local_part", 5, shapes, (pos, q, k, v, halo), after)
    return list(zip(outs[: len(sizes)], outs[len(sizes) :]))


def column_kernel(pos_ref, x2, x3a, x3b, hq, hk, hv, wq, wk, wv, nq, nk, nv, *rest):
    out_refs, scratch = rest[:-3], rest[-3:]
    owners, message, width = scratch[0].shape
    groups = message // (ROWS * SUB)
    for h, w, near, a in zip((hq, hk, hv), (wq, wk, wv), (nq, nk, nv), scratch):
        total = h[...] + dot(x2[...], w[2 * width : 3 * width, :])
        diagonal = [dot(x[...], w[3 * width :, :]) for x in (x3a, x3b)]
        total = total + jnp.concatenate(diagonal, 0)
        a[:NEAR] = near[...].reshape(NEAR, message, width)
        a[NEAR:] = total.astype(BF16).reshape(owners - NEAR, message, width)
    part = ROWS * SUB
    size = owners * part

    def row_and_class(dim):
        i = lax.broadcasted_iota(jnp.int32, (size, size), dim)
        return ((i // part) ^ pos_ref[0]) * ROWS + (i % part) // SUB, i % SUB

    (row_j, class_j), (row_i, class_i) = row_and_class(0), row_and_class(1)
    earlier = jnp.logical_and(class_i == class_j, row_i > row_j)
    stats = []
    heads = [slice(h * DH, (h + 1) * DH) for h in range(HEADS)]
    for pair in range(0, groups, 2):
        tiles = [(g, h) for g in range(pair, pair + 2) for h in range(HEADS)]
        operands = [
            [a[:, g * part : (g + 1) * part, heads[h]].reshape(size, DH) for a in scratch]
            for g, h in tiles
        ]
        scores = [jnp.where(earlier, dot_t(k, q), -1e30) for q, k, _ in operands]
        parts = [softmax_columns(s) for s in scores]
        results = [
            dot_l(v, p.astype(BF16)) * (1.0 / total)
            for (_, _, v), (p, total, _) in zip(operands, parts)
        ]
        lses = [lse for _, _, lse in parts]
        for (g, h), o in zip(tiles, results):
            o = o.T.astype(BF16)
            to = h * message + g * part
            for n in range(owners):
                out_refs[n][to : to + part, :] = o[n * part : (n + 1) * part]
        for some in (lses[:HEADS], lses[HEADS:]):
            stats.append(jnp.concatenate(some + some, 0))
    upper = lax.broadcasted_iota(jnp.int32, (8, 128), 0) < HEADS
    blank = [jnp.zeros((8, 128 - message), F32)] if message < 128 else []
    for n in range(owners):
        x = jnp.concatenate([s[:, n * part : (n + 1) * part] for s in stats] + blank, 1)
        hi = x.astype(BF16).astype(F32)
        mid = (x - hi).astype(BF16).astype(F32)
        lo = x - hi - mid
        tail = jnp.concatenate([jnp.where(upper, hi, lo), jnp.where(upper, mid, 0.0)], 0)
        to = HEADS * message
        out_refs[n][to : to + 16, :] = tail.astype(BF16)


def column_part(pos, across, halves, weights, near, owners, after):
    tokens, width = across.shape
    message = tokens // (owners - NEAR)
    shapes = [shape((HEADS * message + 16, DH))] * owners
    scratch = [pltpu.VMEM((owners, message, width), BF16)] * 3
    middle = tokens // 2
    diagonal = [swap(x, 1) for x in (across[:middle], across[middle:])]
    args = (pos, across, *diagonal, *halves, *weights, *near)
    return call(column_kernel, "column_part", 0, shapes, args, after, scratch)


def mix_kernel(share, pos_ref, *refs):
    count = 2 * len(CHUNKS)
    local_refs, col_refs, (own_ref, send_ref) = refs[:count], refs[count:-2], refs[-2:]
    per_owner = own_ref.shape[1] // len(share)
    first_core = pos_ref[1] == 0
    base = 0
    for chunk, loc_ref, lse_ref in zip(CHUNKS, local_refs[::2], local_refs[1::2]):
        message = loc_ref.shape[1]
        size = HEADS * message + 16
        tiles = [jnp.zeros((8, 128), F32)] * 16
        for k, col_ref in zip(share, col_refs):
            tail = col_ref[base + HEADS * message : base + size, :].astype(F32)
            tiles[k] = tail[:8] + tail[8:]
        turned = jnp.concatenate(tiles, 0).T[:message]
        col_lse = turned + pltpu.roll(turned, 124, 1)
        loc_lse = lse_ref[...]
        top = jnp.maximum(col_lse, loc_lse)
        w_col = jnp.exp2(col_lse - top)
        w_loc = jnp.exp2(loc_lse - top)
        scale = 1.0 / (w_col + w_loc)
        w_col = w_col * scale
        w_loc = w_loc * scale
        for n, (k, col_ref) in enumerate(zip(share, col_refs)):
            d = pos_ref[0] ^ k
            for h in range(HEADS):
                cols = slice(h * DH, (h + 1) * DH)
                at = slice(8 * k + h, 8 * k + h + 1)
                col = col_ref[base + h * message : base + (h + 1) * message, :].astype(F32)
                both = loc_ref[d, :, cols] * w_loc[:, at] + col * w_col[:, at]
                rows = []
                for r in range(ROWS):
                    starts = [(m * ROWS + r) * SUB for m in range(len(chunk))]
                    rows.append(jnp.concatenate([both[t : t + SUB] for t in starts], 0))
                to = n * per_owner + chunk[0] * SUB
                spot = slice(to, to + len(chunk) * SUB)
                for x in range(2):
                    even, odd = rows[2 * x], rows[2 * x + 1]
                    own_ref[x, spot, cols] = jnp.where(first_core, even, odd).astype(BF16)
                    send_ref[x, spot, cols] = jnp.where(first_core, odd, even).astype(BF16)
        base += size


def mix(pos, share, columns, locals_, after):
    owners, _, width = locals_[0][0].shape
    tokens = len(share) * STRIDE // owners
    shapes = [shape((2, tokens, width))] * 2
    args = (pos, *[x for pair in locals_ for x in pair], *columns)
    return call(functools.partial(mix_kernel, share), "mix", 2, shapes, args, after)


def out_kernel(here, pos_ref, a_ref, b_ref, wa_ref, wb_ref, out_ref):
    side = pos_ref[2] if here else 1 - pos_ref[2]
    a, b = a_ref[side], b_ref[side]
    tile = 512
    for n in range(0, out_ref.shape[1], tile):
        at = slice(n, n + tile)
        total = dot(a, wa_ref[:, at]) + dot(b, wb_ref[:, at])
        out_ref[:, at] = total.astype(out_ref.dtype)


def out_project(pos, here, own, other, w_own, w_other):
    dims = shape((own.shape[1], w_own.shape[1]), F32 if here else BF16)
    body = functools.partial(out_kernel, here)
    return call(body, "out_project", 2, dims, (pos, own, other, w_own, w_other))


def join_kernel(share, pos_ref, keep, got, *rest):
    out_hbm, joined, sems = rest[-3:]
    span = keep.shape[0] // len(share)
    joined[...] = (keep[...] + got[...].astype(F32)).astype(BF16)
    copies = []
    for n, k in enumerate(share):
        to = pl.ds(pl.multiple_of((pos_ref[0] ^ k) * span, span), span)
        rows = slice(n * span, (n + 1) * span)
        copies.append(pltpu.make_async_copy(joined.at[rows], out_hbm.at[to], sems.at[n]))
    for c in copies:
        c.start()
    for c in copies:
        c.wait()


def join(pos, share, keep, got, earlier):
    return pl.pallas_call(
        functools.partial(join_kernel, share),
        in_specs=[IN_SMEM, IN_VMEM, IN_VMEM] + [ANYWHERE] * len(earlier),
        out_specs=ANYWHERE,
        out_shape=shape((STRIDE, keep.shape[1])),
        input_output_aliases={3: 0} if earlier else {},
        scratch_shapes=[pltpu.VMEM(keep.shape, BF16), pltpu.SemaphoreType.DMA((len(share),))],
        compiler_params=pltpu.CompilerParams(vmem_limit_bytes=16 * MIB),
        cost_estimate=pl.CostEstimate(flops=int(1.1e9), bytes_accessed=0, transcendentals=0),
        name="join",
    )(pos, keep, got, *earlier)


def swap(value, distance):
    return lax.ppermute(value, "head", [(i, i ^ distance) for i in range(4)])


def exchange(messages):
    peers = lax.axis_size("seq")

    def move(value, k):
        return lax.ppermute(value, "seq", [(i, i ^ k) for i in range(peers)]) if k else value

    return [move(m, k) for k, m in enumerate(messages)]


def chunked(tokens, w_query, w_key, w_value, w_out):
    owners = lax.axis_size("seq")
    head = lax.axis_index("head")
    block = lax.axis_index("seq")
    order = jnp.bitwise_xor(jnp.arange(4, dtype=jnp.int32), head.astype(jnp.int32))
    pos = jnp.stack([block, head % 2, head // 2]).astype(jnp.int32)
    rows, width = tokens.shape

    across = swap(tokens, 2)
    block_tokens, sent = pack(pos, tokens, owners)
    messages = exchange(sent)
    near_own = jnp.concatenate(messages[:NEAR], 0)
    near_core, near_across = swap(near_own, 1), swap(near_own, 2)
    far_own = jnp.concatenate(messages[NEAR:], 0)
    far_core, far_across = swap(far_own, 1), swap(far_own, 2)
    *weights, w_own = stage(order, (w_query, w_key, w_value, w_out), messages[1])
    w_other = swap(w_own, 1)
    block_core = swap(fence(block_tokens, near_own, far_own), 1)
    across = fence(across, near_across, far_own)
    pieces = (block_tokens, block_core, across, swap(across, 1))
    own_halo = call(
        halo_kernel, "project_halo", 1.5, shape((2 * STRIDE, width)), (*pieces, *weights[1:])
    )
    halo = lax.ppermute(own_halo, "seq", [(i, i + 1) for i in range(owners - 1)])
    q = call(
        query_kernel,
        "project_query",
        0,
        shape((rows, width)),
        (*pieces, weights[0]),
        (far_own,),
    )
    near = call(
        near_kernel,
        "project_near",
        0,
        [shape(near_own.shape)] * 3,
        (near_own, near_core, near_across, swap(near_across, 1), *weights),
        (q,),
    )
    far_half = half_sums(far_own, far_core, weights, (near[0],))
    far_across = fence(far_across, near[0])
    columns = column_part(pos, far_across, far_half, weights, near, owners, (w_other,))
    k, v = call(
        key_kernel,
        "project_key",
        0,
        [shape((rows, width))] * 2,
        (*pieces, *weights[1:], own_halo),
        (columns[0], halo),
    )
    locals_ = local_part(pos, q, k, v, halo, owners, (columns[0],))
    columns = list(columns)
    columns = exchange(columns)
    sums, after = [], ()
    for share in SHARES:
        own, send = mix(pos, share, [columns[n] for n in share], locals_, after)
        other = swap(send, 1)
        out = out_project(pos, False, own, other, w_own, w_other)
        keep = out_project(pos, True, own, other, w_own, w_other)
        sums.append((keep, swap(out, 2)))
        after = (out,)
    result = ()
    for share, (keep, got) in zip(SHARES, sums):
        result = (join(pos, share, keep, got, result),)
    return result[0]


def from_behind(value, axis, by):
    peers = lax.axis_size(axis)
    pairs = [(i, i + by) for i in range(peers) if 0 <= i + by < peers]
    return lax.ppermute(value, axis, pairs)


def general(tokens, w_query, w_key, w_value, w_out):
    tok_rows = tokens.shape[0]
    head_width = w_query.shape[1]
    head_count = head_width // DH
    score_scale = DH ** (-0.5)
    shard_piece = lax.all_gather(tokens, "head", axis=1, tiled=True)
    query_full, key_full, value_full = tuple(
        (
            jnp.dot(shard_piece, weight, preferred_element_type=jnp.float32)
            for weight in (w_query, w_key, w_value)
        )
    )
    query = query_full.astype(jnp.bfloat16).reshape(tok_rows, head_count, DH)
    key_heads = key_full.astype(jnp.bfloat16).reshape(tok_rows, head_count, DH)
    value_heads = value_full.astype(jnp.bfloat16).reshape(tok_rows, head_count, DH)
    prev_keys, prev_values = from_behind((key_heads[-STRIDE:], value_heads[-STRIDE:]), "seq", 1)
    blocks = tok_rows // STRIDE
    extended_keys = jnp.concatenate([prev_keys, key_heads], 0)
    extended_values = jnp.concatenate([prev_values, value_heads], 0)
    window_keys = jnp.concatenate(
        [
            extended_keys[:tok_rows].reshape(blocks, STRIDE, head_count, DH),
            extended_keys[STRIDE:].reshape(blocks, STRIDE, head_count, DH),
        ],
        1,
    )
    window_values = jnp.concatenate(
        [
            extended_values[:tok_rows].reshape(blocks, STRIDE, head_count, DH),
            extended_values[STRIDE:].reshape(blocks, STRIDE, head_count, DH),
        ],
        1,
    )
    query_blocks = query.reshape(blocks, STRIDE, head_count, DH)
    scores = (
        jnp.einsum("bthd,buhd->bhtu", query_blocks, window_keys, preferred_element_type=jnp.float32)
        * score_scale
    )
    first_position = lax.axis_index("seq") * tok_rows
    block_index = jnp.arange(blocks)[:, None, None, None]
    query_index = jnp.arange(STRIDE)[None, None, :, None]
    key_index = jnp.arange(2 * STRIDE)[None, None, None, :]
    allowed = (
        (key_index > query_index)
        & (key_index <= query_index + STRIDE)
        & (first_position + block_index * STRIDE + key_index - STRIDE >= 0)
    )
    local_top = jnp.max(jnp.where(allowed, scores, -1e30), axis=-1)
    local_weights = jnp.where(allowed, jnp.exp(scores - local_top[..., None]), 0.0)
    local_total = jnp.sum(local_weights, axis=-1)
    local_out = jnp.einsum(
        "bhtu,buhd->bthd",
        local_weights.astype(jnp.bfloat16),
        window_values,
        preferred_element_type=jnp.float32,
    )
    local_out = local_out.reshape(tok_rows, head_count, DH)
    local_top = local_top.transpose(0, 2, 1).reshape(tok_rows, head_count)
    local_total = local_total.transpose(0, 2, 1).reshape(tok_rows, head_count)
    row_count = tok_rows // STRIDE
    query_class = lax.all_to_all(
        query.reshape(row_count, STRIDE, head_count, DH),
        "seq",
        split_axis=1,
        concat_axis=0,
        tiled=True,
    )
    key_class = lax.all_to_all(
        key_heads.reshape(row_count, STRIDE, head_count, DH),
        "seq",
        split_axis=1,
        concat_axis=0,
        tiled=True,
    )
    value_class = lax.all_to_all(
        value_heads.reshape(row_count, STRIDE, head_count, DH),
        "seq",
        split_axis=1,
        concat_axis=0,
        tiled=True,
    )
    row_total = query_class.shape[0]
    class_scores = (
        jnp.einsum("rchd,schd->chrs", query_class, key_class, preferred_element_type=jnp.float32)
        * score_scale
    )
    earlier = (
        jnp.arange(row_total)[None, None, :, None] > jnp.arange(row_total)[None, None, None, :]
    )
    class_top = jnp.max(jnp.where(earlier, class_scores, -1e30), axis=-1)
    class_weights = jnp.where(earlier, jnp.exp(class_scores - class_top[..., None]), 0.0)
    class_total = jnp.sum(class_weights, axis=-1)
    summed = jnp.einsum(
        "chrs,schd->rchd",
        class_weights.astype(jnp.bfloat16),
        value_class,
        preferred_element_type=jnp.float32,
    )
    floor_total = jnp.maximum(class_total, 1.0).transpose(2, 0, 1)
    class_out = (summed / floor_total[..., None]).astype(jnp.bfloat16)
    class_top_rows = class_top.transpose(2, 0, 1)
    class_total_rows = class_total.transpose(2, 0, 1)
    column_out = class_out
    column_top = class_top_rows
    column_total = class_total_rows
    column_out, column_top, column_total = (
        lax.all_to_all(column_out, "seq", split_axis=0, concat_axis=1, tiled=True),
        lax.all_to_all(
            column_top.astype(jnp.bfloat16), "seq", split_axis=0, concat_axis=1, tiled=True
        ).astype(column_top.dtype),
        lax.all_to_all(
            column_total.astype(jnp.bfloat16), "seq", split_axis=0, concat_axis=1, tiled=True
        ).astype(column_total.dtype),
    )
    column_out = column_out.reshape(tok_rows, head_count, DH)
    column_top = column_top.reshape(tok_rows, head_count)
    column_total = column_total.reshape(tok_rows, head_count)
    top_score = jnp.maximum(local_top, column_top)
    local_weight = jnp.exp(local_top - top_score)
    column_weight = column_total * jnp.exp(column_top - top_score)
    denominator = local_total * local_weight + column_weight
    mixed = (
        local_out * local_weight[..., None]
        + column_out.astype(jnp.float32) * column_weight[..., None]
    ) / denominator[..., None]
    mixed = mixed.astype(jnp.bfloat16).reshape(tok_rows, head_width)
    return lax.psum_scatter(
        jnp.dot(mixed, w_out, preferred_element_type=jnp.float32).astype(jnp.bfloat16),
        "head",
        scatter_dimension=0,
        tiled=True,
    )


def shards(tokens, w_query, w_key, w_value, w_out):
    rows, width = w_query.shape
    fits = (
        lax.axis_size("seq") == PEERS
        and lax.axis_size("head") == 4
        and tokens.shape == (ROWS * STRIDE, HEADS * DH)
        and (rows, width) == (4 * HEADS * DH, HEADS * DH)
    )
    plan = chunked if fits else general
    return plan(tokens, w_query, w_key, w_value, w_out)


def solution(mesh):
    in_specs = (
        P("seq", "head"),
        P(None, "head"),
        P(None, "head"),
        P(None, "head"),
        P("head", None),
    )
    out_specs = P(("seq", "head"), None)
    return jax.shard_map(shards, mesh=mesh, in_specs=in_specs, out_specs=out_specs, check_vma=False)
```

```python
import functools

import jax
import jax.numpy as jnp
from jax import lax
from jax.experimental import pallas as pl
from jax.experimental.pallas import tpu as pltpu
from jax.sharding import PartitionSpec as P

DH = 128
STRIDE = 256
HEADS = 4
ROWS = 4
SUB = 8
CHUNKS = ((0, 1, 2, 3),)
NEAR = 4
PEERS = 8
SHARES = ((4, 5, 3, 2, 1, 0), (6, 7))
SCALE2 = DH ** (-0.5) * 1.4426950408889634
FLOOR = -1e29
MIB = 1024 * 1024
F32 = jnp.float32
BF16 = jnp.bfloat16


ANYWHERE = pl.BlockSpec(memory_space=pl.ANY)
IN_VMEM = pl.BlockSpec(memory_space=pltpu.VMEM)
IN_SMEM = pl.BlockSpec(memory_space=pltpu.SMEM)


def call(body, name, micros, out_shape, args, after=(), scratch=(), mib=24):
    specs = [IN_SMEM if x.dtype == jnp.int32 else IN_VMEM for x in args]
    extra = len(after)

    def run(*refs):
        n = len(args)
        body(*refs[:n], *refs[n + extra :])

    return pl.pallas_call(
        run,
        in_specs=specs + [ANYWHERE] * extra,
        out_specs=jax.tree.map(lambda _: IN_VMEM, out_shape),
        out_shape=out_shape,
        scratch_shapes=list(scratch),
        compiler_params=pltpu.CompilerParams(vmem_limit_bytes=mib * MIB),
        cost_estimate=pl.CostEstimate(
            flops=int(micros * 1.1e9), bytes_accessed=0, transcendentals=0
        ),
        name=name,
    )(*args, *after)


def fence(value, *after):
    return pl.pallas_call(
        lambda *refs: None,
        in_specs=[ANYWHERE] * (1 + len(after)),
        out_specs=ANYWHERE,
        out_shape=jax.ShapeDtypeStruct(value.shape, value.dtype),
        input_output_aliases={0: 0},
        compiler_params=pltpu.CompilerParams(vmem_limit_bytes=MIB),
        cost_estimate=pl.CostEstimate(flops=0, bytes_accessed=0, transcendentals=0),
        name="fence",
    )(value, *after)


def in_hbm(value):
    return pltpu.with_memory_space_constraint(value, pltpu.HBM)


def shape(dims, dtype=BF16):
    return jax.ShapeDtypeStruct(tuple(dims), dtype)


def dot(a, b):
    return jnp.dot(a, b, preferred_element_type=F32)


def dot_t(a, b):
    return lax.dot_general(a, b, (((1,), (1,)), ((), ())), preferred_element_type=F32)


def dot_l(a, b):
    return lax.dot_general(a, b, (((0,), (0,)), ((), ())), preferred_element_type=F32)


def pack_kernel(pos_ref, tok_hbm, tok_ref, *rest):
    out_refs, sems = rest[:-1], rest[-1]
    spans = [slice(r * STRIDE, (r + 1) * STRIDE) for r in range(ROWS)]
    copies = [
        pltpu.make_async_copy(tok_hbm.at[at], tok_ref.at[at], sems.at[r])
        for r, at in enumerate(spans)
    ]
    for c in copies:
        c.start()
    for c in copies:
        c.wait()
    per_owner = STRIDE // len(out_refs)
    part = ROWS * SUB
    for k, out_ref in enumerate(out_refs):
        d = pos_ref[0] ^ k
        rows = [
            tok_ref[pl.ds(pl.multiple_of(r * STRIDE + d * per_owner, per_owner), per_owner), :]
            for r in range(ROWS)
        ]
        rows = [x.astype(F32) for x in rows]
        for g in range(per_owner // SUB):
            piece = jnp.concatenate([x[g * SUB : (g + 1) * SUB] for x in rows], 0)
            out_ref[g * part : (g + 1) * part, :] = piece.astype(BF16)


def pack(pos, tokens, owners):
    message = shape((tokens.shape[0] // owners, tokens.shape[1]))
    outs = pl.pallas_call(
        pack_kernel,
        in_specs=[IN_SMEM, ANYWHERE],
        out_specs=[IN_VMEM] * (1 + owners),
        out_shape=[shape(tokens.shape)] + [message] * owners,
        scratch_shapes=[pltpu.SemaphoreType.DMA((ROWS,))],
        compiler_params=pltpu.CompilerParams(vmem_limit_bytes=8 * MIB),
        cost_estimate=pl.CostEstimate(flops=0, bytes_accessed=2 * MIB, transcendentals=0),
        name="pack_tokens",
    )(pos, in_hbm(tokens))
    return outs[0], outs[1:]


def stage_kernel(order_ref, wq, wk, wv, wo, after, oq, ok, ov, oo, sems):
    copies = []
    for w, o in ((wq, oq), (wk, ok), (wv, ov), (wo, oo)):
        part = w.shape[0] // 4
        for p in range(4):
            place = p if w is wo else order_ref[p]
            rows = pl.ds(pl.multiple_of(place * part, part), part)
            to = slice(p * part, (p + 1) * part)
            sem = sems.at[len(copies)]
            copies.append(pltpu.make_async_copy(w.at[rows], o.at[to], sem))
    for c in copies:
        c.start()
    for c in copies:
        c.wait()


def stage(order, weights, after):
    return pl.pallas_call(
        stage_kernel,
        in_specs=[IN_SMEM] + [ANYWHERE] * 5,
        out_specs=[IN_VMEM] * 4,
        out_shape=[shape(w.shape) for w in weights],
        scratch_shapes=[pltpu.SemaphoreType.DMA((16,))],
        compiler_params=pltpu.CompilerParams(vmem_limit_bytes=16 * MIB),
        cost_estimate=pl.CostEstimate(flops=0, bytes_accessed=0, transcendentals=0),
        name="stage_weights",
    )(order, *weights, after)


def gathered(x_refs, at, w_ref):
    width = x_refs[0].shape[1]
    total = None
    for p, x_ref in enumerate(x_refs):
        term = dot(x_ref[at, :], w_ref[p * width : (p + 1) * width, :])
        total = term if total is None else total + term
    return total.astype(BF16)


def half_kernel(x0, x1, wq, wk, wv, *outs):
    width = x0.shape[1]
    for w, out in zip((wq, wk, wv), outs):
        out[...] = dot(x0[...], w[:width, :]) + dot(x1[...], w[width : 2 * width, :])


def half_sums(own, core, weights, after):
    shapes = [shape(own.shape, F32)] * 3
    return call(half_kernel, "half_sums", 0, shapes, (own, core, *weights), after)


def near_kernel(x0, x1, x2, x3, wq, wk, wv, *outs):
    everything = slice(0, x0.shape[0])
    for w, out in zip((wq, wk, wv), outs):
        out[...] = gathered((x0, x1, x2, x3), everything, w)


def halo_kernel(x0, x1, x2, x3, wk, wv, out_ref):
    rows = x0.shape[0]
    at = slice(rows - STRIDE, rows)
    out_ref[:STRIDE, :] = gathered((x0, x1, x2, x3), at, wk)
    out_ref[STRIDE:, :] = gathered((x0, x1, x2, x3), at, wv)


def query_kernel(x0, x1, x2, x3, wq, q_ref):
    q_ref[...] = gathered((x0, x1, x2, x3), slice(0, x0.shape[0]), wq)


def key_kernel(x0, x1, x2, x3, wk, wv, halo, k_ref, v_ref):
    upto = x0.shape[0] - STRIDE
    k_ref[upto:, :] = halo[:STRIDE, :]
    v_ref[upto:, :] = halo[STRIDE:, :]
    for w, out in ((wk, k_ref), (wv, v_ref)):
        out[:upto, :] = gathered((x0, x1, x2, x3), slice(0, upto), w)


def softmax_columns(s):
    m = jnp.maximum(jnp.max(s, 0, keepdims=True), FLOOR)
    p = jnp.exp2((s - m) * SCALE2)
    total = jnp.maximum(jnp.sum(p, 0, keepdims=True), 1.0)
    return p, total, m * SCALE2 + jnp.log2(total)


def local_kernel(pos_ref, q_ref, k_ref, v_ref, halo_ref, *outs):
    out_refs, lse_refs = outs[: len(CHUNKS)], outs[len(CHUNKS) :]
    owners = out_refs[0].shape[0]
    groups = STRIDE // owners // SUB
    block = pos_ref[0]
    u = lax.broadcasted_iota(jnp.int32, (STRIDE, STRIDE), 0)
    t = lax.broadcasted_iota(jnp.int32, (STRIDE, STRIDE), 1)
    current = u <= t
    low = jnp.where(block == 0, -1e30, 0.0).astype(F32)
    for r in range(ROWS):
        lses = []
        here = slice(r * STRIDE, (r + 1) * STRIDE)
        back = slice((r - 1) * STRIDE, r * STRIDE)
        heads = [slice(h * DH, (h + 1) * DH) for h in range(HEADS)]
        scores = []
        for cols in heads:
            q = q_ref[here, cols]
            s_prev = dot_t(k_ref[back, cols] if r else halo_ref[:STRIDE, cols], q)
            if r == 0:
                s_prev = s_prev + low
            scores.append(jnp.where(current, dot_t(k_ref[here, cols], q), s_prev))
        parts = []
        for p, total, lse in [softmax_columns(s) for s in scores]:
            now = jnp.where(current, p, 0.0).astype(BF16)
            before = jnp.where(current, 0.0, p).astype(BF16)
            parts.append((now, before, 1.0 / total))
            lses.append(lse)
        results = []
        for cols, (now, before, share) in zip(heads, parts):
            v_prev = v_ref[back, cols] if r else halo_ref[STRIDE:, cols]
            results.append((dot_l(v_ref[here, cols], now) + dot_l(v_prev, before)) * share)
        for cols, o in zip(heads, results):
            o = o.T
            for d in range(owners):
                for chunk, out_ref in zip(CHUNKS, out_refs):
                    for n, g in enumerate(chunk):
                        at = (d * groups + g) * SUB
                        to = (n * ROWS + r) * SUB
                        out_ref[d, to : to + SUB, cols] = o[at : at + SUB]
        lses.append(jnp.zeros((128 - HEADS, STRIDE), F32))
        turned = jnp.concatenate(lses, 0).T
        for chunk, lse_ref in zip(CHUNKS, lse_refs):
            for n, g in enumerate(chunk):
                total = None
                for d in range(owners):
                    at = (d * groups + g) * SUB
                    moved = pltpu.roll(turned[at : at + SUB], 8 * (block ^ d), 1)
                    total = moved if total is None else total + moved
                to = (n * ROWS + r) * SUB
                lse_ref[to : to + SUB, :] = total


def local_part(pos, q, k, v, halo, owners, after):
    rows, width = q.shape
    sizes = [len(chunk) * ROWS * SUB for chunk in CHUNKS]
    shapes = [shape((owners, m, width), F32) for m in sizes] + [shape((m, 128), F32) for m in sizes]
    outs = call(local_kernel, "local_part", 5, shapes, (pos, q, k, v, halo), after)
    return list(zip(outs[: len(sizes)], outs[len(sizes) :]))


def column_kernel(pos_ref, x2, x3a, x3b, hq, hk, hv, wq, wk, wv, nq, nk, nv, *rest):
    out_refs, scratch = rest[:-3], rest[-3:]
    owners, message, width = scratch[0].shape
    groups = message // (ROWS * SUB)
    for h, w, near, a in zip((hq, hk, hv), (wq, wk, wv), (nq, nk, nv), scratch):
        total = h[...] + dot(x2[...], w[2 * width : 3 * width, :])
        diagonal = [dot(x[...], w[3 * width :, :]) for x in (x3a, x3b)]
        total = total + jnp.concatenate(diagonal, 0)
        a[:NEAR] = near[...].reshape(NEAR, message, width)
        a[NEAR:] = total.astype(BF16).reshape(owners - NEAR, message, width)
    part = ROWS * SUB
    size = owners * part

    def row_and_class(dim):
        i = lax.broadcasted_iota(jnp.int32, (size, size), dim)
        return ((i // part) ^ pos_ref[0]) * ROWS + (i % part) // SUB, i % SUB

    (row_j, class_j), (row_i, class_i) = row_and_class(0), row_and_class(1)
    earlier = jnp.logical_and(class_i == class_j, row_i > row_j)
    stats = []
    heads = [slice(h * DH, (h + 1) * DH) for h in range(HEADS)]
    for pair in range(0, groups, 2):
        tiles = [(g, h) for g in range(pair, pair + 2) for h in range(HEADS)]
        operands = [
            [a[:, g * part : (g + 1) * part, heads[h]].reshape(size, DH) for a in scratch]
            for g, h in tiles
        ]
        scores = [jnp.where(earlier, dot_t(k, q), -1e30) for q, k, _ in operands]
        parts = [softmax_columns(s) for s in scores]
        results = [
            dot_l(v, p.astype(BF16)) * (1.0 / total)
            for (_, _, v), (p, total, _) in zip(operands, parts)
        ]
        lses = [lse for _, _, lse in parts]
        for (g, h), o in zip(tiles, results):
            o = o.T.astype(BF16)
            to = h * message + g * part
            for n in range(owners):
                out_refs[n][to : to + part, :] = o[n * part : (n + 1) * part]
        for some in (lses[:HEADS], lses[HEADS:]):
            stats.append(jnp.concatenate(some + some, 0))
    upper = lax.broadcasted_iota(jnp.int32, (8, 128), 0) < HEADS
    blank = [jnp.zeros((8, 128 - message), F32)] if message < 128 else []
    for n in range(owners):
        x = jnp.concatenate([s[:, n * part : (n + 1) * part] for s in stats] + blank, 1)
        hi = x.astype(BF16).astype(F32)
        mid = (x - hi).astype(BF16).astype(F32)
        lo = x - hi - mid
        tail = jnp.concatenate([jnp.where(upper, hi, lo), jnp.where(upper, mid, 0.0)], 0)
        to = HEADS * message
        out_refs[n][to : to + 16, :] = tail.astype(BF16)


def column_part(pos, across, halves, weights, near, owners, after):
    tokens, width = across.shape
    message = tokens // (owners - NEAR)
    shapes = [shape((HEADS * message + 16, DH))] * owners
    scratch = [pltpu.VMEM((owners, message, width), BF16)] * 3
    middle = tokens // 2
    diagonal = [swap(x, 1) for x in (across[:middle], across[middle:])]
    args = (pos, across, *diagonal, *halves, *weights, *near)
    return call(column_kernel, "column_part", 0, shapes, args, after, scratch)


def mix_kernel(share, pos_ref, *refs):
    count = 2 * len(CHUNKS)
    local_refs, col_refs, (own_ref, send_ref) = refs[:count], refs[count:-2], refs[-2:]
    per_owner = own_ref.shape[1] // len(share)
    first_core = pos_ref[1] == 0
    base = 0
    for chunk, loc_ref, lse_ref in zip(CHUNKS, local_refs[::2], local_refs[1::2]):
        message = loc_ref.shape[1]
        size = HEADS * message + 16
        tiles = [jnp.zeros((8, 128), F32)] * 16
        for k, col_ref in zip(share, col_refs):
            tail = col_ref[base + HEADS * message : base + size, :].astype(F32)
            tiles[k] = tail[:8] + tail[8:]
        turned = jnp.concatenate(tiles, 0).T[:message]
        col_lse = turned + pltpu.roll(turned, 124, 1)
        loc_lse = lse_ref[...]
        top = jnp.maximum(col_lse, loc_lse)
        w_col = jnp.exp2(col_lse - top)
        w_loc = jnp.exp2(loc_lse - top)
        scale = 1.0 / (w_col + w_loc)
        w_col = w_col * scale
        w_loc = w_loc * scale
        for n, (k, col_ref) in enumerate(zip(share, col_refs)):
            d = pos_ref[0] ^ k
            for h in range(HEADS):
                cols = slice(h * DH, (h + 1) * DH)
                at = slice(8 * k + h, 8 * k + h + 1)
                col = col_ref[base + h * message : base + (h + 1) * message, :].astype(F32)
                both = loc_ref[d, :, cols] * w_loc[:, at] + col * w_col[:, at]
                rows = []
                for r in range(ROWS):
                    starts = [(m * ROWS + r) * SUB for m in range(len(chunk))]
                    rows.append(jnp.concatenate([both[t : t + SUB] for t in starts], 0))
                to = n * per_owner + chunk[0] * SUB
                spot = slice(to, to + len(chunk) * SUB)
                for x in range(2):
                    even, odd = rows[2 * x], rows[2 * x + 1]
                    own_ref[x, spot, cols] = jnp.where(first_core, even, odd).astype(BF16)
                    send_ref[x, spot, cols] = jnp.where(first_core, odd, even).astype(BF16)
        base += size


def mix(pos, share, columns, locals_, after):
    owners, _, width = locals_[0][0].shape
    tokens = len(share) * STRIDE // owners
    shapes = [shape((2, tokens, width))] * 2
    args = (pos, *[x for pair in locals_ for x in pair], *columns)
    return call(functools.partial(mix_kernel, share), "mix", 2, shapes, args, after)


def out_kernel(here, pos_ref, a_ref, b_ref, wa_ref, wb_ref, out_ref):
    side = pos_ref[2] if here else 1 - pos_ref[2]
    a, b = a_ref[side], b_ref[side]
    tile = 512
    for n in range(0, out_ref.shape[1], tile):
        at = slice(n, n + tile)
        total = dot(a, wa_ref[:, at]) + dot(b, wb_ref[:, at])
        out_ref[:, at] = total.astype(out_ref.dtype)


def out_project(pos, here, own, other, w_own, w_other):
    dims = shape((own.shape[1], w_own.shape[1]), F32 if here else BF16)
    body = functools.partial(out_kernel, here)
    return call(body, "out_project", 2, dims, (pos, own, other, w_own, w_other))


def join_kernel(share, pos_ref, keep, got, *rest):
    out_hbm, joined, sems = rest[-3:]
    span = keep.shape[0] // len(share)
    joined[...] = (keep[...] + got[...].astype(F32)).astype(BF16)
    copies = []
    for n, k in enumerate(share):
        to = pl.ds(pl.multiple_of((pos_ref[0] ^ k) * span, span), span)
        rows = slice(n * span, (n + 1) * span)
        copies.append(pltpu.make_async_copy(joined.at[rows], out_hbm.at[to], sems.at[n]))
    for c in copies:
        c.start()
    for c in copies:
        c.wait()


def join(pos, share, keep, got, earlier):
    return pl.pallas_call(
        functools.partial(join_kernel, share),
        in_specs=[IN_SMEM, IN_VMEM, IN_VMEM] + [ANYWHERE] * len(earlier),
        out_specs=ANYWHERE,
        out_shape=shape((STRIDE, keep.shape[1])),
        input_output_aliases={3: 0} if earlier else {},
        scratch_shapes=[pltpu.VMEM(keep.shape, BF16), pltpu.SemaphoreType.DMA((len(share),))],
        compiler_params=pltpu.CompilerParams(vmem_limit_bytes=16 * MIB),
        cost_estimate=pl.CostEstimate(flops=int(1.1e9), bytes_accessed=0, transcendentals=0),
        name="join",
    )(pos, keep, got, *earlier)


def swap(value, distance):
    return lax.ppermute(value, "head", [(i, i ^ distance) for i in range(4)])


def exchange(messages):
    peers = lax.axis_size("seq")

    def move(value, k):
        return lax.ppermute(value, "seq", [(i, i ^ k) for i in range(peers)]) if k else value

    return [move(m, k) for k, m in enumerate(messages)]


def chunked(tokens, w_query, w_key, w_value, w_out):
    owners = lax.axis_size("seq")
    head = lax.axis_index("head")
    block = lax.axis_index("seq")
    order = jnp.bitwise_xor(jnp.arange(4, dtype=jnp.int32), head.astype(jnp.int32))
    pos = jnp.stack([block, head % 2, head // 2]).astype(jnp.int32)
    rows, width = tokens.shape

    across = swap(tokens, 2)
    block_tokens, sent = pack(pos, tokens, owners)
    messages = exchange(sent)
    near_own = jnp.concatenate(messages[:NEAR], 0)
    near_core, near_across = swap(near_own, 1), swap(near_own, 2)
    far_own = jnp.concatenate(messages[NEAR:], 0)
    far_core, far_across = swap(far_own, 1), swap(far_own, 2)
    *weights, w_own = stage(order, (w_query, w_key, w_value, w_out), messages[1])
    w_other = swap(w_own, 1)
    block_core = swap(fence(block_tokens, near_own, far_own), 1)
    across = fence(across, near_across, far_own)
    pieces = (block_tokens, block_core, across, swap(across, 1))
    own_halo = call(
        halo_kernel, "project_halo", 1.5, shape((2 * STRIDE, width)), (*pieces, *weights[1:])
    )
    halo = lax.ppermute(own_halo, "seq", [(i, i + 1) for i in range(owners - 1)])
    q = call(
        query_kernel,
        "project_query",
        0,
        shape((rows, width)),
        (*pieces, weights[0]),
        (far_own,),
    )
    near = call(
        near_kernel,
        "project_near",
        0,
        [shape(near_own.shape)] * 3,
        (near_own, near_core, near_across, swap(near_across, 1), *weights),
        (q,),
    )
    far_half = half_sums(far_own, far_core, weights, (near[0],))
    far_across = fence(far_across, near[0])
    columns = column_part(pos, far_across, far_half, weights, near, owners, (w_other,))
    k, v = call(
        key_kernel,
        "project_key",
        0,
        [shape((rows, width))] * 2,
        (*pieces, *weights[1:], own_halo),
        (columns[0], halo),
    )
    locals_ = local_part(pos, q, k, v, halo, owners, (columns[0],))
    columns = list(columns)
    columns = exchange(columns)
    sums, after = [], ()
    for share in SHARES:
        own, send = mix(pos, share, [columns[n] for n in share], locals_, after)
        other = swap(send, 1)
        out = out_project(pos, False, own, other, w_own, w_other)
        keep = out_project(pos, True, own, other, w_own, w_other)
        sums.append((keep, swap(out, 2)))
        after = (out,)
    result = ()
    for share, (keep, got) in zip(SHARES, sums):
        result = (join(pos, share, keep, got, result),)
    return result[0]


def from_behind(value, axis, by):
    peers = lax.axis_size(axis)
    pairs = [(i, i + by) for i in range(peers) if 0 <= i + by < peers]
    return lax.ppermute(value, axis, pairs)


def general(tokens, w_query, w_key, w_value, w_out):
    tok_rows = tokens.shape[0]
    head_width = w_query.shape[1]
    head_count = head_width // DH
    score_scale = DH ** (-0.5)
    shard_piece = lax.all_gather(tokens, "head", axis=1, tiled=True)
    query_full, key_full, value_full = tuple(
        (
            jnp.dot(shard_piece, weight, preferred_element_type=jnp.float32)
            for weight in (w_query, w_key, w_value)
        )
    )
    query = query_full.astype(jnp.bfloat16).reshape(tok_rows, head_count, DH)
    key_heads = key_full.astype(jnp.bfloat16).reshape(tok_rows, head_count, DH)
    value_heads = value_full.astype(jnp.bfloat16).reshape(tok_rows, head_count, DH)
    prev_keys, prev_values = from_behind((key_heads[-STRIDE:], value_heads[-STRIDE:]), "seq", 1)
    blocks = tok_rows // STRIDE
    extended_keys = jnp.concatenate([prev_keys, key_heads], 0)
    extended_values = jnp.concatenate([prev_values, value_heads], 0)
    window_keys = jnp.concatenate(
        [
            extended_keys[:tok_rows].reshape(blocks, STRIDE, head_count, DH),
            extended_keys[STRIDE:].reshape(blocks, STRIDE, head_count, DH),
        ],
        1,
    )
    window_values = jnp.concatenate(
        [
            extended_values[:tok_rows].reshape(blocks, STRIDE, head_count, DH),
            extended_values[STRIDE:].reshape(blocks, STRIDE, head_count, DH),
        ],
        1,
    )
    query_blocks = query.reshape(blocks, STRIDE, head_count, DH)
    scores = (
        jnp.einsum("bthd,buhd->bhtu", query_blocks, window_keys, preferred_element_type=jnp.float32)
        * score_scale
    )
    first_position = lax.axis_index("seq") * tok_rows
    block_index = jnp.arange(blocks)[:, None, None, None]
    query_index = jnp.arange(STRIDE)[None, None, :, None]
    key_index = jnp.arange(2 * STRIDE)[None, None, None, :]
    allowed = (
        (key_index > query_index)
        & (key_index <= query_index + STRIDE)
        & (first_position + block_index * STRIDE + key_index - STRIDE >= 0)
    )
    local_top = jnp.max(jnp.where(allowed, scores, -1e30), axis=-1)
    local_weights = jnp.where(allowed, jnp.exp(scores - local_top[..., None]), 0.0)
    local_total = jnp.sum(local_weights, axis=-1)
    local_out = jnp.einsum(
        "bhtu,buhd->bthd",
        local_weights.astype(jnp.bfloat16),
        window_values,
        preferred_element_type=jnp.float32,
    )
    local_out = local_out.reshape(tok_rows, head_count, DH)
    local_top = local_top.transpose(0, 2, 1).reshape(tok_rows, head_count)
    local_total = local_total.transpose(0, 2, 1).reshape(tok_rows, head_count)
    row_count = tok_rows // STRIDE
    query_class = lax.all_to_all(
        query.reshape(row_count, STRIDE, head_count, DH),
        "seq",
        split_axis=1,
        concat_axis=0,
        tiled=True,
    )
    key_class = lax.all_to_all(
        key_heads.reshape(row_count, STRIDE, head_count, DH),
        "seq",
        split_axis=1,
        concat_axis=0,
        tiled=True,
    )
    value_class = lax.all_to_all(
        value_heads.reshape(row_count, STRIDE, head_count, DH),
        "seq",
        split_axis=1,
        concat_axis=0,
        tiled=True,
    )
    row_total = query_class.shape[0]
    class_scores = (
        jnp.einsum("rchd,schd->chrs", query_class, key_class, preferred_element_type=jnp.float32)
        * score_scale
    )
    earlier = (
        jnp.arange(row_total)[None, None, :, None] > jnp.arange(row_total)[None, None, None, :]
    )
    class_top = jnp.max(jnp.where(earlier, class_scores, -1e30), axis=-1)
    class_weights = jnp.where(earlier, jnp.exp(class_scores - class_top[..., None]), 0.0)
    class_total = jnp.sum(class_weights, axis=-1)
    summed = jnp.einsum(
        "chrs,schd->rchd",
        class_weights.astype(jnp.bfloat16),
        value_class,
        preferred_element_type=jnp.float32,
    )
    floor_total = jnp.maximum(class_total, 1.0).transpose(2, 0, 1)
    class_out = (summed / floor_total[..., None]).astype(jnp.bfloat16)
    class_top_rows = class_top.transpose(2, 0, 1)
    class_total_rows = class_total.transpose(2, 0, 1)
    column_out = class_out
    column_top = class_top_rows
    column_total = class_total_rows
    column_out, column_top, column_total = (
        lax.all_to_all(column_out, "seq", split_axis=0, concat_axis=1, tiled=True),
        lax.all_to_all(
            column_top.astype(jnp.bfloat16), "seq", split_axis=0, concat_axis=1, tiled=True
        ).astype(column_top.dtype),
        lax.all_to_all(
            column_total.astype(jnp.bfloat16), "seq", split_axis=0, concat_axis=1, tiled=True
        ).astype(column_total.dtype),
    )
    column_out = column_out.reshape(tok_rows, head_count, DH)
    column_top = column_top.reshape(tok_rows, head_count)
    column_total = column_total.reshape(tok_rows, head_count)
    top_score = jnp.maximum(local_top, column_top)
    local_weight = jnp.exp(local_top - top_score)
    column_weight = column_total * jnp.exp(column_top - top_score)
    denominator = local_total * local_weight + column_weight
    mixed = (
        local_out * local_weight[..., None]
        + column_out.astype(jnp.float32) * column_weight[..., None]
    ) / denominator[..., None]
    mixed = mixed.astype(jnp.bfloat16).reshape(tok_rows, head_width)
    return lax.psum_scatter(
        jnp.dot(mixed, w_out, preferred_element_type=jnp.float32).astype(jnp.bfloat16),
        "head",
        scatter_dimension=0,
        tiled=True,
    )


def shards(tokens, w_query, w_key, w_value, w_out):
    rows, width = w_query.shape
    fits = (
        lax.axis_size("seq") == PEERS
        and lax.axis_size("head") == 4
        and tokens.shape == (ROWS * STRIDE, HEADS * DH)
        and (rows, width) == (4 * HEADS * DH, HEADS * DH)
    )
    plan = chunked if fits else general
    return plan(tokens, w_query, w_key, w_value, w_out)


def solution(mesh):
    in_specs = (
        P("seq", "head"),
        P(None, "head"),
        P(None, "head"),
        P(None, "head"),
        P("head", None),
    )
    out_specs = P(("seq", "head"), None)
    return jax.shard_map(shards, mesh=mesh, in_specs=in_specs, out_specs=out_specs, check_vma=False)
```

```python
import functools

import jax
import jax.numpy as jnp
from jax import lax
from jax.experimental import pallas as pl
from jax.experimental.pallas import tpu as pltpu
from jax.sharding import PartitionSpec as P

DH = 128
STRIDE = 256
HEADS = 4
ROWS = 4
SUB = 8
CHUNKS = ((0, 1, 2, 3),)
NEAR = 4
PEERS = 8
SHARES = ((1, 4, 5, 3, 2, 0), (6, 7))
SCALE2 = DH ** (-0.5) * 1.4426950408889634
FLOOR = -1e29
MIB = 1024 * 1024
F32 = jnp.float32
BF16 = jnp.bfloat16


ANYWHERE = pl.BlockSpec(memory_space=pl.ANY)
IN_VMEM = pl.BlockSpec(memory_space=pltpu.VMEM)
IN_SMEM = pl.BlockSpec(memory_space=pltpu.SMEM)


def call(body, name, micros, out_shape, args, after=(), scratch=(), mib=24):
    specs = [IN_SMEM if x.dtype == jnp.int32 else IN_VMEM for x in args]
    extra = len(after)

    def run(*refs):
        n = len(args)
        body(*refs[:n], *refs[n + extra :])

    return pl.pallas_call(
        run,
        in_specs=specs + [ANYWHERE] * extra,
        out_specs=jax.tree.map(lambda _: IN_VMEM, out_shape),
        out_shape=out_shape,
        scratch_shapes=list(scratch),
        compiler_params=pltpu.CompilerParams(vmem_limit_bytes=mib * MIB),
        cost_estimate=pl.CostEstimate(
            flops=int(micros * 1.1e9), bytes_accessed=0, transcendentals=0
        ),
        name=name,
    )(*args, *after)


def fence(value, *after):
    return pl.pallas_call(
        lambda *refs: None,
        in_specs=[ANYWHERE] * (1 + len(after)),
        out_specs=ANYWHERE,
        out_shape=jax.ShapeDtypeStruct(value.shape, value.dtype),
        input_output_aliases={0: 0},
        compiler_params=pltpu.CompilerParams(vmem_limit_bytes=MIB),
        cost_estimate=pl.CostEstimate(flops=0, bytes_accessed=0, transcendentals=0),
        name="fence",
    )(value, *after)


def in_hbm(value):
    return pltpu.with_memory_space_constraint(value, pltpu.HBM)


def shape(dims, dtype=BF16):
    return jax.ShapeDtypeStruct(tuple(dims), dtype)


def dot(a, b):
    return jnp.dot(a, b, preferred_element_type=F32)


def dot_t(a, b):
    return lax.dot_general(a, b, (((1,), (1,)), ((), ())), preferred_element_type=F32)


def dot_l(a, b):
    return lax.dot_general(a, b, (((0,), (0,)), ((), ())), preferred_element_type=F32)


def pack_kernel(pos_ref, tok_hbm, tok_ref, *rest):
    out_refs, sems = rest[:-1], rest[-1]
    spans = [slice(r * STRIDE, (r + 1) * STRIDE) for r in range(ROWS)]
    copies = [
        pltpu.make_async_copy(tok_hbm.at[at], tok_ref.at[at], sems.at[r])
        for r, at in enumerate(spans)
    ]
    for c in copies:
        c.start()
    for c in copies:
        c.wait()
    per_owner = STRIDE // len(out_refs)
    part = ROWS * SUB
    for k, out_ref in enumerate(out_refs):
        d = pos_ref[0] ^ k
        rows = [
            tok_ref[pl.ds(pl.multiple_of(r * STRIDE + d * per_owner, per_owner), per_owner), :]
            for r in range(ROWS)
        ]
        rows = [x.astype(F32) for x in rows]
        for g in range(per_owner // SUB):
            piece = jnp.concatenate([x[g * SUB : (g + 1) * SUB] for x in rows], 0)
            out_ref[g * part : (g + 1) * part, :] = piece.astype(BF16)


def pack(pos, tokens, owners):
    message = shape((tokens.shape[0] // owners, tokens.shape[1]))
    outs = pl.pallas_call(
        pack_kernel,
        in_specs=[IN_SMEM, ANYWHERE],
        out_specs=[IN_VMEM] * (1 + owners),
        out_shape=[shape(tokens.shape)] + [message] * owners,
        scratch_shapes=[pltpu.SemaphoreType.DMA((ROWS,))],
        compiler_params=pltpu.CompilerParams(vmem_limit_bytes=8 * MIB),
        cost_estimate=pl.CostEstimate(flops=0, bytes_accessed=2 * MIB, transcendentals=0),
        name="pack_tokens",
    )(pos, in_hbm(tokens))
    return outs[0], outs[1:]


def stage_kernel(order_ref, wq, wk, wv, wo, after, oq, ok, ov, oo, sems):
    copies = []
    for w, o in ((wq, oq), (wk, ok), (wv, ov), (wo, oo)):
        part = w.shape[0] // 4
        for p in range(4):
            place = p if w is wo else order_ref[p]
            rows = pl.ds(pl.multiple_of(place * part, part), part)
            to = slice(p * part, (p + 1) * part)
            sem = sems.at[len(copies)]
            copies.append(pltpu.make_async_copy(w.at[rows], o.at[to], sem))
    for c in copies:
        c.start()
    for c in copies:
        c.wait()


def stage(order, weights, after):
    return pl.pallas_call(
        stage_kernel,
        in_specs=[IN_SMEM] + [ANYWHERE] * 5,
        out_specs=[IN_VMEM] * 4,
        out_shape=[shape(w.shape) for w in weights],
        scratch_shapes=[pltpu.SemaphoreType.DMA((16,))],
        compiler_params=pltpu.CompilerParams(vmem_limit_bytes=16 * MIB),
        cost_estimate=pl.CostEstimate(flops=0, bytes_accessed=0, transcendentals=0),
        name="stage_weights",
    )(order, *weights, after)


def gathered(x_refs, at, w_ref):
    width = x_refs[0].shape[1]
    total = None
    for p, x_ref in enumerate(x_refs):
        term = dot(x_ref[at, :], w_ref[p * width : (p + 1) * width, :])
        total = term if total is None else total + term
    return total.astype(BF16)


def half_kernel(x0, x1, wq, wk, wv, *outs):
    width = x0.shape[1]
    for w, out in zip((wq, wk, wv), outs):
        out[...] = dot(x0[...], w[:width, :]) + dot(x1[...], w[width : 2 * width, :])


def half_sums(own, core, weights, after):
    shapes = [shape(own.shape, F32)] * 3
    return call(half_kernel, "half_sums", 0, shapes, (own, core, *weights), after)


def near_kernel(x0, x1, x2, x3, wq, wk, wv, *outs):
    everything = slice(0, x0.shape[0])
    for w, out in zip((wq, wk, wv), outs):
        out[...] = gathered((x0, x1, x2, x3), everything, w)


def halo_kernel(x0, x1, x2, x3, wk, wv, out_ref):
    rows = x0.shape[0]
    at = slice(rows - STRIDE, rows)
    out_ref[:STRIDE, :] = gathered((x0, x1, x2, x3), at, wk)
    out_ref[STRIDE:, :] = gathered((x0, x1, x2, x3), at, wv)


def query_kernel(x0, x1, x2, x3, wq, q_ref):
    q_ref[...] = gathered((x0, x1, x2, x3), slice(0, x0.shape[0]), wq)


def key_kernel(x0, x1, x2, x3, wk, wv, halo, k_ref, v_ref):
    upto = x0.shape[0] - STRIDE
    k_ref[upto:, :] = halo[:STRIDE, :]
    v_ref[upto:, :] = halo[STRIDE:, :]
    for w, out in ((wk, k_ref), (wv, v_ref)):
        out[:upto, :] = gathered((x0, x1, x2, x3), slice(0, upto), w)


def softmax_columns(s):
    m = jnp.maximum(jnp.max(s, 0, keepdims=True), FLOOR)
    p = jnp.exp2((s - m) * SCALE2)
    total = jnp.maximum(jnp.sum(p, 0, keepdims=True), 1.0)
    return p, total, m * SCALE2 + jnp.log2(total)


def local_kernel(pos_ref, q_ref, k_ref, v_ref, halo_ref, *outs):
    out_refs, lse_refs = outs[: len(CHUNKS)], outs[len(CHUNKS) :]
    owners = out_refs[0].shape[0]
    groups = STRIDE // owners // SUB
    block = pos_ref[0]
    u = lax.broadcasted_iota(jnp.int32, (STRIDE, STRIDE), 0)
    t = lax.broadcasted_iota(jnp.int32, (STRIDE, STRIDE), 1)
    current = u <= t
    low = jnp.where(block == 0, -1e30, 0.0).astype(F32)
    for r in range(ROWS):
        lses = []
        here = slice(r * STRIDE, (r + 1) * STRIDE)
        back = slice((r - 1) * STRIDE, r * STRIDE)
        heads = [slice(h * DH, (h + 1) * DH) for h in range(HEADS)]
        scores = []
        for cols in heads:
            q = q_ref[here, cols]
            s_prev = dot_t(k_ref[back, cols] if r else halo_ref[:STRIDE, cols], q)
            if r == 0:
                s_prev = s_prev + low
            scores.append(jnp.where(current, dot_t(k_ref[here, cols], q), s_prev))
        parts = []
        for p, total, lse in [softmax_columns(s) for s in scores]:
            now = jnp.where(current, p, 0.0).astype(BF16)
            before = jnp.where(current, 0.0, p).astype(BF16)
            parts.append((now, before, 1.0 / total))
            lses.append(lse)
        results = []
        for cols, (now, before, share) in zip(heads, parts):
            v_prev = v_ref[back, cols] if r else halo_ref[STRIDE:, cols]
            results.append((dot_l(v_ref[here, cols], now) + dot_l(v_prev, before)) * share)
        for cols, o in zip(heads, results):
            o = o.T
            for d in range(owners):
                for chunk, out_ref in zip(CHUNKS, out_refs):
                    for n, g in enumerate(chunk):
                        at = (d * groups + g) * SUB
                        to = (n * ROWS + r) * SUB
                        out_ref[d, to : to + SUB, cols] = o[at : at + SUB]
        lses.append(jnp.zeros((128 - HEADS, STRIDE), F32))
        turned = jnp.concatenate(lses, 0).T
        for chunk, lse_ref in zip(CHUNKS, lse_refs):
            for n, g in enumerate(chunk):
                total = None
                for d in range(owners):
                    at = (d * groups + g) * SUB
                    moved = pltpu.roll(turned[at : at + SUB], 8 * (block ^ d), 1)
                    total = moved if total is None else total + moved
                to = (n * ROWS + r) * SUB
                lse_ref[to : to + SUB, :] = total


def local_part(pos, q, k, v, halo, owners, after):
    rows, width = q.shape
    sizes = [len(chunk) * ROWS * SUB for chunk in CHUNKS]
    shapes = [shape((owners, m, width), F32) for m in sizes] + [shape((m, 128), F32) for m in sizes]
    outs = call(local_kernel, "local_part", 5, shapes, (pos, q, k, v, halo), after)
    return list(zip(outs[: len(sizes)], outs[len(sizes) :]))


def column_kernel(pos_ref, x2, x3a, x3b, hq, hk, hv, wq, wk, wv, nq, nk, nv, *rest):
    out_refs, scratch = rest[:-3], rest[-3:]
    owners, message, width = scratch[0].shape
    groups = message // (ROWS * SUB)
    for h, w, near, a in zip((hq, hk, hv), (wq, wk, wv), (nq, nk, nv), scratch):
        total = h[...] + dot(x2[...], w[2 * width : 3 * width, :])
        diagonal = [dot(x[...], w[3 * width :, :]) for x in (x3a, x3b)]
        total = total + jnp.concatenate(diagonal, 0)
        a[:NEAR] = near[...].reshape(NEAR, message, width)
        a[NEAR:] = total.astype(BF16).reshape(owners - NEAR, message, width)
    part = ROWS * SUB
    size = owners * part

    def row_and_class(dim):
        i = lax.broadcasted_iota(jnp.int32, (size, size), dim)
        return ((i // part) ^ pos_ref[0]) * ROWS + (i % part) // SUB, i % SUB

    (row_j, class_j), (row_i, class_i) = row_and_class(0), row_and_class(1)
    earlier = jnp.logical_and(class_i == class_j, row_i > row_j)
    stats = []
    heads = [slice(h * DH, (h + 1) * DH) for h in range(HEADS)]
    for pair in range(0, groups, 2):
        tiles = [(g, h) for g in range(pair, pair + 2) for h in range(HEADS)]
        operands = [
            [a[:, g * part : (g + 1) * part, heads[h]].reshape(size, DH) for a in scratch]
            for g, h in tiles
        ]
        scores = [jnp.where(earlier, dot_t(k, q), -1e30) for q, k, _ in operands]
        parts = [softmax_columns(s) for s in scores]
        results = [
            dot_l(v, p.astype(BF16)) * (1.0 / total)
            for (_, _, v), (p, total, _) in zip(operands, parts)
        ]
        lses = [lse for _, _, lse in parts]
        for (g, h), o in zip(tiles, results):
            o = o.T.astype(BF16)
            to = h * message + g * part
            for n in range(owners):
                out_refs[n][to : to + part, :] = o[n * part : (n + 1) * part]
        for some in (lses[:HEADS], lses[HEADS:]):
            stats.append(jnp.concatenate(some + some, 0))
    upper = lax.broadcasted_iota(jnp.int32, (8, 128), 0) < HEADS
    blank = [jnp.zeros((8, 128 - message), F32)] if message < 128 else []
    for n in range(owners):
        x = jnp.concatenate([s[:, n * part : (n + 1) * part] for s in stats] + blank, 1)
        hi = x.astype(BF16).astype(F32)
        mid = (x - hi).astype(BF16).astype(F32)
        lo = x - hi - mid
        tail = jnp.concatenate([jnp.where(upper, hi, lo), jnp.where(upper, mid, 0.0)], 0)
        to = HEADS * message
        out_refs[n][to : to + 16, :] = tail.astype(BF16)


def column_part(pos, across, halves, weights, near, owners, after):
    tokens, width = across.shape
    message = tokens // (owners - NEAR)
    shapes = [shape((HEADS * message + 16, DH))] * owners
    scratch = [pltpu.VMEM((owners, message, width), BF16)] * 3
    middle = tokens // 2
    diagonal = [swap(x, 1) for x in (across[:middle], across[middle:])]
    args = (pos, across, *diagonal, *halves, *weights, *near)
    return call(column_kernel, "column_part", 0, shapes, args, after, scratch)


def mix_kernel(share, pos_ref, *refs):
    count = 2 * len(CHUNKS)
    local_refs, col_refs, (own_ref, send_ref) = refs[:count], refs[count:-2], refs[-2:]
    per_owner = own_ref.shape[1] // len(share)
    first_core = pos_ref[1] == 0
    base = 0
    for chunk, loc_ref, lse_ref in zip(CHUNKS, local_refs[::2], local_refs[1::2]):
        message = loc_ref.shape[1]
        size = HEADS * message + 16
        tiles = [jnp.zeros((8, 128), F32)] * 16
        for k, col_ref in zip(share, col_refs):
            tail = col_ref[base + HEADS * message : base + size, :].astype(F32)
            tiles[k] = tail[:8] + tail[8:]
        turned = jnp.concatenate(tiles, 0).T[:message]
        col_lse = turned + pltpu.roll(turned, 124, 1)
        loc_lse = lse_ref[...]
        top = jnp.maximum(col_lse, loc_lse)
        w_col = jnp.exp2(col_lse - top)
        w_loc = jnp.exp2(loc_lse - top)
        scale = 1.0 / (w_col + w_loc)
        w_col = w_col * scale
        w_loc = w_loc * scale
        for n, (k, col_ref) in enumerate(zip(share, col_refs)):
            d = pos_ref[0] ^ k
            for h in range(HEADS):
                cols = slice(h * DH, (h + 1) * DH)
                at = slice(8 * k + h, 8 * k + h + 1)
                col = col_ref[base + h * message : base + (h + 1) * message, :].astype(F32)
                both = loc_ref[d, :, cols] * w_loc[:, at] + col * w_col[:, at]
                rows = []
                for r in range(ROWS):
                    starts = [(m * ROWS + r) * SUB for m in range(len(chunk))]
                    rows.append(jnp.concatenate([both[t : t + SUB] for t in starts], 0))
                to = n * per_owner + chunk[0] * SUB
                spot = slice(to, to + len(chunk) * SUB)
                for x in range(2):
                    even, odd = rows[2 * x], rows[2 * x + 1]
                    own_ref[x, spot, cols] = jnp.where(first_core, even, odd).astype(BF16)
                    send_ref[x, spot, cols] = jnp.where(first_core, odd, even).astype(BF16)
        base += size


def mix(pos, share, columns, locals_, after):
    owners, _, width = locals_[0][0].shape
    tokens = len(share) * STRIDE // owners
    shapes = [shape((2, tokens, width))] * 2
    args = (pos, *[x for pair in locals_ for x in pair], *columns)
    return call(functools.partial(mix_kernel, share), "mix", 2, shapes, args, after)


def out_kernel(here, pos_ref, a_ref, b_ref, wa_ref, wb_ref, out_ref):
    side = pos_ref[2] if here else 1 - pos_ref[2]
    a, b = a_ref[side], b_ref[side]
    tile = 512
    for n in range(0, out_ref.shape[1], tile):
        at = slice(n, n + tile)
        total = dot(a, wa_ref[:, at]) + dot(b, wb_ref[:, at])
        out_ref[:, at] = total.astype(out_ref.dtype)


def out_project(pos, here, own, other, w_own, w_other):
    dims = shape((own.shape[1], w_own.shape[1]), F32 if here else BF16)
    body = functools.partial(out_kernel, here)
    return call(body, "out_project", 2, dims, (pos, own, other, w_own, w_other))


def join_kernel(share, pos_ref, keep, got, *rest):
    out_hbm, joined, sems = rest[-3:]
    span = keep.shape[0] // len(share)
    joined[...] = (keep[...] + got[...].astype(F32)).astype(BF16)
    copies = []
    for n, k in enumerate(share):
        to = pl.ds(pl.multiple_of((pos_ref[0] ^ k) * span, span), span)
        rows = slice(n * span, (n + 1) * span)
        copies.append(pltpu.make_async_copy(joined.at[rows], out_hbm.at[to], sems.at[n]))
    for c in copies:
        c.start()
    for c in copies:
        c.wait()


def join(pos, share, keep, got, earlier):
    return pl.pallas_call(
        functools.partial(join_kernel, share),
        in_specs=[IN_SMEM, IN_VMEM, IN_VMEM] + [ANYWHERE] * len(earlier),
        out_specs=ANYWHERE,
        out_shape=shape((STRIDE, keep.shape[1])),
        input_output_aliases={3: 0} if earlier else {},
        scratch_shapes=[pltpu.VMEM(keep.shape, BF16), pltpu.SemaphoreType.DMA((len(share),))],
        compiler_params=pltpu.CompilerParams(vmem_limit_bytes=16 * MIB),
        cost_estimate=pl.CostEstimate(flops=int(1.1e9), bytes_accessed=0, transcendentals=0),
        name="join",
    )(pos, keep, got, *earlier)


def swap(value, distance):
    return lax.ppermute(value, "head", [(i, i ^ distance) for i in range(4)])


def exchange(messages):
    peers = lax.axis_size("seq")

    def move(value, k):
        return lax.ppermute(value, "seq", [(i, i ^ k) for i in range(peers)]) if k else value

    return [move(m, k) for k, m in enumerate(messages)]


def chunked(tokens, w_query, w_key, w_value, w_out):
    owners = lax.axis_size("seq")
    head = lax.axis_index("head")
    block = lax.axis_index("seq")
    order = jnp.bitwise_xor(jnp.arange(4, dtype=jnp.int32), head.astype(jnp.int32))
    pos = jnp.stack([block, head % 2, head // 2]).astype(jnp.int32)
    rows, width = tokens.shape

    across = swap(tokens, 2)
    block_tokens, sent = pack(pos, tokens, owners)
    messages = exchange(sent)
    near_own = jnp.concatenate(messages[:NEAR], 0)
    near_core, near_across = swap(near_own, 1), swap(near_own, 2)
    far_own = jnp.concatenate(messages[NEAR:], 0)
    far_core, far_across = swap(far_own, 1), swap(far_own, 2)
    *weights, w_own = stage(order, (w_query, w_key, w_value, w_out), messages[1])
    w_other = swap(w_own, 1)
    block_core = swap(fence(block_tokens, near_own, far_own), 1)
    across = fence(across, near_across, far_own)
    pieces = (block_tokens, block_core, across, swap(across, 1))
    own_halo = call(
        halo_kernel, "project_halo", 1.5, shape((2 * STRIDE, width)), (*pieces, *weights[1:])
    )
    halo = lax.ppermute(own_halo, "seq", [(i, i + 1) for i in range(owners - 1)])
    q = call(
        query_kernel,
        "project_query",
        0,
        shape((rows, width)),
        (*pieces, weights[0]),
        (far_own,),
    )
    near = call(
        near_kernel,
        "project_near",
        0,
        [shape(near_own.shape)] * 3,
        (near_own, near_core, near_across, swap(near_across, 1), *weights),
        (q,),
    )
    far_half = half_sums(far_own, far_core, weights, (near[0],))
    far_across = fence(far_across, near[0])
    columns = column_part(pos, far_across, far_half, weights, near, owners, (w_other,))
    k, v = call(
        key_kernel,
        "project_key",
        0,
        [shape((rows, width))] * 2,
        (*pieces, *weights[1:], own_halo),
        (columns[0], halo),
    )
    locals_ = local_part(pos, q, k, v, halo, owners, (columns[0],))
    columns = list(columns)
    columns = exchange(columns)
    sums, after = [], ()
    for share in SHARES:
        own, send = mix(pos, share, [columns[n] for n in share], locals_, after)
        other = swap(send, 1)
        out = out_project(pos, False, own, other, w_own, w_other)
        keep = out_project(pos, True, own, other, w_own, w_other)
        sums.append((keep, swap(out, 2)))
        after = (out,)
    result = ()
    for share, (keep, got) in zip(SHARES, sums):
        result = (join(pos, share, keep, got, result),)
    return result[0]


def from_behind(value, axis, by):
    peers = lax.axis_size(axis)
    pairs = [(i, i + by) for i in range(peers) if 0 <= i + by < peers]
    return lax.ppermute(value, axis, pairs)


def general(tokens, w_query, w_key, w_value, w_out):
    tok_rows = tokens.shape[0]
    head_width = w_query.shape[1]
    head_count = head_width // DH
    score_scale = DH ** (-0.5)
    shard_piece = lax.all_gather(tokens, "head", axis=1, tiled=True)
    query_full, key_full, value_full = tuple(
        (
            jnp.dot(shard_piece, weight, preferred_element_type=jnp.float32)
            for weight in (w_query, w_key, w_value)
        )
    )
    query = query_full.astype(jnp.bfloat16).reshape(tok_rows, head_count, DH)
    key_heads = key_full.astype(jnp.bfloat16).reshape(tok_rows, head_count, DH)
    value_heads = value_full.astype(jnp.bfloat16).reshape(tok_rows, head_count, DH)
    prev_keys, prev_values = from_behind((key_heads[-STRIDE:], value_heads[-STRIDE:]), "seq", 1)
    blocks = tok_rows // STRIDE
    extended_keys = jnp.concatenate([prev_keys, key_heads], 0)
    extended_values = jnp.concatenate([prev_values, value_heads], 0)
    window_keys = jnp.concatenate(
        [
            extended_keys[:tok_rows].reshape(blocks, STRIDE, head_count, DH),
            extended_keys[STRIDE:].reshape(blocks, STRIDE, head_count, DH),
        ],
        1,
    )
    window_values = jnp.concatenate(
        [
            extended_values[:tok_rows].reshape(blocks, STRIDE, head_count, DH),
            extended_values[STRIDE:].reshape(blocks, STRIDE, head_count, DH),
        ],
        1,
    )
    query_blocks = query.reshape(blocks, STRIDE, head_count, DH)
    scores = (
        jnp.einsum("bthd,buhd->bhtu", query_blocks, window_keys, preferred_element_type=jnp.float32)
        * score_scale
    )
    first_position = lax.axis_index("seq") * tok_rows
    block_index = jnp.arange(blocks)[:, None, None, None]
    query_index = jnp.arange(STRIDE)[None, None, :, None]
    key_index = jnp.arange(2 * STRIDE)[None, None, None, :]
    allowed = (
        (key_index > query_index)
        & (key_index <= query_index + STRIDE)
        & (first_position + block_index * STRIDE + key_index - STRIDE >= 0)
    )
    local_top = jnp.max(jnp.where(allowed, scores, -1e30), axis=-1)
    local_weights = jnp.where(allowed, jnp.exp(scores - local_top[..., None]), 0.0)
    local_total = jnp.sum(local_weights, axis=-1)
    local_out = jnp.einsum(
        "bhtu,buhd->bthd",
        local_weights.astype(jnp.bfloat16),
        window_values,
        preferred_element_type=jnp.float32,
    )
    local_out = local_out.reshape(tok_rows, head_count, DH)
    local_top = local_top.transpose(0, 2, 1).reshape(tok_rows, head_count)
    local_total = local_total.transpose(0, 2, 1).reshape(tok_rows, head_count)
    row_count = tok_rows // STRIDE
    query_class = lax.all_to_all(
        query.reshape(row_count, STRIDE, head_count, DH),
        "seq",
        split_axis=1,
        concat_axis=0,
        tiled=True,
    )
    key_class = lax.all_to_all(
        key_heads.reshape(row_count, STRIDE, head_count, DH),
        "seq",
        split_axis=1,
        concat_axis=0,
        tiled=True,
    )
    value_class = lax.all_to_all(
        value_heads.reshape(row_count, STRIDE, head_count, DH),
        "seq",
        split_axis=1,
        concat_axis=0,
        tiled=True,
    )
    row_total = query_class.shape[0]
    class_scores = (
        jnp.einsum("rchd,schd->chrs", query_class, key_class, preferred_element_type=jnp.float32)
        * score_scale
    )
    earlier = (
        jnp.arange(row_total)[None, None, :, None] > jnp.arange(row_total)[None, None, None, :]
    )
    class_top = jnp.max(jnp.where(earlier, class_scores, -1e30), axis=-1)
    class_weights = jnp.where(earlier, jnp.exp(class_scores - class_top[..., None]), 0.0)
    class_total = jnp.sum(class_weights, axis=-1)
    summed = jnp.einsum(
        "chrs,schd->rchd",
        class_weights.astype(jnp.bfloat16),
        value_class,
        preferred_element_type=jnp.float32,
    )
    floor_total = jnp.maximum(class_total, 1.0).transpose(2, 0, 1)
    class_out = (summed / floor_total[..., None]).astype(jnp.bfloat16)
    class_top_rows = class_top.transpose(2, 0, 1)
    class_total_rows = class_total.transpose(2, 0, 1)
    column_out = class_out
    column_top = class_top_rows
    column_total = class_total_rows
    column_out, column_top, column_total = (
        lax.all_to_all(column_out, "seq", split_axis=0, concat_axis=1, tiled=True),
        lax.all_to_all(
            column_top.astype(jnp.bfloat16), "seq", split_axis=0, concat_axis=1, tiled=True
        ).astype(column_top.dtype),
        lax.all_to_all(
            column_total.astype(jnp.bfloat16), "seq", split_axis=0, concat_axis=1, tiled=True
        ).astype(column_total.dtype),
    )
    column_out = column_out.reshape(tok_rows, head_count, DH)
    column_top = column_top.reshape(tok_rows, head_count)
    column_total = column_total.reshape(tok_rows, head_count)
    top_score = jnp.maximum(local_top, column_top)
    local_weight = jnp.exp(local_top - top_score)
    column_weight = column_total * jnp.exp(column_top - top_score)
    denominator = local_total * local_weight + column_weight
    mixed = (
        local_out * local_weight[..., None]
        + column_out.astype(jnp.float32) * column_weight[..., None]
    ) / denominator[..., None]
    mixed = mixed.astype(jnp.bfloat16).reshape(tok_rows, head_width)
    return lax.psum_scatter(
        jnp.dot(mixed, w_out, preferred_element_type=jnp.float32).astype(jnp.bfloat16),
        "head",
        scatter_dimension=0,
        tiled=True,
    )


def shards(tokens, w_query, w_key, w_value, w_out):
    rows, width = w_query.shape
    fits = (
        lax.axis_size("seq") == PEERS
        and lax.axis_size("head") == 4
        and tokens.shape == (ROWS * STRIDE, HEADS * DH)
        and (rows, width) == (4 * HEADS * DH, HEADS * DH)
    )
    plan = chunked if fits else general
    return plan(tokens, w_query, w_key, w_value, w_out)


def solution(mesh):
    in_specs = (
        P("seq", "head"),
        P(None, "head"),
        P(None, "head"),
        P(None, "head"),
        P("head", None),
    )
    out_specs = P(("seq", "head"), None)
    return jax.shard_map(shards, mesh=mesh, in_specs=in_specs, out_specs=out_specs, check_vma=False)
```

```python
import functools

import jax
import jax.numpy as jnp
from jax import lax
from jax.experimental import pallas as pl
from jax.experimental.pallas import tpu as pltpu
from jax.sharding import PartitionSpec as P

DH = 128
STRIDE = 256
HEADS = 4
ROWS = 4
SUB = 8
CHUNKS = ((0, 1, 2, 3),)
NEAR = 4
PEERS = 8
SHARES = ((4, 5, 3, 2, 1, 0), (6, 7))
SCALE2 = DH ** (-0.5) * 1.4426950408889634
FLOOR = -1e29
MIB = 1024 * 1024
F32 = jnp.float32
BF16 = jnp.bfloat16


ANYWHERE = pl.BlockSpec(memory_space=pl.ANY)
IN_VMEM = pl.BlockSpec(memory_space=pltpu.VMEM)
IN_SMEM = pl.BlockSpec(memory_space=pltpu.SMEM)


def call(body, name, micros, out_shape, args, after=(), scratch=(), mib=24):
    specs = [IN_SMEM if x.dtype == jnp.int32 else IN_VMEM for x in args]
    extra = len(after)

    def run(*refs):
        n = len(args)
        body(*refs[:n], *refs[n + extra :])

    return pl.pallas_call(
        run,
        in_specs=specs + [ANYWHERE] * extra,
        out_specs=jax.tree.map(lambda _: IN_VMEM, out_shape),
        out_shape=out_shape,
        scratch_shapes=list(scratch),
        compiler_params=pltpu.CompilerParams(vmem_limit_bytes=mib * MIB),
        cost_estimate=pl.CostEstimate(
            flops=int(micros * 1.1e9), bytes_accessed=0, transcendentals=0
        ),
        name=name,
    )(*args, *after)


def fence(value, *after):
    return pl.pallas_call(
        lambda *refs: None,
        in_specs=[ANYWHERE] * (1 + len(after)),
        out_specs=ANYWHERE,
        out_shape=jax.ShapeDtypeStruct(value.shape, value.dtype),
        input_output_aliases={0: 0},
        compiler_params=pltpu.CompilerParams(vmem_limit_bytes=MIB),
        cost_estimate=pl.CostEstimate(flops=0, bytes_accessed=0, transcendentals=0),
        name="fence",
    )(value, *after)


def in_hbm(value):
    return pltpu.with_memory_space_constraint(value, pltpu.HBM)


def shape(dims, dtype=BF16):
    return jax.ShapeDtypeStruct(tuple(dims), dtype)


def dot(a, b):
    return jnp.dot(a, b, preferred_element_type=F32)


def dot_t(a, b):
    return lax.dot_general(a, b, (((1,), (1,)), ((), ())), preferred_element_type=F32)


def dot_l(a, b):
    return lax.dot_general(a, b, (((0,), (0,)), ((), ())), preferred_element_type=F32)


def pack_kernel(pos_ref, tok_hbm, tok_ref, *rest):
    out_refs, sems = rest[:-1], rest[-1]
    spans = [slice(r * STRIDE, (r + 1) * STRIDE) for r in range(ROWS)]
    copies = [
        pltpu.make_async_copy(tok_hbm.at[at], tok_ref.at[at], sems.at[r])
        for r, at in enumerate(spans)
    ]
    for c in copies:
        c.start()
    for c in copies:
        c.wait()
    per_owner = STRIDE // len(out_refs)
    part = ROWS * SUB
    for k, out_ref in enumerate(out_refs):
        d = pos_ref[0] ^ k
        rows = [
            tok_ref[pl.ds(pl.multiple_of(r * STRIDE + d * per_owner, per_owner), per_owner), :]
            for r in range(ROWS)
        ]
        rows = [x.astype(F32) for x in rows]
        for g in range(per_owner // SUB):
            piece = jnp.concatenate([x[g * SUB : (g + 1) * SUB] for x in rows], 0)
            out_ref[g * part : (g + 1) * part, :] = piece.astype(BF16)


def pack(pos, tokens, owners):
    message = shape((tokens.shape[0] // owners, tokens.shape[1]))
    outs = pl.pallas_call(
        pack_kernel,
        in_specs=[IN_SMEM, ANYWHERE],
        out_specs=[IN_VMEM] * (1 + owners),
        out_shape=[shape(tokens.shape)] + [message] * owners,
        scratch_shapes=[pltpu.SemaphoreType.DMA((ROWS,))],
        compiler_params=pltpu.CompilerParams(vmem_limit_bytes=8 * MIB),
        cost_estimate=pl.CostEstimate(flops=0, bytes_accessed=2 * MIB, transcendentals=0),
        name="pack_tokens",
    )(pos, in_hbm(tokens))
    return outs[0], outs[1:]


def stage_kernel(order_ref, wq, wk, wv, wo, after, oq, ok, ov, oo, sems):
    copies = []
    for w, o in ((wq, oq), (wk, ok), (wv, ov), (wo, oo)):
        part = w.shape[0] // 4
        for p in range(4):
            place = p if w is wo else order_ref[p]
            rows = pl.ds(pl.multiple_of(place * part, part), part)
            to = slice(p * part, (p + 1) * part)
            sem = sems.at[len(copies)]
            copies.append(pltpu.make_async_copy(w.at[rows], o.at[to], sem))
    for c in copies:
        c.start()
    for c in copies:
        c.wait()


def stage(order, weights, after):
    return pl.pallas_call(
        stage_kernel,
        in_specs=[IN_SMEM] + [ANYWHERE] * 5,
        out_specs=[IN_VMEM] * 4,
        out_shape=[shape(w.shape) for w in weights],
        scratch_shapes=[pltpu.SemaphoreType.DMA((16,))],
        compiler_params=pltpu.CompilerParams(vmem_limit_bytes=16 * MIB),
        cost_estimate=pl.CostEstimate(flops=0, bytes_accessed=0, transcendentals=0),
        name="stage_weights",
    )(order, *weights, after)


def gathered(x_refs, at, w_ref):
    width = x_refs[0].shape[1]
    total = None
    for p, x_ref in enumerate(x_refs):
        term = dot(x_ref[at, :], w_ref[p * width : (p + 1) * width, :])
        total = term if total is None else total + term
    return total.astype(BF16)


def half_kernel(x0, x1, wq, wk, wv, *outs):
    width = x0.shape[1]
    for w, out in zip((wq, wk, wv), outs):
        out[...] = dot(x0[...], w[:width, :]) + dot(x1[...], w[width : 2 * width, :])


def half_sums(own, core, weights, after):
    shapes = [shape(own.shape, F32)] * 3
    return call(half_kernel, "half_sums", 0, shapes, (own, core, *weights), after)


def near_kernel(x0, x1, x2, x3, wq, wk, wv, *outs):
    everything = slice(0, x0.shape[0])
    for w, out in zip((wq, wk, wv), outs):
        out[...] = gathered((x0, x1, x2, x3), everything, w)


def halo_kernel(x0, x1, x2, x3, wk, wv, out_ref):
    rows = x0.shape[0]
    at = slice(rows - STRIDE, rows)
    out_ref[:STRIDE, :] = gathered((x0, x1, x2, x3), at, wk)
    out_ref[STRIDE:, :] = gathered((x0, x1, x2, x3), at, wv)


def project_kernel(x0, x1, x2, x3, wq, wk, wv, halo, q_ref, k_ref, v_ref):
    rows = x0.shape[0]
    upto = rows - STRIDE
    k_ref[upto:, :] = halo[:STRIDE, :]
    v_ref[upto:, :] = halo[STRIDE:, :]
    for w, out, at in ((wq, q_ref, rows), (wk, k_ref, upto), (wv, v_ref, upto)):
        out[:at, :] = gathered((x0, x1, x2, x3), slice(0, at), w)


def softmax_columns(s):
    m = jnp.maximum(jnp.max(s, 0, keepdims=True), FLOOR)
    p = jnp.exp2((s - m) * SCALE2)
    total = jnp.maximum(jnp.sum(p, 0, keepdims=True), 1.0)
    return p, total, m * SCALE2 + jnp.log2(total)


def local_kernel(pos_ref, q_ref, k_ref, v_ref, halo_ref, *outs):
    out_refs, lse_refs = outs[: len(CHUNKS)], outs[len(CHUNKS) :]
    owners = out_refs[0].shape[0]
    groups = STRIDE // owners // SUB
    block = pos_ref[0]
    u = lax.broadcasted_iota(jnp.int32, (STRIDE, STRIDE), 0)
    t = lax.broadcasted_iota(jnp.int32, (STRIDE, STRIDE), 1)
    current = u <= t
    low = jnp.where(block == 0, -1e30, 0.0).astype(F32)
    for r in range(ROWS):
        lses = []
        here = slice(r * STRIDE, (r + 1) * STRIDE)
        back = slice((r - 1) * STRIDE, r * STRIDE)
        heads = [slice(h * DH, (h + 1) * DH) for h in range(HEADS)]
        scores = []
        for cols in heads:
            q = q_ref[here, cols]
            s_prev = dot_t(k_ref[back, cols] if r else halo_ref[:STRIDE, cols], q)
            if r == 0:
                s_prev = s_prev + low
            scores.append(jnp.where(current, dot_t(k_ref[here, cols], q), s_prev))
        parts = []
        for p, total, lse in [softmax_columns(s) for s in scores]:
            now = jnp.where(current, p, 0.0).astype(BF16)
            before = jnp.where(current, 0.0, p).astype(BF16)
            parts.append((now, before, 1.0 / total))
            lses.append(lse)
        results = []
        for cols, (now, before, share) in zip(heads, parts):
            v_prev = v_ref[back, cols] if r else halo_ref[STRIDE:, cols]
            results.append((dot_l(v_ref[here, cols], now) + dot_l(v_prev, before)) * share)
        for cols, o in zip(heads, results):
            o = o.T
            for d in range(owners):
                for chunk, out_ref in zip(CHUNKS, out_refs):
                    for n, g in enumerate(chunk):
                        at = (d * groups + g) * SUB
                        to = (n * ROWS + r) * SUB
                        out_ref[d, to : to + SUB, cols] = o[at : at + SUB]
        lses.append(jnp.zeros((128 - HEADS, STRIDE), F32))
        turned = jnp.concatenate(lses, 0).T
        for chunk, lse_ref in zip(CHUNKS, lse_refs):
            for n, g in enumerate(chunk):
                total = None
                for d in range(owners):
                    at = (d * groups + g) * SUB
                    moved = pltpu.roll(turned[at : at + SUB], 8 * (block ^ d), 1)
                    total = moved if total is None else total + moved
                to = (n * ROWS + r) * SUB
                lse_ref[to : to + SUB, :] = total


def local_part(pos, q, k, v, halo, owners, after):
    rows, width = q.shape
    sizes = [len(chunk) * ROWS * SUB for chunk in CHUNKS]
    shapes = [shape((owners, m, width), F32) for m in sizes] + [shape((m, 128), F32) for m in sizes]
    outs = call(local_kernel, "local_part", 5, shapes, (pos, q, k, v, halo), after)
    return list(zip(outs[: len(sizes)], outs[len(sizes) :]))


def column_kernel(pos_ref, x2, x3a, x3b, hq, hk, hv, wq, wk, wv, nq, nk, nv, *rest):
    out_refs, scratch = rest[:-3], rest[-3:]
    owners, message, width = scratch[0].shape
    groups = message // (ROWS * SUB)
    for h, w, near, a in zip((hq, hk, hv), (wq, wk, wv), (nq, nk, nv), scratch):
        total = h[...] + dot(x2[...], w[2 * width : 3 * width, :])
        diagonal = [dot(x[...], w[3 * width :, :]) for x in (x3a, x3b)]
        total = total + jnp.concatenate(diagonal, 0)
        a[:NEAR] = near[...].reshape(NEAR, message, width)
        a[NEAR:] = total.astype(BF16).reshape(owners - NEAR, message, width)
    part = ROWS * SUB
    size = owners * part

    def row_and_class(dim):
        i = lax.broadcasted_iota(jnp.int32, (size, size), dim)
        return ((i // part) ^ pos_ref[0]) * ROWS + (i % part) // SUB, i % SUB

    (row_j, class_j), (row_i, class_i) = row_and_class(0), row_and_class(1)
    earlier = jnp.logical_and(class_i == class_j, row_i > row_j)
    stats = []
    heads = [slice(h * DH, (h + 1) * DH) for h in range(HEADS)]
    for pair in range(0, groups, 2):
        tiles = [(g, h) for g in range(pair, pair + 2) for h in range(HEADS)]
        operands = [
            [a[:, g * part : (g + 1) * part, heads[h]].reshape(size, DH) for a in scratch]
            for g, h in tiles
        ]
        scores = [jnp.where(earlier, dot_t(k, q), -1e30) for q, k, _ in operands]
        parts = [softmax_columns(s) for s in scores]
        results = [
            dot_l(v, p.astype(BF16)) * (1.0 / total)
            for (_, _, v), (p, total, _) in zip(operands, parts)
        ]
        lses = [lse for _, _, lse in parts]
        for (g, h), o in zip(tiles, results):
            o = o.T.astype(BF16)
            to = h * message + g * part
            for n in range(owners):
                out_refs[n][to : to + part, :] = o[n * part : (n + 1) * part]
        for some in (lses[:HEADS], lses[HEADS:]):
            stats.append(jnp.concatenate(some + some, 0))
    upper = lax.broadcasted_iota(jnp.int32, (8, 128), 0) < HEADS
    blank = [jnp.zeros((8, 128 - message), F32)] if message < 128 else []
    for n in range(owners):
        x = jnp.concatenate([s[:, n * part : (n + 1) * part] for s in stats] + blank, 1)
        hi = x.astype(BF16).astype(F32)
        mid = (x - hi).astype(BF16).astype(F32)
        lo = x - hi - mid
        tail = jnp.concatenate([jnp.where(upper, hi, lo), jnp.where(upper, mid, 0.0)], 0)
        to = HEADS * message
        out_refs[n][to : to + 16, :] = tail.astype(BF16)


def column_part(pos, across, halves, weights, near, owners, after):
    tokens, width = across.shape
    message = tokens // (owners - NEAR)
    shapes = [shape((HEADS * message + 16, DH))] * owners
    scratch = [pltpu.VMEM((owners, message, width), BF16)] * 3
    middle = tokens // 2
    diagonal = [swap(x, 1) for x in (across[:middle], across[middle:])]
    args = (pos, across, *diagonal, *halves, *weights, *near)
    return call(column_kernel, "column_part", 0, shapes, args, after, scratch)


def mix_kernel(share, pos_ref, *refs):
    count = 2 * len(CHUNKS)
    local_refs, col_refs, (own_ref, send_ref) = refs[:count], refs[count:-2], refs[-2:]
    per_owner = own_ref.shape[1] // len(share)
    first_core = pos_ref[1] == 0
    base = 0
    for chunk, loc_ref, lse_ref in zip(CHUNKS, local_refs[::2], local_refs[1::2]):
        message = loc_ref.shape[1]
        size = HEADS * message + 16
        tiles = [jnp.zeros((8, 128), F32)] * 16
        for k, col_ref in zip(share, col_refs):
            tail = col_ref[base + HEADS * message : base + size, :].astype(F32)
            tiles[k] = tail[:8] + tail[8:]
        turned = jnp.concatenate(tiles, 0).T[:message]
        col_lse = turned + pltpu.roll(turned, 124, 1)
        loc_lse = lse_ref[...]
        top = jnp.maximum(col_lse, loc_lse)
        w_col = jnp.exp2(col_lse - top)
        w_loc = jnp.exp2(loc_lse - top)
        scale = 1.0 / (w_col + w_loc)
        w_col = w_col * scale
        w_loc = w_loc * scale
        for n, (k, col_ref) in enumerate(zip(share, col_refs)):
            d = pos_ref[0] ^ k
            for h in range(HEADS):
                cols = slice(h * DH, (h + 1) * DH)
                at = slice(8 * k + h, 8 * k + h + 1)
                col = col_ref[base + h * message : base + (h + 1) * message, :].astype(F32)
                both = loc_ref[d, :, cols] * w_loc[:, at] + col * w_col[:, at]
                rows = []
                for r in range(ROWS):
                    starts = [(m * ROWS + r) * SUB for m in range(len(chunk))]
                    rows.append(jnp.concatenate([both[t : t + SUB] for t in starts], 0))
                to = n * per_owner + chunk[0] * SUB
                spot = slice(to, to + len(chunk) * SUB)
                for x in range(2):
                    even, odd = rows[2 * x], rows[2 * x + 1]
                    own_ref[x, spot, cols] = jnp.where(first_core, even, odd).astype(BF16)
                    send_ref[x, spot, cols] = jnp.where(first_core, odd, even).astype(BF16)
        base += size


def mix(pos, share, columns, locals_, after):
    owners, _, width = locals_[0][0].shape
    tokens = len(share) * STRIDE // owners
    shapes = [shape((2, tokens, width))] * 2
    args = (pos, *[x for pair in locals_ for x in pair], *columns)
    return call(functools.partial(mix_kernel, share), "mix", 2, shapes, args, after)


def out_kernel(here, pos_ref, a_ref, b_ref, wa_ref, wb_ref, out_ref):
    side = pos_ref[2] if here else 1 - pos_ref[2]
    a, b = a_ref[side], b_ref[side]
    tile = 512
    for n in range(0, out_ref.shape[1], tile):
        at = slice(n, n + tile)
        total = dot(a, wa_ref[:, at]) + dot(b, wb_ref[:, at])
        out_ref[:, at] = total.astype(out_ref.dtype)


def out_project(pos, here, own, other, w_own, w_other):
    dims = shape((own.shape[1], w_own.shape[1]), F32 if here else BF16)
    body = functools.partial(out_kernel, here)
    return call(body, "out_project", 2, dims, (pos, own, other, w_own, w_other))


def join_kernel(share, pos_ref, keep, got, *rest):
    out_hbm, joined, sems = rest[-3:]
    span = keep.shape[0] // len(share)
    joined[...] = (keep[...] + got[...].astype(F32)).astype(BF16)
    copies = []
    for n, k in enumerate(share):
        to = pl.ds(pl.multiple_of((pos_ref[0] ^ k) * span, span), span)
        rows = slice(n * span, (n + 1) * span)
        copies.append(pltpu.make_async_copy(joined.at[rows], out_hbm.at[to], sems.at[n]))
    for c in copies:
        c.start()
    for c in copies:
        c.wait()


def join(pos, share, keep, got, earlier):
    return pl.pallas_call(
        functools.partial(join_kernel, share),
        in_specs=[IN_SMEM, IN_VMEM, IN_VMEM] + [ANYWHERE] * len(earlier),
        out_specs=ANYWHERE,
        out_shape=shape((STRIDE, keep.shape[1])),
        input_output_aliases={3: 0} if earlier else {},
        scratch_shapes=[pltpu.VMEM(keep.shape, BF16), pltpu.SemaphoreType.DMA((len(share),))],
        compiler_params=pltpu.CompilerParams(vmem_limit_bytes=16 * MIB),
        cost_estimate=pl.CostEstimate(flops=int(1.1e9), bytes_accessed=0, transcendentals=0),
        name="join",
    )(pos, keep, got, *earlier)


def swap(value, distance):
    return lax.ppermute(value, "head", [(i, i ^ distance) for i in range(4)])


def exchange(messages):
    peers = lax.axis_size("seq")

    def move(value, k):
        return lax.ppermute(value, "seq", [(i, i ^ k) for i in range(peers)]) if k else value

    return [move(m, k) for k, m in enumerate(messages)]


def chunked(tokens, w_query, w_key, w_value, w_out):
    owners = lax.axis_size("seq")
    head = lax.axis_index("head")
    block = lax.axis_index("seq")
    order = jnp.bitwise_xor(jnp.arange(4, dtype=jnp.int32), head.astype(jnp.int32))
    pos = jnp.stack([block, head % 2, head // 2]).astype(jnp.int32)
    rows, width = tokens.shape

    across = swap(tokens, 2)
    block_tokens, sent = pack(pos, tokens, owners)
    messages = exchange(sent)
    near_own = jnp.concatenate(messages[:NEAR], 0)
    near_core, near_across = swap(near_own, 1), swap(near_own, 2)
    far_own = jnp.concatenate(messages[NEAR:], 0)
    far_core, far_across = swap(far_own, 1), swap(far_own, 2)
    *weights, w_own = stage(order, (w_query, w_key, w_value, w_out), messages[1])
    w_other = swap(w_own, 1)
    block_core = swap(fence(block_tokens, near_own, far_own), 1)
    across = fence(across, near_across, far_own)
    pieces = (block_tokens, block_core, across, swap(across, 1))
    own_halo = call(
        halo_kernel, "project_halo", 1.5, shape((2 * STRIDE, width)), (*pieces, *weights[1:])
    )
    halo = lax.ppermute(own_halo, "seq", [(i, i + 1) for i in range(owners - 1)])
    near = call(
        near_kernel,
        "project_near",
        0,
        [shape(near_own.shape)] * 3,
        (near_own, near_core, near_across, swap(near_across, 1), *weights),
        (own_halo,),
    )
    far_half = half_sums(far_own, far_core, weights, (near[0],))
    far_across = fence(far_across, near[0])
    columns = column_part(pos, far_across, far_half, weights, near, owners, (w_other,))
    q, k, v = call(
        project_kernel,
        "project_block",
        0,
        [shape((rows, width))] * 3,
        (*pieces, *weights, own_halo),
        (columns[0], halo),
    )
    locals_ = local_part(pos, q, k, v, halo, owners, (columns[0],))
    columns = list(columns)
    columns = exchange(columns)
    sums, after = [], ()
    for share in SHARES:
        own, send = mix(pos, share, [columns[n] for n in share], locals_, after)
        other = swap(send, 1)
        out = out_project(pos, False, own, other, w_own, w_other)
        keep = out_project(pos, True, own, other, w_own, w_other)
        sums.append((keep, swap(out, 2)))
        after = (out,)
    result = ()
    for share, (keep, got) in zip(SHARES, sums):
        result = (join(pos, share, keep, got, result),)
    return result[0]


def from_behind(value, axis, by):
    peers = lax.axis_size(axis)
    pairs = [(i, i + by) for i in range(peers) if 0 <= i + by < peers]
    return lax.ppermute(value, axis, pairs)


def general(tokens, w_query, w_key, w_value, w_out):
    tok_rows = tokens.shape[0]
    head_width = w_query.shape[1]
    head_count = head_width // DH
    score_scale = DH ** (-0.5)
    shard_piece = lax.all_gather(tokens, "head", axis=1, tiled=True)
    query_full, key_full, value_full = tuple(
        (
            jnp.dot(shard_piece, weight, preferred_element_type=jnp.float32)
            for weight in (w_query, w_key, w_value)
        )
    )
    query = query_full.astype(jnp.bfloat16).reshape(tok_rows, head_count, DH)
    key_heads = key_full.astype(jnp.bfloat16).reshape(tok_rows, head_count, DH)
    value_heads = value_full.astype(jnp.bfloat16).reshape(tok_rows, head_count, DH)
    prev_keys, prev_values = from_behind((key_heads[-STRIDE:], value_heads[-STRIDE:]), "seq", 1)
    blocks = tok_rows // STRIDE
    extended_keys = jnp.concatenate([prev_keys, key_heads], 0)
    extended_values = jnp.concatenate([prev_values, value_heads], 0)
    window_keys = jnp.concatenate(
        [
            extended_keys[:tok_rows].reshape(blocks, STRIDE, head_count, DH),
            extended_keys[STRIDE:].reshape(blocks, STRIDE, head_count, DH),
        ],
        1,
    )
    window_values = jnp.concatenate(
        [
            extended_values[:tok_rows].reshape(blocks, STRIDE, head_count, DH),
            extended_values[STRIDE:].reshape(blocks, STRIDE, head_count, DH),
        ],
        1,
    )
    query_blocks = query.reshape(blocks, STRIDE, head_count, DH)
    scores = (
        jnp.einsum("bthd,buhd->bhtu", query_blocks, window_keys, preferred_element_type=jnp.float32)
        * score_scale
    )
    first_position = lax.axis_index("seq") * tok_rows
    block_index = jnp.arange(blocks)[:, None, None, None]
    query_index = jnp.arange(STRIDE)[None, None, :, None]
    key_index = jnp.arange(2 * STRIDE)[None, None, None, :]
    allowed = (
        (key_index > query_index)
        & (key_index <= query_index + STRIDE)
        & (first_position + block_index * STRIDE + key_index - STRIDE >= 0)
    )
    local_top = jnp.max(jnp.where(allowed, scores, -1e30), axis=-1)
    local_weights = jnp.where(allowed, jnp.exp(scores - local_top[..., None]), 0.0)
    local_total = jnp.sum(local_weights, axis=-1)
    local_out = jnp.einsum(
        "bhtu,buhd->bthd",
        local_weights.astype(jnp.bfloat16),
        window_values,
        preferred_element_type=jnp.float32,
    )
    local_out = local_out.reshape(tok_rows, head_count, DH)
    local_top = local_top.transpose(0, 2, 1).reshape(tok_rows, head_count)
    local_total = local_total.transpose(0, 2, 1).reshape(tok_rows, head_count)
    row_count = tok_rows // STRIDE
    query_class = lax.all_to_all(
        query.reshape(row_count, STRIDE, head_count, DH),
        "seq",
        split_axis=1,
        concat_axis=0,
        tiled=True,
    )
    key_class = lax.all_to_all(
        key_heads.reshape(row_count, STRIDE, head_count, DH),
        "seq",
        split_axis=1,
        concat_axis=0,
        tiled=True,
    )
    value_class = lax.all_to_all(
        value_heads.reshape(row_count, STRIDE, head_count, DH),
        "seq",
        split_axis=1,
        concat_axis=0,
        tiled=True,
    )
    row_total = query_class.shape[0]
    class_scores = (
        jnp.einsum("rchd,schd->chrs", query_class, key_class, preferred_element_type=jnp.float32)
        * score_scale
    )
    earlier = (
        jnp.arange(row_total)[None, None, :, None] > jnp.arange(row_total)[None, None, None, :]
    )
    class_top = jnp.max(jnp.where(earlier, class_scores, -1e30), axis=-1)
    class_weights = jnp.where(earlier, jnp.exp(class_scores - class_top[..., None]), 0.0)
    class_total = jnp.sum(class_weights, axis=-1)
    summed = jnp.einsum(
        "chrs,schd->rchd",
        class_weights.astype(jnp.bfloat16),
        value_class,
        preferred_element_type=jnp.float32,
    )
    floor_total = jnp.maximum(class_total, 1.0).transpose(2, 0, 1)
    class_out = (summed / floor_total[..., None]).astype(jnp.bfloat16)
    class_top_rows = class_top.transpose(2, 0, 1)
    class_total_rows = class_total.transpose(2, 0, 1)
    column_out = class_out
    column_top = class_top_rows
    column_total = class_total_rows
    column_out, column_top, column_total = (
        lax.all_to_all(column_out, "seq", split_axis=0, concat_axis=1, tiled=True),
        lax.all_to_all(
            column_top.astype(jnp.bfloat16), "seq", split_axis=0, concat_axis=1, tiled=True
        ).astype(column_top.dtype),
        lax.all_to_all(
            column_total.astype(jnp.bfloat16), "seq", split_axis=0, concat_axis=1, tiled=True
        ).astype(column_total.dtype),
    )
    column_out = column_out.reshape(tok_rows, head_count, DH)
    column_top = column_top.reshape(tok_rows, head_count)
    column_total = column_total.reshape(tok_rows, head_count)
    top_score = jnp.maximum(local_top, column_top)
    local_weight = jnp.exp(local_top - top_score)
    column_weight = column_total * jnp.exp(column_top - top_score)
    denominator = local_total * local_weight + column_weight
    mixed = (
        local_out * local_weight[..., None]
        + column_out.astype(jnp.float32) * column_weight[..., None]
    ) / denominator[..., None]
    mixed = mixed.astype(jnp.bfloat16).reshape(tok_rows, head_width)
    return lax.psum_scatter(
        jnp.dot(mixed, w_out, preferred_element_type=jnp.float32).astype(jnp.bfloat16),
        "head",
        scatter_dimension=0,
        tiled=True,
    )


def shards(tokens, w_query, w_key, w_value, w_out):
    rows, width = w_query.shape
    fits = (
        lax.axis_size("seq") == PEERS
        and lax.axis_size("head") == 4
        and tokens.shape == (ROWS * STRIDE, HEADS * DH)
        and (rows, width) == (4 * HEADS * DH, HEADS * DH)
    )
    plan = chunked if fits else general
    return plan(tokens, w_query, w_key, w_value, w_out)


def solution(mesh):
    in_specs = (
        P("seq", "head"),
        P(None, "head"),
        P(None, "head"),
        P(None, "head"),
        P("head", None),
    )
    out_specs = P(("seq", "head"), None)
    return jax.shard_map(shards, mesh=mesh, in_specs=in_specs, out_specs=out_specs, check_vma=False)
```
